32 devices in a mesh: sub: 16 (over z, y, x), crow: 2 (over core), ccol: 1.
Axes of the slice: x: 2, y: 2, z: 4, core: 2. Of those that a mesh axis runs over, the one named last changes fastest.
Arguments:
- loads: bfloat16 [32, 1024, 128], P('sub'), may hold values from -6 to 6
- stiffness: bfloat16 [32, 1024, 1024], P('sub', ('crow', 'ccol'))
- local_inverse: bfloat16 [32, 1024, 1024], P('sub', ('crow', 'ccol'))
- coarse_basis: bfloat16 [32, 1024, 48], P('sub', ('crow', 'ccol')), may hold values from -0.1875 to 0.1875
- coarse_inverse: bfloat16 [1536, 1536], P('sub', ('crow', 'ccol'))
- coarse_index: int32 [32, 48], P('sub'), may hold values from 0 to 1535, as said below
- left_rows: int32 [32, 128], P('sub'), may hold values from 0 to 1023, as said below
- right_rows: int32 [32, 128], P('sub'), may hold values from 0 to 1023, as said below
Outputs:
- second_pass: float32 [32, 1024, 128], P('sub', ('crow', 'ccol'))
- final_residual: float32 [32, 1024, 128], P('sub', ('crow', 'ccol'))
The draws below stay inside these ranges and needn't reach their ends.
Inputs may be any that keep to these rules, and one draw needn't show every extreme that they name: `coarse_index`: every value 0 to 1535 appears exactly once in the whole array. Of the 96 values in the rows of one index of sub, at most 96 lie in one block of 768 consecutive coarse rows starting at a multiple of 768, and that most is reached. In each subdomain the 128 entries of left_rows and the 128 entries of right_rows are 256 distinct rows. `right_rows`: see left_rows.
All inputs are finite; a program needn't handle non-finite values.
Results may differ from the reference program's by a relative error of at most 0.0067.
Values may be sent and summed in bfloat16 or wider, within the bound.
No kernel may reach another device: no remote copies, remote signals or barrier semaphores. Data moves between devices by JAX's collectives and lax.ppermute only.
A program may use at most 64 MiB of HBM per device.

```python
import math
import jax
import jax.numpy as jnp
from jax import lax

IFACE = 1024
FACE = 128
MODES = 48
SUB_DEV = 2
CASES = 128
NSUB = 32
NC = 1536
N_SUB = 16
N_CROW = 2
N_CCOL = 1


def dominant_matrices(key, count, order, low, high, spread):
    key_off, key_diag = jax.random.split(jax.random.fold_in(key, 11))
    off_diag = jax.random.normal(key_off, (count, order, order), jnp.float32) * (spread / math.sqrt(order))
    diagonal = jax.random.uniform(key_diag, (count, order), jnp.float32, low, high)
    return off_diag + diagonal[:, :, None] * jnp.eye(order, dtype=jnp.float32)[None, :, :]


def draw_stiffness(key, part):
    return dominant_matrices(jax.random.fold_in(key, 1), NSUB, IFACE, 1.0, 3.0, 0.5).astype(jnp.bfloat16)


def draw_local_inverse(key, part):
    return dominant_matrices(jax.random.fold_in(key, 2), NSUB, IFACE, 0.3, 1.0, 0.25).astype(jnp.bfloat16)


def draw_coarse_inverse(key, part):
    return dominant_matrices(jax.random.fold_in(key, 3), 1, NC, 1.0, 3.0, 0.5)[0].astype(jnp.bfloat16)


def draw_coarse_index(key, part):
    block_count = N_CROW * N_CCOL
    per_sub = MODES * SUB_DEV
    mean_count = per_sub // block_count
    block_width = NC // block_count
    split_keys = jax.random.split(jax.random.fold_in(key, 4), 3)
    pair_count = N_SUB // 2

    def choose_blocks(one_key):
        return jax.random.permutation(one_key, block_count)[:2]
    chosen = jax.vmap(choose_blocks)(jax.random.split(split_keys[0], pair_count))
    labels = jnp.arange(block_count, dtype=jnp.int32)[None, :]
    swing = (labels == chosen[:, 0:1]).astype(jnp.int32) - (labels == chosen[:, 1:2]).astype(jnp.int32)
    counts = mean_count + mean_count * jnp.stack([swing, -swing], axis=1).reshape(N_SUB, block_count)
    offsets = jnp.cumsum(counts, axis=0) - counts
    block_ends = jnp.cumsum(counts, axis=1)

    def shuffle_block(one_key):
        return jax.random.permutation(one_key, block_width)
    positions_perm = jax.vmap(shuffle_block)(jax.random.split(split_keys[1], block_count))
    slot_index = jnp.arange(per_sub, dtype=jnp.int32)
    block_of = jnp.sum((slot_index[None, :, None] >= block_ends[:, None, :]).astype(jnp.int32), axis=2)
    block_starts = jnp.take_along_axis(block_ends - counts, block_of, axis=1)
    within = slot_index[None, :] - block_starts
    position = jnp.take_along_axis(offsets, block_of, axis=1) + within
    values = block_of * block_width + positions_perm[block_of, position]

    def shuffle_rows(one_key):
        return jax.random.permutation(one_key, per_sub)
    shuffle_order = jax.vmap(shuffle_rows)(jax.random.split(split_keys[2], N_SUB))
    shuffled = jnp.take_along_axis(values, shuffle_order, axis=1)
    return shuffled.reshape(N_SUB * SUB_DEV, MODES).astype(jnp.int32)


def face_rows(key):
    face_key = jax.random.fold_in(key, 7)

    def shuffle_face(one_key):
        return jax.random.permutation(one_key, IFACE)
    orders = jax.vmap(shuffle_face)(jax.random.split(face_key, NSUB))
    return (orders[:, :FACE].astype(jnp.int32), orders[:, FACE:2 * FACE].astype(jnp.int32))


def draw_left_rows(key, part):
    return face_rows(key)[0]


def draw_right_rows(key, part):
    return face_rows(key)[1]


def levels(rng, dims, shards, smallest, largest):
    def one(axis_at, blocks):
        draws = jax.random.uniform(jax.random.fold_in(jax.random.fold_in(rng, 6), axis_at), (blocks,), jnp.float32, smallest / len(shards), largest / len(shards))
        return jnp.repeat(jnp.exp(draws), dims[axis_at] // blocks).reshape((-1,) + (1,) * (len(dims) - axis_at - 1))

    level = one(*shards[0])
    for cut in shards[1:]:
        level = level * one(*cut)
    return level


def noise(rng, dims, scale, most, cuts=(), kind=jnp.bfloat16):
    entries = jax.random.normal(rng, dims, jnp.float32) * scale
    if len(cuts) > 0:
        entries = levels(rng, dims, cuts, -0.22, 0.18) * entries
    return jnp.clip(entries, min=-most, max=most).astype(kind)


def setup_inputs(seed: int = 0) -> dict:
    keys = jax.random.split(jax.random.key(seed), 9)
    loads = noise(keys[0], (NSUB, IFACE, CASES), 1.0, 6.0, ((0, 16),))
    stiffness = draw_stiffness(jax.random.fold_in(keys[8], 71), 0)
    local_inverse = draw_local_inverse(jax.random.fold_in(keys[8], 71), 0)
    coarse_basis = noise(keys[3], (NSUB, IFACE, MODES), IFACE ** -0.5, 0.1875, ((0, 16), (1, 2)))
    coarse_inverse = draw_coarse_inverse(jax.random.fold_in(keys[8], 71), 0)
    coarse_index = draw_coarse_index(jax.random.fold_in(keys[8], 71), 0)
    left_rows = draw_left_rows(jax.random.fold_in(keys[8], 71), 0)
    right_rows = draw_right_rows(jax.random.fold_in(keys[8], 71), 0)
    return {"loads": loads, "stiffness": stiffness, "local_inverse": local_inverse, "coarse_basis": coarse_basis, "coarse_inverse": coarse_inverse, "coarse_index": coarse_index, "left_rows": left_rows, "right_rows": right_rows}


def batched_dot(left_side, right_side):
    def single(operands):
        return jnp.dot(operands[0], operands[1], preferred_element_type=jnp.float32)
    return lax.map(single, (left_side, right_side))


def apply_stiffness(stiffness, iterate, left_rows, right_rows):
    product = batched_dot(stiffness, iterate.astype(jnp.bfloat16))
    rounded = lax.optimization_barrier(product.astype(jnp.bfloat16)).astype(jnp.float32)
    sub_rows = jnp.arange(NSUB, dtype=jnp.int32)[:, None]
    right_values = rounded[sub_rows, right_rows]
    left_values = rounded[sub_rows, left_rows]
    from_before = jnp.roll(right_values, 1, axis=0)
    from_after = jnp.roll(left_values, -1, axis=0)
    assembled = rounded.at[sub_rows, left_rows].add(from_before)
    return assembled.at[sub_rows, right_rows].add(from_after)


def precondition(residual, local_inverse, coarse_basis, coarse_inverse, coarse_index):
    local_part = batched_dot(local_inverse, residual)
    basis_turned = jnp.swapaxes(coarse_basis, 1, 2)
    restricted = batched_dot(basis_turned, residual).astype(jnp.bfloat16)
    flat_index = coarse_index.reshape(-1).astype(jnp.int32)
    ordered = jnp.zeros((NC, CASES), jnp.bfloat16).at[flat_index].set(restricted.reshape(NC, CASES))
    coarse = jnp.dot(coarse_inverse, ordered, preferred_element_type=jnp.float32).astype(jnp.bfloat16)
    picked = coarse[flat_index].reshape(NSUB, MODES, CASES)
    return local_part + batched_dot(coarse_basis, picked)


def reference(loads, stiffness, local_inverse, coarse_basis, coarse_inverse, coarse_index, left_rows, right_rows):
    first_pass = precondition(loads, local_inverse, coarse_basis, coarse_inverse, coarse_index)
    residual = loads.astype(jnp.float32) - apply_stiffness(stiffness, first_pass, left_rows, right_rows)
    second_pass = first_pass + precondition(residual.astype(jnp.bfloat16), local_inverse, coarse_basis, coarse_inverse, coarse_index)
    final_residual = loads.astype(jnp.float32) - apply_stiffness(stiffness, second_pass, left_rows, right_rows)
    return second_pass, final_residual
```

```python
import jax
import jax.numpy as jnp
from jax import lax
from jax.sharding import PartitionSpec as P


def padded(block, sides, width):
    for axis, dim in sides:
        count = lax.axis_size(axis)
        forward = [(i, i + 1) for i in range(count - 1)]
        forward.append((count - 1, 0))
        backward = [(target, source) for source, target in forward]
        low = lax.ppermute(
            lax.slice_in_dim(block, block.shape[dim] - width, None, axis=dim), axis, forward
        )
        high = lax.ppermute(lax.slice_in_dim(block, 0, width, axis=dim), axis, backward)
        block = jnp.concatenate([low, block, high], axis=dim)
    return block


def stages(count):
    widths = []
    stride = 1
    while count > 1:
        factor = 2 if count % 2 == 0 else count
        widths.append((stride, factor))
        stride *= factor
        count //= factor
    return widths


def gather_staged(block, axis):
    count = lax.axis_size(axis)
    out = block[None]
    for stride, factor in stages(count):
        groups = [
            [base + stride * k for k in range(factor)]
            for base in range(count)
            if (base // stride) % factor == 0
        ]
        out = lax.all_gather(out, axis, axis=0, tiled=True, axis_index_groups=groups)
    return out.reshape((count * block.shape[0],) + block.shape[1:])


def gather_direct(block, axis):
    count = lax.axis_size(axis)
    copies = jnp.broadcast_to(block[None], (count,) + block.shape)
    out = lax.all_to_all(copies, axis, 0, 0)
    return out.reshape((count * block.shape[0],) + block.shape[1:])


def fold_product(matrix, gathered_piece):
    return jnp.einsum("sij,sjc->sic", matrix, gathered_piece, preferred_element_type=jnp.float32)


def apply_stiffness(iterate, stiffness, left_rows, right_rows, pick_left, pick_right):
    sub_count, row_count, case_count = iterate.shape
    rounded = iterate.astype(jnp.bfloat16)
    product = fold_product(stiffness, lax.all_gather(rounded, ("crow", "ccol"), axis=1, tiled=True))
    product_b = product.astype(jnp.bfloat16)
    whole_rows = lax.all_gather(product_b, ("crow", "ccol"), axis=1, tiled=True)
    sub_rows = jnp.arange(sub_count, dtype=jnp.int32)[:, None]
    boundary = jnp.stack(
        [whole_rows[sub_rows, left_rows], whole_rows[sub_rows, right_rows]], axis=1
    )
    extended = padded(boundary, (("sub", 0),), 1)
    from_before = extended[:sub_count, 1]
    from_after = extended[2:, 0]
    added_left = jnp.einsum(
        "sfi,sfc->sic", pick_left, from_before, preferred_element_type=jnp.float32
    )
    added_right = jnp.einsum(
        "sfi,sfc->sic", pick_right, from_after, preferred_element_type=jnp.float32
    )
    return product_b.astype(jnp.float32) + added_left + added_right


def coarse_step(restricted, coarse_inverse, coarse_index, spread):
    sub_count, mode_count, case_count = restricted.shape
    flat_rows = restricted.reshape(sub_count * mode_count, case_count)
    flat_index = coarse_index.reshape(-1)
    owned_rows, block_width = coarse_inverse.shape
    block_index = lax.axis_index(("crow", "ccol"))
    arrived, arrived_index = (
        spread(flat_rows, "sub"),
        lax.all_gather(flat_index, "sub", axis=0, tiled=True),
    )
    shifted_place = arrived_index - block_index * block_width
    inside = (shifted_place >= 0) & (shifted_place < block_width)
    arrived_place = jnp.where(inside, shifted_place, block_width)
    ordered = (
        jnp.zeros((block_width + 1, case_count), jnp.bfloat16)
        .at[arrived_place]
        .set(arrived)[:block_width]
    )
    partial_coarse = jnp.dot(coarse_inverse, ordered, preferred_element_type=jnp.float32)
    coarse = lax.psum(partial_coarse, ("crow", "ccol")).astype(jnp.bfloat16)
    everything = spread(coarse, "sub")
    picked = everything[flat_index]
    return picked.reshape(sub_count, mode_count, case_count)


def precondition(local_part, residual_rows, coarse_basis, coarse_inverse, coarse_index, spread):
    partial_modes = jnp.einsum(
        "sik,sic->skc", coarse_basis, residual_rows, preferred_element_type=jnp.float32
    )
    restricted = lax.psum(partial_modes, ("crow", "ccol")).astype(jnp.bfloat16)
    picked = coarse_step(restricted, coarse_inverse, coarse_index, spread)
    return local_part + jnp.einsum(
        "sik,skc->sic", coarse_basis, picked, preferred_element_type=jnp.float32
    )


def body(
    loads,
    stiffness,
    local_inverse,
    coarse_basis,
    coarse_inverse,
    coarse_index,
    left_rows,
    right_rows,
):
    sub_count, row_count, iface_count = stiffness.shape
    group_index = lax.axis_index(("crow", "ccol"))
    first_row = group_index * row_count
    loads_rows = lax.dynamic_slice_in_dim(loads, first_row, row_count, 1)
    local_rows = first_row + jnp.arange(row_count, dtype=jnp.int32)
    pick_left = (left_rows[:, :, None] == local_rows[None, None, :]).astype(jnp.bfloat16)
    pick_right = (right_rows[:, :, None] == local_rows[None, None, :]).astype(jnp.bfloat16)
    first_local = jnp.einsum(
        "sij,sjc->sic", local_inverse, loads, preferred_element_type=jnp.float32
    )
    first_pass = precondition(
        first_local, loads_rows, coarse_basis, coarse_inverse, coarse_index, gather_staged
    )
    image_first = apply_stiffness(
        first_pass, stiffness, left_rows, right_rows, pick_left, pick_right
    )
    residual_b = (loads_rows.astype(jnp.float32) - image_first).astype(jnp.bfloat16)
    second_local = fold_product(
        local_inverse, lax.all_gather(residual_b, ("crow", "ccol"), axis=1, tiled=True)
    )
    second_pass = first_pass + precondition(
        second_local, residual_b, coarse_basis, coarse_inverse, coarse_index, gather_direct
    )
    image_second = apply_stiffness(
        second_pass, stiffness, left_rows, right_rows, pick_left, pick_right
    )
    final_residual = loads_rows.astype(jnp.float32) - image_second
    return (second_pass, final_residual)


def solution(mesh):
    return jax.shard_map(
        body,
        mesh=mesh,
        in_specs=(
            P("sub", None, None),
            P("sub", ("crow", "ccol"), None),
            P("sub", ("crow", "ccol"), None),
            P("sub", ("crow", "ccol"), None),
            P("sub", ("crow", "ccol")),
            P("sub", None),
            P("sub", None),
            P("sub", None),
        ),
        out_specs=(P("sub", ("crow", "ccol"), None), P("sub", ("crow", "ccol"), None)),
        check_vma=False,
    )
```

```python
import functools

import jax
import jax.numpy as jnp
import numpy as np
from jax import lax
from jax.experimental import pallas as pl
from jax.experimental.pallas import tpu as pltpu
from jax.sharding import PartitionSpec as P

GROUP = ("crow", "ccol")
F32 = jnp.float32
BF16 = jnp.bfloat16
VMEM_BYTES = 48 * 1024 * 1024
DIGIT_ROWS = 16
DIGIT = 256


def dot(a, b):
    return lax.dot_general(a, b, (((1,), (0,)), ((), ())), preferred_element_type=F32)


def dot_tn(a, b):
    return lax.dot_general(a, b, (((0,), (0,)), ((), ())), preferred_element_type=F32)


def dot_nt(a, b):
    return lax.dot_general(a, b, (((1,), (1,)), ((), ())), preferred_element_type=F32)


class Sizes:
    def __init__(self, loads, stiffness, coarse_basis, coarse_inverse, left_rows):
        self.n = lax.axis_size("sub")
        self.group = lax.axis_size(GROUP)
        self.subs, self.rows, self.cases = loads.shape
        self.own = stiffness.shape[1]
        self.modes = coarse_basis.shape[2]
        self.owned, self.block = coarse_inverse.shape
        self.total = self.block * self.group
        self.face = left_rows.shape[1]
        self.width = self.cases // self.group
        self.lanes = max(self.cases, -(-self.subs * self.width // 128) * 128)
        self.columns = self.n * self.modes


def lane_mask(z, block, shape):
    lane = lax.broadcasted_iota(jnp.int32, shape, len(shape) - 1)
    return (lane >= block * z.width) & (lane < (block + 1) * z.width)


def select(z, parts):
    out = jnp.zeros_like(parts[0])
    for s, part in enumerate(parts):
        out = jnp.where(lane_mask(z, s, part.shape), part, out)
    return out


def fold(z, packed):
    if z.lanes == z.subs * z.width:
        out = packed
        for k in range(1, z.subs):
            out = out + pltpu.roll(packed, k * z.width, 1)
        return out
    out = packed
    for k in range(1, z.subs):
        out = out + pltpu.roll(packed, k * z.width, 1)
        out = out + pltpu.roll(packed, z.lanes - k * z.width, 1)
    return out


def shift_matrix(z, source, target):
    row = lax.broadcasted_iota(jnp.int32, (z.lanes, z.lanes), 0)
    lane = lax.broadcasted_iota(jnp.int32, (z.lanes, z.lanes), 1)
    hit = (row - source * z.width == lane - target * z.width) & lane_mask(z, target, (z.lanes, z.lanes))
    return jnp.where(hit, 1.0, 0.0).astype(BF16)


def place_matrix(z, block):
    row = lax.broadcasted_iota(jnp.int32, (z.modes, 3 * z.modes), 0)
    lane = lax.broadcasted_iota(jnp.int32, (z.modes, 3 * z.modes), 1)
    return jnp.where(row + block * z.modes == lane, 1.0, 0.0).astype(BF16)


def piece_start(z, k, size):
    place = lax.rem(lax.axis_index(GROUP) + k, z.group)
    return pl.multiple_of(place * size, size)


def scatter_matrix(z, rows_of):
    row = lax.broadcasted_iota(jnp.int32, (z.rows, z.face), 0)
    return jnp.where(row == rows_of, 1.0, 0.0).astype(BF16)


def open_kernel(z, *refs):
    pieces = refs[: z.group]
    loads, digits, load_rows, basis_t, message = refs[z.group :]
    group = lax.axis_index(GROUP)
    for k, piece in enumerate(pieces):
        basis_t[:, :, pl.ds(piece_start(z, k, z.own), z.own)] = piece[...]
    row = lax.broadcasted_iota(jnp.int32, (z.cases, z.lanes), 0)
    lane = lax.broadcasted_iota(jnp.int32, (z.cases, z.lanes), 1)
    packed = jnp.zeros((z.rows, z.lanes), F32)
    for s in range(z.subs):
        hit = (row - group * z.width == lane - s * z.width) & lane_mask(z, s, row.shape)
        packed = packed + dot(loads[s], jnp.where(hit, 1.0, 0.0).astype(BF16))
    packed = packed.astype(BF16)
    load_rows[...] = packed
    modes = select(z, [dot(basis_t[s], packed) for s in range(z.subs)]).astype(BF16)
    for k in range(z.n):
        message[k, : z.modes, :] = modes
        message[k, z.modes :, :] = digits[...]


def multiply(z, pieces, vector, store):
    for k, piece in enumerate(pieces):
        parts = [dot(piece[s], vector) for s in range(z.subs)]
        store(piece_start(z, k, z.own), select(z, parts))


def face_picks(z, image, rows_ref, s):
    return dot_tn(scatter_matrix(z, rows_ref[s : s + 1, :]), image).astype(BF16)


def image_kernel(z, first, *refs):
    inverse, stiffness = refs[: z.group], refs[z.group : 2 * z.group]
    rest = refs[2 * z.group :]
    if first:
        vector, basis_t, left_rows, right_rows = rest[:4]
        solved, image, to_before, to_after, basis, image_basis = rest[4:10]
        rounded = rest[10]
    else:
        vector, base, left_rows, right_rows = rest[:4]
        solved, image, to_before, to_after = rest[4:8]
        rounded = rest[8]
    operand = vector[...]

    def store_solved(start, value):
        if not first:
            value = value + base[pl.ds(start, z.own), :]
        solved[pl.ds(start, z.own), :] = value
        rounded[pl.ds(start, z.own), :] = value.astype(BF16)

    multiply(z, inverse, operand, store_solved)

    def store_image(start, value):
        image[pl.ds(start, z.own), :] = value

    multiply(z, stiffness, rounded[...], store_image)
    if first:
        for s in range(z.subs):
            basis[s] = jnp.transpose(basis_t[s].astype(F32)).astype(BF16)
            for k, piece in enumerate(stiffness):
                start = piece_start(z, k, z.own)
                image_basis[s, pl.ds(start, z.own), :] = dot(piece[s], basis[s]).astype(BF16)
    image_b = image[...].astype(BF16)
    for s in range(z.subs):
        for rows_ref, out, target in (
            (left_rows, to_before, (s - 1) % z.subs),
            (right_rows, to_after, (s + 1) % z.subs),
        ):
            picked = face_picks(z, image_b, rows_ref, s)
            out[s, :, : z.lanes] = dot(picked, shift_matrix(z, s, target)).astype(BF16)
            if first:
                out[s, :, z.lanes : z.lanes + z.modes] = face_picks(z, image_basis[s], rows_ref, s)


def join_kernel(z, first, *refs):
    load_rows, image, to_before, to_after, from_before, from_after, left_rows, right_rows = refs[:8]
    if first:
        image_basis, residual, joined = refs[8:]
    else:
        (residual,) = refs[8:]
    added = []
    for s in range(z.subs):
        before = from_before[...] if s == 0 else to_after[s - 1]
        after = from_after[...] if s == z.subs - 1 else to_before[s + 1]
        left = scatter_matrix(z, left_rows[s : s + 1, :])
        right = scatter_matrix(z, right_rows[s : s + 1, :])
        added.append(dot(left, before[:, : z.lanes]) + dot(right, after[:, : z.lanes]))
        if first:
            cut = slice(z.lanes, z.lanes + z.modes)
            total = dot(left, dot(before[:, cut], place_matrix(z, 0)).astype(BF16))
            total = total + dot(image_basis[s], place_matrix(z, 1))
            total = total + dot(right, dot(after[:, cut], place_matrix(z, 2)).astype(BF16))
            joined[s] = total.astype(BF16)
    residual[...] = load_rows[...].astype(F32) - image[...] - select(z, added)


def coarse_rows(z, ordered_inverse, arrived):
    parts = [dot(ordered_inverse[s], arrived) for s in range(z.subs)]
    rows = fold(z, select(z, parts))
    return select(z, [rows[s * z.modes : (s + 1) * z.modes, :] for s in range(z.subs)]).astype(BF16)


def order_kernel(z, *refs):
    pieces = refs[: z.group]
    arrived, repeat, own_row, ordered_inverse, index, message, whole = refs[z.group :]
    for k, piece in enumerate(pieces):
        whole[:, pl.ds(piece_start(z, k, z.block), z.block)] = piece[...]
    digits = arrived[:, z.modes :, :].astype(F32)
    for s in range(z.subs):
        high = jnp.sum(jnp.where(digit_row(digits.shape, 2 * s), digits, 0.0), axis=1)
        low = jnp.sum(jnp.where(digit_row(digits.shape, 2 * s + 1), digits, 0.0), axis=1)
        index[s] = high * DIGIT + low
        spread = dot(high.astype(BF16), repeat[...]) * DIGIT + dot(low.astype(BF16), repeat[...])
        places = jnp.sum(spread * own_row[...], axis=0, keepdims=True).astype(jnp.int32)
        for at in range(0, z.columns, 768):
            wide = min(768, z.columns - at)
            total = jnp.zeros((z.owned, wide), F32)
            for first in range(0, z.total, 256):
                deep = min(256, z.total - first)
                row = lax.broadcasted_iota(jnp.int32, (deep, wide), 0) + first
                hot = jnp.where(row == places[:, at : at + wide], 1.0, 0.0).astype(BF16)
                total = total + dot(whole[:, first : first + deep], hot)
            ordered_inverse[s, :, at : at + wide] = total.astype(BF16)
    rows = arrived[:, : z.modes, :].reshape(z.columns, z.lanes)
    packed = coarse_rows(z, ordered_inverse, rows)
    for k in range(z.n):
        message[k] = packed


def digit_row(shape, row):
    return lax.broadcasted_iota(jnp.int32, shape, 1) == row


def pick_kernel(z, index, place, picks):
    here = lax.axis_index("sub")
    device = lax.broadcasted_iota(jnp.int32, (z.n, z.lanes), 0)
    for t in range(z.subs + 2):
        if t == 0:
            s, owner = z.subs - 1, lax.rem(here + z.n - 1, z.n)
        elif t == z.subs + 1:
            s, owner = 0, lax.rem(here + 1, z.n)
        else:
            s, owner = t - 1, here
        row = jnp.sum(jnp.where(device == owner, index[s], 0.0), axis=0, keepdims=True)
        column = jnp.transpose(jnp.broadcast_to(row, (z.lanes, z.lanes)))[: z.modes, 0:1]
        column = column.astype(jnp.int32)
        for h in range(z.subs):
            hit = column == place[h : h + 1, :]
            picks[h, t * z.modes : (t + 1) * z.modes, :] = jnp.where(hit, 1.0, 0.0).astype(BF16)


def picked_rows(z, arrived, picks):
    flat = arrived[...].reshape(z.columns, z.lanes)
    return fold(z, select(z, [dot(picks[h], flat) for h in range(z.subs)])).astype(BF16)


def update_kernel(z, arrived, picks, solved, residual, basis, joined, basis_t, first_pass, rounded, message):
    chosen = picked_rows(z, arrived, picks)
    m = z.modes
    first_pass[...] = solved[...] + select(
        z, [dot(basis[s], chosen[(s + 1) * m : (s + 2) * m]) for s in range(z.subs)]
    )
    left = residual[...] - select(z, [dot(joined[s], chosen[s * m : (s + 3) * m]) for s in range(z.subs)])
    left = left.astype(BF16)
    rounded[...] = left
    modes = select(z, [dot(basis_t[s], left) for s in range(z.subs)]).astype(BF16)
    for k in range(z.n):
        message[k] = modes


def coarse_kernel(z, arrived, ordered_inverse, message):
    packed = coarse_rows(z, ordered_inverse, arrived[...].reshape(z.columns, z.lanes))
    for k in range(z.n):
        message[k] = packed


def last_kernel(z, arrived, picks, solved, residual, basis, joined, out):
    chosen = picked_rows(z, arrived, picks)
    m = z.modes
    second = solved[...] + select(
        z, [dot(basis[s], chosen[(s + 1) * m : (s + 2) * m]) for s in range(z.subs)]
    )
    left = residual[...] - select(z, [dot(joined[s], chosen[s * m : (s + 3) * m]) for s in range(z.subs)])
    for k in range(z.group):
        out[k, 0] = second[k * z.own : (k + 1) * z.own, :]
        out[k, 1] = left[k * z.own : (k + 1) * z.own, :]


def unpack_kernel(z, arrived, second_pass, final_residual):
    for at, out in enumerate((second_pass, final_residual)):
        for s in range(z.subs):
            total = jnp.zeros((z.own, z.lanes), F32)
            for k in range(z.group):
                turned = arrived[k, at]
                turn = ((k - s) * z.width) % z.lanes
                if turn:
                    turned = pltpu.roll(turned, turn, 1)
                total = jnp.where(lane_mask(z, k, turned.shape), turned, total)
            out[s] = total[:, : z.cases]


def call(kernel, outs, operands, flops, scratch=(), name=None):
    vmem = pl.BlockSpec(memory_space=pltpu.VMEM)
    moved = sum(int(np.prod(x.shape)) * x.dtype.itemsize for x in (*operands, *outs))
    return pl.pallas_call(
        kernel,
        out_shape=[jax.ShapeDtypeStruct(o.shape, o.dtype) for o in outs],
        in_specs=[vmem] * len(operands),
        out_specs=[vmem] * len(outs),
        scratch_shapes=list(scratch),
        compiler_params=pltpu.CompilerParams(vmem_limit_bytes=VMEM_BYTES),
        cost_estimate=pl.CostEstimate(flops=flops, bytes_accessed=moved, transcendentals=0),
        name=name,
    )(*operands)


def shape(dims, dtype):
    return jax.ShapeDtypeStruct(dims, dtype)


def pieces_of(block, group):
    out = [block]
    for k in range(1, group):
        out.append(lax.ppermute(block, GROUP, [((g + k) % group, g) for g in range(group)]))
    return out


def body(loads, stiffness, local_inverse, coarse_basis, coarse_inverse, coarse_index, left_rows, right_rows):
    z = Sizes(loads, stiffness, coarse_basis, coarse_inverse, left_rows)
    n, group, subs, rows, lanes, modes = z.n, z.group, z.subs, z.rows, z.lanes, z.modes
    own_t = jnp.swapaxes(coarse_basis, 1, 2)
    basis_pieces = pieces_of(own_t, group)
    high, low = coarse_index // DIGIT, coarse_index % DIGIT
    digits = jnp.stack([high, low], axis=1).reshape(2 * subs, modes).astype(BF16)
    digits = jnp.pad(digits, ((0, DIGIT_ROWS - 2 * subs), (0, lanes - modes)))
    column = np.arange(z.columns)
    repeat = jnp.asarray(np.arange(lanes)[:, None] == column[None, :] % modes, BF16)
    own_row = jnp.asarray(np.arange(n)[:, None] == column[None, :] // modes, F32)
    place = jnp.asarray(
        (column // modes * z.owned + column % modes)[None, :] + np.arange(subs)[:, None] * modes, jnp.int32
    )
    packed_f = shape((rows, lanes), F32)
    packed_b = shape((rows, lanes), BF16)
    copies = shape((n, modes, lanes), BF16)
    spread = functools.partial(lax.all_to_all, axis_name="sub", split_axis=0, concat_axis=0)

    load_rows, basis_t, message = call(
        functools.partial(open_kernel, z),
        [packed_b, shape((subs, modes, rows), BF16), shape((n, modes + DIGIT_ROWS, lanes), BF16)],
        [*basis_pieces, loads, digits],
        4 * rows * lanes * lanes,
        name="open",
    )
    restricted = spread(message)

    inverse_pieces = pieces_of(local_inverse, group)
    stiffness_pieces = pieces_of(stiffness, group)
    inverse_columns = pieces_of(coarse_inverse, group)
    work = 4 * subs * rows * rows * lanes
    faces = shape((subs, z.face, 2 * lanes), BF16)
    solved, image, to_before, to_after, basis, image_basis = call(
        functools.partial(image_kernel, z, True),
        [packed_f, packed_f, faces, faces, shape((subs, rows, modes), BF16), shape((subs, rows, modes), BF16)],
        [*inverse_pieces, *stiffness_pieces, load_rows, basis_t, left_rows, right_rows],
        work,
        [pltpu.VMEM((rows, lanes), BF16)],
        name="first_image",
    )
    forward = [(i, (i + 1) % n) for i in range(n)]
    backward = [(target, source) for source, target in forward]
    from_before = lax.ppermute(to_after[subs - 1], "sub", forward)
    from_after = lax.ppermute(to_before[0], "sub", backward)
    residual, joined = call(
        functools.partial(join_kernel, z, True),
        [packed_f, shape((subs, rows, 3 * modes), BF16)],
        [load_rows, image, to_before, to_after, from_before, from_after, left_rows, right_rows, image_basis],
        work // 8,
        name="first_join",
    )

    ordered_inverse, index, message = call(
        functools.partial(order_kernel, z),
        [shape((subs, z.owned, z.columns), BF16), shape((subs, n, lanes), F32), copies],
        [*inverse_columns, restricted, repeat, own_row],
        2 * z.owned * z.total * z.total,
        [pltpu.VMEM((z.owned, z.total), BF16)],
        name="order",
    )
    coarse = spread(message)
    (picks,) = call(
        functools.partial(pick_kernel, z),
        [shape((subs, (subs + 2) * modes, z.columns), BF16)],
        [index, place],
        work // 64,
        name="picks",
    )
    first_pass, rounded, message = call(
        functools.partial(update_kernel, z),
        [packed_f, packed_b, copies],
        [coarse, picks, solved, residual, basis, joined, basis_t],
        work // 8,
        name="update",
    )
    restricted = spread(message)

    faces = shape((subs, z.face, lanes), BF16)
    solved, image, to_before, to_after = call(
        functools.partial(image_kernel, z, False),
        [packed_f, packed_f, faces, faces],
        [*inverse_pieces, *stiffness_pieces, rounded, first_pass, left_rows, right_rows],
        work,
        [pltpu.VMEM((rows, lanes), BF16)],
        name="second_image",
    )
    from_before = lax.ppermute(to_after[subs - 1], "sub", forward)
    from_after = lax.ppermute(to_before[0], "sub", backward)
    (residual,) = call(
        functools.partial(join_kernel, z, False),
        [packed_f],
        [load_rows, image, to_before, to_after, from_before, from_after, left_rows, right_rows],
        work // 8,
        name="second_join",
    )
    (message,) = call(
        functools.partial(coarse_kernel, z), [copies], [restricted, ordered_inverse], work // 64, name="coarse"
    )
    coarse = spread(message)
    (parts,) = call(
        functools.partial(last_kernel, z),
        [shape((group, 2, z.own, lanes), F32)],
        [coarse, picks, solved, residual, basis, joined],
        work // 8,
        name="last",
    )
    parts = lax.all_to_all(parts, GROUP, 0, 0)
    out = shape((subs, z.own, z.cases), F32)
    return tuple(call(functools.partial(unpack_kernel, z), [out, out], [parts], work // 64, name="unpack"))


def solution(mesh):
    return jax.shard_map(
        body,
        mesh=mesh,
        in_specs=(
            P("sub", None, None),
            P("sub", GROUP, None),
            P("sub", GROUP, None),
            P("sub", GROUP, None),
            P("sub", GROUP),
            P("sub", None),
            P("sub", None),
            P("sub", None),
        ),
        out_specs=(P("sub", GROUP, None), P("sub", GROUP, None)),
        check_vma=False,
    )
```

```python
import functools

import jax
import jax.numpy as jnp
import numpy as np
from jax import lax
from jax.experimental import pallas as pl
from jax.experimental.pallas import tpu as pltpu
from jax.sharding import PartitionSpec as P

GROUP = ("crow", "ccol")
F32 = jnp.float32
BF16 = jnp.bfloat16
VMEM_BYTES = 16 * 1024 * 1024
DIGIT_ROWS = 16
DIGIT = 256


def dot(a, b):
    return lax.dot_general(a, b, (((1,), (0,)), ((), ())), preferred_element_type=F32)


def dot_tn(a, b):
    return lax.dot_general(a, b, (((0,), (0,)), ((), ())), preferred_element_type=F32)


def dot_nt(a, b):
    return lax.dot_general(a, b, (((1,), (1,)), ((), ())), preferred_element_type=F32)


class Sizes:
    def __init__(self, loads, stiffness, coarse_basis, coarse_inverse, left_rows):
        self.n = lax.axis_size("sub")
        self.group = lax.axis_size(GROUP)
        self.subs, self.rows, self.cases = loads.shape
        self.own = stiffness.shape[1]
        self.modes = coarse_basis.shape[2]
        self.owned, self.block = coarse_inverse.shape
        self.total = self.block * self.group
        self.face = left_rows.shape[1]
        self.width = self.cases // self.group
        self.lanes = max(self.cases, -(-self.subs * self.width // 128) * 128)
        self.columns = self.n * self.modes
        self.near = 1
        while self.near * self.near < self.n and self.n % (2 * self.near) == 0:
            self.near *= 2
        self.far = self.n // self.near


def lane_mask(z, block, shape):
    lane = lax.broadcasted_iota(jnp.int32, shape, len(shape) - 1)
    return (lane >= block * z.width) & (lane < (block + 1) * z.width)


def select(z, parts):
    out = jnp.zeros_like(parts[0])
    for s, part in enumerate(parts):
        out = jnp.where(lane_mask(z, s, part.shape), part, out)
    return out


def fold(z, packed):
    if z.lanes == z.subs * z.width:
        out = packed
        for k in range(1, z.subs):
            out = out + pltpu.roll(packed, k * z.width, 1)
        return out
    out = packed
    for k in range(1, z.subs):
        out = out + pltpu.roll(packed, k * z.width, 1)
        out = out + pltpu.roll(packed, z.lanes - k * z.width, 1)
    return out


def shift_matrix(z, source, target):
    row = lax.broadcasted_iota(jnp.int32, (z.lanes, z.lanes), 0)
    lane = lax.broadcasted_iota(jnp.int32, (z.lanes, z.lanes), 1)
    hit = (row - source * z.width == lane - target * z.width) & lane_mask(z, target, (z.lanes, z.lanes))
    return jnp.where(hit, 1.0, 0.0).astype(BF16)


def place_matrix(z, block):
    row = lax.broadcasted_iota(jnp.int32, (z.modes, 3 * z.modes), 0)
    lane = lax.broadcasted_iota(jnp.int32, (z.modes, 3 * z.modes), 1)
    return jnp.where(row + block * z.modes == lane, 1.0, 0.0).astype(BF16)


def piece_start(z, k, size):
    place = lax.rem(lax.axis_index(GROUP) + k, z.group)
    return pl.multiple_of(place * size, size)


def scatter_matrix(z, rows_of):
    row = lax.broadcasted_iota(jnp.int32, (z.rows, z.face), 0)
    return jnp.where(row == rows_of, 1.0, 0.0).astype(BF16)


def open_kernel(z, *refs):
    pieces = refs[: z.group]
    loads, digits, load_rows, basis_t, message = refs[z.group :]
    group = lax.axis_index(GROUP)
    for k, piece in enumerate(pieces):
        basis_t[:, :, pl.ds(piece_start(z, k, z.own), z.own)] = piece[...]
    row = lax.broadcasted_iota(jnp.int32, (z.cases, z.lanes), 0)
    lane = lax.broadcasted_iota(jnp.int32, (z.cases, z.lanes), 1)
    packed = jnp.zeros((z.rows, z.lanes), F32)
    for s in range(z.subs):
        hit = (row - group * z.width == lane - s * z.width) & lane_mask(z, s, row.shape)
        packed = packed + dot(loads[s], jnp.where(hit, 1.0, 0.0).astype(BF16))
    packed = packed.astype(BF16)
    load_rows[...] = packed
    modes = select(z, [dot(basis_t[s], packed) for s in range(z.subs)]).astype(BF16)
    for k in range(z.n):
        message[k, : z.modes, :] = modes
        message[k, z.modes :, :] = digits[...]


def multiply(z, pieces, vector, store):
    for k, piece in enumerate(pieces):
        parts = [dot(piece[s], vector) for s in range(z.subs)]
        store(piece_start(z, k, z.own), select(z, parts))


def face_picks(z, image, rows_ref, s):
    return dot_tn(scatter_matrix(z, rows_ref[s : s + 1, :]), image).astype(BF16)


def image_kernel(z, first, *refs):
    inverse, stiffness = refs[: z.group], refs[z.group : 2 * z.group]
    rest = refs[2 * z.group :]
    if first:
        vector, basis_t, left_rows, right_rows = rest[:4]
        solved, image, to_before, to_after, basis, image_basis = rest[4:10]
        rounded = rest[10]
    else:
        vector, base, left_rows, right_rows = rest[:4]
        solved, image, to_before, to_after = rest[4:8]
        rounded = rest[8]
    operand = vector[...]

    def store_solved(start, value):
        if not first:
            value = value + base[pl.ds(start, z.own), :]
        solved[pl.ds(start, z.own), :] = value
        rounded[pl.ds(start, z.own), :] = value.astype(BF16)

    multiply(z, inverse, operand, store_solved)

    def store_image(start, value):
        image[pl.ds(start, z.own), :] = value

    multiply(z, stiffness, rounded[...], store_image)
    if first:
        for s in range(z.subs):
            basis[s] = jnp.transpose(basis_t[s].astype(F32)).astype(BF16)
            for k, piece in enumerate(stiffness):
                start = piece_start(z, k, z.own)
                image_basis[s, pl.ds(start, z.own), :] = dot(piece[s], basis[s]).astype(BF16)
    image_b = image[...].astype(BF16)
    for s in range(z.subs):
        for rows_ref, out, target in (
            (left_rows, to_before, (s - 1) % z.subs),
            (right_rows, to_after, (s + 1) % z.subs),
        ):
            picked = face_picks(z, image_b, rows_ref, s)
            out[s, :, : z.lanes] = dot(picked, shift_matrix(z, s, target)).astype(BF16)
            if first:
                out[s, :, z.lanes : z.lanes + z.modes] = face_picks(z, image_basis[s], rows_ref, s)


def join_kernel(z, first, *refs):
    load_rows, image, to_before, to_after, from_before, from_after, left_rows, right_rows = refs[:8]
    if first:
        image_basis, residual, joined = refs[8:]
    else:
        (residual,) = refs[8:]
    added = []
    for s in range(z.subs):
        before = from_before[...] if s == 0 else to_after[s - 1]
        after = from_after[...] if s == z.subs - 1 else to_before[s + 1]
        left = scatter_matrix(z, left_rows[s : s + 1, :])
        right = scatter_matrix(z, right_rows[s : s + 1, :])
        added.append(dot(left, before[:, : z.lanes]) + dot(right, after[:, : z.lanes]))
        if first:
            cut = slice(z.lanes, z.lanes + z.modes)
            total = dot(left, dot(before[:, cut], place_matrix(z, 0)).astype(BF16))
            total = total + dot(image_basis[s], place_matrix(z, 1))
            total = total + dot(right, dot(after[:, cut], place_matrix(z, 2)).astype(BF16))
            joined[s] = total.astype(BF16)
    residual[...] = load_rows[...].astype(F32) - image[...] - select(z, added)


def coarse_rows(z, ordered_inverse, arrived):
    parts = [dot(ordered_inverse[s], arrived) for s in range(z.subs)]
    rows = fold(z, select(z, parts))
    return select(z, [rows[s * z.modes : (s + 1) * z.modes, :] for s in range(z.subs)]).astype(BF16)


def order_kernel(z, *refs):
    pieces = refs[: z.group]
    arrived, repeat, own_row, ordered_inverse, index, message, whole = refs[z.group :]
    for k, piece in enumerate(pieces):
        whole[:, pl.ds(piece_start(z, k, z.block), z.block)] = piece[...]
    digits = arrived[:, z.modes :, :].astype(F32)
    for s in range(z.subs):
        high = jnp.sum(jnp.where(digit_row(digits.shape, 2 * s), digits, 0.0), axis=1)
        low = jnp.sum(jnp.where(digit_row(digits.shape, 2 * s + 1), digits, 0.0), axis=1)
        index[s] = high * DIGIT + low
        spread = dot(high.astype(BF16), repeat[...]) * DIGIT + dot(low.astype(BF16), repeat[...])
        places = jnp.sum(spread * own_row[...], axis=0, keepdims=True).astype(jnp.int32)
        for at in range(0, z.columns, 768):
            wide = min(768, z.columns - at)
            total = jnp.zeros((z.owned, wide), F32)
            for first in range(0, z.total, 256):
                deep = min(256, z.total - first)
                row = lax.broadcasted_iota(jnp.int32, (deep, wide), 0) + first
                hot = jnp.where(row == places[:, at : at + wide], 1.0, 0.0).astype(BF16)
                total = total + dot(whole[:, first : first + deep], hot)
            ordered_inverse[s, :, at : at + wide] = total.astype(BF16)
    rows = arrived[:, : z.modes, :].reshape(z.columns, z.lanes)
    packed = coarse_rows(z, ordered_inverse, rows)
    for k in range(z.n):
        message[k] = packed


def digit_row(shape, row):
    return lax.broadcasted_iota(jnp.int32, shape, 1) == row


def pick_kernel(z, index, place, picks):
    here = lax.axis_index("sub")
    device = lax.broadcasted_iota(jnp.int32, (z.n, z.lanes), 0)
    for t in range(z.subs + 2):
        if t == 0:
            s, owner = z.subs - 1, lax.rem(here + z.n - 1, z.n)
        elif t == z.subs + 1:
            s, owner = 0, lax.rem(here + 1, z.n)
        else:
            s, owner = t - 1, here
        row = jnp.sum(jnp.where(device == owner, index[s], 0.0), axis=0, keepdims=True)
        column = jnp.transpose(jnp.broadcast_to(row, (z.lanes, z.lanes)))[: z.modes, 0:1]
        column = column.astype(jnp.int32)
        for h in range(z.subs):
            hit = column == place[h : h + 1, :]
            picks[h, t * z.modes : (t + 1) * z.modes, :] = jnp.where(hit, 1.0, 0.0).astype(BF16)


def picked_rows(z, arrived, picks):
    flat = in_order(z, arrived)
    return fold(z, select(z, [dot(picks[h], flat) for h in range(z.subs)])).astype(BF16)


def update_kernel(z, arrived, picks, solved, residual, basis, joined, basis_t, first_pass, rounded, message):
    chosen = picked_rows(z, arrived, picks)
    m = z.modes
    first_pass[...] = solved[...] + select(
        z, [dot(basis[s], chosen[(s + 1) * m : (s + 2) * m]) for s in range(z.subs)]
    )
    left = residual[...] - select(z, [dot(joined[s], chosen[s * m : (s + 3) * m]) for s in range(z.subs)])
    left = left.astype(BF16)
    rounded[...] = left
    modes = select(z, [dot(basis_t[s], left) for s in range(z.subs)]).astype(BF16)
    for k in range(message.shape[0]):
        message[k] = modes


def in_order(z, arrived):
    if len(arrived.shape) == 3:
        return arrived[...].reshape(z.columns, z.lanes)
    return jnp.concatenate([arrived[a, b] for b in range(z.far) for a in range(z.near)], axis=0)


def coarse_kernel(z, arrived, ordered_inverse, message):
    packed = coarse_rows(z, ordered_inverse, in_order(z, arrived))
    for k in range(message.shape[0]):
        message[k] = packed


def last_kernel(z, arrived, picks, solved, residual, basis, joined, out):
    chosen = picked_rows(z, arrived, picks)
    m = z.modes
    second = solved[...] + select(
        z, [dot(basis[s], chosen[(s + 1) * m : (s + 2) * m]) for s in range(z.subs)]
    )
    left = residual[...] - select(z, [dot(joined[s], chosen[s * m : (s + 3) * m]) for s in range(z.subs)])
    for k in range(z.group):
        out[k, 0] = second[k * z.own : (k + 1) * z.own, :]
        out[k, 1] = left[k * z.own : (k + 1) * z.own, :]


def unpack_kernel(z, arrived, second_pass, final_residual):
    for at, out in enumerate((second_pass, final_residual)):
        for s in range(z.subs):
            total = jnp.zeros((z.own, z.lanes), F32)
            for k in range(z.group):
                turned = arrived[k, at]
                turn = ((k - s) * z.width) % z.lanes
                if turn:
                    turned = pltpu.roll(turned, turn, 1)
                total = jnp.where(lane_mask(z, k, turned.shape), turned, total)
            out[s] = total[:, : z.cases]


def call(kernel, outs, operands, flops, scratch=(), name=None):
    vmem = pl.BlockSpec(memory_space=pltpu.VMEM)
    moved = sum(int(np.prod(x.shape)) * x.dtype.itemsize for x in (*operands, *outs))
    return pl.pallas_call(
        kernel,
        out_shape=[jax.ShapeDtypeStruct(o.shape, o.dtype) for o in outs],
        in_specs=[vmem] * len(operands),
        out_specs=[vmem] * len(outs),
        scratch_shapes=list(scratch),
        compiler_params=pltpu.CompilerParams(vmem_limit_bytes=VMEM_BYTES),
        cost_estimate=pl.CostEstimate(flops=flops, bytes_accessed=moved, transcendentals=0),
        name=name,
    )(*operands)


def shape(dims, dtype):
    return jax.ShapeDtypeStruct(dims, dtype)


def pieces_of(block, group):
    out = [block]
    for k in range(1, group):
        out.append(lax.ppermute(block, GROUP, [((g + k) % group, g) for g in range(group)]))
    return out


def body(loads, stiffness, local_inverse, coarse_basis, coarse_inverse, coarse_index, left_rows, right_rows):
    z = Sizes(loads, stiffness, coarse_basis, coarse_inverse, left_rows)
    n, group, subs, rows, lanes, modes = z.n, z.group, z.subs, z.rows, z.lanes, z.modes
    own_t = jnp.swapaxes(coarse_basis, 1, 2)
    basis_pieces = pieces_of(own_t, group)
    high, low = coarse_index // DIGIT, coarse_index % DIGIT
    digits = jnp.stack([high, low], axis=1).reshape(2 * subs, modes).astype(BF16)
    digits = jnp.pad(digits, ((0, DIGIT_ROWS - 2 * subs), (0, lanes - modes)))
    column = np.arange(z.columns)
    repeat = jnp.asarray(np.arange(lanes)[:, None] == column[None, :] % modes, BF16)
    own_row = jnp.asarray(np.arange(n)[:, None] == column[None, :] // modes, F32)
    place = jnp.asarray(
        (column // modes * z.owned + column % modes)[None, :] + np.arange(subs)[:, None] * modes, jnp.int32
    )
    packed_f = shape((rows, lanes), F32)
    packed_b = shape((rows, lanes), BF16)
    copies = shape((n, modes, lanes), BF16)
    few = shape((z.far, modes, lanes), BF16)
    spread = functools.partial(lax.all_to_all, axis_name="sub", split_axis=0, concat_axis=0)
    far_groups = [[a + z.near * b for b in range(z.far)] for a in range(z.near)]
    near_groups = [[a + z.near * b for a in range(z.near)] for b in range(z.far)]

    def spread_staged(message):
        part = spread(message, axis_index_groups=far_groups)
        return spread(jnp.broadcast_to(part[None], (z.near, *part.shape)), axis_index_groups=near_groups)


    load_rows, basis_t, message = call(
        functools.partial(open_kernel, z),
        [packed_b, shape((subs, modes, rows), BF16), shape((n, modes + DIGIT_ROWS, lanes), BF16)],
        [*basis_pieces, loads, digits],
        4 * rows * lanes * lanes,
        name="open",
    )
    restricted = spread(message)

    inverse_pieces = pieces_of(local_inverse, group)
    stiffness_pieces = pieces_of(stiffness, group)
    inverse_columns = pieces_of(coarse_inverse, group)
    work = 4 * subs * rows * rows * lanes
    faces = shape((subs, z.face, 2 * lanes), BF16)
    solved, image, to_before, to_after, basis, image_basis = call(
        functools.partial(image_kernel, z, True),
        [packed_f, packed_f, faces, faces, shape((subs, rows, modes), BF16), shape((subs, rows, modes), BF16)],
        [*inverse_pieces, *stiffness_pieces, load_rows, basis_t, left_rows, right_rows],
        work,
        [pltpu.VMEM((rows, lanes), BF16)],
        name="first_image",
    )
    forward = [(i, (i + 1) % n) for i in range(n)]
    backward = [(target, source) for source, target in forward]
    from_before = lax.ppermute(to_after[subs - 1], "sub", forward)
    from_after = lax.ppermute(to_before[0], "sub", backward)
    residual, joined = call(
        functools.partial(join_kernel, z, True),
        [packed_f, shape((subs, rows, 3 * modes), BF16)],
        [load_rows, image, to_before, to_after, from_before, from_after, left_rows, right_rows, image_basis],
        work // 8,
        name="first_join",
    )

    ordered_inverse, index, message = call(
        functools.partial(order_kernel, z),
        [shape((subs, z.owned, z.columns), BF16), shape((subs, n, lanes), F32), copies],
        [*inverse_columns, restricted, repeat, own_row],
        2 * z.owned * z.total * z.total,
        [pltpu.VMEM((z.owned, z.total), BF16)],
        name="order",
    )
    coarse = spread(message)
    (picks,) = call(
        functools.partial(pick_kernel, z),
        [shape((subs, (subs + 2) * modes, z.columns), BF16)],
        [index, place],
        work // 64,
        name="picks",
    )
    first_pass, rounded, message = call(
        functools.partial(update_kernel, z),
        [packed_f, packed_b, few],
        [coarse, picks, solved, residual, basis, joined, basis_t],
        work // 8,
        name="update",
    )
    restricted = spread_staged(message)

    faces = shape((subs, z.face, lanes), BF16)
    solved, image, to_before, to_after = call(
        functools.partial(image_kernel, z, False),
        [packed_f, packed_f, faces, faces],
        [*inverse_pieces, *stiffness_pieces, rounded, first_pass, left_rows, right_rows],
        work,
        [pltpu.VMEM((rows, lanes), BF16)],
        name="second_image",
    )
    from_before = lax.ppermute(to_after[subs - 1], "sub", forward)
    from_after = lax.ppermute(to_before[0], "sub", backward)
    (residual,) = call(
        functools.partial(join_kernel, z, False),
        [packed_f],
        [load_rows, image, to_before, to_after, from_before, from_after, left_rows, right_rows],
        work // 8,
        name="second_join",
    )
    (message,) = call(
        functools.partial(coarse_kernel, z), [few], [restricted, ordered_inverse], work // 64, name="coarse"
    )
    coarse = spread_staged(message)
    (parts,) = call(
        functools.partial(last_kernel, z),
        [shape((group, 2, z.own, lanes), F32)],
        [coarse, picks, solved, residual, basis, joined],
        work // 8,
        name="last",
    )
    parts = lax.all_to_all(parts, GROUP, 0, 0)
    out = shape((subs, z.own, z.cases), F32)
    return tuple(call(functools.partial(unpack_kernel, z), [out, out], [parts], work // 64, name="unpack"))


def solution(mesh):
    return jax.shard_map(
        body,
        mesh=mesh,
        in_specs=(
            P("sub", None, None),
            P("sub", GROUP, None),
            P("sub", GROUP, None),
            P("sub", GROUP, None),
            P("sub", GROUP),
            P("sub", None),
            P("sub", None),
            P("sub", None),
        ),
        out_specs=(P("sub", GROUP, None), P("sub", GROUP, None)),
        check_vma=False,
    )
```

```python
import functools

import jax
import jax.numpy as jnp
import numpy as np
from jax import lax
from jax.experimental import pallas as pl
from jax.experimental.pallas import tpu as pltpu
from jax.sharding import PartitionSpec as P

GROUP = ("crow", "ccol")
F32 = jnp.float32
BF16 = jnp.bfloat16
VMEM_BYTES = 40 * 1024 * 1024
DIGIT_ROWS = 16
DIGIT = 256


def dot(a, b):
    return lax.dot_general(a, b, (((1,), (0,)), ((), ())), preferred_element_type=F32)


def dot_tn(a, b):
    return lax.dot_general(a, b, (((0,), (0,)), ((), ())), preferred_element_type=F32)


def dot_nt(a, b):
    return lax.dot_general(a, b, (((1,), (1,)), ((), ())), preferred_element_type=F32)


class Sizes:
    def __init__(self, loads, stiffness, coarse_basis, coarse_inverse, left_rows):
        self.n = lax.axis_size("sub")
        self.group = lax.axis_size(GROUP)
        self.subs, self.rows, self.cases = loads.shape
        self.own = stiffness.shape[1]
        self.modes = coarse_basis.shape[2]
        self.owned, self.block = coarse_inverse.shape
        self.total = self.block * self.group
        self.face = left_rows.shape[1]
        self.width = self.cases // self.group
        self.lanes = max(self.cases, -(-self.subs * self.width // 128) * 128)
        self.columns = self.n * self.modes


def lane_mask(z, block, shape):
    lane = lax.broadcasted_iota(jnp.int32, shape, len(shape) - 1)
    return (lane >= block * z.width) & (lane < (block + 1) * z.width)


def select(z, parts):
    out = jnp.zeros_like(parts[0])
    for s, part in enumerate(parts):
        out = jnp.where(lane_mask(z, s, part.shape), part, out)
    return out


def fold(z, packed):
    if z.lanes == z.subs * z.width:
        out = packed
        for k in range(1, z.subs):
            out = out + pltpu.roll(packed, k * z.width, 1)
        return out
    out = packed
    for k in range(1, z.subs):
        out = out + pltpu.roll(packed, k * z.width, 1)
        out = out + pltpu.roll(packed, z.lanes - k * z.width, 1)
    return out


def shift_matrix(z, source, target):
    row = lax.broadcasted_iota(jnp.int32, (z.lanes, z.lanes), 0)
    lane = lax.broadcasted_iota(jnp.int32, (z.lanes, z.lanes), 1)
    hit = (row - source * z.width == lane - target * z.width) & lane_mask(z, target, (z.lanes, z.lanes))
    return jnp.where(hit, 1.0, 0.0).astype(BF16)


def place_matrix(z, block):
    row = lax.broadcasted_iota(jnp.int32, (z.modes, 3 * z.modes), 0)
    lane = lax.broadcasted_iota(jnp.int32, (z.modes, 3 * z.modes), 1)
    return jnp.where(row + block * z.modes == lane, 1.0, 0.0).astype(BF16)


def piece_start(z, k, size):
    place = lax.rem(lax.axis_index(GROUP) + k, z.group)
    return pl.multiple_of(place * size, size)


def scatter_matrix(z, rows_of):
    row = lax.broadcasted_iota(jnp.int32, (z.rows, z.face), 0)
    return jnp.where(row == rows_of, 1.0, 0.0).astype(BF16)


def open_kernel(z, *refs):
    pieces = refs[: z.group]
    loads, digits, load_rows, basis_t, message = refs[z.group :]
    group = lax.axis_index(GROUP)
    for k, piece in enumerate(pieces):
        basis_t[:, :, pl.ds(piece_start(z, k, z.own), z.own)] = piece[...]
    row = lax.broadcasted_iota(jnp.int32, (z.cases, z.lanes), 0)
    lane = lax.broadcasted_iota(jnp.int32, (z.cases, z.lanes), 1)
    packed = jnp.zeros((z.rows, z.lanes), F32)
    for s in range(z.subs):
        hit = (row - group * z.width == lane - s * z.width) & lane_mask(z, s, row.shape)
        packed = packed + dot(loads[s], jnp.where(hit, 1.0, 0.0).astype(BF16))
    packed = packed.astype(BF16)
    load_rows[...] = packed
    modes = select(z, [dot(basis_t[s], packed) for s in range(z.subs)]).astype(BF16)
    for k in range(z.n):
        message[k, : z.modes, :] = modes
        message[k, z.modes :, :] = digits[...]


def multiply(z, pieces, vector, store):
    for k, piece in enumerate(pieces):
        parts = [dot(piece[s], vector) for s in range(z.subs)]
        store(piece_start(z, k, z.own), select(z, parts))


def face_picks(z, image, rows_ref, s):
    return dot_tn(scatter_matrix(z, rows_ref[s : s + 1, :]), image).astype(BF16)


def image_kernel(z, first, wait, *refs):
    inverse, stiffness = refs[: z.group], refs[z.group : 2 * z.group]
    rest = refs[2 * z.group :]
    if first:
        vector, basis_t, left_rows, right_rows = rest[:4]
        solved, image, to_before, to_after, basis, image_basis = rest[4:10]
        rounded = rest[10]
    else:
        vector, base, left_rows, right_rows = rest[:4]
        solved, image, to_before, to_after = rest[4:8]
        rounded = rest[8]
    operand = vector[...]

    def store_solved(start, value):
        if not first:
            value = value + base[pl.ds(start, z.own), :]
        solved[pl.ds(start, z.own), :] = value
        rounded[pl.ds(start, z.own), :] = value.astype(BF16)

    multiply(z, inverse, operand, store_solved)

    def store_image(start, value):
        image[pl.ds(start, z.own), :] = value

    for k in range(z.group):
        wait(z.group + k)
    multiply(z, stiffness, rounded[...], store_image)
    if first:
        for s in range(z.subs):
            basis[s] = jnp.transpose(basis_t[s].astype(F32)).astype(BF16)
            for k, piece in enumerate(stiffness):
                start = piece_start(z, k, z.own)
                image_basis[s, pl.ds(start, z.own), :] = dot(piece[s], basis[s]).astype(BF16)
    image_b = image[...].astype(BF16)
    for s in range(z.subs):
        for rows_ref, out, target in (
            (left_rows, to_before, (s - 1) % z.subs),
            (right_rows, to_after, (s + 1) % z.subs),
        ):
            picked = face_picks(z, image_b, rows_ref, s)
            out[s, :, : z.lanes] = dot(picked, shift_matrix(z, s, target)).astype(BF16)
            if first:
                out[s, :, z.lanes : z.lanes + z.modes] = face_picks(z, image_basis[s], rows_ref, s)


def join_kernel(z, first, *refs):
    load_rows, image, to_before, to_after, from_before, from_after, left_rows, right_rows = refs[:8]
    if first:
        image_basis, residual, joined = refs[8:]
    else:
        (residual,) = refs[8:]
    added = []
    for s in range(z.subs):
        before = from_before[...] if s == 0 else to_after[s - 1]
        after = from_after[...] if s == z.subs - 1 else to_before[s + 1]
        left = scatter_matrix(z, left_rows[s : s + 1, :])
        right = scatter_matrix(z, right_rows[s : s + 1, :])
        added.append(dot(left, before[:, : z.lanes]) + dot(right, after[:, : z.lanes]))
        if first:
            cut = slice(z.lanes, z.lanes + z.modes)
            total = dot(left, dot(before[:, cut], place_matrix(z, 0)).astype(BF16))
            total = total + dot(image_basis[s], place_matrix(z, 1))
            total = total + dot(right, dot(after[:, cut], place_matrix(z, 2)).astype(BF16))
            joined[s] = total.astype(BF16)
    residual[...] = load_rows[...].astype(F32) - image[...] - select(z, added)


def digit_row(shape, row):
    return lax.broadcasted_iota(jnp.int32, shape, 1) == row


def choose_kernel(z, block, arrived, repeat, own_row, chosen, rows):
    digits = arrived[:, z.modes :, :].astype(F32)
    high = [jnp.sum(jnp.where(digit_row(digits.shape, 2 * s), digits, 0.0), axis=1) for s in range(z.subs)]
    low = [jnp.sum(jnp.where(digit_row(digits.shape, 2 * s + 1), digits, 0.0), axis=1) for s in range(z.subs)]
    here = lax.axis_index("sub")
    device = lax.broadcasted_iota(jnp.int32, (z.n, z.lanes), 0)
    row_of = lax.broadcasted_iota(jnp.int32, (z.modes, z.total), 1)
    for t in range(z.subs + 2):
        if t == 0:
            s, owner = z.subs - 1, lax.rem(here + z.n - 1, z.n)
        elif t == z.subs + 1:
            s, owner = 0, lax.rem(here + 1, z.n)
        else:
            s, owner = t - 1, here
        places = high[s] * DIGIT + low[s]
        row = jnp.sum(jnp.where(device == owner, places, 0.0), axis=0, keepdims=True)
        column = jnp.transpose(jnp.broadcast_to(row, (z.lanes, z.lanes)))[: z.modes, 0:1].astype(jnp.int32)
        hot = jnp.where(row_of == column, 1.0, 0.0).astype(BF16)
        rows[t * z.modes : (t + 1) * z.modes, :] = dot(hot, block[...]).astype(BF16)
    first = lax.axis_index(GROUP) * z.block
    for s in range(z.subs):
        spread = dot(high[s].astype(BF16), repeat[...]) * DIGIT + dot(low[s].astype(BF16), repeat[...])
        places = jnp.sum(spread * own_row[...], axis=0, keepdims=True).astype(jnp.int32) - first
        for at in range(0, z.columns, 768):
            wide = min(768, z.columns - at)
            total = jnp.zeros((rows.shape[0], wide), F32)
            for start in range(0, z.block, 256):
                deep = min(256, z.block - start)
                row = lax.broadcasted_iota(jnp.int32, (deep, wide), 0) + start
                hot = jnp.where(row == places[:, at : at + wide], 1.0, 0.0).astype(BF16)
                total = total + dot(rows[:, start : start + deep], hot)
            chosen[s, :, at : at + wide] = total.astype(BF16)


def coarse_rows(z, chosen, arrived):
    flat = arrived[:, : z.modes, :].reshape(z.columns, z.lanes)
    return fold(z, select(z, [dot(chosen[s], flat) for s in range(z.subs)])).astype(BF16)


def update_kernel(z, *refs):
    pieces = refs[: z.group]
    arrived, solved, residual, basis, joined, basis_t, first_pass, rounded, message, chosen = refs[z.group :]
    for s in range(z.subs):
        total = pieces[0][s].astype(F32)
        for piece in pieces[1:]:
            total = total + piece[s].astype(F32)
        chosen[s] = total.astype(BF16)
    coarse = coarse_rows(z, chosen, arrived)
    m = z.modes
    first_pass[...] = solved[...] + select(
        z, [dot(basis[s], coarse[(s + 1) * m : (s + 2) * m]) for s in range(z.subs)]
    )
    left = residual[...] - select(z, [dot(joined[s], coarse[s * m : (s + 3) * m]) for s in range(z.subs)])
    left = left.astype(BF16)
    rounded[...] = left
    modes = select(z, [dot(basis_t[s], left) for s in range(z.subs)]).astype(BF16)
    for k in range(z.n):
        message[k] = modes


def last_kernel(z, arrived, chosen, solved, residual, basis, joined, *outs):
    coarse = coarse_rows(z, chosen, arrived)
    m = z.modes
    second = solved[...] + select(
        z, [dot(basis[s], coarse[(s + 1) * m : (s + 2) * m]) for s in range(z.subs)]
    )
    left = residual[...] - select(z, [dot(joined[s], coarse[s * m : (s + 3) * m]) for s in range(z.subs)])
    *outs, whole = outs
    whole[0] = second
    whole[1] = left
    for k, out in enumerate(outs):
        out[...] = whole[:, pl.ds(piece_start(z, k, z.own), z.own), :]


def unpack_kernel(z, *refs):
    pieces, outs = refs[: z.group], refs[z.group :]
    for at, out in enumerate(outs):
        for s in range(z.subs):
            total = jnp.zeros((z.own, z.lanes), F32)
            for k, piece in enumerate(pieces):
                place = lax.rem(lax.axis_index(GROUP) + k, z.group)
                turn = lax.rem((place - s + z.subs * z.group) * z.width, z.lanes)
                turned = pltpu.roll(piece[at], turn, 1)
                total = jnp.where(lane_mask(z, place, turned.shape), turned, total)
            out[s] = total[:, : z.cases]


def call(kernel, outs, operands, flops, scratch=(), late=(), name=None):
    moved = sum(int(np.prod(x.shape)) * x.dtype.itemsize for x in (*operands, *outs))
    n_in, n_out = len(operands), len(outs)

    def whole(*refs):
        hbm, refs = refs[: n_in + n_out], refs[n_in + n_out :]
        vmem, refs = refs[: n_in + n_out], refs[n_in + n_out :]
        in_sems, out_sems, *rest = refs
        arriving = [pltpu.make_async_copy(hbm[i], vmem[i], in_sems.at[i]) for i in range(n_in)]
        for copy in arriving:
            copy.start()
        for i, copy in enumerate(arriving):
            if i not in late:
                copy.wait()
        extra = [lambda i: arriving[i].wait()] if late else []
        kernel(*extra, *vmem, *rest)
        leaving = [pltpu.make_async_copy(vmem[n_in + i], hbm[n_in + i], out_sems.at[i]) for i in range(n_out)]
        for copy in leaving:
            copy.start()
        for copy in leaving:
            copy.wait()

    anywhere = pl.BlockSpec(memory_space=pl.ANY)
    return pl.pallas_call(
        whole,
        out_shape=[jax.ShapeDtypeStruct(o.shape, o.dtype) for o in outs],
        in_specs=[anywhere] * n_in,
        out_specs=[anywhere] * n_out,
        scratch_shapes=[
            *[pltpu.VMEM(x.shape, x.dtype) for x in (*operands, *outs)],
            pltpu.SemaphoreType.DMA((n_in,)),
            pltpu.SemaphoreType.DMA((n_out,)),
            *scratch,
        ],
        compiler_params=pltpu.CompilerParams(vmem_limit_bytes=VMEM_BYTES),
        cost_estimate=pl.CostEstimate(flops=flops, bytes_accessed=moved, transcendentals=0),
        name=name,
    )(*operands)


def shape(dims, dtype):
    return jax.ShapeDtypeStruct(dims, dtype)


def pieces_of(block, group):
    out = [block]
    for k in range(1, group):
        out.append(lax.ppermute(block, GROUP, [((g + k) % group, g) for g in range(group)]))
    return out


def body(loads, stiffness, local_inverse, coarse_basis, coarse_inverse, coarse_index, left_rows, right_rows):
    z = Sizes(loads, stiffness, coarse_basis, coarse_inverse, left_rows)
    n, group, subs, rows, lanes, modes = z.n, z.group, z.subs, z.rows, z.lanes, z.modes
    own_t = jnp.swapaxes(coarse_basis, 1, 2)
    gathered = lax.all_gather(coarse_inverse, "sub", axis=0, tiled=True)
    basis_pieces = pieces_of(own_t, group)
    high, low = coarse_index // DIGIT, coarse_index % DIGIT
    digits = jnp.stack([high, low], axis=1).reshape(2 * subs, modes).astype(BF16)
    digits = jnp.pad(digits, ((0, DIGIT_ROWS - 2 * subs), (0, lanes - modes)))
    column = np.arange(z.columns)
    repeat = jnp.asarray(np.arange(lanes)[:, None] == column[None, :] % modes, BF16)
    own_row = jnp.asarray(np.arange(n)[:, None] == column[None, :] // modes, F32)
    packed_f = shape((rows, lanes), F32)
    packed_b = shape((rows, lanes), BF16)
    copies = shape((n, modes, lanes), BF16)
    spread = functools.partial(lax.all_to_all, axis_name="sub", split_axis=0, concat_axis=0)

    load_rows, basis_t, message = call(
        functools.partial(open_kernel, z),
        [packed_b, shape((subs, modes, rows), BF16), shape((n, modes + DIGIT_ROWS, lanes), BF16)],
        [*basis_pieces, loads, digits],
        4 * rows * lanes * lanes,
        name="open",
    )
    restricted = spread(message)

    inverse_pieces = pieces_of(local_inverse, group)
    stiffness_pieces = pieces_of(stiffness, group)
    work = 4 * subs * rows * rows * lanes
    faces = shape((subs, z.face, 2 * lanes), BF16)
    solved, image, to_before, to_after, basis, image_basis = call(
        functools.partial(image_kernel, z, True),
        [packed_f, packed_f, faces, faces, shape((subs, rows, modes), BF16), shape((subs, rows, modes), BF16)],
        [*inverse_pieces, *stiffness_pieces, load_rows, basis_t, left_rows, right_rows],
        work,
        [pltpu.VMEM((rows, lanes), BF16)],
        range(group, 2 * group),
        name="first_image",
    )
    forward = [(i, (i + 1) % n) for i in range(n)]
    backward = [(target, source) for source, target in forward]
    from_before = lax.ppermute(to_after[subs - 1], "sub", forward)
    from_after = lax.ppermute(to_before[0], "sub", backward)
    residual, joined = call(
        functools.partial(join_kernel, z, True),
        [packed_f, shape((subs, rows, 3 * modes), BF16)],
        [load_rows, image, to_before, to_after, from_before, from_after, left_rows, right_rows, image_basis],
        work // 8,
        name="first_join",
    )

    near = (subs + 2) * modes
    columns = shape((subs, near, z.columns), BF16)
    (chosen,) = call(
        functools.partial(choose_kernel, z),
        [columns],
        [gathered, restricted, repeat, own_row],
        2 * near * z.total * z.total,
        [pltpu.VMEM((near, z.block), BF16)],
        name="choose",
    )
    first_pass, rounded, message, chosen = call(
        functools.partial(update_kernel, z),
        [packed_f, packed_b, copies, columns],
        [*pieces_of(chosen, group), restricted, solved, residual, basis, joined, basis_t],
        work // 8,
        name="update",
    )
    restricted = spread(message)

    faces = shape((subs, z.face, lanes), BF16)
    solved, image, to_before, to_after = call(
        functools.partial(image_kernel, z, False),
        [packed_f, packed_f, faces, faces],
        [*inverse_pieces, *stiffness_pieces, rounded, first_pass, left_rows, right_rows],
        work,
        [pltpu.VMEM((rows, lanes), BF16)],
        range(group, 2 * group),
        name="second_image",
    )
    from_before = lax.ppermute(to_after[subs - 1], "sub", forward)
    from_after = lax.ppermute(to_before[0], "sub", backward)
    (residual,) = call(
        functools.partial(join_kernel, z, False),
        [packed_f],
        [load_rows, image, to_before, to_after, from_before, from_after, left_rows, right_rows],
        work // 8,
        name="second_join",
    )
    parts = shape((2, z.own, lanes), F32)
    parts = call(
        functools.partial(last_kernel, z),
        [parts] * group,
        [restricted, chosen, solved, residual, basis, joined],
        work // 8,
        [pltpu.VMEM((2, rows, lanes), F32)],
        name="last",
    )
    swapped = [parts[0]]
    for k in range(1, group):
        swapped.append(lax.ppermute(parts[k], GROUP, [(g, (g + k) % group) for g in range(group)]))
    swapped = [swapped[(group - k) % group] for k in range(group)]
    out = shape((subs, z.own, z.cases), F32)
    return tuple(call(functools.partial(unpack_kernel, z), [out, out], swapped, work // 64, name="unpack"))


def solution(mesh):
    return jax.shard_map(
        body,
        mesh=mesh,
        in_specs=(
            P("sub", None, None),
            P("sub", GROUP, None),
            P("sub", GROUP, None),
            P("sub", GROUP, None),
            P("sub", GROUP),
            P("sub", None),
            P("sub", None),
            P("sub", None),
        ),
        out_specs=(P("sub", GROUP, None), P("sub", GROUP, None)),
        check_vma=False,
    )
```

```python
import functools

import jax
import jax.numpy as jnp
import numpy as np
from jax import lax
from jax.experimental import pallas as pl
from jax.experimental.pallas import tpu as pltpu
from jax.sharding import PartitionSpec as P

GROUP = ("crow", "ccol")
F32 = jnp.float32
BF16 = jnp.bfloat16
VMEM_BYTES = 48 * 1024 * 1024
DIGIT_ROWS = 16
DIGIT = 256


def dot(a, b):
    return lax.dot_general(a, b, (((1,), (0,)), ((), ())), preferred_element_type=F32)


def dot_tn(a, b):
    return lax.dot_general(a, b, (((0,), (0,)), ((), ())), preferred_element_type=F32)


def dot_nt(a, b):
    return lax.dot_general(a, b, (((1,), (1,)), ((), ())), preferred_element_type=F32)


class Sizes:
    def __init__(self, loads, stiffness, coarse_basis, coarse_inverse, left_rows):
        self.n = lax.axis_size("sub")
        self.group = lax.axis_size(GROUP)
        self.subs, self.rows, self.cases = loads.shape
        self.own = stiffness.shape[1]
        self.modes = coarse_basis.shape[2]
        self.owned, self.block = coarse_inverse.shape
        self.total = self.block * self.group
        self.face = left_rows.shape[1]
        self.width = self.cases // self.group
        self.lanes = max(self.cases, -(-self.subs * self.width // 128) * 128)
        self.columns = self.n * self.modes
        self.near = 1
        while self.near * self.near < self.n and self.n % (2 * self.near) == 0:
            self.near *= 2
        self.far = self.n // self.near


def lane_mask(z, block, shape):
    lane = lax.broadcasted_iota(jnp.int32, shape, len(shape) - 1)
    return (lane >= block * z.width) & (lane < (block + 1) * z.width)


def select(z, parts):
    out = jnp.zeros_like(parts[0])
    for s, part in enumerate(parts):
        out = jnp.where(lane_mask(z, s, part.shape), part, out)
    return out


def fold(z, packed):
    if z.lanes == z.subs * z.width:
        out = packed
        for k in range(1, z.subs):
            out = out + pltpu.roll(packed, k * z.width, 1)
        return out
    out = packed
    for k in range(1, z.subs):
        out = out + pltpu.roll(packed, k * z.width, 1)
        out = out + pltpu.roll(packed, z.lanes - k * z.width, 1)
    return out


def shift_matrix(z, source, target):
    row = lax.broadcasted_iota(jnp.int32, (z.lanes, z.lanes), 0)
    lane = lax.broadcasted_iota(jnp.int32, (z.lanes, z.lanes), 1)
    hit = (row - source * z.width == lane - target * z.width) & lane_mask(z, target, (z.lanes, z.lanes))
    return jnp.where(hit, 1.0, 0.0).astype(BF16)


def place_matrix(z, block):
    row = lax.broadcasted_iota(jnp.int32, (z.modes, 3 * z.modes), 0)
    lane = lax.broadcasted_iota(jnp.int32, (z.modes, 3 * z.modes), 1)
    return jnp.where(row + block * z.modes == lane, 1.0, 0.0).astype(BF16)


def piece_start(z, k, size):
    place = lax.rem(lax.axis_index(GROUP) + k, z.group)
    return pl.multiple_of(place * size, size)


def scatter_matrix(z, rows_of):
    row = lax.broadcasted_iota(jnp.int32, (z.rows, z.face), 0)
    return jnp.where(row == rows_of, 1.0, 0.0).astype(BF16)


def open_kernel(z, *refs):
    pieces = refs[: z.group]
    loads, digits, load_rows, basis_t, message = refs[z.group :]
    group = lax.axis_index(GROUP)
    for k, piece in enumerate(pieces):
        basis_t[:, :, pl.ds(piece_start(z, k, z.own), z.own)] = piece[...]
    row = lax.broadcasted_iota(jnp.int32, (z.cases, z.lanes), 0)
    lane = lax.broadcasted_iota(jnp.int32, (z.cases, z.lanes), 1)
    packed = jnp.zeros((z.rows, z.lanes), F32)
    for s in range(z.subs):
        hit = (row - group * z.width == lane - s * z.width) & lane_mask(z, s, row.shape)
        packed = packed + dot(loads[s], jnp.where(hit, 1.0, 0.0).astype(BF16))
    packed = packed.astype(BF16)
    load_rows[...] = packed
    modes = select(z, [dot(basis_t[s], packed) for s in range(z.subs)]).astype(BF16)
    for k in range(z.n):
        message[k, : z.modes, :] = modes
        message[k, z.modes :, :] = digits[...]


def multiply(z, pieces, vector, store):
    for k, piece in enumerate(pieces):
        parts = [dot(piece[s], vector) for s in range(z.subs)]
        store(piece_start(z, k, z.own), select(z, parts))


def face_picks(z, image, rows_ref, s):
    return dot_tn(scatter_matrix(z, rows_ref[s : s + 1, :]), image).astype(BF16)


def image_kernel(z, first, wait, *refs):
    inverse, stiffness = refs[: z.group], refs[z.group : 2 * z.group]
    rest = refs[2 * z.group :]
    if first:
        vector, basis_t, left_rows, right_rows = rest[:4]
        solved, image, to_before, to_after, basis, image_basis = rest[4:10]
        rounded = rest[10]
    else:
        vector, base, left_rows, right_rows = rest[:4]
        solved, image, to_before, to_after = rest[4:8]
        rounded = rest[8]
    operand = vector[...]

    def store_solved(start, value):
        if not first:
            value = value + base[pl.ds(start, z.own), :]
        solved[pl.ds(start, z.own), :] = value
        rounded[pl.ds(start, z.own), :] = value.astype(BF16)

    multiply(z, inverse, operand, store_solved)

    def store_image(start, value):
        image[pl.ds(start, z.own), :] = value

    for k in range(z.group):
        wait(z.group + k)
    multiply(z, stiffness, rounded[...], store_image)
    if first:
        for s in range(z.subs):
            basis[s] = jnp.transpose(basis_t[s].astype(F32)).astype(BF16)
            for k, piece in enumerate(stiffness):
                start = piece_start(z, k, z.own)
                image_basis[s, pl.ds(start, z.own), :] = dot(piece[s], basis[s]).astype(BF16)
    image_b = image[...].astype(BF16)
    for s in range(z.subs):
        for rows_ref, out, target in (
            (left_rows, to_before, (s - 1) % z.subs),
            (right_rows, to_after, (s + 1) % z.subs),
        ):
            picked = face_picks(z, image_b, rows_ref, s)
            out[s, :, : z.lanes] = dot(picked, shift_matrix(z, s, target)).astype(BF16)
            if first:
                out[s, :, z.lanes : z.lanes + z.modes] = face_picks(z, image_basis[s], rows_ref, s)


def join_kernel(z, first, *refs):
    load_rows, image, to_before, to_after, from_before, from_after, left_rows, right_rows = refs[:8]
    if first:
        image_basis, residual, joined = refs[8:]
    else:
        (residual,) = refs[8:]
    added = []
    for s in range(z.subs):
        before = from_before[...] if s == 0 else to_after[s - 1]
        after = from_after[...] if s == z.subs - 1 else to_before[s + 1]
        left = scatter_matrix(z, left_rows[s : s + 1, :])
        right = scatter_matrix(z, right_rows[s : s + 1, :])
        added.append(dot(left, before[:, : z.lanes]) + dot(right, after[:, : z.lanes]))
        if first:
            cut = slice(z.lanes, z.lanes + z.modes)
            total = dot(left, dot(before[:, cut], place_matrix(z, 0)).astype(BF16))
            total = total + dot(image_basis[s], place_matrix(z, 1))
            total = total + dot(right, dot(after[:, cut], place_matrix(z, 2)).astype(BF16))
            joined[s] = total.astype(BF16)
    residual[...] = load_rows[...].astype(F32) - image[...] - select(z, added)


def digit_row(shape, row):
    return lax.broadcasted_iota(jnp.int32, shape, 1) == row


def coarse_rows(z, ordered_inverse, arrived, message):
    flat = arrived[:, : z.modes, :].reshape(z.columns, z.lanes)
    rows = fold(z, select(z, [dot(ordered_inverse[s], flat) for s in range(z.subs)]))
    for k in range(z.far):
        place = lax.rem(lax.axis_index("sub") // z.near + k, z.far)
        start = k * z.owned
        packed = select(
            z, [rows[start + s * z.modes : start + (s + 1) * z.modes, :] for s in range(z.subs)]
        ).astype(BF16)
        for a in range(z.near):
            message[a, place] = packed


def order_kernel(z, *refs):
    blocks = refs[: z.group]
    arrived, repeat, own_row, ordered_inverse, index, message = refs[z.group :]
    digits = arrived[:, z.modes :, :].astype(F32)
    for s in range(z.subs):
        high = jnp.sum(jnp.where(digit_row(digits.shape, 2 * s), digits, 0.0), axis=1)
        low = jnp.sum(jnp.where(digit_row(digits.shape, 2 * s + 1), digits, 0.0), axis=1)
        index[s] = high * DIGIT + low
        spread = dot(high.astype(BF16), repeat[...]) * DIGIT + dot(low.astype(BF16), repeat[...])
        places = jnp.sum(spread * own_row[...], axis=0, keepdims=True).astype(jnp.int32)
        for at in range(0, z.columns, 768):
            wide = min(768, z.columns - at)
            total = jnp.zeros((z.far * z.owned, wide), F32)
            for k, block in enumerate(blocks):
                inside = places[:, at : at + wide] - piece_start(z, k, z.block)
                for first in range(0, z.block, 768):
                    deep = min(768, z.block - first)
                    row = lax.broadcasted_iota(jnp.int32, (deep, wide), 0) + first
                    hot = jnp.where(row == inside, 1.0, 0.0).astype(BF16)
                    rows = block[:, :, first : first + deep].reshape(z.far * z.owned, deep)
                    total = total + dot(rows, hot)
            ordered_inverse[s, :, at : at + wide] = total.astype(BF16)
    coarse_rows(z, ordered_inverse, arrived, message)


def coarse_kernel(z, arrived, ordered_inverse, message):
    coarse_rows(z, ordered_inverse, arrived, message)


def pick_kernel(z, index, place, picks):
    here = lax.axis_index("sub")
    device = lax.broadcasted_iota(jnp.int32, (z.n, z.lanes), 0)
    for t in range(z.subs + 2):
        if t == 0:
            s, owner = z.subs - 1, lax.rem(here + z.n - 1, z.n)
        elif t == z.subs + 1:
            s, owner = 0, lax.rem(here + 1, z.n)
        else:
            s, owner = t - 1, here
        row = jnp.sum(jnp.where(device == owner, index[s], 0.0), axis=0, keepdims=True)
        column = jnp.transpose(jnp.broadcast_to(row, (z.lanes, z.lanes)))[: z.modes, 0:1]
        column = column.astype(jnp.int32)
        for h in range(z.subs):
            hit = column == place[h : h + 1, :]
            picks[h, t * z.modes : (t + 1) * z.modes, :] = jnp.where(hit, 1.0, 0.0).astype(BF16)


def picked_rows(z, arrived, picks):
    flat = jnp.concatenate([arrived[a, b] for b in range(z.far) for a in range(z.near)], axis=0)
    return fold(z, select(z, [dot(picks[h], flat) for h in range(z.subs)])).astype(BF16)


def update_kernel(z, arrived, picks, solved, residual, basis, joined, basis_t, first_pass, rounded, message):
    chosen = picked_rows(z, arrived, picks)
    m = z.modes
    first_pass[...] = solved[...] + select(
        z, [dot(basis[s], chosen[(s + 1) * m : (s + 2) * m]) for s in range(z.subs)]
    )
    left = residual[...] - select(z, [dot(joined[s], chosen[s * m : (s + 3) * m]) for s in range(z.subs)])
    left = left.astype(BF16)
    rounded[...] = left
    modes = select(z, [dot(basis_t[s], left) for s in range(z.subs)]).astype(BF16)
    for k in range(z.n):
        message[k] = modes


def last_kernel(z, arrived, picks, solved, residual, basis, joined, *outs):
    chosen = picked_rows(z, arrived, picks)
    m = z.modes
    second = solved[...] + select(
        z, [dot(basis[s], chosen[(s + 1) * m : (s + 2) * m]) for s in range(z.subs)]
    )
    left = residual[...] - select(z, [dot(joined[s], chosen[s * m : (s + 3) * m]) for s in range(z.subs)])
    *outs, whole = outs
    whole[0] = second
    whole[1] = left
    for k, out in enumerate(outs):
        out[...] = whole[:, pl.ds(piece_start(z, k, z.own), z.own), :]


def unpack_kernel(z, *refs):
    pieces, outs = refs[: z.group], refs[z.group :]
    for at, out in enumerate(outs):
        for s in range(z.subs):
            total = jnp.zeros((z.own, z.lanes), F32)
            for k, piece in enumerate(pieces):
                place = lax.rem(lax.axis_index(GROUP) + k, z.group)
                turn = lax.rem((place - s + z.subs * z.group) * z.width, z.lanes)
                turned = pltpu.roll(piece[at], turn, 1)
                total = jnp.where(lane_mask(z, place, turned.shape), turned, total)
            out[s] = total[:, : z.cases]


def call(kernel, outs, operands, flops, scratch=(), late=(), after=(), loose=(), name=None):
    moved = sum(int(np.prod(x.shape)) * x.dtype.itemsize for x in (*operands, *outs))
    n_in, n_out = len(operands), len(outs)

    def whole(*refs):
        hbm, refs = (*refs[:n_in], *refs[n_in + len(after) :][:n_out]), refs[n_in + len(after) + n_out :]
        vmem, refs = refs[: n_in + n_out], refs[n_in + n_out :]
        in_sems, out_sems, *rest = refs
        arriving = [pltpu.make_async_copy(hbm[i], vmem[i], in_sems.at[i]) for i in range(n_in)]
        for copy in arriving:
            copy.start()
        for i, copy in enumerate(arriving):
            if i not in late:
                copy.wait()
        extra = [lambda i: arriving[i].wait()] if late else []
        kernel(*extra, *vmem, *rest)
        leaving = [pltpu.make_async_copy(vmem[n_in + i], hbm[n_in + i], out_sems.at[i]) for i in range(n_out)]
        for copy in leaving:
            copy.start()
        for copy in leaving:
            copy.wait()

    hbm_spec = pl.BlockSpec(memory_space=pltpu.HBM)
    any_spec = pl.BlockSpec(memory_space=pl.ANY)
    placed = [
        x if i in loose else pltpu.with_memory_space_constraint(x, pltpu.HBM) for i, x in enumerate(operands)
    ]
    return pl.pallas_call(
        whole,
        out_shape=[pltpu.HBM(o.shape, o.dtype) for o in outs],
        in_specs=[*[any_spec if i in loose else hbm_spec for i in range(n_in)], *[any_spec] * len(after)],
        out_specs=[hbm_spec] * n_out,
        scratch_shapes=[
            *[pltpu.VMEM(x.shape, x.dtype) for x in (*operands, *outs)],
            pltpu.SemaphoreType.DMA((n_in,)),
            pltpu.SemaphoreType.DMA((n_out,)),
            *scratch,
        ],
        compiler_params=pltpu.CompilerParams(vmem_limit_bytes=VMEM_BYTES),
        cost_estimate=pl.CostEstimate(flops=flops, bytes_accessed=moved, transcendentals=0),
        name=name,
    )(*placed, *after)


def shape(dims, dtype):
    return jax.ShapeDtypeStruct(dims, dtype)


def pieces_of(block, group):
    out = [block]
    for k in range(1, group):
        out.append(lax.ppermute(block, GROUP, [((g + k) % group, g) for g in range(group)]))
    return out


def body(loads, stiffness, local_inverse, coarse_basis, coarse_inverse, coarse_index, left_rows, right_rows):
    z = Sizes(loads, stiffness, coarse_basis, coarse_inverse, left_rows)
    n, group, subs, rows, lanes, modes = z.n, z.group, z.subs, z.rows, z.lanes, z.modes
    own_t = jnp.swapaxes(coarse_basis, 1, 2)
    basis_pieces = pieces_of(own_t, group)
    high, low = coarse_index // DIGIT, coarse_index % DIGIT
    digits = jnp.stack([high, low], axis=1).reshape(2 * subs, modes).astype(BF16)
    digits = jnp.pad(digits, ((0, DIGIT_ROWS - 2 * subs), (0, lanes - modes)))
    column = np.arange(z.columns)
    repeat = jnp.asarray(np.arange(lanes)[:, None] == column[None, :] % modes, BF16)
    own_row = jnp.asarray(np.arange(n)[:, None] == column[None, :] // modes, F32)
    place = jnp.asarray(
        (column // modes * z.owned + column % modes)[None, :] + np.arange(subs)[:, None] * modes, jnp.int32
    )
    packed_f = shape((rows, lanes), F32)
    packed_b = shape((rows, lanes), BF16)
    copies = shape((n, modes, lanes), BF16)
    few = shape((z.near, z.far, modes, lanes), BF16)
    spread = functools.partial(lax.all_to_all, axis_name="sub", split_axis=0, concat_axis=0)
    groups = [[a + z.near * b for a in range(z.near)] for b in range(z.far)]
    spread_near = functools.partial(spread, axis_index_groups=groups)
    shared = [coarse_inverse]
    for k in range(1, z.far):
        shared.append(lax.ppermute(coarse_inverse, "sub", [((i + k * z.near) % n, i) for i in range(n)]))
    shared = jnp.stack(shared)

    load_rows, basis_t, message = call(
        functools.partial(open_kernel, z),
        [packed_b, shape((subs, modes, rows), BF16), shape((n, modes + DIGIT_ROWS, lanes), BF16)],
        [*basis_pieces, loads, digits],
        4 * rows * lanes * lanes,
        loose=range(1, group),
        name="open",
    )
    restricted = spread(message)

    inverse_pieces = pieces_of(local_inverse, group)
    stiffness_pieces = pieces_of(stiffness, group)
    work = 4 * subs * rows * rows * lanes
    faces = shape((subs, z.face, 2 * lanes), BF16)
    solved, image, to_before, to_after, basis, image_basis = call(
        functools.partial(image_kernel, z, True),
        [packed_f, packed_f, faces, faces, shape((subs, rows, modes), BF16), shape((subs, rows, modes), BF16)],
        [*inverse_pieces, *stiffness_pieces, load_rows, basis_t, left_rows, right_rows],
        work,
        [pltpu.VMEM((rows, lanes), BF16)],
        range(group, 2 * group),
        loose=[*range(1, group), *range(group + 1, 2 * group)],
        name="first_image",
    )
    forward = [(i, (i + 1) % n) for i in range(n)]
    backward = [(target, source) for source, target in forward]
    from_before = lax.ppermute(to_after[subs - 1], "sub", forward)
    from_after = lax.ppermute(to_before[0], "sub", backward)
    residual, joined = call(
        functools.partial(join_kernel, z, True),
        [packed_f, shape((subs, rows, 3 * modes), BF16)],
        [load_rows, image, to_before, to_after, from_before, from_after, left_rows, right_rows, image_basis],
        work // 8,
        loose=[4, 5],
        name="first_join",
    )

    ordered_inverse, index, message = call(
        functools.partial(order_kernel, z),
        [shape((subs, z.far * z.owned, z.columns), BF16), shape((subs, n, lanes), F32), few],
        [*pieces_of(shared, group), restricted, repeat, own_row],
        2 * z.far * z.owned * z.total * z.total,
        after=[to_before],
        loose=range(1, group),
        name="order",
    )
    coarse = spread_near(message)
    (picks,) = call(
        functools.partial(pick_kernel, z),
        [shape((subs, (subs + 2) * modes, z.columns), BF16)],
        [index, place],
        work // 64,
        name="picks",
    )
    first_pass, rounded, message = call(
        functools.partial(update_kernel, z),
        [packed_f, packed_b, copies],
        [coarse, picks, solved, residual, basis, joined, basis_t],
        work // 8,
        name="update",
    )
    restricted = spread(message)

    faces = shape((subs, z.face, lanes), BF16)
    solved, image, to_before, to_after = call(
        functools.partial(image_kernel, z, False),
        [packed_f, packed_f, faces, faces],
        [*inverse_pieces, *stiffness_pieces, rounded, first_pass, left_rows, right_rows],
        work,
        [pltpu.VMEM((rows, lanes), BF16)],
        range(group, 2 * group),
        loose=[*range(1, group), *range(group + 1, 2 * group)],
        name="second_image",
    )
    from_before = lax.ppermute(to_after[subs - 1], "sub", forward)
    from_after = lax.ppermute(to_before[0], "sub", backward)
    (residual,) = call(
        functools.partial(join_kernel, z, False),
        [packed_f],
        [load_rows, image, to_before, to_after, from_before, from_after, left_rows, right_rows],
        work // 8,
        loose=[4, 5],
        name="second_join",
    )
    (message,) = call(
        functools.partial(coarse_kernel, z),
        [few],
        [restricted, ordered_inverse],
        work // 64,
        after=[to_before],
        name="coarse",
    )
    coarse = spread_near(message)
    parts = shape((2, z.own, lanes), F32)
    parts = call(
        functools.partial(last_kernel, z),
        [parts] * group,
        [coarse, picks, solved, residual, basis, joined],
        work // 8,
        [pltpu.VMEM((2, rows, lanes), F32)],
        name="last",
    )
    swapped = [parts[0]]
    for k in range(1, group):
        swapped.append(lax.ppermute(parts[k], GROUP, [(g, (g + k) % group) for g in range(group)]))
    swapped = [swapped[(group - k) % group] for k in range(group)]
    out = shape((subs, z.own, z.cases), F32)
    return tuple(call(functools.partial(unpack_kernel, z), [out, out], swapped, work // 64, loose=range(1, group), name="unpack"))


def solution(mesh):
    return jax.shard_map(
        body,
        mesh=mesh,
        in_specs=(
            P("sub", None, None),
            P("sub", GROUP, None),
            P("sub", GROUP, None),
            P("sub", GROUP, None),
            P("sub", GROUP),
            P("sub", None),
            P("sub", None),
            P("sub", None),
        ),
        out_specs=(P("sub", GROUP, None), P("sub", GROUP, None)),
        check_vma=False,
    )
```

```python
import functools

import jax
import jax.numpy as jnp
import numpy as np
from jax import lax
from jax.experimental import pallas as pl
from jax.experimental.pallas import tpu as pltpu
from jax.sharding import PartitionSpec as P

GROUP = ("crow", "ccol")
F32 = jnp.float32
BF16 = jnp.bfloat16
VMEM_BYTES = 48 * 1024 * 1024
DIGIT_ROWS = 16
DIGIT_BITS = 8
DIGIT = 1 << DIGIT_BITS


def dot(a, b):
    return lax.dot_general(a, b, (((1,), (0,)), ((), ())), preferred_element_type=F32)


def dot_tn(a, b):
    return lax.dot_general(a, b, (((0,), (0,)), ((), ())), preferred_element_type=F32)


def dot_nt(a, b):
    return lax.dot_general(a, b, (((1,), (1,)), ((), ())), preferred_element_type=F32)


class Sizes:
    def __init__(self, loads, stiffness, coarse_basis, coarse_inverse, left_rows):
        self.n = lax.axis_size("sub")
        self.group = lax.axis_size(GROUP)
        self.subs, self.rows, self.cases = loads.shape
        self.own = stiffness.shape[1]
        self.modes = coarse_basis.shape[2]
        self.owned, self.block = coarse_inverse.shape
        self.total = self.block * self.group
        self.face = left_rows.shape[1]
        self.width = self.cases // self.group
        self.lanes = max(self.cases, -(-self.subs * self.width // 128) * 128)
        self.columns = self.n * self.modes
        self.near = 1
        while self.near * self.near < self.n and self.n % (2 * self.near) == 0:
            self.near *= 2
        self.far = self.n // self.near


def lane_mask(z, block, shape):
    lane = lax.broadcasted_iota(jnp.int32, shape, len(shape) - 1)
    return (lane >= block * z.width) & (lane < (block + 1) * z.width)


def select(z, parts):
    out = jnp.zeros_like(parts[0])
    for s, part in enumerate(parts):
        out = jnp.where(lane_mask(z, s, part.shape), part, out)
    return out


def fold(z, packed):
    if z.lanes == z.subs * z.width:
        out = packed
        for k in range(1, z.subs):
            out = out + pltpu.roll(packed, k * z.width, 1)
        return out
    out = packed
    for k in range(1, z.subs):
        out = out + pltpu.roll(packed, k * z.width, 1)
        out = out + pltpu.roll(packed, z.lanes - k * z.width, 1)
    return out


def shift_matrix(z, source, target):
    row = lax.broadcasted_iota(jnp.int32, (z.lanes, z.lanes), 0)
    lane = lax.broadcasted_iota(jnp.int32, (z.lanes, z.lanes), 1)
    hit = (row - source * z.width == lane - target * z.width) & lane_mask(z, target, (z.lanes, z.lanes))
    return jnp.where(hit, 1.0, 0.0).astype(BF16)


def piece_start(z, k, size):
    place = lax.rem(lax.axis_index(GROUP) + k, z.group)
    return pl.multiple_of(place * size, size)


def scatter_matrix(z, rows_of):
    row = lax.broadcasted_iota(jnp.int32, (z.rows, z.face), 0)
    return jnp.where(row == rows_of, 1.0, 0.0).astype(BF16)


def open_kernel(z, *refs):
    pieces = refs[: z.group]
    loads, index, load_rows, basis_t, message, digits = refs[z.group :]
    group = lax.axis_index(GROUP)
    for k, piece in enumerate(pieces):
        basis_t[:, :, pl.ds(piece_start(z, k, z.own), z.own)] = piece[...]
    row = lax.broadcasted_iota(jnp.int32, (z.cases, z.lanes), 0)
    lane = lax.broadcasted_iota(jnp.int32, (z.cases, z.lanes), 1)
    packed = jnp.zeros((z.rows, z.lanes), F32)
    for s in range(z.subs):
        hit = (row - group * z.width == lane - s * z.width) & lane_mask(z, s, row.shape)
        packed = packed + dot(loads[s], jnp.where(hit, 1.0, 0.0).astype(BF16))
    packed = packed.astype(BF16)
    load_rows[...] = packed
    modes = select(z, [dot(basis_t[s], packed) for s in range(z.subs)]).astype(BF16)
    digits[...] = jnp.zeros(digits.shape, F32)
    for s in range(z.subs):
        places = index[s : s + 1, :]
        digits[2 * s : 2 * s + 1, : z.modes] = (places >> DIGIT_BITS).astype(F32)
        digits[2 * s + 1 : 2 * s + 2, : z.modes] = (places & (DIGIT - 1)).astype(F32)
    for k in range(z.n):
        message[k, : z.modes, :] = modes
        message[k, z.modes :, :] = digits[...].astype(BF16)


def stack_kernel(z, *refs):
    *blocks, out = refs
    for k, block in enumerate(blocks):
        out[k] = block[...]


def multiply(z, pieces, vector, store):
    for k, piece in enumerate(pieces):
        parts = [dot(piece[s], vector) for s in range(z.subs)]
        store(piece_start(z, k, z.own), select(z, parts))


def face_rows(z, image_b, rows_ref, s, target):
    picked = dot_tn(scatter_matrix(z, rows_ref[s : s + 1, :]), image_b).astype(BF16)
    return dot(picked, shift_matrix(z, s, target)).astype(BF16)


def sides(z, before, after, outer_before, outer_after, s):
    return (outer_before if s == 0 else after.at[s - 1]), (outer_after if s == z.subs - 1 else before.at[s + 1])


def shares(z, s, chosen, values, bases):
    m = z.modes
    out = []
    for value, base, at in ((values[0], bases[0], s), (values[1], bases[1], s + 2)):
        total = value[:, : z.lanes].astype(F32)
        total = total + dot(base[:, z.lanes : z.lanes + m], chosen[at * m : (at + 1) * m])
        out.append(total.astype(BF16))
    return out


def correction(z, s, chosen, image_basis, both, left_rows, right_rows):
    total = dot(image_basis[s], chosen[(s + 1) * z.modes : (s + 2) * z.modes])
    total = total + dot(scatter_matrix(z, left_rows[s : s + 1, :]), both[0])
    return total + dot(scatter_matrix(z, right_rows[s : s + 1, :]), both[1])


def first_image_kernel(z, wait, *refs):
    inverse, stiffness = refs[: z.group], refs[z.group : 2 * z.group]
    load_rows, basis_t, left_rows, right_rows = refs[2 * z.group : 2 * z.group + 4]
    outs = refs[2 * z.group + 4 :]
    solved, image, before, after, first_face, last_face, basis, image_basis, left_t, right_t, inner, start_modes = outs[:12]
    rounded = outs[12]

    def store_solved(start, value):
        solved[pl.ds(start, z.own), :] = value
        rounded[pl.ds(start, z.own), :] = value.astype(BF16)

    multiply(z, inverse, load_rows[...], store_solved)
    for s in range(z.subs):
        basis[s] = jnp.transpose(basis_t[s].astype(F32)).astype(BF16)

    def store_image(start, value):
        image[pl.ds(start, z.own), :] = value

    for k in range(z.group):
        wait(z.group + k)
    multiply(z, stiffness, rounded[...], store_image)
    for s in range(z.subs):
        for k, piece in enumerate(stiffness):
            image_basis[s, pl.ds(piece_start(z, k, z.own), z.own), :] = dot(piece[s], basis[s]).astype(BF16)
    image_b = image[...].astype(BF16)
    left = (load_rows[...].astype(F32) - image[...]).astype(BF16)
    start_modes[...] = select(z, [dot(basis_t[s], left) for s in range(z.subs)])
    for s in range(z.subs):
        inner[s] = dot(basis_t[s], image_basis[s]).astype(BF16)
        for rows_ref, out, side_t, target in (
            (left_rows, before, left_t, (s - 1) % z.subs),
            (right_rows, after, right_t, (s + 1) % z.subs),
        ):
            scatter = scatter_matrix(z, rows_ref[s : s + 1, :])
            side_t[s] = dot(basis_t[s], scatter).astype(BF16)
            out[s, :, : z.lanes] = face_rows(z, image_b, rows_ref, s, target)
            out[s, :, z.lanes : z.lanes + z.modes] = dot_tn(scatter, image_basis[s]).astype(BF16)
            out[s, :, z.lanes + z.modes :] = jnp.zeros((z.face, z.lanes - z.modes), BF16)
    first_face[...] = before[0]
    last_face[...] = after[z.subs - 1]


def second_image_kernel(z, wait, *refs):
    inverse, stiffness = refs[: z.group], refs[z.group : 2 * z.group]
    rest = refs[2 * z.group :]
    load_rows, old_image, image_basis, old_solved, basis, chosen = rest[:6]
    before, after, outer_before, outer_after, left_rows, right_rows = rest[6:12]
    solved, image, new_before, new_after, first_face, last_face, rounded = rest[12:]
    parts = []
    for s in range(z.subs):
        faces = sides(z, before, after, outer_before, outer_after, s)
        both = shares(z, s, chosen, faces, faces)
        parts.append(correction(z, s, chosen, image_basis, both, left_rows, right_rows))
    residual = (load_rows[...].astype(F32) - old_image[...] - select(z, parts)).astype(BF16)
    m = z.modes
    solved[...] = old_solved[...] + select(
        z, [dot(basis[s], chosen[(s + 1) * m : (s + 2) * m]) for s in range(z.subs)]
    )
    for k in range(z.group):
        wait(k)

    def store_solved(start, value):
        value = value + solved[pl.ds(start, z.own), :]
        solved[pl.ds(start, z.own), :] = value
        rounded[pl.ds(start, z.own), :] = value.astype(BF16)

    multiply(z, inverse, residual, store_solved)

    def store_image(start, value):
        image[pl.ds(start, z.own), :] = value

    for k in range(z.group):
        wait(z.group + k)
    multiply(z, stiffness, rounded[...], store_image)
    image_b = image[...].astype(BF16)
    for s in range(z.subs):
        new_before[s] = face_rows(z, image_b, left_rows, s, (s - 1) % z.subs)
        new_after[s] = face_rows(z, image_b, right_rows, s, (s + 1) % z.subs)
    first_face[...] = new_before[0]
    last_face[...] = new_after[z.subs - 1]


def digit_row(shape, row):
    return lax.broadcasted_iota(jnp.int32, shape, 1) == row


def coarse_rows(z, ordered_inverse, arrived, message):
    flat = arrived[:, : z.modes, :].reshape(z.columns, z.lanes)
    rows = fold(z, select(z, [dot(ordered_inverse[s], flat) for s in range(z.subs)]))
    for k in range(z.far):
        place = lax.rem(lax.axis_index("sub") // z.near + k, z.far)
        start = k * z.owned
        packed = select(
            z, [rows[start + s * z.modes : start + (s + 1) * z.modes, :] for s in range(z.subs)]
        ).astype(BF16)
        for a in range(z.near):
            message[a, place] = packed


def order_kernel(z, *refs):
    blocks = refs[: z.group]
    arrived, repeat, own_row, ordered_inverse, index, message = refs[z.group :]
    digits = arrived[:, z.modes :, :].astype(F32)
    for s in range(z.subs):
        high = jnp.sum(jnp.where(digit_row(digits.shape, 2 * s), digits, 0.0), axis=1)
        low = jnp.sum(jnp.where(digit_row(digits.shape, 2 * s + 1), digits, 0.0), axis=1)
        index[s] = high * DIGIT + low
        spread = dot(high.astype(BF16), repeat[...]) * DIGIT + dot(low.astype(BF16), repeat[...])
        places = jnp.sum(spread * own_row[...], axis=0, keepdims=True).astype(jnp.int32)
        for at in range(0, z.columns, 768):
            wide = min(768, z.columns - at)
            total = jnp.zeros((z.far * z.owned, wide), F32)
            for k, block in enumerate(blocks):
                inside = places[:, at : at + wide] - piece_start(z, k, z.block)
                for first in range(0, z.block, 768):
                    deep = min(768, z.block - first)
                    row = lax.broadcasted_iota(jnp.int32, (deep, wide), 0) + first
                    hot = jnp.where(row == inside, 1.0, 0.0).astype(BF16)
                    rows = block[:, :, first : first + deep].reshape(z.far * z.owned, deep)
                    total = total + dot(rows, hot)
            ordered_inverse[s, :, at : at + wide] = total.astype(BF16)
    coarse_rows(z, ordered_inverse, arrived, message)


def coarse_kernel(z, arrived, ordered_inverse, last_face, message, face):
    coarse_rows(z, ordered_inverse, arrived, message)
    face[...] = last_face[...]


def pick_kernel(z, index, place, last_face, picks, face):
    face[...] = last_face[...]
    here = lax.axis_index("sub")
    device = lax.broadcasted_iota(jnp.int32, (z.n, z.lanes), 0)
    for t in range(z.subs + 2):
        if t == 0:
            s, owner = z.subs - 1, lax.rem(here + z.n - 1, z.n)
        elif t == z.subs + 1:
            s, owner = 0, lax.rem(here + 1, z.n)
        else:
            s, owner = t - 1, here
        row = jnp.sum(jnp.where(device == owner, index[s], 0.0), axis=0, keepdims=True)
        column = jnp.transpose(jnp.broadcast_to(row, (z.lanes, z.lanes)))[: z.modes, 0:1]
        column = column.astype(jnp.int32)
        for h in range(z.subs):
            hit = column == place[h : h + 1, :]
            picks[h, t * z.modes : (t + 1) * z.modes, :] = jnp.where(hit, 1.0, 0.0).astype(BF16)


def picked_rows(z, arrived, picks):
    flat = jnp.concatenate([arrived[a, b] for b in range(z.far) for a in range(z.near)], axis=0)
    return fold(z, select(z, [dot(picks[h], flat) for h in range(z.subs)])).astype(BF16)


def update_kernel(z, *refs):
    arrived, picks, start_modes, inner, left_t, right_t, before, after, outer_before, outer_after = refs[:10]
    chosen, message = refs[10:]
    rows = picked_rows(z, arrived, picks)
    chosen[...] = rows
    m = z.modes
    parts = []
    for s in range(z.subs):
        faces = sides(z, before, after, outer_before, outer_after, s)
        both = shares(z, s, rows, faces, faces)
        total = dot(inner[s], rows[(s + 1) * m : (s + 2) * m])
        parts.append(total + dot(left_t[s], both[0]) + dot(right_t[s], both[1]))
    modes = (start_modes[...] - select(z, parts)).astype(BF16)
    for k in range(z.n):
        message[k] = modes


def last_kernel(z, *refs):
    arrived, picks, load_rows, image, image_basis, solved, basis = refs[:7]
    before, after, outer_before, outer_after = refs[7:11]
    base_before, base_after, base_outer_before, base_outer_after, left_rows, right_rows = refs[11:17]
    *outs, whole = refs[17:]
    chosen = picked_rows(z, arrived, picks)
    m = z.modes
    parts = []
    for s in range(z.subs):
        values = sides(z, before, after, outer_before, outer_after, s)
        bases = sides(z, base_before, base_after, base_outer_before, base_outer_after, s)
        both = shares(z, s, chosen, values, bases)
        parts.append(correction(z, s, chosen, image_basis, both, left_rows, right_rows))
    whole[0] = solved[...] + select(
        z, [dot(basis[s], chosen[(s + 1) * m : (s + 2) * m]) for s in range(z.subs)]
    )
    whole[1] = load_rows[...].astype(F32) - image[...] - select(z, parts)
    for k, out in enumerate(outs):
        out[...] = whole[:, pl.ds(piece_start(z, k, z.own), z.own), :]


def unpack_kernel(z, *refs):
    pieces, outs = refs[: z.group], refs[z.group :]
    for at, out in enumerate(outs):
        for s in range(z.subs):
            total = jnp.zeros((z.own, z.lanes), F32)
            for k, piece in enumerate(pieces):
                place = lax.rem(lax.axis_index(GROUP) + k, z.group)
                turn = lax.rem((place - s + z.subs * z.group) * z.width, z.lanes)
                turned = pltpu.roll(piece[at], turn, 1)
                total = jnp.where(lane_mask(z, place, turned.shape), turned, total)
            out[s] = total[:, : z.cases]


def call(kernel, outs, operands, flops, scratch=(), late=(), after=(), loose=(), name=None):
    moved = sum(int(np.prod(x.shape)) * x.dtype.itemsize for x in (*operands, *outs))
    n_in, n_out = len(operands), len(outs)

    def whole(*refs):
        hbm, refs = (*refs[:n_in], *refs[n_in + len(after) :][:n_out]), refs[n_in + len(after) + n_out :]
        vmem, refs = refs[: n_in + n_out], refs[n_in + n_out :]
        in_sems, out_sems, *rest = refs
        arriving = [pltpu.make_async_copy(hbm[i], vmem[i], in_sems.at[i]) for i in range(n_in)]
        for copy in arriving:
            copy.start()
        for i, copy in enumerate(arriving):
            if i not in late:
                copy.wait()
        extra = [lambda i: arriving[i].wait()] if late else []
        kernel(*extra, *vmem, *rest)
        leaving = [pltpu.make_async_copy(vmem[n_in + i], hbm[n_in + i], out_sems.at[i]) for i in range(n_out)]
        for copy in leaving:
            copy.start()
        for copy in leaving:
            copy.wait()

    hbm_spec = pl.BlockSpec(memory_space=pltpu.HBM)
    any_spec = pl.BlockSpec(memory_space=pl.ANY)
    placed = [
        x if i in loose else pltpu.with_memory_space_constraint(x, pltpu.HBM) for i, x in enumerate(operands)
    ]
    return pl.pallas_call(
        whole,
        out_shape=[pltpu.HBM(o.shape, o.dtype) for o in outs],
        in_specs=[*[any_spec if i in loose else hbm_spec for i in range(n_in)], *[any_spec] * len(after)],
        out_specs=[hbm_spec] * n_out,
        scratch_shapes=[
            *[pltpu.VMEM(x.shape, x.dtype) for x in (*operands, *outs)],
            pltpu.SemaphoreType.DMA((n_in,)),
            pltpu.SemaphoreType.DMA((n_out,)),
            *scratch,
        ],
        compiler_params=pltpu.CompilerParams(vmem_limit_bytes=VMEM_BYTES),
        cost_estimate=pl.CostEstimate(flops=flops, bytes_accessed=moved, transcendentals=0),
        name=name,
    )(*placed, *after)


def shape(dims, dtype):
    return jax.ShapeDtypeStruct(dims, dtype)


def pieces_of(block, group):
    out = [block]
    for k in range(1, group):
        out.append(lax.ppermute(block, GROUP, [((g + k) % group, g) for g in range(group)]))
    return out


def body(loads, stiffness, local_inverse, coarse_basis, coarse_inverse, coarse_index, left_rows, right_rows):
    z = Sizes(loads, stiffness, coarse_basis, coarse_inverse, left_rows)
    n, group, subs, rows, lanes, modes, face = z.n, z.group, z.subs, z.rows, z.lanes, z.modes, z.face
    basis_pieces = pieces_of(jnp.swapaxes(coarse_basis, 1, 2), group)
    column = np.arange(z.columns)
    repeat = jnp.asarray(np.arange(lanes)[:, None] == column[None, :] % modes, BF16)
    own_row = jnp.asarray(np.arange(n)[:, None] == column[None, :] // modes, F32)
    place = jnp.asarray(
        (column // modes * z.owned + column % modes)[None, :] + np.arange(subs)[:, None] * modes, jnp.int32
    )
    packed_f = shape((rows, lanes), F32)
    packed_b = shape((rows, lanes), BF16)
    copies = shape((n, modes, lanes), BF16)
    few = shape((z.near, z.far, modes, lanes), BF16)
    tall = shape((subs, rows, modes), BF16)
    spread = functools.partial(lax.all_to_all, axis_name="sub", split_axis=0, concat_axis=0)
    groups = [[a + z.near * b for a in range(z.near)] for b in range(z.far)]
    spread_near = functools.partial(spread, axis_index_groups=groups)
    forward = [(i, (i + 1) % n) for i in range(n)]
    backward = [(target, source) for source, target in forward]
    work = 4 * subs * rows * rows * lanes

    load_rows, basis_t, message = call(
        functools.partial(open_kernel, z),
        [packed_b, shape((subs, modes, rows), BF16), shape((n, modes + DIGIT_ROWS, lanes), BF16)],
        [*basis_pieces, loads, coarse_index],
        4 * rows * lanes * lanes,
        [pltpu.VMEM((DIGIT_ROWS, lanes), F32)],
        loose=range(1, group),
        name="open",
    )
    restricted = spread(message)

    shared = [coarse_inverse]
    for k in range(1, z.far):
        shared.append(lax.ppermute(coarse_inverse, "sub", [((i + k * z.near) % n, i) for i in range(n)]))
    (shared,) = call(
        functools.partial(stack_kernel, z),
        [shape((z.far, z.owned, z.block), BF16)],
        shared,
        0,
        after=[message],
        loose=range(1, z.far),
        name="stack",
    )
    shared = pieces_of(shared, group)

    inverse_pieces = pieces_of(local_inverse, group)
    stiffness_pieces = pieces_of(stiffness, group)
    arrivals = [*range(1, group), *range(group + 1, 2 * group)]
    faces = shape((subs, face, 2 * lanes), BF16)
    outer = shape((face, 2 * lanes), BF16)
    side = shape((subs, modes, face), BF16)
    (
        solved, image, before, after, first_face, last_face, basis, image_basis, left_t, right_t, inner, start_modes
    ) = call(
        functools.partial(first_image_kernel, z),
        [
            packed_f, packed_f, faces, faces, outer, outer, tall, tall, side, side,
            shape((subs, modes, modes), BF16), shape((modes, lanes), F32),
        ],
        [*inverse_pieces, *stiffness_pieces, load_rows, basis_t, left_rows, right_rows],
        work,
        [pltpu.VMEM((rows, lanes), BF16)],
        late=range(group, 2 * group),
        loose=arrivals,
        name="first_image",
    )
    outer_after = lax.ppermute(first_face, "sub", backward)
    ordered_inverse, index, message = call(
        functools.partial(order_kernel, z),
        [shape((subs, z.far * z.owned, z.columns), BF16), shape((subs, n, lanes), F32), few],
        [*shared, restricted, repeat, own_row],
        2 * z.far * z.owned * z.total * z.total,
        after=[first_face],
        loose=range(1, group),
        name="order",
    )
    coarse = spread_near(message)
    picks, last_face = call(
        functools.partial(pick_kernel, z),
        [shape((subs, (subs + 2) * modes, z.columns), BF16), outer],
        [index, place, last_face],
        work // 64,
        name="picks",
    )
    outer_before = lax.ppermute(last_face, "sub", forward)
    chosen, message = call(
        functools.partial(update_kernel, z),
        [shape(((subs + 2) * modes, lanes), BF16), copies],
        [coarse, picks, start_modes, inner, left_t, right_t, before, after, outer_before, outer_after],
        work // 64,
        loose=[8, 9],
        name="update",
    )
    restricted = spread(message)

    bases = [before, after, outer_before, outer_after]
    faces = shape((subs, face, lanes), BF16)
    outer = shape((face, lanes), BF16)
    solved, image, before, after, first_face, last_face = call(
        functools.partial(second_image_kernel, z),
        [packed_f, packed_f, faces, faces, outer, outer],
        [
            *inverse_pieces, *stiffness_pieces, load_rows, image, image_basis, solved, basis, chosen,
            *bases, left_rows, right_rows,
        ],
        work,
        [pltpu.VMEM((rows, lanes), BF16)],
        late=range(2 * group),
        loose=[*arrivals, 2 * group + 8, 2 * group + 9],
        name="second_image",
    )
    outer_after = lax.ppermute(first_face, "sub", backward)
    message, last_face = call(
        functools.partial(coarse_kernel, z),
        [few, outer],
        [restricted, ordered_inverse, last_face],
        work // 64,
        name="coarse",
    )
    coarse = spread_near(message)
    outer_before = lax.ppermute(last_face, "sub", forward)
    parts = call(
        functools.partial(last_kernel, z),
        [shape((2, z.own, lanes), F32)] * group,
        [
            coarse, picks, load_rows, image, image_basis, solved, basis,
            before, after, outer_before, outer_after, *bases, left_rows, right_rows,
        ],
        work // 8,
        [pltpu.VMEM((2, rows, lanes), F32)],
        loose=[9, 10, 13, 14],
        name="last",
    )
    swapped = [parts[0]]
    for k in range(1, group):
        swapped.append(lax.ppermute(parts[k], GROUP, [(g, (g + k) % group) for g in range(group)]))
    swapped = [swapped[(group - k) % group] for k in range(group)]
    out = shape((subs, z.own, z.cases), F32)
    return tuple(
        call(
            functools.partial(unpack_kernel, z), [out, out], swapped, work // 64, loose=range(1, group), name="unpack"
        )
    )


def solution(mesh):
    return jax.shard_map(
        body,
        mesh=mesh,
        in_specs=(
            P("sub", None, None),
            P("sub", GROUP, None),
            P("sub", GROUP, None),
            P("sub", GROUP, None),
            P("sub", GROUP),
            P("sub", None),
            P("sub", None),
            P("sub", None),
        ),
        out_specs=(P("sub", GROUP, None), P("sub", GROUP, None)),
        check_vma=False,
    )
```

```python
import functools

import jax
import jax.numpy as jnp
import numpy as np
from jax import lax
from jax.experimental import pallas as pl
from jax.experimental.pallas import tpu as pltpu
from jax.sharding import PartitionSpec as P

GROUP = ("crow", "ccol")
F32 = jnp.float32
BF16 = jnp.bfloat16
VMEM_BYTES = 48 * 1024 * 1024
DIGIT_ROWS = 16
DIGIT_BITS = 8
DIGIT = 1 << DIGIT_BITS


def dot(a, b):
    return lax.dot_general(a, b, (((1,), (0,)), ((), ())), preferred_element_type=F32)


def dot_tn(a, b):
    return lax.dot_general(a, b, (((0,), (0,)), ((), ())), preferred_element_type=F32)


def dot_nt(a, b):
    return lax.dot_general(a, b, (((1,), (1,)), ((), ())), preferred_element_type=F32)


class Sizes:
    def __init__(self, loads, stiffness, coarse_basis, coarse_inverse, left_rows):
        self.n = lax.axis_size("sub")
        self.group = lax.axis_size(GROUP)
        self.subs, self.rows, self.cases = loads.shape
        self.own = stiffness.shape[1]
        self.modes = coarse_basis.shape[2]
        self.owned, self.block = coarse_inverse.shape
        self.total = self.block * self.group
        self.face = left_rows.shape[1]
        self.width = self.cases // self.group
        self.lanes = max(self.cases, -(-self.subs * self.width // 128) * 128)
        self.columns = self.n * self.modes


def lane_mask(z, block, shape):
    lane = lax.broadcasted_iota(jnp.int32, shape, len(shape) - 1)
    return (lane >= block * z.width) & (lane < (block + 1) * z.width)


def select(z, parts):
    out = jnp.zeros_like(parts[0])
    for s, part in enumerate(parts):
        out = jnp.where(lane_mask(z, s, part.shape), part, out)
    return out


def fold(z, packed):
    if z.lanes == z.subs * z.width:
        out = packed
        for k in range(1, z.subs):
            out = out + pltpu.roll(packed, k * z.width, 1)
        return out
    out = packed
    for k in range(1, z.subs):
        out = out + pltpu.roll(packed, k * z.width, 1)
        out = out + pltpu.roll(packed, z.lanes - k * z.width, 1)
    return out


def shift_matrix(z, source, target):
    row = lax.broadcasted_iota(jnp.int32, (z.lanes, z.lanes), 0)
    lane = lax.broadcasted_iota(jnp.int32, (z.lanes, z.lanes), 1)
    hit = (row - source * z.width == lane - target * z.width) & lane_mask(z, target, (z.lanes, z.lanes))
    return jnp.where(hit, 1.0, 0.0).astype(BF16)


def piece_start(z, k, size):
    place = lax.rem(lax.axis_index(GROUP) + k, z.group)
    return pl.multiple_of(place * size, size)


def scatter_matrix(z, rows_of):
    row = lax.broadcasted_iota(jnp.int32, (z.rows, z.face), 0)
    return jnp.where(row == rows_of, 1.0, 0.0).astype(BF16)


def case_matrix(z, s):
    row = lax.broadcasted_iota(jnp.int32, (z.cases, z.lanes), 0)
    lane = lax.broadcasted_iota(jnp.int32, (z.cases, z.lanes), 1)
    hit = (row - lax.axis_index(GROUP) * z.width == lane - s * z.width) & lane_mask(z, s, row.shape)
    return jnp.where(hit, 1.0, 0.0).astype(BF16)


def join_basis(z, pieces, basis_t):
    for k, piece in enumerate(pieces):
        basis_t[:, :, pl.ds(piece_start(z, k, z.own), z.own)] = piece[...]


def open_kernel(z, *refs):
    pieces = refs[: z.group]
    loads, index, message, digits, basis_t = refs[z.group :]
    join_basis(z, pieces, basis_t)
    total = jnp.zeros((z.modes, z.lanes), F32)
    for s in range(z.subs):
        total = total + dot(dot(basis_t[s], loads[s]).astype(BF16), case_matrix(z, s))
    modes = total.astype(BF16)
    digits[...] = jnp.zeros(digits.shape, F32)
    for s in range(z.subs):
        places = index[s : s + 1, :]
        digits[2 * s : 2 * s + 1, : z.modes] = (places >> DIGIT_BITS).astype(F32)
        digits[2 * s + 1 : 2 * s + 2, : z.modes] = (places & (DIGIT - 1)).astype(F32)
    for k in range(z.n):
        message[k, : z.modes, :] = modes
        message[k, z.modes :, :] = digits[...].astype(BF16)


def multiply(z, pieces, vector, store):
    for k, piece in enumerate(pieces):
        parts = [dot(piece[s], vector) for s in range(z.subs)]
        store(piece_start(z, k, z.own), select(z, parts))


def face_rows(z, image_b, rows_ref, s, target):
    picked = dot_tn(scatter_matrix(z, rows_ref[s : s + 1, :]), image_b).astype(BF16)
    return dot(picked, shift_matrix(z, s, target)).astype(BF16)


def sides(z, before, after, outer_before, outer_after, s):
    return (outer_before if s == 0 else after.at[s - 1]), (outer_after if s == z.subs - 1 else before.at[s + 1])


def shares(z, s, chosen, values, bases):
    m = z.modes
    out = []
    for value, base, at in ((values[0], bases[0], s), (values[1], bases[1], s + 2)):
        total = value[:, : z.lanes].astype(F32)
        total = total + dot(base[:, z.lanes : z.lanes + m], chosen[at * m : (at + 1) * m])
        out.append(total.astype(BF16))
    return out


def correction(z, s, chosen, image_basis, both, left_rows, right_rows):
    total = dot(image_basis[s], chosen[(s + 1) * z.modes : (s + 2) * z.modes])
    total = total + dot(scatter_matrix(z, left_rows[s : s + 1, :]), both[0])
    return total + dot(scatter_matrix(z, right_rows[s : s + 1, :]), both[1])


def first_image_kernel(z, wait, *refs):
    inverse, stiffness = refs[: z.group], refs[z.group : 2 * z.group]
    pieces = refs[2 * z.group : 3 * z.group]
    loads, left_rows, right_rows = refs[3 * z.group : 3 * z.group + 3]
    load_rows, solved, image, before, after, first_face, last_face = refs[3 * z.group + 3 : 3 * z.group + 10]
    basis, image_basis, left_t, right_t, inner, start_modes, rounded, basis_t = refs[3 * z.group + 10 :]
    join_basis(z, pieces, basis_t)
    packed = dot(loads[0], case_matrix(z, 0))
    for s in range(1, z.subs):
        packed = packed + dot(loads[s], case_matrix(z, s))
    load_rows[...] = packed.astype(BF16)
    for k in range(z.group):
        wait(k)

    def store_solved(start, value):
        solved[pl.ds(start, z.own), :] = value
        rounded[pl.ds(start, z.own), :] = value.astype(BF16)

    multiply(z, inverse, load_rows[...], store_solved)
    for s in range(z.subs):
        basis[s] = jnp.transpose(basis_t[s].astype(F32)).astype(BF16)

    def store_image(start, value):
        image[pl.ds(start, z.own), :] = value

    for k in range(z.group):
        wait(z.group + k)
    multiply(z, stiffness, rounded[...], store_image)
    for s in range(z.subs):
        for k, piece in enumerate(stiffness):
            image_basis[s, pl.ds(piece_start(z, k, z.own), z.own), :] = dot(piece[s], basis[s]).astype(BF16)
    image_b = image[...].astype(BF16)
    left = (load_rows[...].astype(F32) - image[...]).astype(BF16)
    start_modes[...] = select(z, [dot(basis_t[s], left) for s in range(z.subs)])
    for s in range(z.subs):
        inner[s] = dot(basis_t[s], image_basis[s]).astype(BF16)
        for rows_ref, out, side_t, target in (
            (left_rows, before, left_t, (s - 1) % z.subs),
            (right_rows, after, right_t, (s + 1) % z.subs),
        ):
            scatter = scatter_matrix(z, rows_ref[s : s + 1, :])
            side_t[s] = dot(basis_t[s], scatter).astype(BF16)
            out[s, :, : z.lanes] = face_rows(z, image_b, rows_ref, s, target)
            out[s, :, z.lanes : z.lanes + z.modes] = dot_tn(scatter, image_basis[s]).astype(BF16)
            out[s, :, z.lanes + z.modes :] = jnp.zeros((z.face, z.lanes - z.modes), BF16)
    first_face[...] = before[0]
    last_face[...] = after[z.subs - 1]


def second_image_kernel(z, wait, *refs):
    inverse, stiffness = refs[: z.group], refs[z.group : 2 * z.group]
    rest = refs[2 * z.group :]
    load_rows, old_image, image_basis, old_solved, basis, chosen = rest[:6]
    before, after, outer_before, outer_after, left_rows, right_rows = rest[6:12]
    solved, image, new_before, new_after, first_face, last_face, rounded = rest[12:]
    parts = []
    for s in range(z.subs):
        faces = sides(z, before, after, outer_before, outer_after, s)
        both = shares(z, s, chosen, faces, faces)
        parts.append(correction(z, s, chosen, image_basis, both, left_rows, right_rows))
    residual = (load_rows[...].astype(F32) - old_image[...] - select(z, parts)).astype(BF16)
    m = z.modes
    solved[...] = old_solved[...] + select(
        z, [dot(basis[s], chosen[(s + 1) * m : (s + 2) * m]) for s in range(z.subs)]
    )
    for k in range(z.group):
        wait(k)

    def store_solved(start, value):
        value = value + solved[pl.ds(start, z.own), :]
        solved[pl.ds(start, z.own), :] = value
        rounded[pl.ds(start, z.own), :] = value.astype(BF16)

    multiply(z, inverse, residual, store_solved)

    def store_image(start, value):
        image[pl.ds(start, z.own), :] = value

    for k in range(z.group):
        wait(z.group + k)
    multiply(z, stiffness, rounded[...], store_image)
    image_b = image[...].astype(BF16)
    for s in range(z.subs):
        new_before[s] = face_rows(z, image_b, left_rows, s, (s - 1) % z.subs)
        new_after[s] = face_rows(z, image_b, right_rows, s, (s + 1) % z.subs)
    first_face[...] = new_before[0]
    last_face[...] = new_after[z.subs - 1]


def digit_row(shape, row):
    return lax.broadcasted_iota(jnp.int32, shape, 1) == row


def coarse_rows(z, ordered_inverse, arrived, message):
    flat = arrived[:, : z.modes, :].reshape(z.columns, z.lanes)
    rows = fold(z, select(z, [dot(ordered_inverse[s], flat) for s in range(z.subs)]))
    packed = select(z, [rows[s * z.modes : (s + 1) * z.modes, :] for s in range(z.subs)]).astype(BF16)
    for k in range(z.n):
        message[k] = packed


def order_kernel(z, *refs):
    blocks = refs[: z.group]
    arrived, repeat, own_row, ordered_inverse, index, message = refs[z.group :]
    digits = arrived[:, z.modes :, :].astype(F32)
    for s in range(z.subs):
        high = jnp.sum(jnp.where(digit_row(digits.shape, 2 * s), digits, 0.0), axis=1)
        low = jnp.sum(jnp.where(digit_row(digits.shape, 2 * s + 1), digits, 0.0), axis=1)
        index[s] = high * DIGIT + low
        spread = dot(high.astype(BF16), repeat[...]) * DIGIT + dot(low.astype(BF16), repeat[...])
        places = jnp.sum(spread * own_row[...], axis=0, keepdims=True).astype(jnp.int32)
        for at in range(0, z.columns, 768):
            wide = min(768, z.columns - at)
            total = jnp.zeros((z.owned, wide), F32)
            for k, block in enumerate(blocks):
                inside = places[:, at : at + wide] - piece_start(z, k, z.block)
                for first in range(0, z.block, 768):
                    deep = min(768, z.block - first)
                    row = lax.broadcasted_iota(jnp.int32, (deep, wide), 0) + first
                    hot = jnp.where(row == inside, 1.0, 0.0).astype(BF16)
                    total = total + dot(block[:, first : first + deep], hot)
            ordered_inverse[s, :, at : at + wide] = total.astype(BF16)
    coarse_rows(z, ordered_inverse, arrived, message)


def coarse_kernel(z, arrived, ordered_inverse, last_face, message, face):
    coarse_rows(z, ordered_inverse, arrived, message)
    face[...] = last_face[...]


def pick_kernel(z, index, place, last_face, picks, face):
    face[...] = last_face[...]
    here = lax.axis_index("sub")
    device = lax.broadcasted_iota(jnp.int32, (z.n, z.lanes), 0)
    for t in range(z.subs + 2):
        if t == 0:
            s, owner = z.subs - 1, lax.rem(here + z.n - 1, z.n)
        elif t == z.subs + 1:
            s, owner = 0, lax.rem(here + 1, z.n)
        else:
            s, owner = t - 1, here
        row = jnp.sum(jnp.where(device == owner, index[s], 0.0), axis=0, keepdims=True)
        column = jnp.transpose(jnp.broadcast_to(row, (z.lanes, z.lanes)))[: z.modes, 0:1]
        column = column.astype(jnp.int32)
        for h in range(z.subs):
            hit = column == place[h : h + 1, :]
            picks[h, t * z.modes : (t + 1) * z.modes, :] = jnp.where(hit, 1.0, 0.0).astype(BF16)


def picked_rows(z, arrived, picks):
    flat = arrived[...].reshape(z.columns, z.lanes)
    return fold(z, select(z, [dot(picks[h], flat) for h in range(z.subs)])).astype(BF16)


def update_kernel(z, *refs):
    arrived, picks, start_modes, inner, left_t, right_t, before, after, outer_before, outer_after = refs[:10]
    chosen, message = refs[10:]
    rows = picked_rows(z, arrived, picks)
    chosen[...] = rows
    m = z.modes
    parts = []
    for s in range(z.subs):
        faces = sides(z, before, after, outer_before, outer_after, s)
        both = shares(z, s, rows, faces, faces)
        total = dot(inner[s], rows[(s + 1) * m : (s + 2) * m])
        parts.append(total + dot(left_t[s], both[0]) + dot(right_t[s], both[1]))
    modes = (start_modes[...] - select(z, parts)).astype(BF16)
    for k in range(z.n):
        message[k] = modes


def last_kernel(z, *refs):
    arrived, picks, load_rows, image, image_basis, solved, basis = refs[:7]
    before, after, outer_before, outer_after = refs[7:11]
    base_before, base_after, base_outer_before, base_outer_after, left_rows, right_rows = refs[11:17]
    *outs, whole = refs[17:]
    chosen = picked_rows(z, arrived, picks)
    m = z.modes
    parts = []
    for s in range(z.subs):
        values = sides(z, before, after, outer_before, outer_after, s)
        bases = sides(z, base_before, base_after, base_outer_before, base_outer_after, s)
        both = shares(z, s, chosen, values, bases)
        parts.append(correction(z, s, chosen, image_basis, both, left_rows, right_rows))
    whole[0] = solved[...] + select(
        z, [dot(basis[s], chosen[(s + 1) * m : (s + 2) * m]) for s in range(z.subs)]
    )
    whole[1] = load_rows[...].astype(F32) - image[...] - select(z, parts)
    for k, out in enumerate(outs):
        out[...] = whole[:, pl.ds(piece_start(z, k, z.own), z.own), :]


def unpack_kernel(z, *refs):
    pieces, outs = refs[: z.group], refs[z.group :]
    for at, out in enumerate(outs):
        for s in range(z.subs):
            total = jnp.zeros((z.own, z.lanes), F32)
            for k, piece in enumerate(pieces):
                place = lax.rem(lax.axis_index(GROUP) + k, z.group)
                turn = lax.rem((place - s + z.subs * z.group) * z.width, z.lanes)
                turned = pltpu.roll(piece[at], turn, 1)
                total = jnp.where(lane_mask(z, place, turned.shape), turned, total)
            out[s] = total[:, : z.cases]


def call(kernel, outs, operands, flops, scratch=(), late=(), after=(), loose=(), name=None):
    moved = sum(int(np.prod(x.shape)) * x.dtype.itemsize for x in (*operands, *outs))
    n_in, n_out = len(operands), len(outs)

    def whole(*refs):
        hbm, refs = (*refs[:n_in], *refs[n_in + len(after) :][:n_out]), refs[n_in + len(after) + n_out :]
        vmem, refs = refs[: n_in + n_out], refs[n_in + n_out :]
        in_sems, out_sems, *rest = refs
        arriving = [pltpu.make_async_copy(hbm[i], vmem[i], in_sems.at[i]) for i in range(n_in)]
        for copy in arriving:
            copy.start()
        for i, copy in enumerate(arriving):
            if i not in late:
                copy.wait()
        extra = [lambda i: arriving[i].wait()] if late else []
        kernel(*extra, *vmem, *rest)
        leaving = [pltpu.make_async_copy(vmem[n_in + i], hbm[n_in + i], out_sems.at[i]) for i in range(n_out)]
        for copy in leaving:
            copy.start()
        for copy in leaving:
            copy.wait()

    hbm_spec = pl.BlockSpec(memory_space=pltpu.HBM)
    any_spec = pl.BlockSpec(memory_space=pl.ANY)
    placed = [
        x if i in loose else pltpu.with_memory_space_constraint(x, pltpu.HBM) for i, x in enumerate(operands)
    ]
    return pl.pallas_call(
        whole,
        out_shape=[pltpu.HBM(o.shape, o.dtype) for o in outs],
        in_specs=[*[any_spec if i in loose else hbm_spec for i in range(n_in)], *[any_spec] * len(after)],
        out_specs=[hbm_spec] * n_out,
        scratch_shapes=[
            *[pltpu.VMEM(x.shape, x.dtype) for x in (*operands, *outs)],
            pltpu.SemaphoreType.DMA((n_in,)),
            pltpu.SemaphoreType.DMA((n_out,)),
            *scratch,
        ],
        compiler_params=pltpu.CompilerParams(vmem_limit_bytes=VMEM_BYTES),
        cost_estimate=pl.CostEstimate(flops=flops, bytes_accessed=moved, transcendentals=0),
        name=name,
    )(*placed, *after)


def shape(dims, dtype):
    return jax.ShapeDtypeStruct(dims, dtype)


def pieces_of(block, group):
    out = [block]
    for k in range(1, group):
        out.append(lax.ppermute(block, GROUP, [((g + k) % group, g) for g in range(group)]))
    return out


def body(loads, stiffness, local_inverse, coarse_basis, coarse_inverse, coarse_index, left_rows, right_rows):
    z = Sizes(loads, stiffness, coarse_basis, coarse_inverse, left_rows)
    n, group, subs, rows, lanes, modes, face = z.n, z.group, z.subs, z.rows, z.lanes, z.modes, z.face
    basis_pieces = pieces_of(jnp.swapaxes(coarse_basis, 1, 2), group)
    column = np.arange(z.columns)
    repeat = jnp.asarray(np.arange(lanes)[:, None] == column[None, :] % modes, BF16)
    own_row = jnp.asarray(np.arange(n)[:, None] == column[None, :] // modes, F32)
    place = jnp.asarray(
        (column // modes * z.owned + column % modes)[None, :] + np.arange(subs)[:, None] * modes, jnp.int32
    )
    packed_f = shape((rows, lanes), F32)
    packed_b = shape((rows, lanes), BF16)
    copies = shape((n, modes, lanes), BF16)
    tall = shape((subs, rows, modes), BF16)
    spread = functools.partial(lax.all_to_all, axis_name="sub", split_axis=0, concat_axis=0)
    forward = [(i, (i + 1) % n) for i in range(n)]
    backward = [(target, source) for source, target in forward]
    work = 4 * subs * rows * rows * lanes

    (message,) = call(
        functools.partial(open_kernel, z),
        [shape((n, modes + DIGIT_ROWS, lanes), BF16)],
        [*basis_pieces, loads, coarse_index],
        4 * rows * lanes * lanes,
        [pltpu.VMEM((DIGIT_ROWS, lanes), F32), pltpu.VMEM((subs, modes, rows), BF16)],
        loose=range(1, group),
        name="open",
    )
    restricted = spread(message)

    inverse_columns = pieces_of(coarse_inverse, group)
    inverse_pieces = pieces_of(local_inverse, group)
    stiffness_pieces = pieces_of(stiffness, group)
    arrivals = [*range(1, group), *range(group + 1, 2 * group)]
    faces = shape((subs, face, 2 * lanes), BF16)
    outer = shape((face, 2 * lanes), BF16)
    side = shape((subs, modes, face), BF16)
    (
        load_rows, solved, image, before, after, first_face, last_face, basis, image_basis, left_t, right_t, inner, start_modes
    ) = call(
        functools.partial(first_image_kernel, z),
        [
            packed_b, packed_f, packed_f, faces, faces, outer, outer, tall, tall, side, side,
            shape((subs, modes, modes), BF16), shape((modes, lanes), F32),
        ],
        [*inverse_pieces, *stiffness_pieces, *basis_pieces, loads, left_rows, right_rows],
        work,
        [pltpu.VMEM((rows, lanes), BF16), pltpu.VMEM((subs, modes, rows), BF16)],
        late=range(2 * group),
        loose=[*arrivals, *range(2 * group + 1, 3 * group)],
        name="first_image",
    )
    outer_after = lax.ppermute(first_face, "sub", backward)
    ordered_inverse, index, message = call(
        functools.partial(order_kernel, z),
        [shape((subs, z.owned, z.columns), BF16), shape((subs, n, lanes), F32), copies],
        [*inverse_columns, restricted, repeat, own_row],
        2 * z.owned * z.total * z.total,
        after=[first_face],
        loose=range(1, group + 1),
        name="order",
    )
    coarse = spread(message)
    picks, last_face = call(
        functools.partial(pick_kernel, z),
        [shape((subs, (subs + 2) * modes, z.columns), BF16), outer],
        [index, place, last_face],
        work // 64,
        name="picks",
    )
    outer_before = lax.ppermute(last_face, "sub", forward)
    chosen, message = call(
        functools.partial(update_kernel, z),
        [shape(((subs + 2) * modes, lanes), BF16), copies],
        [coarse, picks, start_modes, inner, left_t, right_t, before, after, outer_before, outer_after],
        work // 64,
        loose=[0, 8, 9],
        name="update",
    )
    restricted = spread(message)

    bases = [before, after, outer_before, outer_after]
    faces = shape((subs, face, lanes), BF16)
    outer = shape((face, lanes), BF16)
    solved, image, before, after, first_face, last_face = call(
        functools.partial(second_image_kernel, z),
        [packed_f, packed_f, faces, faces, outer, outer],
        [
            *inverse_pieces, *stiffness_pieces, load_rows, image, image_basis, solved, basis, chosen,
            *bases, left_rows, right_rows,
        ],
        work,
        [pltpu.VMEM((rows, lanes), BF16)],
        late=range(2 * group),
        loose=[*arrivals, 2 * group + 8, 2 * group + 9],
        name="second_image",
    )
    outer_after = lax.ppermute(first_face, "sub", backward)
    message, last_face = call(
        functools.partial(coarse_kernel, z),
        [copies, outer],
        [restricted, ordered_inverse, last_face],
        work // 64,
        loose=[0],
        name="coarse",
    )
    coarse = spread(message)
    outer_before = lax.ppermute(last_face, "sub", forward)
    parts = call(
        functools.partial(last_kernel, z),
        [shape((2, z.own, lanes), F32)] * group,
        [
            coarse, picks, load_rows, image, image_basis, solved, basis,
            before, after, outer_before, outer_after, *bases, left_rows, right_rows,
        ],
        work // 8,
        [pltpu.VMEM((2, rows, lanes), F32)],
        loose=[0, 9, 10, 13, 14],
        name="last",
    )
    swapped = [parts[0]]
    for k in range(1, group):
        swapped.append(lax.ppermute(parts[k], GROUP, [(g, (g + k) % group) for g in range(group)]))
    swapped = [swapped[(group - k) % group] for k in range(group)]
    out = shape((subs, z.own, z.cases), F32)
    return tuple(
        call(
            functools.partial(unpack_kernel, z), [out, out], swapped, work // 64, loose=range(1, group), name="unpack"
        )
    )


def solution(mesh):
    return jax.shard_map(
        body,
        mesh=mesh,
        in_specs=(
            P("sub", None, None),
            P("sub", GROUP, None),
            P("sub", GROUP, None),
            P("sub", GROUP, None),
            P("sub", GROUP),
            P("sub", None),
            P("sub", None),
            P("sub", None),
        ),
        out_specs=(P("sub", GROUP, None), P("sub", GROUP, None)),
        check_vma=False,
    )
```

```python
import functools

import jax
import jax.numpy as jnp
import numpy as np
from jax import lax
from jax.experimental import pallas as pl
from jax.experimental.pallas import tpu as pltpu
from jax.sharding import PartitionSpec as P

GROUP = ("crow", "ccol")
F32 = jnp.float32
BF16 = jnp.bfloat16
VMEM_BYTES = 48 * 1024 * 1024
DIGIT_ROWS = 16
DIGIT_BITS = 8
DIGIT = 1 << DIGIT_BITS


def dot(a, b):
    return lax.dot_general(a, b, (((1,), (0,)), ((), ())), preferred_element_type=F32)


def dot_tn(a, b):
    return lax.dot_general(a, b, (((0,), (0,)), ((), ())), preferred_element_type=F32)


def dot_nt(a, b):
    return lax.dot_general(a, b, (((1,), (1,)), ((), ())), preferred_element_type=F32)


class Sizes:
    def __init__(self, loads, stiffness, coarse_basis, coarse_inverse, left_rows):
        self.n = lax.axis_size("sub")
        self.group = lax.axis_size(GROUP)
        self.subs, self.rows, self.cases = loads.shape
        self.own = stiffness.shape[1]
        self.modes = coarse_basis.shape[2]
        self.owned, self.block = coarse_inverse.shape
        self.total = self.block * self.group
        self.face = left_rows.shape[1]
        self.width = self.cases // self.group
        self.lanes = max(self.cases, -(-self.subs * self.width // 128) * 128)
        self.columns = self.n * self.modes


def lane_mask(z, block, shape):
    lane = lax.broadcasted_iota(jnp.int32, shape, len(shape) - 1)
    return (lane >= block * z.width) & (lane < (block + 1) * z.width)


def select(z, parts):
    out = jnp.zeros_like(parts[0])
    for s, part in enumerate(parts):
        out = jnp.where(lane_mask(z, s, part.shape), part, out)
    return out


def fold(z, packed):
    if z.lanes == z.subs * z.width:
        out = packed
        for k in range(1, z.subs):
            out = out + pltpu.roll(packed, k * z.width, 1)
        return out
    out = packed
    for k in range(1, z.subs):
        out = out + pltpu.roll(packed, k * z.width, 1)
        out = out + pltpu.roll(packed, z.lanes - k * z.width, 1)
    return out


def shift_matrix(z, source, target):
    row = lax.broadcasted_iota(jnp.int32, (z.lanes, z.lanes), 0)
    lane = lax.broadcasted_iota(jnp.int32, (z.lanes, z.lanes), 1)
    hit = (row - source * z.width == lane - target * z.width) & lane_mask(z, target, (z.lanes, z.lanes))
    return jnp.where(hit, 1.0, 0.0).astype(BF16)


def piece_start(z, k, size):
    place = lax.rem(lax.axis_index(GROUP) + k, z.group)
    return pl.multiple_of(place * size, size)


def scatter_matrix(z, rows_of):
    row = lax.broadcasted_iota(jnp.int32, (z.rows, z.face), 0)
    return jnp.where(row == rows_of, 1.0, 0.0).astype(BF16)


def pick_matrix(z, rows_of):
    column = jnp.transpose(jnp.broadcast_to(rows_of.astype(F32), (z.face, z.face)))[:, 0:1].astype(jnp.int32)
    row = lax.broadcasted_iota(jnp.int32, (z.face, z.rows), 1)
    return jnp.where(row == column, 1.0, 0.0).astype(BF16)


def even():
    return lax.rem(lax.axis_index("sub"), 2) == 0


def case_matrix(z, s):
    row = lax.broadcasted_iota(jnp.int32, (z.cases, z.lanes), 0)
    lane = lax.broadcasted_iota(jnp.int32, (z.cases, z.lanes), 1)
    hit = (row - lax.axis_index(GROUP) * z.width == lane - s * z.width) & lane_mask(z, s, row.shape)
    return jnp.where(hit, 1.0, 0.0).astype(BF16)


def join_basis(z, pieces, basis_t):
    for k, piece in enumerate(pieces):
        basis_t[:, :, pl.ds(piece_start(z, k, z.own), z.own)] = piece[...]


def open_kernel(z, *refs):
    pieces = refs[: z.group]
    loads, index, message, digits, basis_t = refs[z.group :]
    join_basis(z, pieces, basis_t)
    total = jnp.zeros((z.modes, z.lanes), F32)
    for s in range(z.subs):
        total = total + dot(dot(basis_t[s], loads[s]).astype(BF16), case_matrix(z, s))
    modes = total.astype(BF16)
    digits[...] = jnp.zeros(digits.shape, F32)
    for s in range(z.subs):
        places = index[s : s + 1, :]
        digits[2 * s : 2 * s + 1, : z.modes] = (places >> DIGIT_BITS).astype(F32)
        digits[2 * s + 1 : 2 * s + 2, : z.modes] = (places & (DIGIT - 1)).astype(F32)
    for k in range(z.n):
        message[k, : z.modes, :] = modes
        message[k, z.modes :, :] = digits[...].astype(BF16)


def multiply(z, pieces, vector, store):
    for k, piece in enumerate(pieces):
        parts = [dot(piece[s], vector) for s in range(z.subs)]
        store(piece_start(z, k, z.own), select(z, parts))


def face_rows(z, image_b, rows_ref, s, target):
    picked = dot(pick_matrix(z, rows_ref[s : s + 1, :]), image_b).astype(BF16)
    return dot(picked, shift_matrix(z, s, target)).astype(BF16)


def store_faces(z, before, after, first_pair, second_pair):
    first, last = before[0], after[z.subs - 1]
    first_pair[...] = jnp.where(even(), last, first)
    second_pair[...] = jnp.where(even(), first, last)


def sides(z, before, after, first_pair, second_pair, s):
    if s == 0:
        from_before = jnp.where(even(), second_pair[...], first_pair[...])
    else:
        from_before = after[s - 1]
    if s == z.subs - 1:
        from_after = jnp.where(even(), first_pair[...], second_pair[...])
    else:
        from_after = before[s + 1]
    return from_before, from_after


def shares(z, s, chosen, values, bases):
    m = z.modes
    out = []
    for value, base, at in ((values[0], bases[0], s), (values[1], bases[1], s + 2)):
        total = value[:, : z.lanes].astype(F32)
        total = total + dot(base[:, z.lanes : z.lanes + m], chosen[at * m : (at + 1) * m])
        out.append(total.astype(BF16))
    return out


def correction(z, s, chosen, image_basis, both, left_rows, right_rows):
    total = dot(image_basis[s], chosen[(s + 1) * z.modes : (s + 2) * z.modes])
    total = total + dot(scatter_matrix(z, left_rows[s : s + 1, :]), both[0])
    return total + dot(scatter_matrix(z, right_rows[s : s + 1, :]), both[1])


def first_image_kernel(z, wait, *refs):
    inverse, stiffness = refs[: z.group], refs[z.group : 2 * z.group]
    pieces = refs[2 * z.group : 3 * z.group]
    loads, left_rows, right_rows = refs[3 * z.group : 3 * z.group + 3]
    load_rows, solved, image, before, after, first_pair, second_pair = refs[3 * z.group + 3 : 3 * z.group + 10]
    basis, image_basis, left_t, right_t, inner, start_modes, rounded, basis_t, both, images = refs[3 * z.group + 10 :]
    join_basis(z, pieces, basis_t)
    packed = dot(loads[0], case_matrix(z, 0))
    for s in range(1, z.subs):
        packed = packed + dot(loads[s], case_matrix(z, s))
    load_rows[...] = packed.astype(BF16)
    for k in range(z.group):
        wait(k)

    def store_solved(start, value):
        solved[pl.ds(start, z.own), :] = value
        rounded[pl.ds(start, z.own), :] = value.astype(BF16)

    multiply(z, inverse, load_rows[...], store_solved)
    solved_b = rounded[...]
    for s in range(z.subs):
        basis[s] = jnp.transpose(basis_t[s].astype(F32)).astype(BF16)
        both[s, :, : z.lanes] = solved_b
        both[s, :, z.lanes : z.lanes + z.modes] = basis[s]
        both[s, :, z.lanes + z.modes :] = jnp.zeros((z.rows, z.lanes - z.modes), BF16)
    for k, piece in enumerate(stiffness):
        wait(z.group + k)
        start = piece_start(z, k, z.own)
        parts = [dot(piece[s], both[s]) for s in range(z.subs)]
        image[pl.ds(start, z.own), :] = select(z, [part[:, : z.lanes] for part in parts])
        for s in range(z.subs):
            images[s, pl.ds(start, z.own), :] = parts[s].astype(BF16)
    left = (load_rows[...].astype(F32) - image[...]).astype(BF16)
    start_modes[...] = select(z, [dot(basis_t[s], left) for s in range(z.subs)])
    for s in range(z.subs):
        image_basis[s] = images[s, :, z.lanes : z.lanes + z.modes]
        inner[s] = dot(basis_t[s], image_basis[s]).astype(BF16)
        for rows_ref, out, side_t, target in (
            (left_rows, before, left_t, (s - 1) % z.subs),
            (right_rows, after, right_t, (s + 1) % z.subs),
        ):
            pick = pick_matrix(z, rows_ref[s : s + 1, :])
            side_t[s] = dot_nt(basis_t[s], pick).astype(BF16)
            picked = dot(pick, images[s]).astype(BF16)
            out[s, :, : z.lanes] = dot(picked[:, : z.lanes], shift_matrix(z, s, target)).astype(BF16)
            out[s, :, z.lanes :] = picked[:, z.lanes :]
    store_faces(z, before, after, first_pair, second_pair)


def second_image_kernel(z, wait, *refs):
    inverse, stiffness = refs[: z.group], refs[z.group : 2 * z.group]
    rest = refs[2 * z.group :]
    load_rows, old_image, image_basis, old_solved, basis, chosen = rest[:6]
    before, after, first_got, second_got, left_rows, right_rows = rest[6:12]
    solved, image, new_before, new_after, first_pair, second_pair, rounded = rest[12:]
    parts = []
    for s in range(z.subs):
        faces = sides(z, before, after, first_got, second_got, s)
        both = shares(z, s, chosen, faces, faces)
        parts.append(correction(z, s, chosen, image_basis, both, left_rows, right_rows))
    residual = (load_rows[...].astype(F32) - old_image[...] - select(z, parts)).astype(BF16)
    m = z.modes
    solved[...] = old_solved[...] + select(
        z, [dot(basis[s], chosen[(s + 1) * m : (s + 2) * m]) for s in range(z.subs)]
    )
    for k in range(z.group):
        wait(k)

    def store_solved(start, value):
        value = value + solved[pl.ds(start, z.own), :]
        solved[pl.ds(start, z.own), :] = value
        rounded[pl.ds(start, z.own), :] = value.astype(BF16)

    multiply(z, inverse, residual, store_solved)

    def store_image(start, value):
        image[pl.ds(start, z.own), :] = value

    for k in range(z.group):
        wait(z.group + k)
    multiply(z, stiffness, rounded[...], store_image)
    image_b = image[...].astype(BF16)
    for s in range(z.subs):
        new_before[s] = face_rows(z, image_b, left_rows, s, (s - 1) % z.subs)
        new_after[s] = face_rows(z, image_b, right_rows, s, (s + 1) % z.subs)
    store_faces(z, new_before, new_after, first_pair, second_pair)


def digit_row(shape, row):
    return lax.broadcasted_iota(jnp.int32, shape, 1) == row


def coarse_rows(z, ordered_inverse, arrived, message):
    flat = arrived[:, : z.modes, :].reshape(z.columns, z.lanes)
    rows = fold(z, select(z, [dot(ordered_inverse[s], flat) for s in range(z.subs)]))
    packed = select(z, [rows[s * z.modes : (s + 1) * z.modes, :] for s in range(z.subs)]).astype(BF16)
    for k in range(z.n):
        message[k] = packed


def order_kernel(z, *refs):
    blocks = refs[: z.group]
    arrived, repeat, own_row, ordered_inverse, index, message = refs[z.group :]
    digits = arrived[:, z.modes :, :].astype(F32)
    for s in range(z.subs):
        high = jnp.sum(jnp.where(digit_row(digits.shape, 2 * s), digits, 0.0), axis=1)
        low = jnp.sum(jnp.where(digit_row(digits.shape, 2 * s + 1), digits, 0.0), axis=1)
        index[s] = high * DIGIT + low
        spread = dot(high.astype(BF16), repeat[...]) * DIGIT + dot(low.astype(BF16), repeat[...])
        places = jnp.sum(spread * own_row[...], axis=0, keepdims=True).astype(jnp.int32)
        for at in range(0, z.columns, 768):
            wide = min(768, z.columns - at)
            total = jnp.zeros((z.owned, wide), F32)
            for k, block in enumerate(blocks):
                inside = places[:, at : at + wide] - piece_start(z, k, z.block)
                for first in range(0, z.block, 768):
                    deep = min(768, z.block - first)
                    row = lax.broadcasted_iota(jnp.int32, (deep, wide), 0) + first
                    hot = jnp.where(row == inside, 1.0, 0.0).astype(BF16)
                    total = total + dot(block[:, first : first + deep], hot)
            ordered_inverse[s, :, at : at + wide] = total.astype(BF16)
    coarse_rows(z, ordered_inverse, arrived, message)


def coarse_kernel(z, arrived, ordered_inverse, pair, message, face):
    coarse_rows(z, ordered_inverse, arrived, message)
    face[...] = pair[...]


def pick_kernel(z, index, place, pair, picks, face):
    face[...] = pair[...]
    here = lax.axis_index("sub")
    device = lax.broadcasted_iota(jnp.int32, (z.n, z.lanes), 0)
    for t in range(z.subs + 2):
        if t == 0:
            s, owner = z.subs - 1, lax.rem(here + z.n - 1, z.n)
        elif t == z.subs + 1:
            s, owner = 0, lax.rem(here + 1, z.n)
        else:
            s, owner = t - 1, here
        row = jnp.sum(jnp.where(device == owner, index[s], 0.0), axis=0, keepdims=True)
        column = jnp.transpose(jnp.broadcast_to(row, (z.lanes, z.lanes)))[: z.modes, 0:1]
        column = column.astype(jnp.int32)
        for h in range(z.subs):
            hit = column == place[h : h + 1, :]
            picks[h, t * z.modes : (t + 1) * z.modes, :] = jnp.where(hit, 1.0, 0.0).astype(BF16)


def picked_rows(z, arrived, picks):
    flat = arrived[...].reshape(z.columns, z.lanes)
    return fold(z, select(z, [dot(picks[h], flat) for h in range(z.subs)])).astype(BF16)


def update_kernel(z, *refs):
    arrived, picks, start_modes, inner, left_t, right_t, before, after, first_got, second_got = refs[:10]
    chosen, message = refs[10:]
    rows = picked_rows(z, arrived, picks)
    chosen[...] = rows
    m = z.modes
    parts = []
    for s in range(z.subs):
        faces = sides(z, before, after, first_got, second_got, s)
        both = shares(z, s, rows, faces, faces)
        total = dot(inner[s], rows[(s + 1) * m : (s + 2) * m])
        parts.append(total + dot(left_t[s], both[0]) + dot(right_t[s], both[1]))
    modes = (start_modes[...] - select(z, parts)).astype(BF16)
    for k in range(z.n):
        message[k] = modes


def last_kernel(z, *refs):
    arrived, picks, load_rows, image, image_basis, solved, basis = refs[:7]
    before, after, first_got, second_got = refs[7:11]
    base_before, base_after, base_first, base_second, left_rows, right_rows = refs[11:17]
    *outs, whole = refs[17:]
    chosen = picked_rows(z, arrived, picks)
    m = z.modes
    parts = []
    for s in range(z.subs):
        values = sides(z, before, after, first_got, second_got, s)
        bases = sides(z, base_before, base_after, base_first, base_second, s)
        both = shares(z, s, chosen, values, bases)
        parts.append(correction(z, s, chosen, image_basis, both, left_rows, right_rows))
    whole[0] = solved[...] + select(
        z, [dot(basis[s], chosen[(s + 1) * m : (s + 2) * m]) for s in range(z.subs)]
    )
    whole[1] = load_rows[...].astype(F32) - image[...] - select(z, parts)
    for k, out in enumerate(outs):
        out[...] = whole[:, pl.ds(piece_start(z, k, z.own), z.own), :]


def unpack_kernel(z, *refs):
    pieces, outs = refs[: z.group], refs[z.group :]
    for at, out in enumerate(outs):
        for s in range(z.subs):
            total = jnp.zeros((z.own, z.lanes), F32)
            for k, piece in enumerate(pieces):
                place = lax.rem(lax.axis_index(GROUP) + k, z.group)
                turn = lax.rem((place - s + z.subs * z.group) * z.width, z.lanes)
                turned = pltpu.roll(piece[at], turn, 1)
                total = jnp.where(lane_mask(z, place, turned.shape), turned, total)
            out[s] = total[:, : z.cases]


def call(kernel, outs, operands, flops, scratch=(), late=(), loose=(), name=None):
    moved = sum(int(np.prod(x.shape)) * x.dtype.itemsize for x in (*operands, *outs))
    n_in, n_out = len(operands), len(outs)

    def whole(*refs):
        hbm, refs = refs[: n_in + n_out], refs[n_in + n_out :]
        vmem, refs = refs[: n_in + n_out], refs[n_in + n_out :]
        in_sems, out_sems, *rest = refs
        arriving = [pltpu.make_async_copy(hbm[i], vmem[i], in_sems.at[i]) for i in range(n_in)]
        for copy in arriving:
            copy.start()
        for i, copy in enumerate(arriving):
            if i not in late:
                copy.wait()
        extra = [lambda i: arriving[i].wait()] if late else []
        kernel(*extra, *vmem, *rest)
        leaving = [pltpu.make_async_copy(vmem[n_in + i], hbm[n_in + i], out_sems.at[i]) for i in range(n_out)]
        for copy in leaving:
            copy.start()
        for copy in leaving:
            copy.wait()

    hbm_spec = pl.BlockSpec(memory_space=pltpu.HBM)
    any_spec = pl.BlockSpec(memory_space=pl.ANY)
    placed = [
        x if i in loose else pltpu.with_memory_space_constraint(x, pltpu.HBM) for i, x in enumerate(operands)
    ]
    return pl.pallas_call(
        whole,
        out_shape=[pltpu.HBM(o.shape, o.dtype) for o in outs],
        in_specs=[any_spec if i in loose else hbm_spec for i in range(n_in)],
        out_specs=[hbm_spec] * n_out,
        scratch_shapes=[
            *[pltpu.VMEM(x.shape, x.dtype) for x in (*operands, *outs)],
            pltpu.SemaphoreType.DMA((n_in,)),
            pltpu.SemaphoreType.DMA((n_out,)),
            *scratch,
        ],
        compiler_params=pltpu.CompilerParams(vmem_limit_bytes=VMEM_BYTES),
        cost_estimate=pl.CostEstimate(flops=flops, bytes_accessed=moved, transcendentals=0),
        name=name,
    )(*placed)


def shape(dims, dtype):
    return jax.ShapeDtypeStruct(dims, dtype)


def pieces_of(block, group):
    out = [block]
    for k in range(1, group):
        out.append(lax.ppermute(block, GROUP, [((g + k) % group, g) for g in range(group)]))
    return out


def body(loads, stiffness, local_inverse, coarse_basis, coarse_inverse, coarse_index, left_rows, right_rows):
    z = Sizes(loads, stiffness, coarse_basis, coarse_inverse, left_rows)
    n, group, subs, rows, lanes, modes, face = z.n, z.group, z.subs, z.rows, z.lanes, z.modes, z.face
    basis_pieces = pieces_of(jnp.swapaxes(coarse_basis, 1, 2), group)
    column = np.arange(z.columns)
    repeat = jnp.asarray(np.arange(lanes)[:, None] == column[None, :] % modes, BF16)
    own_row = jnp.asarray(np.arange(n)[:, None] == column[None, :] // modes, F32)
    place = jnp.asarray(
        (column // modes * z.owned + column % modes)[None, :] + np.arange(subs)[:, None] * modes, jnp.int32
    )
    packed_f = shape((rows, lanes), F32)
    packed_b = shape((rows, lanes), BF16)
    copies = shape((n, modes, lanes), BF16)
    tall = shape((subs, rows, modes), BF16)
    spread = functools.partial(lax.all_to_all, axis_name="sub", split_axis=0, concat_axis=0)
    first_pairs = [(i, i + 1 if i % 2 == 0 else i - 1) for i in range(n)]
    second_pairs = [(i, (i + (1 if i % 2 else -1)) % n) for i in range(n)]
    work = 4 * subs * rows * rows * lanes

    (message,) = call(
        functools.partial(open_kernel, z),
        [shape((n, modes + DIGIT_ROWS, lanes), BF16)],
        [*basis_pieces, loads, coarse_index],
        4 * rows * lanes * lanes,
        [pltpu.VMEM((DIGIT_ROWS, lanes), F32), pltpu.VMEM((subs, modes, rows), BF16)],
        loose=range(1, group),
        name="open",
    )
    inverse_columns = pieces_of(coarse_inverse, group)
    message, local_inverse, stiffness = lax.optimization_barrier((message, local_inverse, stiffness))
    inverse_pieces = pieces_of(local_inverse, group)
    stiffness_pieces = pieces_of(stiffness, group)
    restricted = spread(message)
    arrivals = [*range(1, group), *range(group + 1, 2 * group)]
    faces = shape((subs, face, 2 * lanes), BF16)
    outer = shape((face, 2 * lanes), BF16)
    side = shape((subs, modes, face), BF16)
    (
        load_rows, solved, image, before, after, first_pair, second_pair, basis, image_basis, left_t, right_t, inner, start_modes
    ) = call(
        functools.partial(first_image_kernel, z),
        [
            packed_b, packed_f, packed_f, faces, faces, outer, outer, tall, tall, side, side,
            shape((subs, modes, modes), BF16), shape((modes, lanes), F32),
        ],
        [*inverse_pieces, *stiffness_pieces, *basis_pieces, loads, left_rows, right_rows],
        work,
        [
            pltpu.VMEM((rows, lanes), BF16), pltpu.VMEM((subs, modes, rows), BF16),
            pltpu.VMEM((subs, rows, 2 * lanes), BF16), pltpu.VMEM((subs, rows, 2 * lanes), BF16),
        ],
        late=range(2 * group),
        loose=[*arrivals, *range(2 * group + 1, 3 * group)],
        name="first_image",
    )
    second_got = lax.ppermute(second_pair, "sub", second_pairs)
    restricted, second_pair = lax.optimization_barrier((restricted, second_pair))
    ordered_inverse, index, message = call(
        functools.partial(order_kernel, z),
        [shape((subs, z.owned, z.columns), BF16), shape((subs, n, lanes), F32), copies],
        [*inverse_columns, restricted, repeat, own_row],
        2 * z.owned * z.total * z.total,
        loose=range(1, group + 1),
        name="order",
    )
    coarse = spread(message)
    picks, first_pair = call(
        functools.partial(pick_kernel, z),
        [shape((subs, (subs + 2) * modes, z.columns), BF16), outer],
        [index, place, first_pair],
        work // 64,
        name="picks",
    )
    first_got = lax.ppermute(first_pair, "sub", first_pairs)
    chosen, message = call(
        functools.partial(update_kernel, z),
        [shape(((subs + 2) * modes, lanes), BF16), copies],
        [coarse, picks, start_modes, inner, left_t, right_t, before, after, first_got, second_got],
        work // 64,
        loose=[0, 8, 9],
        name="update",
    )
    restricted = spread(message)

    bases = [before, after, first_got, second_got]
    faces = shape((subs, face, lanes), BF16)
    outer = shape((face, lanes), BF16)
    solved, image, before, after, first_pair, second_pair = call(
        functools.partial(second_image_kernel, z),
        [packed_f, packed_f, faces, faces, outer, outer],
        [
            *inverse_pieces, *stiffness_pieces, load_rows, image, image_basis, solved, basis, chosen,
            *bases, left_rows, right_rows,
        ],
        work,
        [pltpu.VMEM((rows, lanes), BF16)],
        late=range(2 * group),
        loose=[*arrivals, 2 * group + 8, 2 * group + 9],
        name="second_image",
    )
    second_got = lax.ppermute(second_pair, "sub", second_pairs)
    message, first_pair = call(
        functools.partial(coarse_kernel, z),
        [copies, outer],
        [restricted, ordered_inverse, first_pair],
        work // 64,
        loose=[0],
        name="coarse",
    )
    coarse = spread(message)
    first_got = lax.ppermute(first_pair, "sub", first_pairs)
    parts = call(
        functools.partial(last_kernel, z),
        [shape((2, z.own, lanes), F32)] * group,
        [
            coarse, picks, load_rows, image, image_basis, solved, basis,
            before, after, first_got, second_got, *bases, left_rows, right_rows,
        ],
        work // 8,
        [pltpu.VMEM((2, rows, lanes), F32)],
        loose=[0, 9, 10, 13, 14],
        name="last",
    )
    swapped = [parts[0]]
    for k in range(1, group):
        swapped.append(lax.ppermute(parts[k], GROUP, [(g, (g + k) % group) for g in range(group)]))
    swapped = [swapped[(group - k) % group] for k in range(group)]
    out = shape((subs, z.own, z.cases), F32)
    return tuple(
        call(
            functools.partial(unpack_kernel, z), [out, out], swapped, work // 64, loose=range(1, group), name="unpack"
        )
    )


def solution(mesh):
    return jax.shard_map(
        body,
        mesh=mesh,
        in_specs=(
            P("sub", None, None),
            P("sub", GROUP, None),
            P("sub", GROUP, None),
            P("sub", GROUP, None),
            P("sub", GROUP),
            P("sub", None),
            P("sub", None),
            P("sub", None),
        ),
        out_specs=(P("sub", GROUP, None), P("sub", GROUP, None)),
        check_vma=False,
    )
```

```python
import functools

import jax
import jax.numpy as jnp
import numpy as np
from jax import lax
from jax.experimental import pallas as pl
from jax.experimental.pallas import tpu as pltpu
from jax.sharding import PartitionSpec as P

GROUP = ("crow", "ccol")
F32 = jnp.float32
BF16 = jnp.bfloat16
VMEM_BYTES = 48 * 1024 * 1024
DIGIT_ROWS = 16
DIGIT_BITS = 8
DIGIT = 1 << DIGIT_BITS


def dot(a, b):
    return lax.dot_general(a, b, (((1,), (0,)), ((), ())), preferred_element_type=F32)


def dot_tn(a, b):
    return lax.dot_general(a, b, (((0,), (0,)), ((), ())), preferred_element_type=F32)


def dot_nt(a, b):
    return lax.dot_general(a, b, (((1,), (1,)), ((), ())), preferred_element_type=F32)


class Sizes:
    def __init__(self, loads, stiffness, coarse_basis, coarse_inverse, left_rows):
        self.n = lax.axis_size("sub")
        self.group = lax.axis_size(GROUP)
        self.subs, self.rows, self.cases = loads.shape
        self.own = stiffness.shape[1]
        self.modes = coarse_basis.shape[2]
        self.owned, self.block = coarse_inverse.shape
        self.total = self.block * self.group
        self.face = left_rows.shape[1]
        self.width = self.cases // self.group
        self.lanes = max(self.cases, -(-self.subs * self.width // 128) * 128)
        self.columns = self.n * self.modes


def lane_mask(z, block, shape):
    lane = lax.broadcasted_iota(jnp.int32, shape, len(shape) - 1)
    return (lane >= block * z.width) & (lane < (block + 1) * z.width)


def select(z, parts):
    out = jnp.zeros_like(parts[0])
    for s, part in enumerate(parts):
        out = jnp.where(lane_mask(z, s, part.shape), part, out)
    return out


def fold(z, packed):
    if z.lanes == z.subs * z.width:
        out = packed
        for k in range(1, z.subs):
            out = out + pltpu.roll(packed, k * z.width, 1)
        return out
    out = packed
    for k in range(1, z.subs):
        out = out + pltpu.roll(packed, k * z.width, 1)
        out = out + pltpu.roll(packed, z.lanes - k * z.width, 1)
    return out


def shift_matrix(z, source, target):
    row = lax.broadcasted_iota(jnp.int32, (z.lanes, z.lanes), 0)
    lane = lax.broadcasted_iota(jnp.int32, (z.lanes, z.lanes), 1)
    hit = (row - source * z.width == lane - target * z.width) & lane_mask(z, target, (z.lanes, z.lanes))
    return jnp.where(hit, 1.0, 0.0).astype(BF16)


def piece_start(z, k, size):
    place = lax.rem(lax.axis_index(GROUP) + k, z.group)
    return pl.multiple_of(place * size, size)


def scatter_matrix(z, rows_of):
    row = lax.broadcasted_iota(jnp.int32, (z.rows, z.face), 0)
    return jnp.where(row == rows_of, 1.0, 0.0).astype(BF16)


def pick_matrix(z, rows_of):
    column = jnp.transpose(jnp.broadcast_to(rows_of.astype(F32), (z.face, z.face)))[:, 0:1].astype(jnp.int32)
    row = lax.broadcasted_iota(jnp.int32, (z.face, z.rows), 1)
    return jnp.where(row == column, 1.0, 0.0).astype(BF16)


def even():
    return lax.rem(lax.axis_index("sub"), 2) == 0


def case_matrix(z, s):
    row = lax.broadcasted_iota(jnp.int32, (z.cases, z.lanes), 0)
    lane = lax.broadcasted_iota(jnp.int32, (z.cases, z.lanes), 1)
    hit = (row - lax.axis_index(GROUP) * z.width == lane - s * z.width) & lane_mask(z, s, row.shape)
    return jnp.where(hit, 1.0, 0.0).astype(BF16)


def join_basis(z, pieces, basis_t):
    for k, piece in enumerate(pieces):
        basis_t[:, :, pl.ds(piece_start(z, k, z.own), z.own)] = piece[...]


def open_kernel(z, *refs):
    pieces = refs[: z.group]
    loads, index, message, digits, basis_t = refs[z.group :]
    join_basis(z, pieces, basis_t)
    total = jnp.zeros((z.modes, z.lanes), F32)
    for s in range(z.subs):
        total = total + dot(dot(basis_t[s], loads[s]).astype(BF16), case_matrix(z, s))
    modes = total.astype(BF16)
    digits[...] = jnp.zeros(digits.shape, F32)
    for s in range(z.subs):
        places = index[s : s + 1, :]
        digits[2 * s : 2 * s + 1, : z.modes] = (places >> DIGIT_BITS).astype(F32)
        digits[2 * s + 1 : 2 * s + 2, : z.modes] = (places & (DIGIT - 1)).astype(F32)
    for k in range(z.n):
        message[k, : z.modes, :] = modes
        message[k, z.modes :, :] = digits[...].astype(BF16)


def multiply(z, pieces, vector, store):
    for k, piece in enumerate(pieces):
        parts = [dot(piece[s], vector) for s in range(z.subs)]
        store(piece_start(z, k, z.own), select(z, parts))


def face_rows(z, image_b, rows_ref, s, target):
    picked = dot(pick_matrix(z, rows_ref[s : s + 1, :]), image_b).astype(BF16)
    return dot(picked, shift_matrix(z, s, target)).astype(BF16)


def store_faces(z, before, after, first_pair, second_pair):
    first, last = before[0], after[z.subs - 1]
    first_pair[...] = jnp.where(even(), last, first)
    second_pair[...] = jnp.where(even(), first, last)


def sides(z, before, after, first_pair, second_pair, s):
    if s == 0:
        from_before = jnp.where(even(), second_pair[...], first_pair[...])
    else:
        from_before = after[s - 1]
    if s == z.subs - 1:
        from_after = jnp.where(even(), first_pair[...], second_pair[...])
    else:
        from_after = before[s + 1]
    return from_before, from_after


def shares(z, s, chosen, values, bases):
    m = z.modes
    out = []
    for value, base, at in ((values[0], bases[0], s), (values[1], bases[1], s + 2)):
        total = value[:, : z.lanes].astype(F32)
        total = total + dot(base[:, z.lanes : z.lanes + m], chosen[at * m : (at + 1) * m])
        out.append(total.astype(BF16))
    return out


def corrected(z, chosen, tall, both, left_rows, right_rows):
    images, steps = [], []
    m, at = z.modes, z.lanes // 2
    for s in range(z.subs):
        own = chosen[(s + 1) * m : (s + 2) * m]
        none = jnp.zeros((at - m, z.lanes), BF16)
        nil = jnp.zeros((at, z.lanes), BF16)
        left = jnp.concatenate([tall[s], scatter_matrix(z, left_rows[s : s + 1, :])], axis=1)
        right = scatter_matrix(z, right_rows[s : s + 1, :])
        image = jnp.concatenate([own, none, nil, both[s][0]], axis=0)
        step = jnp.concatenate([nil, own, none, jnp.zeros((z.face, z.lanes), BF16)], axis=0)
        total = dot(left, jnp.concatenate([image, step], axis=1))
        images.append(total[:, : z.lanes] + dot(right, both[s][1]))
        steps.append(total[:, z.lanes :])
    return select(z, steps), select(z, images)


def first_image_kernel(z, wait, *refs):
    inverse, stiffness = refs[: z.group], refs[z.group : 2 * z.group]
    pieces = refs[2 * z.group : 3 * z.group]
    loads, left_rows, right_rows = refs[3 * z.group : 3 * z.group + 3]
    load_rows, solved, image, before, after, first_pair, second_pair = refs[3 * z.group + 3 : 3 * z.group + 10]
    tall, left_t, right_t, inner, start_modes, rounded, basis_t, both, images = refs[3 * z.group + 10 :]
    join_basis(z, pieces, basis_t)
    packed = dot(loads[0], case_matrix(z, 0))
    for s in range(1, z.subs):
        packed = packed + dot(loads[s], case_matrix(z, s))
    load_rows[...] = packed.astype(BF16)
    for k in range(z.group):
        wait(k)

    def store_solved(start, value):
        solved[pl.ds(start, z.own), :] = value
        rounded[pl.ds(start, z.own), :] = value.astype(BF16)

    multiply(z, inverse, load_rows[...], store_solved)
    solved_b = rounded[...]
    half = z.lanes // 2
    for s in range(z.subs):
        basis = jnp.transpose(basis_t[s].astype(F32)).astype(BF16)
        tall[s, :, half : half + z.modes] = basis
        tall[s, :, half + z.modes :] = jnp.zeros((z.rows, half - z.modes), BF16)
        both[s, :, : z.lanes] = solved_b
        both[s, :, z.lanes : z.lanes + z.modes] = basis
        both[s, :, z.lanes + z.modes :] = jnp.zeros((z.rows, z.lanes - z.modes), BF16)
    for k, piece in enumerate(stiffness):
        wait(z.group + k)
        start = piece_start(z, k, z.own)
        parts = [dot(piece[s], both[s]) for s in range(z.subs)]
        image[pl.ds(start, z.own), :] = select(z, [part[:, : z.lanes] for part in parts])
        for s in range(z.subs):
            images[s, pl.ds(start, z.own), :] = parts[s].astype(BF16)
    left = (load_rows[...].astype(F32) - image[...]).astype(BF16)
    start_modes[...] = select(z, [dot(basis_t[s], left) for s in range(z.subs)])
    for s in range(z.subs):
        image_basis = images[s, :, z.lanes :]
        tall[s, :, :half] = image_basis[:, :half]
        inner[s] = dot(basis_t[s], image_basis)[:, : z.modes].astype(BF16)
        for rows_ref, out, side_t, target in (
            (left_rows, before, left_t, (s - 1) % z.subs),
            (right_rows, after, right_t, (s + 1) % z.subs),
        ):
            pick = pick_matrix(z, rows_ref[s : s + 1, :])
            side_t[s] = dot_nt(basis_t[s], pick).astype(BF16)
            picked = dot(pick, images[s]).astype(BF16)
            out[s, :, : z.lanes] = dot(picked[:, : z.lanes], shift_matrix(z, s, target)).astype(BF16)
            out[s, :, z.lanes :] = picked[:, z.lanes :]
    store_faces(z, before, after, first_pair, second_pair)


def second_image_kernel(z, wait, *refs):
    inverse, stiffness = refs[: z.group], refs[z.group : 2 * z.group]
    rest = refs[2 * z.group :]
    load_rows, old_image, tall, old_solved, chosen = rest[:5]
    before, after, first_got, second_got, left_rows, right_rows = rest[5:11]
    solved, remaining, new_before, new_after, first_pair, second_pair, rounded, image = rest[11:]
    both = []
    for s in range(z.subs):
        faces = sides(z, before, after, first_got, second_got, s)
        both.append(shares(z, s, chosen, faces, faces))
    step, added = corrected(z, chosen, tall, both, left_rows, right_rows)
    residual = (load_rows[...].astype(F32) - old_image[...] - added).astype(BF16)
    solved[...] = old_solved[...] + step
    for k in range(z.group):
        wait(k)

    def store_solved(start, value):
        value = value + solved[pl.ds(start, z.own), :]
        solved[pl.ds(start, z.own), :] = value
        rounded[pl.ds(start, z.own), :] = value.astype(BF16)

    multiply(z, inverse, residual, store_solved)

    def store_image(start, value):
        place = pl.ds(start, z.own)
        remaining[place, :] = load_rows[place, :].astype(F32) - value
        image[place, :] = value.astype(BF16)

    for k in range(z.group):
        wait(z.group + k)
    multiply(z, stiffness, rounded[...], store_image)
    image_b = image[...]
    for s in range(z.subs):
        new_before[s] = face_rows(z, image_b, left_rows, s, (s - 1) % z.subs)
        new_after[s] = face_rows(z, image_b, right_rows, s, (s + 1) % z.subs)
    store_faces(z, new_before, new_after, first_pair, second_pair)


def digit_row(shape, row):
    return lax.broadcasted_iota(jnp.int32, shape, 1) == row


def coarse_rows(z, ordered_inverse, arrived, message):
    flat = arrived[:, : z.modes, :].reshape(z.columns, z.lanes)
    rows = fold(z, select(z, [dot(ordered_inverse[s], flat) for s in range(z.subs)]))
    packed = select(z, [rows[s * z.modes : (s + 1) * z.modes, :] for s in range(z.subs)]).astype(BF16)
    for k in range(z.n):
        message[k] = packed


def order_kernel(z, *refs):
    blocks = refs[: z.group]
    arrived, repeat, own_row, place, ordered_inverse, picks, message = refs[z.group :]
    digits = arrived[:, z.modes :, :].astype(F32)
    index = []
    for s in range(z.subs):
        high = jnp.sum(jnp.where(digit_row(digits.shape, 2 * s), digits, 0.0), axis=1)
        low = jnp.sum(jnp.where(digit_row(digits.shape, 2 * s + 1), digits, 0.0), axis=1)
        index.append(high * DIGIT + low)
        spread = dot(high.astype(BF16), repeat[...]) * DIGIT + dot(low.astype(BF16), repeat[...])
        places = jnp.sum(spread * own_row[...], axis=0, keepdims=True).astype(jnp.int32)
        for at in range(0, z.columns, 768):
            wide = min(768, z.columns - at)
            total = jnp.zeros((z.owned, wide), F32)
            for k, block in enumerate(blocks):
                inside = places[:, at : at + wide] - piece_start(z, k, z.block)
                for first in range(0, z.block, 768):
                    deep = min(768, z.block - first)
                    row = lax.broadcasted_iota(jnp.int32, (deep, wide), 0) + first
                    hot = jnp.where(row == inside, 1.0, 0.0).astype(BF16)
                    total = total + dot(block[:, first : first + deep], hot)
            ordered_inverse[s, :, at : at + wide] = total.astype(BF16)
    coarse_rows(z, ordered_inverse, arrived, message)
    here = lax.axis_index("sub")
    device = lax.broadcasted_iota(jnp.int32, (z.n, z.lanes), 0)
    for t in range(z.subs + 2):
        if t == 0:
            s, owner = z.subs - 1, lax.rem(here + z.n - 1, z.n)
        elif t == z.subs + 1:
            s, owner = 0, lax.rem(here + 1, z.n)
        else:
            s, owner = t - 1, here
        row = jnp.sum(jnp.where(device == owner, index[s], 0.0), axis=0, keepdims=True)
        column = jnp.transpose(jnp.broadcast_to(row, (z.lanes, z.lanes)))[: z.modes, 0:1].astype(jnp.int32)
        for h in range(z.subs):
            hit = column == place[h : h + 1, :]
            picks[h, t * z.modes : (t + 1) * z.modes, :] = jnp.where(hit, 1.0, 0.0).astype(BF16)


def coarse_kernel(z, arrived, ordered_inverse, message):
    coarse_rows(z, ordered_inverse, arrived, message)


def picked_rows(z, arrived, picks):
    flat = arrived[...].reshape(z.columns, z.lanes)
    return fold(z, select(z, [dot(picks[h], flat) for h in range(z.subs)])).astype(BF16)


def update_kernel(z, *refs):
    arrived, picks, start_modes, inner, left_t, right_t, before, after, first_got, second_got = refs[:10]
    chosen, message = refs[10:]
    rows = picked_rows(z, arrived, picks)
    chosen[...] = rows
    m = z.modes
    parts = []
    for s in range(z.subs):
        faces = sides(z, before, after, first_got, second_got, s)
        both = shares(z, s, rows, faces, faces)
        total = dot(inner[s], rows[(s + 1) * m : (s + 2) * m])
        parts.append(total + dot(left_t[s], both[0]) + dot(right_t[s], both[1]))
    modes = (start_modes[...] - select(z, parts)).astype(BF16)
    for k in range(z.n):
        message[k] = modes


def last_kernel(z, *refs):
    arrived, picks, remaining, solved, tall = refs[:5]
    before, after, first_got, second_got = refs[5:9]
    base_before, base_after, base_first, base_second, left_rows, right_rows = refs[9:15]
    *outs, whole = refs[15:]
    chosen = picked_rows(z, arrived, picks)
    both = []
    for s in range(z.subs):
        values = sides(z, before, after, first_got, second_got, s)
        bases = sides(z, base_before, base_after, base_first, base_second, s)
        both.append(shares(z, s, chosen, values, bases))
    step, added = corrected(z, chosen, tall, both, left_rows, right_rows)
    whole[0] = solved[...] + step
    whole[1] = remaining[...] - added
    for k, out in enumerate(outs):
        out[...] = whole[:, pl.ds(piece_start(z, k, z.own), z.own), :]


def unpack_kernel(z, *refs):
    pieces, outs = refs[: z.group], refs[z.group :]
    for at, out in enumerate(outs):
        for s in range(z.subs):
            total = jnp.zeros((z.own, z.lanes), F32)
            for k, piece in enumerate(pieces):
                place = lax.rem(lax.axis_index(GROUP) + k, z.group)
                turn = lax.rem((place - s + z.subs * z.group) * z.width, z.lanes)
                turned = pltpu.roll(piece[at], turn, 1)
                total = jnp.where(lane_mask(z, place, turned.shape), turned, total)
            out[s] = total[:, : z.cases]


def call(kernel, outs, operands, flops, scratch=(), late=(), loose=(), name=None):
    moved = sum(int(np.prod(x.shape)) * x.dtype.itemsize for x in (*operands, *outs))
    n_in, n_out = len(operands), len(outs)

    def whole(*refs):
        hbm, refs = refs[: n_in + n_out], refs[n_in + n_out :]
        vmem, refs = refs[: n_in + n_out], refs[n_in + n_out :]
        in_sems, out_sems, *rest = refs
        arriving = [pltpu.make_async_copy(hbm[i], vmem[i], in_sems.at[i]) for i in range(n_in)]
        for i in sorted(range(n_in), key=lambda i: i in late):
            arriving[i].start()
        for i, copy in enumerate(arriving):
            if i not in late:
                copy.wait()
        extra = [lambda i: arriving[i].wait()] if late else []
        kernel(*extra, *vmem, *rest)
        leaving = [pltpu.make_async_copy(vmem[n_in + i], hbm[n_in + i], out_sems.at[i]) for i in range(n_out)]
        for copy in leaving:
            copy.start()
        for copy in leaving:
            copy.wait()

    hbm_spec = pl.BlockSpec(memory_space=pltpu.HBM)
    any_spec = pl.BlockSpec(memory_space=pl.ANY)
    placed = [
        x if i in loose else pltpu.with_memory_space_constraint(x, pltpu.HBM) for i, x in enumerate(operands)
    ]
    return pl.pallas_call(
        whole,
        out_shape=[pltpu.HBM(o.shape, o.dtype) for o in outs],
        in_specs=[any_spec if i in loose else hbm_spec for i in range(n_in)],
        out_specs=[hbm_spec] * n_out,
        scratch_shapes=[
            *[pltpu.VMEM(x.shape, x.dtype) for x in (*operands, *outs)],
            pltpu.SemaphoreType.DMA((n_in,)),
            pltpu.SemaphoreType.DMA((n_out,)),
            *scratch,
        ],
        compiler_params=pltpu.CompilerParams(vmem_limit_bytes=VMEM_BYTES),
        cost_estimate=pl.CostEstimate(flops=flops, bytes_accessed=moved, transcendentals=0),
        name=name,
    )(*placed)


def shape(dims, dtype):
    return jax.ShapeDtypeStruct(dims, dtype)


def pieces_of(block, group):
    out = [block]
    for k in range(1, group):
        out.append(lax.ppermute(block, GROUP, [((g + k) % group, g) for g in range(group)]))
    return out


def body(loads, stiffness, local_inverse, coarse_basis, coarse_inverse, coarse_index, left_rows, right_rows):
    z = Sizes(loads, stiffness, coarse_basis, coarse_inverse, left_rows)
    n, group, subs, rows, lanes, modes, face = z.n, z.group, z.subs, z.rows, z.lanes, z.modes, z.face
    basis_pieces = pieces_of(jnp.swapaxes(coarse_basis, 1, 2), group)
    column = np.arange(z.columns)
    repeat = jnp.asarray(np.arange(lanes)[:, None] == column[None, :] % modes, BF16)
    own_row = jnp.asarray(np.arange(n)[:, None] == column[None, :] // modes, F32)
    place = jnp.asarray(
        (column // modes * z.owned + column % modes)[None, :] + np.arange(subs)[:, None] * modes, jnp.int32
    )
    packed_f = shape((rows, lanes), F32)
    packed_b = shape((rows, lanes), BF16)
    copies = shape((n, modes, lanes), BF16)
    tall = shape((subs, rows, lanes), BF16)
    spread = functools.partial(lax.all_to_all, axis_name="sub", split_axis=0, concat_axis=0)
    first_pairs = [(i, i + 1 if i % 2 == 0 else i - 1) for i in range(n)]
    second_pairs = [(i, (i + (1 if i % 2 else -1)) % n) for i in range(n)]
    work = 4 * subs * rows * rows * lanes

    (message,) = call(
        functools.partial(open_kernel, z),
        [shape((n, modes + DIGIT_ROWS, lanes), BF16)],
        [*basis_pieces, loads, coarse_index],
        4 * rows * lanes * lanes,
        [pltpu.VMEM((DIGIT_ROWS, lanes), F32), pltpu.VMEM((subs, modes, rows), BF16)],
        loose=range(1, group),
        name="open",
    )
    inverse_columns = pieces_of(coarse_inverse, group)
    message, local_inverse, stiffness = lax.optimization_barrier((message, local_inverse, stiffness))
    inverse_pieces = pieces_of(local_inverse, group)
    stiffness_pieces = pieces_of(stiffness, group)
    restricted = spread(message)
    arrivals = [*range(1, group), *range(group + 1, 2 * group)]
    faces = shape((subs, face, 2 * lanes), BF16)
    outer = shape((face, 2 * lanes), BF16)
    side = shape((subs, modes, face), BF16)
    (
        load_rows, solved, image, before, after, first_pair, second_pair, tall, left_t, right_t, inner, start_modes
    ) = call(
        functools.partial(first_image_kernel, z),
        [
            packed_b, packed_f, packed_f, faces, faces, outer, outer, tall, side, side,
            shape((subs, modes, modes), BF16), shape((modes, lanes), F32),
        ],
        [*inverse_pieces, *stiffness_pieces, *basis_pieces, loads, left_rows, right_rows],
        work,
        [
            pltpu.VMEM((rows, lanes), BF16), pltpu.VMEM((subs, modes, rows), BF16),
            pltpu.VMEM((subs, rows, 2 * lanes), BF16), pltpu.VMEM((subs, rows, 2 * lanes), BF16),
        ],
        late=range(2 * group),
        loose=[*arrivals, *range(2 * group + 1, 3 * group)],
        name="first_image",
    )
    second_got = lax.ppermute(second_pair, "sub", second_pairs)
    restricted, second_pair = lax.optimization_barrier((restricted, second_pair))
    near = (subs + 2) * modes
    ordered_inverse, picks, message = call(
        functools.partial(order_kernel, z),
        [shape((subs, z.owned, z.columns), BF16), shape((subs, near, z.columns), BF16), copies],
        [*inverse_columns, restricted, repeat, own_row, place],
        2 * z.owned * z.total * z.total,
        loose=range(1, group + 1),
        name="order",
    )
    coarse = spread(message)
    first_got = lax.ppermute(first_pair, "sub", first_pairs)
    chosen, message = call(
        functools.partial(update_kernel, z),
        [shape((near, lanes), BF16), copies],
        [coarse, picks, start_modes, inner, left_t, right_t, before, after, first_got, second_got],
        work // 64,
        loose=[0, 8, 9],
        name="update",
    )
    restricted = spread(message)

    bases = [before, after, first_got, second_got]
    faces = shape((subs, face, lanes), BF16)
    outer = shape((face, lanes), BF16)
    solved, remaining, before, after, first_pair, second_pair = call(
        functools.partial(second_image_kernel, z),
        [packed_f, packed_f, faces, faces, outer, outer],
        [
            *inverse_pieces, *stiffness_pieces, load_rows, image, tall, solved, chosen,
            *bases, left_rows, right_rows,
        ],
        work,
        [pltpu.VMEM((rows, lanes), BF16), pltpu.VMEM((rows, lanes), BF16)],
        late=range(2 * group),
        loose=[*arrivals, 2 * group + 7, 2 * group + 8],
        name="second_image",
    )
    second_got = lax.ppermute(second_pair, "sub", second_pairs)
    (message,) = call(
        functools.partial(coarse_kernel, z),
        [copies],
        [restricted, ordered_inverse],
        work // 64,
        loose=[0],
        name="coarse",
    )
    coarse = spread(message)
    first_got = lax.ppermute(first_pair, "sub", first_pairs)
    parts = call(
        functools.partial(last_kernel, z),
        [shape((2, z.own, lanes), F32)] * group,
        [
            coarse, picks, remaining, solved, tall,
            before, after, first_got, second_got, *bases, left_rows, right_rows,
        ],
        work // 8,
        [pltpu.VMEM((2, rows, lanes), F32)],
        loose=[0, 7, 8, 11, 12],
        name="last",
    )
    swapped = [parts[0]]
    for k in range(1, group):
        swapped.append(lax.ppermute(parts[k], GROUP, [(g, (g + k) % group) for g in range(group)]))
    swapped = [swapped[(group - k) % group] for k in range(group)]
    out = shape((subs, z.own, z.cases), F32)
    return tuple(
        call(
            functools.partial(unpack_kernel, z), [out, out], swapped, work // 64, loose=range(1, group), name="unpack"
        )
    )


def solution(mesh):
    return jax.shard_map(
        body,
        mesh=mesh,
        in_specs=(
            P("sub", None, None),
            P("sub", GROUP, None),
            P("sub", GROUP, None),
            P("sub", GROUP, None),
            P("sub", GROUP),
            P("sub", None),
            P("sub", None),
            P("sub", None),
        ),
        out_specs=(P("sub", GROUP, None), P("sub", GROUP, None)),
        check_vma=False,
    )
```

```python
import functools

import jax
import jax.numpy as jnp
import numpy as np
from jax import lax
from jax.experimental import pallas as pl
from jax.experimental.pallas import tpu as pltpu
from jax.sharding import PartitionSpec as P

GROUP = ("crow", "ccol")
F32 = jnp.float32
BF16 = jnp.bfloat16
VMEM_BYTES = 48 * 1024 * 1024
DIGIT_ROWS = 16
DIGIT_BITS = 8
DIGIT = 1 << DIGIT_BITS


def dot(a, b):
    return lax.dot_general(a, b, (((1,), (0,)), ((), ())), preferred_element_type=F32)


def dot_tn(a, b):
    return lax.dot_general(a, b, (((0,), (0,)), ((), ())), preferred_element_type=F32)


def dot_nt(a, b):
    return lax.dot_general(a, b, (((1,), (1,)), ((), ())), preferred_element_type=F32)


class Sizes:
    def __init__(self, loads, stiffness, coarse_basis, coarse_inverse, left_rows):
        self.n = lax.axis_size("sub")
        self.group = lax.axis_size(GROUP)
        self.subs, self.rows, self.cases = loads.shape
        self.own = stiffness.shape[1]
        self.modes = coarse_basis.shape[2]
        self.owned, self.block = coarse_inverse.shape
        self.total = self.block * self.group
        self.face = left_rows.shape[1]
        self.width = self.cases // self.group
        self.lanes = max(self.cases, -(-self.subs * self.width // 128) * 128)
        self.columns = self.n * self.modes


def lane_mask(z, block, shape):
    lane = lax.broadcasted_iota(jnp.int32, shape, len(shape) - 1)
    return (lane >= block * z.width) & (lane < (block + 1) * z.width)


def select(z, parts):
    out = jnp.zeros_like(parts[0])
    for s, part in enumerate(parts):
        out = jnp.where(lane_mask(z, s, part.shape), part, out)
    return out


def fold(z, packed):
    if z.lanes == z.subs * z.width:
        out = packed
        for k in range(1, z.subs):
            out = out + pltpu.roll(packed, k * z.width, 1)
        return out
    out = packed
    for k in range(1, z.subs):
        out = out + pltpu.roll(packed, k * z.width, 1)
        out = out + pltpu.roll(packed, z.lanes - k * z.width, 1)
    return out


def lane_matrix(z, source, target):
    row = lax.broadcasted_iota(jnp.int32, (z.lanes, z.lanes), 0)
    lane = lax.broadcasted_iota(jnp.int32, (z.lanes, z.lanes), 1)
    hit = (row - source == lane - target) & (lane >= target) & (lane < target + z.width)
    return jnp.where(hit, 1.0, 0.0).astype(BF16)


def piece_start(z, k, size):
    place = lax.rem(lax.axis_index(GROUP) + k, z.group)
    return pl.multiple_of(place * size, size)


def scatter_matrix(z, rows_of):
    row = lax.broadcasted_iota(jnp.int32, (z.rows, z.face), 0)
    return jnp.where(row == rows_of, 1.0, 0.0).astype(BF16)


def pick_matrix(z, rows_of):
    column = jnp.transpose(jnp.broadcast_to(rows_of.astype(F32), (z.face, z.face)))[:, 0:1].astype(jnp.int32)
    row = lax.broadcasted_iota(jnp.int32, (z.face, z.rows), 1)
    return jnp.where(row == column, 1.0, 0.0).astype(BF16)


def even():
    return lax.rem(lax.axis_index("sub"), 2) == 0


def case_matrix(z, s):
    row = lax.broadcasted_iota(jnp.int32, (z.cases, z.lanes), 0)
    lane = lax.broadcasted_iota(jnp.int32, (z.cases, z.lanes), 1)
    hit = (row - lax.axis_index(GROUP) * z.width == lane - s * z.width) & lane_mask(z, s, row.shape)
    return jnp.where(hit, 1.0, 0.0).astype(BF16)


def join_basis(z, pieces, basis_t):
    for k, piece in enumerate(pieces):
        basis_t[:, :, pl.ds(piece_start(z, k, z.own), z.own)] = piece[...]


def open_kernel(z, *refs):
    pieces = refs[: z.group]
    loads, index, message, digits, basis_t = refs[z.group :]
    join_basis(z, pieces, basis_t)
    total = jnp.zeros((z.modes, z.lanes), F32)
    for s in range(z.subs):
        total = total + dot(dot(basis_t[s], loads[s]).astype(BF16), case_matrix(z, s))
    modes = total.astype(BF16)
    digits[...] = jnp.zeros(digits.shape, F32)
    for s in range(z.subs):
        places = index[s : s + 1, :]
        digits[2 * s : 2 * s + 1, : z.modes] = (places >> DIGIT_BITS).astype(F32)
        digits[2 * s + 1 : 2 * s + 2, : z.modes] = (places & (DIGIT - 1)).astype(F32)
    for k in range(z.n):
        message[k, : z.modes, :] = modes
        message[k, z.modes :, :] = digits[...].astype(BF16)


def multiply(z, pieces, vector, store):
    for k, piece in enumerate(pieces):
        parts = [dot(piece[s], vector) for s in range(z.subs)]
        store(piece_start(z, k, z.own), select(z, parts))


def face_rows(z, pick, image_b, s):
    return dot(dot(pick, image_b).astype(BF16), lane_matrix(z, s * z.width, 0))


def store_faces(z, before, after, first_pair, second_pair):
    first, last = before[0], after[z.subs - 1]
    first_pair[...] = jnp.where(even(), last, first)
    second_pair[...] = jnp.where(even(), first, last)


def sides(z, before, after, first_pair, second_pair, s):
    if s == 0:
        from_before = jnp.where(even(), second_pair[...], first_pair[...])
    else:
        from_before = after[s - 1]
    if s == z.subs - 1:
        from_after = jnp.where(even(), first_pair[...], second_pair[...])
    else:
        from_after = before[s + 1]
    return from_before, from_after


def shares(z, s, chosen, faces, bases=None):
    m, half = z.modes, z.lanes // 2
    moved = lane_matrix(z, 0, s * z.width)
    out = []
    for side, at in ((0, s), (1, s + 2)):
        own = chosen[at * m : (at + 1) * m]
        below = jnp.concatenate([own, jnp.zeros((half - m, z.lanes), BF16)], axis=0)
        if bases is None:
            total = dot(faces[side], jnp.concatenate([moved[:half], below], axis=0))
        else:
            above = jnp.zeros((half, z.lanes), BF16)
            total = dot(faces[side], moved) + dot(bases[side], jnp.concatenate([above, below], axis=0))
        out.append(total.astype(BF16))
    return out


def corrected(z, chosen, tall, both, left_rows, right_rows):
    images, steps = [], []
    m, at = z.modes, z.lanes // 2
    for s in range(z.subs):
        own = chosen[(s + 1) * m : (s + 2) * m]
        none = jnp.zeros((at - m, z.lanes), BF16)
        nil = jnp.zeros((at, z.lanes), BF16)
        left = jnp.concatenate([tall[s], scatter_matrix(z, left_rows[s : s + 1, :])], axis=1)
        right = scatter_matrix(z, right_rows[s : s + 1, :])
        image = jnp.concatenate([own, none, nil, both[s][0]], axis=0)
        step = jnp.concatenate([nil, own, none, jnp.zeros((z.face, z.lanes), BF16)], axis=0)
        total = dot(left, jnp.concatenate([image, step], axis=1))
        images.append(total[:, : z.lanes] + dot(right, both[s][1]))
        steps.append(total[:, z.lanes :])
    return select(z, steps), select(z, images)


def first_image_kernel(z, wait, *refs):
    inverse, stiffness = refs[: z.group], refs[z.group : 2 * z.group]
    pieces = refs[2 * z.group : 3 * z.group]
    loads, left_rows, right_rows = refs[3 * z.group : 3 * z.group + 3]
    load_rows, solved, image, before, after, first_pair, second_pair = refs[3 * z.group + 3 : 3 * z.group + 10]
    tall, left_t, right_t, inner, start_modes, rounded, basis_t, both, images = refs[3 * z.group + 10 :]
    join_basis(z, pieces, basis_t)
    packed = dot(loads[0], case_matrix(z, 0))
    for s in range(1, z.subs):
        packed = packed + dot(loads[s], case_matrix(z, s))
    load_rows[...] = packed.astype(BF16)
    for k in range(z.group):
        wait(k)

    def store_solved(start, value):
        solved[pl.ds(start, z.own), :] = value
        rounded[pl.ds(start, z.own), :] = value.astype(BF16)

    multiply(z, inverse, load_rows[...], store_solved)
    solved_b = rounded[...]
    half = z.lanes // 2
    for s in range(z.subs):
        basis = jnp.transpose(basis_t[s].astype(F32)).astype(BF16)
        tall[s, :, half : half + z.modes] = basis
        tall[s, :, half + z.modes :] = jnp.zeros((z.rows, half - z.modes), BF16)
        both[s, :, : z.lanes] = solved_b
        both[s, :, z.lanes : z.lanes + z.modes] = basis
        both[s, :, z.lanes + z.modes :] = jnp.zeros((z.rows, z.lanes - z.modes), BF16)
    for k, piece in enumerate(stiffness):
        wait(z.group + k)
        start = piece_start(z, k, z.own)
        parts = [dot(piece[s], both[s]) for s in range(z.subs)]
        image[pl.ds(start, z.own), :] = select(z, [part[:, : z.lanes] for part in parts])
        for s in range(z.subs):
            images[s, pl.ds(start, z.own), :] = parts[s].astype(BF16)
    left = (load_rows[...].astype(F32) - image[...]).astype(BF16)
    start_modes[...] = select(z, [dot(basis_t[s], left) for s in range(z.subs)])
    for s in range(z.subs):
        image_basis = images[s, :, z.lanes :]
        tall[s, :, :half] = image_basis[:, :half]
        inner[s] = dot(basis_t[s], image_basis)[:, : z.modes].astype(BF16)
        placed = jnp.concatenate([jnp.zeros((z.rows, half), BF16), image_basis[:, :half]], axis=1)
        for rows_ref, out, side_t in ((left_rows, before, left_t), (right_rows, after, right_t)):
            pick = pick_matrix(z, rows_ref[s : s + 1, :])
            side_t[s] = dot_nt(basis_t[s], pick).astype(BF16)
            out[s] = (face_rows(z, pick, images[s, :, : z.lanes], s) + dot(pick, placed)).astype(BF16)
    store_faces(z, before, after, first_pair, second_pair)


def second_image_kernel(z, wait, *refs):
    inverse, stiffness = refs[: z.group], refs[z.group : 2 * z.group]
    rest = refs[2 * z.group :]
    load_rows, old_image, tall, old_solved, chosen = rest[:5]
    before, after, first_got, second_got, left_rows, right_rows = rest[5:11]
    solved, remaining, new_before, new_after, first_pair, second_pair, rounded, image = rest[11:]
    both = []
    for s in range(z.subs):
        faces = sides(z, before, after, first_got, second_got, s)
        both.append(shares(z, s, chosen, faces))
    step, added = corrected(z, chosen, tall, both, left_rows, right_rows)
    residual = (load_rows[...].astype(F32) - old_image[...] - added).astype(BF16)
    solved[...] = old_solved[...] + step
    for k in range(z.group):
        wait(k)

    def store_solved(start, value):
        value = value + solved[pl.ds(start, z.own), :]
        solved[pl.ds(start, z.own), :] = value
        rounded[pl.ds(start, z.own), :] = value.astype(BF16)

    multiply(z, inverse, residual, store_solved)

    def store_image(start, value):
        place = pl.ds(start, z.own)
        remaining[place, :] = load_rows[place, :].astype(F32) - value
        image[place, :] = value.astype(BF16)

    for k in range(z.group):
        wait(z.group + k)
    multiply(z, stiffness, rounded[...], store_image)
    image_b = image[...]
    for s in range(z.subs):
        new_before[s] = face_rows(z, pick_matrix(z, left_rows[s : s + 1, :]), image_b, s).astype(BF16)
        new_after[s] = face_rows(z, pick_matrix(z, right_rows[s : s + 1, :]), image_b, s).astype(BF16)
    store_faces(z, new_before, new_after, first_pair, second_pair)


def digit_row(shape, row):
    return lax.broadcasted_iota(jnp.int32, shape, 1) == row


def coarse_rows(z, ordered_inverse, arrived, message):
    flat = arrived[:, : z.modes, :].reshape(z.columns, z.lanes)
    rows = fold(z, select(z, [dot(ordered_inverse[s], flat) for s in range(z.subs)]))
    packed = select(z, [rows[s * z.modes : (s + 1) * z.modes, :] for s in range(z.subs)]).astype(BF16)
    for k in range(z.n):
        message[k] = packed


def order_kernel(z, *refs):
    blocks = refs[: z.group]
    arrived, repeat, own_row, place, ordered_inverse, picks, message = refs[z.group :]
    digits = arrived[:, z.modes :, :].astype(F32)
    index = []
    for s in range(z.subs):
        high = jnp.sum(jnp.where(digit_row(digits.shape, 2 * s), digits, 0.0), axis=1)
        low = jnp.sum(jnp.where(digit_row(digits.shape, 2 * s + 1), digits, 0.0), axis=1)
        index.append(high * DIGIT + low)
        spread = dot(high.astype(BF16), repeat[...]) * DIGIT + dot(low.astype(BF16), repeat[...])
        places = jnp.sum(spread * own_row[...], axis=0, keepdims=True).astype(jnp.int32)
        for at in range(0, z.columns, 768):
            wide = min(768, z.columns - at)
            total = jnp.zeros((z.owned, wide), F32)
            for k, block in enumerate(blocks):
                inside = places[:, at : at + wide] - piece_start(z, k, z.block)
                for first in range(0, z.block, 768):
                    deep = min(768, z.block - first)
                    row = lax.broadcasted_iota(jnp.int32, (deep, wide), 0) + first
                    hot = jnp.where(row == inside, 1.0, 0.0).astype(BF16)
                    total = total + dot(block[:, first : first + deep], hot)
            ordered_inverse[s, :, at : at + wide] = total.astype(BF16)
    coarse_rows(z, ordered_inverse, arrived, message)
    here = lax.axis_index("sub")
    device = lax.broadcasted_iota(jnp.int32, (z.n, z.lanes), 0)
    for t in range(z.subs + 2):
        if t == 0:
            s, owner = z.subs - 1, lax.rem(here + z.n - 1, z.n)
        elif t == z.subs + 1:
            s, owner = 0, lax.rem(here + 1, z.n)
        else:
            s, owner = t - 1, here
        row = jnp.sum(jnp.where(device == owner, index[s], 0.0), axis=0, keepdims=True)
        column = jnp.transpose(jnp.broadcast_to(row, (z.lanes, z.lanes)))[: z.modes, 0:1].astype(jnp.int32)
        for h in range(z.subs):
            hit = column == place[h : h + 1, :]
            picks[h, t * z.modes : (t + 1) * z.modes, :] = jnp.where(hit, 1.0, 0.0).astype(BF16)


def coarse_kernel(z, arrived, ordered_inverse, message):
    coarse_rows(z, ordered_inverse, arrived, message)


def picked_rows(z, arrived, picks):
    flat = arrived[...].reshape(z.columns, z.lanes)
    return fold(z, select(z, [dot(picks[h], flat) for h in range(z.subs)])).astype(BF16)


def update_kernel(z, *refs):
    arrived, picks, start_modes, inner, left_t, right_t, before, after, first_got, second_got = refs[:10]
    chosen, message = refs[10:]
    rows = picked_rows(z, arrived, picks)
    chosen[...] = rows
    m = z.modes
    parts = []
    for s in range(z.subs):
        faces = sides(z, before, after, first_got, second_got, s)
        both = shares(z, s, rows, faces)
        total = dot(inner[s], rows[(s + 1) * m : (s + 2) * m])
        parts.append(total + dot(left_t[s], both[0]) + dot(right_t[s], both[1]))
    modes = (start_modes[...] - select(z, parts)).astype(BF16)
    for k in range(z.n):
        message[k] = modes


def last_kernel(z, *refs):
    arrived, picks, remaining, solved, tall = refs[:5]
    before, after, first_got, second_got = refs[5:9]
    base_before, base_after, base_first, base_second, left_rows, right_rows = refs[9:15]
    *outs, whole = refs[15:]
    chosen = picked_rows(z, arrived, picks)
    both = []
    for s in range(z.subs):
        values = sides(z, before, after, first_got, second_got, s)
        bases = sides(z, base_before, base_after, base_first, base_second, s)
        both.append(shares(z, s, chosen, values, bases))
    step, added = corrected(z, chosen, tall, both, left_rows, right_rows)
    whole[0] = solved[...] + step
    whole[1] = remaining[...] - added
    for k, out in enumerate(outs):
        out[...] = whole[:, pl.ds(piece_start(z, k, z.own), z.own), :]


def unpack_kernel(z, *refs):
    pieces, outs = refs[: z.group], refs[z.group :]
    for at, out in enumerate(outs):
        for s in range(z.subs):
            total = jnp.zeros((z.own, z.lanes), F32)
            for k, piece in enumerate(pieces):
                place = lax.rem(lax.axis_index(GROUP) + k, z.group)
                turn = lax.rem((place - s + z.subs * z.group) * z.width, z.lanes)
                turned = pltpu.roll(piece[at], turn, 1)
                total = jnp.where(lane_mask(z, place, turned.shape), turned, total)
            out[s] = total[:, : z.cases]


def call(kernel, outs, operands, flops, scratch=(), late=(), loose=(), name=None):
    moved = sum(int(np.prod(x.shape)) * x.dtype.itemsize for x in (*operands, *outs))
    n_in, n_out = len(operands), len(outs)

    def whole(*refs):
        hbm, refs = refs[: n_in + n_out], refs[n_in + n_out :]
        vmem, refs = refs[: n_in + n_out], refs[n_in + n_out :]
        in_sems, out_sems, *rest = refs
        arriving = [pltpu.make_async_copy(hbm[i], vmem[i], in_sems.at[i]) for i in range(n_in)]
        for i in sorted(range(n_in), key=lambda i: i in late):
            arriving[i].start()
        for i, copy in enumerate(arriving):
            if i not in late:
                copy.wait()
        extra = [lambda i: arriving[i].wait()] if late else []
        kernel(*extra, *vmem, *rest)
        leaving = [pltpu.make_async_copy(vmem[n_in + i], hbm[n_in + i], out_sems.at[i]) for i in range(n_out)]
        for copy in leaving:
            copy.start()
        for copy in leaving:
            copy.wait()

    hbm_spec = pl.BlockSpec(memory_space=pltpu.HBM)
    any_spec = pl.BlockSpec(memory_space=pl.ANY)
    placed = [
        x if i in loose else pltpu.with_memory_space_constraint(x, pltpu.HBM) for i, x in enumerate(operands)
    ]
    return pl.pallas_call(
        whole,
        out_shape=[pltpu.HBM(o.shape, o.dtype) for o in outs],
        in_specs=[any_spec if i in loose else hbm_spec for i in range(n_in)],
        out_specs=[hbm_spec] * n_out,
        scratch_shapes=[
            *[pltpu.VMEM(x.shape, x.dtype) for x in (*operands, *outs)],
            pltpu.SemaphoreType.DMA((n_in,)),
            pltpu.SemaphoreType.DMA((n_out,)),
            *scratch,
        ],
        compiler_params=pltpu.CompilerParams(vmem_limit_bytes=VMEM_BYTES),
        cost_estimate=pl.CostEstimate(flops=flops, bytes_accessed=moved, transcendentals=0),
        name=name,
    )(*placed)


def shape(dims, dtype):
    return jax.ShapeDtypeStruct(dims, dtype)


def pieces_of(block, group):
    out = [block]
    for k in range(1, group):
        out.append(lax.ppermute(block, GROUP, [((g + k) % group, g) for g in range(group)]))
    return out


def body(loads, stiffness, local_inverse, coarse_basis, coarse_inverse, coarse_index, left_rows, right_rows):
    z = Sizes(loads, stiffness, coarse_basis, coarse_inverse, left_rows)
    n, group, subs, rows, lanes, modes, face = z.n, z.group, z.subs, z.rows, z.lanes, z.modes, z.face
    basis_pieces = pieces_of(jnp.swapaxes(coarse_basis, 1, 2), group)
    basis_pieces, local_inverse, stiffness = lax.optimization_barrier((basis_pieces, local_inverse, stiffness))
    column = np.arange(z.columns)
    repeat = jnp.asarray(np.arange(lanes)[:, None] == column[None, :] % modes, BF16)
    own_row = jnp.asarray(np.arange(n)[:, None] == column[None, :] // modes, F32)
    place = jnp.asarray(
        (column // modes * z.owned + column % modes)[None, :] + np.arange(subs)[:, None] * modes, jnp.int32
    )
    packed_f = shape((rows, lanes), F32)
    packed_b = shape((rows, lanes), BF16)
    copies = shape((n, modes, lanes), BF16)
    tall = shape((subs, rows, lanes), BF16)
    spread = functools.partial(lax.all_to_all, axis_name="sub", split_axis=0, concat_axis=0)
    first_pairs = [(i, i + 1 if i % 2 == 0 else i - 1) for i in range(n)]
    second_pairs = [(i, (i + (1 if i % 2 else -1)) % n) for i in range(n)]
    work = 4 * subs * rows * rows * lanes

    (message,) = call(
        functools.partial(open_kernel, z),
        [shape((n, modes + DIGIT_ROWS, lanes), BF16)],
        [*basis_pieces, loads, coarse_index],
        4 * rows * lanes * lanes,
        [pltpu.VMEM((DIGIT_ROWS, lanes), F32), pltpu.VMEM((subs, modes, rows), BF16)],
        loose=range(1, group),
        name="open",
    )
    inverse_columns = pieces_of(coarse_inverse, group)
    inverse_pieces = pieces_of(local_inverse, group)
    stiffness_pieces = pieces_of(stiffness, group)
    restricted = spread(message)
    arrivals = [*range(1, group), *range(group + 1, 2 * group)]
    faces = shape((subs, face, lanes), BF16)
    outer = shape((face, lanes), BF16)
    side = shape((subs, modes, face), BF16)
    (
        load_rows, solved, image, before, after, first_pair, second_pair, tall, left_t, right_t, inner, start_modes
    ) = call(
        functools.partial(first_image_kernel, z),
        [
            packed_b, packed_f, packed_f, faces, faces, outer, outer, tall, side, side,
            shape((subs, modes, modes), BF16), shape((modes, lanes), F32),
        ],
        [*inverse_pieces, *stiffness_pieces, *basis_pieces, loads, left_rows, right_rows],
        work,
        [
            pltpu.VMEM((rows, lanes), BF16), pltpu.VMEM((subs, modes, rows), BF16),
            pltpu.VMEM((subs, rows, 2 * lanes), BF16), pltpu.VMEM((subs, rows, 2 * lanes), BF16),
        ],
        late=range(2 * group),
        loose=[*arrivals, *range(2 * group + 1, 3 * group)],
        name="first_image",
    )
    second_got = lax.ppermute(second_pair, "sub", second_pairs)
    restricted, second_pair = lax.optimization_barrier((restricted, second_pair))
    near = (subs + 2) * modes
    ordered_inverse, picks, message = call(
        functools.partial(order_kernel, z),
        [shape((subs, z.owned, z.columns), BF16), shape((subs, near, z.columns), BF16), copies],
        [*inverse_columns, restricted, repeat, own_row, place],
        2 * z.owned * z.total * z.total,
        loose=range(1, group + 1),
        name="order",
    )
    coarse = spread(message)
    first_got = lax.ppermute(first_pair, "sub", first_pairs)
    chosen, message = call(
        functools.partial(update_kernel, z),
        [shape((near, lanes), BF16), copies],
        [coarse, picks, start_modes, inner, left_t, right_t, before, after, first_got, second_got],
        work // 64,
        loose=[0, 8, 9],
        name="update",
    )
    restricted = spread(message)

    bases = [before, after, first_got, second_got]
    solved, remaining, before, after, first_pair, second_pair = call(
        functools.partial(second_image_kernel, z),
        [packed_f, packed_f, faces, faces, outer, outer],
        [
            *inverse_pieces, *stiffness_pieces, load_rows, image, tall, solved, chosen,
            *bases, left_rows, right_rows,
        ],
        work,
        [pltpu.VMEM((rows, lanes), BF16), pltpu.VMEM((rows, lanes), BF16)],
        late=range(2 * group),
        loose=[*arrivals, 2 * group + 7, 2 * group + 8],
        name="second_image",
    )
    second_got = lax.ppermute(second_pair, "sub", second_pairs)
    restricted, remaining = lax.optimization_barrier((restricted, remaining))
    (message,) = call(
        functools.partial(coarse_kernel, z),
        [copies],
        [restricted, ordered_inverse],
        work // 64,
        loose=[0],
        name="coarse",
    )
    coarse = spread(message)
    first_got = lax.ppermute(first_pair, "sub", first_pairs)
    parts = call(
        functools.partial(last_kernel, z),
        [shape((2, z.own, lanes), F32)] * group,
        [
            coarse, picks, remaining, solved, tall,
            before, after, first_got, second_got, *bases, left_rows, right_rows,
        ],
        work // 8,
        [pltpu.VMEM((2, rows, lanes), F32)],
        loose=[0, 7, 8, 11, 12],
        name="last",
    )
    swapped = [parts[0]]
    for k in range(1, group):
        swapped.append(lax.ppermute(parts[k], GROUP, [(g, (g + k) % group) for g in range(group)]))
    swapped = [swapped[(group - k) % group] for k in range(group)]
    out = shape((subs, z.own, z.cases), F32)
    return tuple(
        call(
            functools.partial(unpack_kernel, z), [out, out], swapped, work // 64, loose=range(1, group), name="unpack"
        )
    )


def solution(mesh):
    return jax.shard_map(
        body,
        mesh=mesh,
        in_specs=(
            P("sub", None, None),
            P("sub", GROUP, None),
            P("sub", GROUP, None),
            P("sub", GROUP, None),
            P("sub", GROUP),
            P("sub", None),
            P("sub", None),
            P("sub", None),
        ),
        out_specs=(P("sub", GROUP, None), P("sub", GROUP, None)),
        check_vma=False,
    )
```

```python
import functools

import jax
import jax.numpy as jnp
import numpy as np
from jax import lax
from jax.experimental import pallas as pl
from jax.experimental.pallas import tpu as pltpu
from jax.sharding import PartitionSpec as P

GROUP = ("crow", "ccol")
F32 = jnp.float32
BF16 = jnp.bfloat16
VMEM_BYTES = 48 * 1024 * 1024
DIGIT_ROWS = 16
DIGIT_BITS = 8
DIGIT = 1 << DIGIT_BITS


def dot(a, b):
    return lax.dot_general(a, b, (((1,), (0,)), ((), ())), preferred_element_type=F32)


def dot_tn(a, b):
    return lax.dot_general(a, b, (((0,), (0,)), ((), ())), preferred_element_type=F32)


def dot_nt(a, b):
    return lax.dot_general(a, b, (((1,), (1,)), ((), ())), preferred_element_type=F32)


class Sizes:
    def __init__(self, loads, stiffness, coarse_basis, coarse_inverse, left_rows):
        self.n = lax.axis_size("sub")
        self.group = lax.axis_size(GROUP)
        self.subs, self.rows, self.cases = loads.shape
        self.own = stiffness.shape[1]
        self.modes = coarse_basis.shape[2]
        self.owned, self.block = coarse_inverse.shape
        self.total = self.block * self.group
        self.face = left_rows.shape[1]
        self.width = self.cases // self.group
        self.lanes = max(self.cases, -(-self.subs * self.width // 128) * 128)
        self.columns = self.n * self.modes


def lane_mask(z, block, shape):
    lane = lax.broadcasted_iota(jnp.int32, shape, len(shape) - 1)
    return (lane >= block * z.width) & (lane < (block + 1) * z.width)


def select(z, parts):
    out = jnp.zeros_like(parts[0])
    for s, part in enumerate(parts):
        out = jnp.where(lane_mask(z, s, part.shape), part, out)
    return out


def fold(z, packed):
    if z.lanes == z.subs * z.width:
        out = packed
        for k in range(1, z.subs):
            out = out + pltpu.roll(packed, k * z.width, 1)
        return out
    out = packed
    for k in range(1, z.subs):
        out = out + pltpu.roll(packed, k * z.width, 1)
        out = out + pltpu.roll(packed, z.lanes - k * z.width, 1)
    return out


def lane_matrix(z, source, target, width=None):
    row = lax.broadcasted_iota(jnp.int32, (z.lanes, z.lanes), 0)
    lane = lax.broadcasted_iota(jnp.int32, (z.lanes, z.lanes), 1)
    hit = (row - source == lane - target) & (lane >= target) & (lane < target + (width or z.width))
    return jnp.where(hit, 1.0, 0.0).astype(BF16)


def piece_start(z, k, size):
    place = lax.rem(lax.axis_index(GROUP) + k, z.group)
    return pl.multiple_of(place * size, size)


def pick_matrix(z, rows_of):
    column = jnp.transpose(jnp.broadcast_to(rows_of.astype(F32), (z.face, z.face)))[:, 0:1].astype(jnp.int32)
    row = lax.broadcasted_iota(jnp.int32, (z.face, z.rows), 1)
    return jnp.where(row == column, 1.0, 0.0).astype(BF16)


def even():
    return lax.rem(lax.axis_index("sub"), 2) == 0


def case_matrix(z, s):
    row = lax.broadcasted_iota(jnp.int32, (z.cases, z.lanes), 0)
    lane = lax.broadcasted_iota(jnp.int32, (z.cases, z.lanes), 1)
    hit = (row - lax.axis_index(GROUP) * z.width == lane - s * z.width) & lane_mask(z, s, row.shape)
    return jnp.where(hit, 1.0, 0.0).astype(BF16)


def join_basis(z, pieces, basis_t):
    for k, piece in enumerate(pieces):
        basis_t[:, :, pl.ds(piece_start(z, k, z.own), z.own)] = piece[...]


def open_kernel(z, *refs):
    pieces = refs[: z.group]
    loads, index, message, digits, basis_t = refs[z.group :]
    join_basis(z, pieces, basis_t)
    total = jnp.zeros((z.modes, z.lanes), F32)
    for s in range(z.subs):
        total = total + dot(dot(basis_t[s], loads[s]).astype(BF16), case_matrix(z, s))
    modes = total.astype(BF16)
    digits[...] = jnp.zeros(digits.shape, F32)
    for s in range(z.subs):
        places = index[s : s + 1, :]
        digits[2 * s : 2 * s + 1, : z.modes] = (places >> DIGIT_BITS).astype(F32)
        digits[2 * s + 1 : 2 * s + 2, : z.modes] = (places & (DIGIT - 1)).astype(F32)
    for k in range(z.n):
        message[k, : z.modes, :] = modes
        message[k, z.modes :, :] = digits[...].astype(BF16)


def multiply(z, pieces, vector, store):
    for k, piece in enumerate(pieces):
        parts = [dot(piece[s], vector) for s in range(z.subs)]
        store(k, piece_start(z, k, z.own), select(z, parts))


def pick_both(z, left_rows, right_rows, s):
    return jnp.concatenate(
        [pick_matrix(z, left_rows[s : s + 1, :]), pick_matrix(z, right_rows[s : s + 1, :])], axis=0
    )


def store_faces(z, before, after, first_pair, second_pair):
    first, last = before[0], after[z.subs - 1]
    first_pair[...] = jnp.where(even(), last, first)
    second_pair[...] = jnp.where(even(), first, last)


def sides(z, before, after, first_pair, second_pair, s):
    if s == 0:
        from_before = jnp.where(even(), second_pair[...], first_pair[...])
    else:
        from_before = after[s - 1]
    if s == z.subs - 1:
        from_after = jnp.where(even(), first_pair[...], second_pair[...])
    else:
        from_after = before[s + 1]
    return from_before, from_after


def shares(z, s, chosen, faces, bases=None):
    m, half = z.modes, z.lanes // 2
    moved = lane_matrix(z, 0, s * z.width)
    out = []
    for side, at in ((0, s), (1, s + 2)):
        own = chosen[at * m : (at + 1) * m]
        below = jnp.concatenate([own, jnp.zeros((half - m, z.lanes), BF16)], axis=0)
        if bases is None:
            total = dot(faces[side], jnp.concatenate([moved[:half], below], axis=0))
        else:
            above = jnp.zeros((half, z.lanes), BF16)
            total = dot(faces[side], moved) + dot(bases[side], jnp.concatenate([above, below], axis=0))
        out.append(total)
    return out


def correction_side(z, chosen, s, share):
    m, half = z.modes, z.lanes // 2
    own = chosen[(s + 1) * m : (s + 2) * m]
    none = jnp.zeros((half - m, z.lanes), BF16)
    nil = jnp.zeros((half, z.lanes), BF16)
    image = jnp.concatenate([own, none, nil, share], axis=0)
    step = jnp.concatenate([nil, own, none, jnp.zeros((z.face, z.lanes), BF16)], axis=0)
    return jnp.concatenate([image, step], axis=1)


def scatter_matrix(z, rows_of, start, count):
    row = lax.broadcasted_iota(jnp.int32, (count, z.face), 0) + start
    return jnp.where(row == rows_of, 1.0, 0.0).astype(BF16)


def first_image_kernel(z, wait, *refs):
    inverse, stiffness = refs[: z.group], refs[z.group : 2 * z.group]
    pieces = refs[2 * z.group : 3 * z.group]
    loads, left_rows, right_rows = refs[3 * z.group : 3 * z.group + 3]
    load_rows, solved, image, before, after, first_pair, second_pair = refs[3 * z.group + 3 : 3 * z.group + 10]
    tall, left_t, right_t, inner, start_modes, rounded, basis_t, both, images = refs[3 * z.group + 10 :]
    join_basis(z, pieces, basis_t)
    packed = dot(loads[0], case_matrix(z, 0))
    for s in range(1, z.subs):
        packed = packed + dot(loads[s], case_matrix(z, s))
    load_rows[...] = packed.astype(BF16)
    for k in range(z.group):
        wait(k)

    def store_solved(k, start, value):
        solved[pl.ds(start, z.own), :] = value
        rounded[pl.ds(start, z.own), :] = value.astype(BF16)

    multiply(z, inverse, load_rows[...], store_solved)
    solved_b = rounded[...]
    half = z.lanes // 2
    for s in range(z.subs):
        basis = jnp.transpose(basis_t[s].astype(F32)).astype(BF16)
        tall[s, :, half : half + z.modes] = basis
        tall[s, :, half + z.modes :] = jnp.zeros((z.rows, half - z.modes), BF16)
        both[s, :, : z.lanes] = solved_b
        both[s, :, z.lanes : z.lanes + z.modes] = basis
        both[s, :, z.lanes + z.modes :] = jnp.zeros((z.rows, z.lanes - z.modes), BF16)
    for k, piece in enumerate(stiffness):
        wait(z.group + k)
        start = piece_start(z, k, z.own)
        parts = [dot(piece[s], both[s]) for s in range(z.subs)]
        image[pl.ds(start, z.own), :] = select(z, [part[:, : z.lanes] for part in parts])
        for s in range(z.subs):
            images[s, pl.ds(start, z.own), :] = parts[s].astype(BF16)
    left = (load_rows[...].astype(F32) - image[...]).astype(BF16)
    begun = []
    for s in range(z.subs):
        image_basis = images[s, :, z.lanes :]
        tall[s, :, :half] = image_basis[:, :half]
        restricted = dot(basis_t[s], jnp.concatenate([left, image_basis], axis=1))
        begun.append(restricted[:, : z.lanes])
        inner[s] = restricted[:, z.lanes : z.lanes + z.modes].astype(BF16)
        pick = pick_both(z, left_rows, right_rows, s)
        sides_t = dot_nt(basis_t[s], pick).astype(BF16)
        left_t[s] = sides_t[:, : z.face]
        right_t[s] = sides_t[:, z.face :]
        picked = dot(pick, images[s]).astype(BF16)
        faces = dot(picked[:, : z.lanes], lane_matrix(z, s * z.width, 0))
        faces = (faces + dot(picked[:, z.lanes :], lane_matrix(z, 0, half, z.modes))).astype(BF16)
        before[s] = faces[: z.face]
        after[s] = faces[z.face :]
    start_modes[...] = select(z, begun)
    store_faces(z, before, after, first_pair, second_pair)


def second_image_kernel(z, wait, *refs):
    inverse, stiffness = refs[: z.group], refs[z.group : 2 * z.group]
    rest = refs[2 * z.group :]
    load_rows, old_image, tall, old_solved, chosen = rest[:5]
    before, after, first_got, second_got, left_rows, right_rows = rest[5:11]
    new_before, new_after, first_pair, second_pair = rest[11:15]
    values = rest[15 : 15 + z.group]
    base, rounded, image = rest[15 + z.group :]
    steps, images = [], []
    for s in range(z.subs):
        faces = sides(z, before, after, first_got, second_got, s)
        both = [share.astype(BF16) for share in shares(z, s, chosen, faces)]
        left = jnp.concatenate([tall[s], scatter_matrix(z, left_rows[s : s + 1, :], 0, z.rows)], axis=1)
        total = dot(left, correction_side(z, chosen, s, both[0]))
        steps.append(total[:, z.lanes :])
        images.append(total[:, : z.lanes] + dot(scatter_matrix(z, right_rows[s : s + 1, :], 0, z.rows), both[1]))
    residual = (load_rows[...].astype(F32) - old_image[...] - select(z, images)).astype(BF16)
    base[...] = old_solved[...] + select(z, steps)
    for k in range(z.group):
        wait(k)

    def store_solved(k, start, value):
        value = value + base[pl.ds(start, z.own), :]
        values[k][0] = value
        rounded[pl.ds(start, z.own), :] = value.astype(BF16)

    multiply(z, inverse, residual, store_solved)

    def store_image(k, start, value):
        place = pl.ds(start, z.own)
        values[k][1] = load_rows[place, :].astype(F32) - value
        image[place, :] = value.astype(BF16)

    for k in range(z.group):
        wait(z.group + k)
    multiply(z, stiffness, rounded[...], store_image)
    pick = jnp.concatenate([pick_both(z, left_rows, right_rows, s) for s in range(z.subs)], axis=0)
    picked = dot(pick, image[...]).astype(BF16)
    for s in range(z.subs):
        own = picked[2 * s * z.face : 2 * (s + 1) * z.face]
        faces = dot(own, lane_matrix(z, s * z.width, 0)).astype(BF16)
        new_before[s] = faces[: z.face]
        new_after[s] = faces[z.face :]
    store_faces(z, new_before, new_after, first_pair, second_pair)


def digit_row(shape, row):
    return lax.broadcasted_iota(jnp.int32, shape, 1) == row


def coarse_rows(z, ordered_inverse, arrived, message):
    flat = arrived[:, : z.modes, :].reshape(z.columns, z.lanes)
    rows = fold(z, select(z, [dot(ordered_inverse[s], flat) for s in range(z.subs)]))
    packed = select(z, [rows[s * z.modes : (s + 1) * z.modes, :] for s in range(z.subs)]).astype(BF16)
    for k in range(z.n):
        message[k] = packed


def order_kernel(z, *refs):
    blocks = refs[: z.group]
    arrived, repeat, own_row, place, ordered_inverse, picks, message = refs[z.group :]
    digits = arrived[:, z.modes :, :].astype(F32)
    index = []
    for s in range(z.subs):
        high = jnp.sum(jnp.where(digit_row(digits.shape, 2 * s), digits, 0.0), axis=1)
        low = jnp.sum(jnp.where(digit_row(digits.shape, 2 * s + 1), digits, 0.0), axis=1)
        index.append(high * DIGIT + low)
        spread = dot(high.astype(BF16), repeat[...]) * DIGIT + dot(low.astype(BF16), repeat[...])
        places = jnp.sum(spread * own_row[...], axis=0, keepdims=True).astype(jnp.int32)
        for at in range(0, z.columns, 768):
            wide = min(768, z.columns - at)
            total = jnp.zeros((z.owned, wide), F32)
            for k, block in enumerate(blocks):
                inside = places[:, at : at + wide] - piece_start(z, k, z.block)
                for first in range(0, z.block, 768):
                    deep = min(768, z.block - first)
                    row = lax.broadcasted_iota(jnp.int32, (deep, wide), 0) + first
                    hot = jnp.where(row == inside, 1.0, 0.0).astype(BF16)
                    total = total + dot(block[:, first : first + deep], hot)
            ordered_inverse[s, :, at : at + wide] = total.astype(BF16)
    coarse_rows(z, ordered_inverse, arrived, message)
    here = lax.axis_index("sub")
    device = lax.broadcasted_iota(jnp.int32, (z.n, z.lanes), 0)
    for t in range(z.subs + 2):
        if t == 0:
            s, owner = z.subs - 1, lax.rem(here + z.n - 1, z.n)
        elif t == z.subs + 1:
            s, owner = 0, lax.rem(here + 1, z.n)
        else:
            s, owner = t - 1, here
        row = jnp.sum(jnp.where(device == owner, index[s], 0.0), axis=0, keepdims=True)
        column = jnp.transpose(jnp.broadcast_to(row, (z.lanes, z.lanes)))[: z.modes, 0:1].astype(jnp.int32)
        for h in range(z.subs):
            hit = column == place[h : h + 1, :]
            picks[h, t * z.modes : (t + 1) * z.modes, :] = jnp.where(hit, 1.0, 0.0).astype(BF16)


def coarse_kernel(z, arrived, ordered_inverse, message):
    coarse_rows(z, ordered_inverse, arrived, message)


def picked_rows(z, arrived, picks):
    flat = arrived[...].reshape(z.columns, z.lanes)
    return fold(z, select(z, [dot(picks[h], flat) for h in range(z.subs)])).astype(BF16)


def update_kernel(z, *refs):
    arrived, picks, start_modes, inner, left_t, right_t, before, after, first_got, second_got = refs[:10]
    chosen, message = refs[10:]
    rows = picked_rows(z, arrived, picks)
    chosen[...] = rows
    m = z.modes
    parts = []
    for s in range(z.subs):
        faces = sides(z, before, after, first_got, second_got, s)
        both = shares(z, s, rows, faces)
        total = dot(inner[s], rows[(s + 1) * m : (s + 2) * m])
        parts.append(total + dot(left_t[s], both[0].astype(BF16)) + dot(right_t[s], both[1].astype(BF16)))
    modes = (start_modes[...] - select(z, parts)).astype(BF16)
    for k in range(z.n):
        message[k] = modes


def pick_kernel(z, *refs):
    arrived, picks, before, after, first_got, second_got = refs[:6]
    base_before, base_after, base_first, base_second, out = refs[6:]
    chosen = picked_rows(z, arrived, picks)
    near = chosen.shape[0]
    lefts, rights = [], []
    for s in range(z.subs):
        values = sides(z, before, after, first_got, second_got, s)
        bases = sides(z, base_before, base_after, base_first, base_second, s)
        left, right = shares(z, s, chosen, values, bases)
        lefts.append(left)
        rights.append(right)
    out[:near] = chosen
    out[near : near + z.face] = select(z, lefts).astype(BF16)
    out[near + z.face :] = select(z, rights).astype(BF16)


def last_kernel(z, *refs):
    chosen, values = refs[: z.group], refs[z.group : 2 * z.group]
    tall, left_rows, right_rows, second_pass, final_residual = refs[2 * z.group :]
    start = piece_start(z, 0, z.own)
    near = (z.subs + 2) * z.modes
    lefts, rights = [], []
    for s in range(z.subs):
        scatter = scatter_matrix(z, left_rows[s : s + 1, :], start, z.own)
        lefts.append(jnp.concatenate([tall[s, pl.ds(start, z.own), :], scatter], axis=1))
        rights.append(scatter_matrix(z, right_rows[s : s + 1, :], start, z.own))
    done = [jnp.zeros((z.own, z.lanes), F32) for _ in range(2 * z.subs)]
    for k in range(z.group):
        rows = chosen[k][:near]
        left, right = chosen[k][near : near + z.face], chosen[k][near + z.face :]
        steps, images = [], []
        for s in range(z.subs):
            total = dot(lefts[s], correction_side(z, rows, s, left))
            steps.append(total[:, z.lanes :])
            images.append(total[:, : z.lanes] + dot(rights[s], right))
        pair = values[k][0] + select(z, steps), values[k][1] - select(z, images)
        place = lax.rem(lax.axis_index(GROUP) + k, z.group)
        for at, packed in enumerate(pair):
            for s in range(z.subs):
                turn = lax.rem((place - s + z.subs * z.group) * z.width, z.lanes)
                turned = pltpu.roll(packed, turn, 1)
                here = at * z.subs + s
                done[here] = jnp.where(lane_mask(z, place, turned.shape), turned, done[here])
    for s in range(z.subs):
        second_pass[s] = done[s][:, : z.cases]
        final_residual[s] = done[z.subs + s][:, : z.cases]


def call(kernel, outs, operands, flops, scratch=(), late=(), loose=(), name=None):
    moved = sum(int(np.prod(x.shape)) * x.dtype.itemsize for x in (*operands, *outs))
    n_in, n_out = len(operands), len(outs)

    def whole(*refs):
        hbm, refs = refs[: n_in + n_out], refs[n_in + n_out :]
        vmem, refs = refs[: n_in + n_out], refs[n_in + n_out :]
        in_sems, out_sems, *rest = refs
        arriving = [pltpu.make_async_copy(hbm[i], vmem[i], in_sems.at[i]) for i in range(n_in)]
        for i in sorted(range(n_in), key=lambda i: i in late):
            arriving[i].start()
        for i, copy in enumerate(arriving):
            if i not in late:
                copy.wait()
        extra = [lambda i: arriving[i].wait()] if late else []
        kernel(*extra, *vmem, *rest)
        leaving = [pltpu.make_async_copy(vmem[n_in + i], hbm[n_in + i], out_sems.at[i]) for i in range(n_out)]
        for copy in leaving:
            copy.start()
        for copy in leaving:
            copy.wait()

    hbm_spec = pl.BlockSpec(memory_space=pltpu.HBM)
    any_spec = pl.BlockSpec(memory_space=pl.ANY)
    placed = [
        x if i in loose else pltpu.with_memory_space_constraint(x, pltpu.HBM) for i, x in enumerate(operands)
    ]
    return pl.pallas_call(
        whole,
        out_shape=[pltpu.HBM(o.shape, o.dtype) for o in outs],
        in_specs=[any_spec if i in loose else hbm_spec for i in range(n_in)],
        out_specs=[hbm_spec] * n_out,
        scratch_shapes=[
            *[pltpu.VMEM(x.shape, x.dtype) for x in (*operands, *outs)],
            pltpu.SemaphoreType.DMA((n_in,)),
            pltpu.SemaphoreType.DMA((n_out,)),
            *scratch,
        ],
        compiler_params=pltpu.CompilerParams(vmem_limit_bytes=VMEM_BYTES),
        cost_estimate=pl.CostEstimate(flops=flops, bytes_accessed=moved, transcendentals=0),
        name=name,
    )(*placed)


def shape(dims, dtype):
    return jax.ShapeDtypeStruct(dims, dtype)


def pieces_of(block, group):
    out = [block]
    for k in range(1, group):
        out.append(lax.ppermute(block, GROUP, [((g + k) % group, g) for g in range(group)]))
    return out


def body(loads, stiffness, local_inverse, coarse_basis, coarse_inverse, coarse_index, left_rows, right_rows):
    z = Sizes(loads, stiffness, coarse_basis, coarse_inverse, left_rows)
    n, group, subs, rows, lanes, modes, face = z.n, z.group, z.subs, z.rows, z.lanes, z.modes, z.face
    basis_pieces = pieces_of(jnp.swapaxes(coarse_basis, 1, 2), group)
    basis_pieces, local_inverse, stiffness = lax.optimization_barrier((basis_pieces, local_inverse, stiffness))
    column = np.arange(z.columns)
    repeat = jnp.asarray(np.arange(lanes)[:, None] == column[None, :] % modes, BF16)
    own_row = jnp.asarray(np.arange(n)[:, None] == column[None, :] // modes, F32)
    place = jnp.asarray(
        (column // modes * z.owned + column % modes)[None, :] + np.arange(subs)[:, None] * modes, jnp.int32
    )
    packed_f = shape((rows, lanes), F32)
    packed_b = shape((rows, lanes), BF16)
    copies = shape((n, modes, lanes), BF16)
    tall = shape((subs, rows, lanes), BF16)
    spread = functools.partial(lax.all_to_all, axis_name="sub", split_axis=0, concat_axis=0)
    first_pairs = [(i, i + 1 if i % 2 == 0 else i - 1) for i in range(n)]
    second_pairs = [(i, (i + (1 if i % 2 else -1)) % n) for i in range(n)]
    work = 4 * subs * rows * rows * lanes

    (message,) = call(
        functools.partial(open_kernel, z),
        [shape((n, modes + DIGIT_ROWS, lanes), BF16)],
        [*basis_pieces, loads, coarse_index],
        4 * rows * lanes * lanes,
        [pltpu.VMEM((DIGIT_ROWS, lanes), F32), pltpu.VMEM((subs, modes, rows), BF16)],
        loose=range(1, group),
        name="open",
    )
    inverse_columns = pieces_of(coarse_inverse, group)
    inverse_pieces = pieces_of(local_inverse, group)
    stiffness_pieces = pieces_of(stiffness, group)
    restricted = spread(message)
    arrivals = [*range(1, group), *range(group + 1, 2 * group)]
    faces = shape((subs, face, lanes), BF16)
    outer = shape((face, lanes), BF16)
    side = shape((subs, modes, face), BF16)
    (
        load_rows, solved, image, before, after, first_pair, second_pair, tall, left_t, right_t, inner, start_modes
    ) = call(
        functools.partial(first_image_kernel, z),
        [
            packed_b, packed_f, packed_f, faces, faces, outer, outer, tall, side, side,
            shape((subs, modes, modes), BF16), shape((modes, lanes), F32),
        ],
        [*inverse_pieces, *stiffness_pieces, *basis_pieces, loads, left_rows, right_rows],
        work,
        [
            pltpu.VMEM((rows, lanes), BF16), pltpu.VMEM((subs, modes, rows), BF16),
            pltpu.VMEM((subs, rows, 2 * lanes), BF16), pltpu.VMEM((subs, rows, 2 * lanes), BF16),
        ],
        late=range(2 * group),
        loose=[*arrivals, *range(2 * group + 1, 3 * group)],
        name="first_image",
    )
    second_got = lax.ppermute(second_pair, "sub", second_pairs)
    restricted, second_pair = lax.optimization_barrier((restricted, second_pair))
    near = (subs + 2) * modes
    ordered_inverse, picks, message = call(
        functools.partial(order_kernel, z),
        [shape((subs, z.owned, z.columns), BF16), shape((subs, near, z.columns), BF16), copies],
        [*inverse_columns, restricted, repeat, own_row, place],
        2 * z.owned * z.total * z.total,
        loose=range(1, group + 1),
        name="order",
    )
    coarse = spread(message)
    first_got = lax.ppermute(first_pair, "sub", first_pairs)
    chosen, message = call(
        functools.partial(update_kernel, z),
        [shape((near, lanes), BF16), copies],
        [coarse, picks, start_modes, inner, left_t, right_t, before, after, first_got, second_got],
        work // 64,
        loose=[0, 8, 9],
        name="update",
    )
    restricted = spread(message)

    bases = [before, after, first_got, second_got]
    before, after, first_pair, second_pair, *values = call(
        functools.partial(second_image_kernel, z),
        [faces, faces, outer, outer, *[shape((2, z.own, lanes), F32)] * group],
        [
            *inverse_pieces, *stiffness_pieces, load_rows, image, tall, solved, chosen,
            *bases, left_rows, right_rows,
        ],
        work,
        [pltpu.VMEM((rows, lanes), F32), pltpu.VMEM((rows, lanes), BF16), pltpu.VMEM((rows, lanes), BF16)],
        late=range(2 * group),
        loose=[*arrivals, 2 * group + 7, 2 * group + 8],
        name="second_image",
    )
    second_got = lax.ppermute(second_pair, "sub", second_pairs)
    restricted, before = lax.optimization_barrier((restricted, before))
    (message,) = call(
        functools.partial(coarse_kernel, z),
        [copies],
        [restricted, ordered_inverse],
        work // 64,
        loose=[0],
        name="coarse",
    )
    coarse = spread(message)
    first_got = lax.ppermute(first_pair, "sub", first_pairs)
    swapped = [values[0]]
    for k in range(1, group):
        swapped.append(lax.ppermute(values[k], GROUP, [(g, (g + k) % group) for g in range(group)]))
    swapped = [swapped[(group - k) % group] for k in range(group)]
    (chosen,) = call(
        functools.partial(pick_kernel, z),
        [shape((near + 2 * face, lanes), BF16)],
        [coarse, picks, before, after, first_got, second_got, *bases],
        work // 64,
        loose=[0, 4, 5, 8, 9],
        name="pick",
    )
    out = shape((subs, z.own, z.cases), F32)
    return tuple(
        call(
            functools.partial(last_kernel, z),
            [out, out],
            [*pieces_of(chosen, group), *swapped, tall, left_rows, right_rows],
            work // 8,
            loose=[*range(1, group), *range(group + 1, 2 * group)],
            name="last",
        )
    )


def solution(mesh):
    return jax.shard_map(
        body,
        mesh=mesh,
        in_specs=(
            P("sub", None, None),
            P("sub", GROUP, None),
            P("sub", GROUP, None),
            P("sub", GROUP, None),
            P("sub", GROUP),
            P("sub", None),
            P("sub", None),
            P("sub", None),
        ),
        out_specs=(P("sub", GROUP, None), P("sub", GROUP, None)),
        check_vma=False,
    )
```

```python
import functools

import jax
import jax.numpy as jnp
import numpy as np
from jax import lax
from jax.experimental import pallas as pl
from jax.experimental.pallas import tpu as pltpu
from jax.sharding import PartitionSpec as P

GROUP = ("crow", "ccol")
F32 = jnp.float32
BF16 = jnp.bfloat16
VMEM_BYTES = 28 * 1024 * 1024
DIGIT_ROWS = 16
DIGIT_BITS = 8
DIGIT = 1 << DIGIT_BITS


def dot(a, b):
    return lax.dot_general(a, b, (((1,), (0,)), ((), ())), preferred_element_type=F32)


def dot_tn(a, b):
    return lax.dot_general(a, b, (((0,), (0,)), ((), ())), preferred_element_type=F32)


def dot_nt(a, b):
    return lax.dot_general(a, b, (((1,), (1,)), ((), ())), preferred_element_type=F32)


class Sizes:
    def __init__(self, loads, stiffness, coarse_basis, coarse_inverse, left_rows):
        self.n = lax.axis_size("sub")
        self.group = lax.axis_size(GROUP)
        self.subs, self.rows, self.cases = loads.shape
        self.own = stiffness.shape[1]
        self.modes = coarse_basis.shape[2]
        self.owned, self.block = coarse_inverse.shape
        self.total = self.block * self.group
        self.face = left_rows.shape[1]
        self.width = self.cases // self.group
        self.lanes = max(self.cases, -(-self.subs * self.width // 128) * 128)
        self.columns = self.n * self.modes


def lane_mask(z, block, shape):
    lane = lax.broadcasted_iota(jnp.int32, shape, len(shape) - 1)
    return (lane >= block * z.width) & (lane < (block + 1) * z.width)


def select(z, parts):
    out = jnp.zeros_like(parts[0])
    for s, part in enumerate(parts):
        out = jnp.where(lane_mask(z, s, part.shape), part, out)
    return out


def fold(z, packed):
    if z.lanes == z.subs * z.width:
        out = packed
        for k in range(1, z.subs):
            out = out + pltpu.roll(packed, k * z.width, 1)
        return out
    out = packed
    for k in range(1, z.subs):
        out = out + pltpu.roll(packed, k * z.width, 1)
        out = out + pltpu.roll(packed, z.lanes - k * z.width, 1)
    return out


def lane_matrix(z, source, target, width=None):
    row = lax.broadcasted_iota(jnp.int32, (z.lanes, z.lanes), 0)
    lane = lax.broadcasted_iota(jnp.int32, (z.lanes, z.lanes), 1)
    hit = (row - source == lane - target) & (lane >= target) & (lane < target + (width or z.width))
    return jnp.where(hit, 1.0, 0.0).astype(BF16)


def piece_start(z, k, size):
    place = lax.rem(lax.axis_index(GROUP) + k, z.group)
    return pl.multiple_of(place * size, size)


def pick_matrix(z, rows_of):
    column = jnp.transpose(jnp.broadcast_to(rows_of.astype(F32), (z.face, z.face)))[:, 0:1].astype(jnp.int32)
    row = lax.broadcasted_iota(jnp.int32, (z.face, z.rows), 1)
    return jnp.where(row == column, 1.0, 0.0).astype(BF16)


def even():
    return lax.rem(lax.axis_index("sub"), 2) == 0


def case_matrix(z, s):
    row = lax.broadcasted_iota(jnp.int32, (z.cases, z.lanes), 0)
    lane = lax.broadcasted_iota(jnp.int32, (z.cases, z.lanes), 1)
    hit = (row - lax.axis_index(GROUP) * z.width == lane - s * z.width) & lane_mask(z, s, row.shape)
    return jnp.where(hit, 1.0, 0.0).astype(BF16)


def join_basis(z, pieces, basis_t):
    for k, piece in enumerate(pieces):
        basis_t[:, :, pl.ds(piece_start(z, k, z.own), z.own)] = piece[...]


def open_kernel(z, *refs):
    pieces = refs[: z.group]
    loads, index, message, digits, basis_t = refs[z.group :]
    join_basis(z, pieces, basis_t)
    total = jnp.zeros((z.modes, z.lanes), F32)
    for s in range(z.subs):
        total = total + dot(dot(basis_t[s], loads[s]).astype(BF16), case_matrix(z, s))
    modes = total.astype(BF16)
    digits[...] = jnp.zeros(digits.shape, F32)
    for s in range(z.subs):
        places = index[s : s + 1, :]
        digits[2 * s : 2 * s + 1, : z.modes] = (places >> DIGIT_BITS).astype(F32)
        digits[2 * s + 1 : 2 * s + 2, : z.modes] = (places & (DIGIT - 1)).astype(F32)
    for k in range(z.n):
        message[k, : z.modes, :] = modes
        message[k, z.modes :, :] = digits[...].astype(BF16)


def multiply(z, pieces, vector, store):
    for k, piece in enumerate(pieces):
        parts = [dot(piece[s], vector) for s in range(z.subs)]
        store(k, piece_start(z, k, z.own), select(z, parts))


def pick_both(z, left_rows, right_rows, s):
    return jnp.concatenate(
        [pick_matrix(z, left_rows[s : s + 1, :]), pick_matrix(z, right_rows[s : s + 1, :])], axis=0
    )


def store_faces(z, before, after, first_pair, second_pair):
    first, last = before[0], after[z.subs - 1]
    first_pair[...] = jnp.where(even(), last, first)
    second_pair[...] = jnp.where(even(), first, last)


def sides(z, before, after, first_pair, second_pair, s):
    if s == 0:
        from_before = jnp.where(even(), second_pair[...], first_pair[...])
    else:
        from_before = after[s - 1]
    if s == z.subs - 1:
        from_after = jnp.where(even(), first_pair[...], second_pair[...])
    else:
        from_after = before[s + 1]
    return from_before, from_after


def shares(z, s, chosen, faces, bases=None):
    m, half = z.modes, z.lanes // 2
    moved = lane_matrix(z, 0, s * z.width)
    out = []
    for side, at in ((0, s), (1, s + 2)):
        own = chosen[at * m : (at + 1) * m]
        below = jnp.concatenate([own, jnp.zeros((half - m, z.lanes), BF16)], axis=0)
        if bases is None:
            total = dot(faces[side], jnp.concatenate([moved[:half], below], axis=0))
        else:
            above = jnp.zeros((half, z.lanes), BF16)
            total = dot(faces[side], moved) + dot(bases[side], jnp.concatenate([above, below], axis=0))
        out.append(total)
    return out


def correction_side(z, chosen, s, share):
    m, half = z.modes, z.lanes // 2
    own = chosen[(s + 1) * m : (s + 2) * m]
    none = jnp.zeros((half - m, z.lanes), BF16)
    nil = jnp.zeros((half, z.lanes), BF16)
    image = jnp.concatenate([own, none, nil, share], axis=0)
    step = jnp.concatenate([nil, own, none, jnp.zeros((z.face, z.lanes), BF16)], axis=0)
    return jnp.concatenate([image, step], axis=1)


def scatter_matrix(z, rows_of, start, count):
    row = lax.broadcasted_iota(jnp.int32, (count, z.face), 0) + start
    return jnp.where(row == rows_of, 1.0, 0.0).astype(BF16)


def first_image_kernel(z, wait, *refs):
    inverse, stiffness = refs[: z.group], refs[z.group : 2 * z.group]
    pieces = refs[2 * z.group : 3 * z.group]
    loads, left_rows, right_rows = refs[3 * z.group : 3 * z.group + 3]
    load_rows, solved, image, before, after, first_pair, second_pair = refs[3 * z.group + 3 : 3 * z.group + 10]
    tall, left_t, right_t, inner, start_modes, rounded, basis_t, both, images = refs[3 * z.group + 10 :]
    join_basis(z, pieces, basis_t)
    packed = dot(loads[0], case_matrix(z, 0))
    for s in range(1, z.subs):
        packed = packed + dot(loads[s], case_matrix(z, s))
    load_rows[...] = packed.astype(BF16)

    def store_solved(k, start, value):
        solved[pl.ds(start, z.own), :] = value
        rounded[pl.ds(start, z.own), :] = value.astype(BF16)

    wait(0)
    multiply(z, inverse, load_rows[...], store_solved)
    solved_b = rounded[...]
    half = z.lanes // 2
    for s in range(z.subs):
        basis = jnp.transpose(basis_t[s].astype(F32)).astype(BF16)
        tall[s, :, half : half + z.modes] = basis
        tall[s, :, half + z.modes :] = jnp.zeros((z.rows, half - z.modes), BF16)
        both[s, :, : z.lanes] = solved_b
        both[s, :, z.lanes : z.lanes + z.modes] = basis
        both[s, :, z.lanes + z.modes :] = jnp.zeros((z.rows, z.lanes - z.modes), BF16)
    wait(z.group)
    for k, piece in enumerate(stiffness):
        start = piece_start(z, k, z.own)
        parts = [dot(piece[s], both[s]) for s in range(z.subs)]
        image[pl.ds(start, z.own), :] = select(z, [part[:, : z.lanes] for part in parts])
        for s in range(z.subs):
            images[s, pl.ds(start, z.own), :] = parts[s].astype(BF16)
    left = (load_rows[...].astype(F32) - image[...]).astype(BF16)
    begun = []
    for s in range(z.subs):
        image_basis = images[s, :, z.lanes :]
        tall[s, :, :half] = image_basis[:, :half]
        restricted = dot(basis_t[s], jnp.concatenate([left, image_basis], axis=1))
        begun.append(restricted[:, : z.lanes])
        inner[s] = restricted[:, z.lanes : z.lanes + z.modes].astype(BF16)
        pick = pick_both(z, left_rows, right_rows, s)
        sides_t = dot_nt(basis_t[s], pick).astype(BF16)
        left_t[s] = sides_t[:, : z.face]
        right_t[s] = sides_t[:, z.face :]
        picked = dot(pick, images[s]).astype(BF16)
        faces = dot(picked[:, : z.lanes], lane_matrix(z, s * z.width, 0))
        faces = (faces + dot(picked[:, z.lanes :], lane_matrix(z, 0, half, z.modes))).astype(BF16)
        before[s] = faces[: z.face]
        after[s] = faces[z.face :]
    start_modes[...] = select(z, begun)
    store_faces(z, before, after, first_pair, second_pair)


def second_image_kernel(z, wait, *refs):
    inverse, stiffness = refs[: z.group], refs[z.group : 2 * z.group]
    rest = refs[2 * z.group :]
    load_rows, old_image, tall, old_solved, chosen = rest[:5]
    before, after, first_got, second_got, left_rows, right_rows = rest[5:11]
    new_before, new_after, first_pair, second_pair = rest[11:15]
    values = rest[15 : 15 + z.group]
    base, rounded, image = rest[15 + z.group :]
    steps, images = [], []
    for s in range(z.subs):
        faces = sides(z, before, after, first_got, second_got, s)
        both = [share.astype(BF16) for share in shares(z, s, chosen, faces)]
        left = jnp.concatenate([tall[s], scatter_matrix(z, left_rows[s : s + 1, :], 0, z.rows)], axis=1)
        total = dot(left, correction_side(z, chosen, s, both[0]))
        steps.append(total[:, z.lanes :])
        images.append(total[:, : z.lanes] + dot(scatter_matrix(z, right_rows[s : s + 1, :], 0, z.rows), both[1]))
    residual = (load_rows[...].astype(F32) - old_image[...] - select(z, images)).astype(BF16)
    base[...] = old_solved[...] + select(z, steps)

    def store_solved(k, start, value):
        value = value + base[pl.ds(start, z.own), :]
        values[k][0] = value
        rounded[pl.ds(start, z.own), :] = value.astype(BF16)

    wait(0)
    multiply(z, inverse, residual, store_solved)

    def store_image(k, start, value):
        place = pl.ds(start, z.own)
        values[k][1] = load_rows[place, :].astype(F32) - value
        image[place, :] = value.astype(BF16)

    wait(z.group)
    multiply(z, stiffness, rounded[...], store_image)
    pick = jnp.concatenate([pick_both(z, left_rows, right_rows, s) for s in range(z.subs)], axis=0)
    picked = dot(pick, image[...]).astype(BF16)
    for s in range(z.subs):
        own = picked[2 * s * z.face : 2 * (s + 1) * z.face]
        faces = dot(own, lane_matrix(z, s * z.width, 0)).astype(BF16)
        new_before[s] = faces[: z.face]
        new_after[s] = faces[z.face :]
    store_faces(z, new_before, new_after, first_pair, second_pair)


def digit_row(shape, row):
    return lax.broadcasted_iota(jnp.int32, shape, 1) == row


def coarse_rows(z, ordered_inverse, arrived, message):
    flat = arrived[:, : z.modes, :].reshape(z.columns, z.lanes)
    rows = fold(z, select(z, [dot(ordered_inverse[s], flat) for s in range(z.subs)]))
    packed = select(z, [rows[s * z.modes : (s + 1) * z.modes, :] for s in range(z.subs)]).astype(BF16)
    for k in range(z.n):
        message[k] = packed


def order_kernel(z, *refs):
    blocks = refs[: z.group]
    arrived, repeat, own_row, place, ordered_inverse, picks, message = refs[z.group :]
    digits = arrived[:, z.modes :, :].astype(F32)
    index = []
    for s in range(z.subs):
        high = jnp.sum(jnp.where(digit_row(digits.shape, 2 * s), digits, 0.0), axis=1)
        low = jnp.sum(jnp.where(digit_row(digits.shape, 2 * s + 1), digits, 0.0), axis=1)
        index.append(high * DIGIT + low)
        spread = dot(high.astype(BF16), repeat[...]) * DIGIT + dot(low.astype(BF16), repeat[...])
        places = jnp.sum(spread * own_row[...], axis=0, keepdims=True).astype(jnp.int32)
        for at in range(0, z.columns, 768):
            wide = min(768, z.columns - at)
            total = jnp.zeros((z.owned, wide), F32)
            for k, block in enumerate(blocks):
                inside = places[:, at : at + wide] - piece_start(z, k, z.block)
                for first in range(0, z.block, 768):
                    deep = min(768, z.block - first)
                    row = lax.broadcasted_iota(jnp.int32, (deep, wide), 0) + first
                    hot = jnp.where(row == inside, 1.0, 0.0).astype(BF16)
                    total = total + dot(block[:, first : first + deep], hot)
            ordered_inverse[s, :, at : at + wide] = total.astype(BF16)
    coarse_rows(z, ordered_inverse, arrived, message)
    here = lax.axis_index("sub")
    device = lax.broadcasted_iota(jnp.int32, (z.n, z.lanes), 0)
    for t in range(z.subs + 2):
        if t == 0:
            s, owner = z.subs - 1, lax.rem(here + z.n - 1, z.n)
        elif t == z.subs + 1:
            s, owner = 0, lax.rem(here + 1, z.n)
        else:
            s, owner = t - 1, here
        row = jnp.sum(jnp.where(device == owner, index[s], 0.0), axis=0, keepdims=True)
        column = jnp.transpose(jnp.broadcast_to(row, (z.lanes, z.lanes)))[: z.modes, 0:1].astype(jnp.int32)
        for h in range(z.subs):
            hit = column == place[h : h + 1, :]
            picks[h, t * z.modes : (t + 1) * z.modes, :] = jnp.where(hit, 1.0, 0.0).astype(BF16)


def coarse_kernel(z, arrived, ordered_inverse, message):
    coarse_rows(z, ordered_inverse, arrived, message)


def picked_rows(z, arrived, picks):
    flat = arrived[...].reshape(z.columns, z.lanes)
    return fold(z, select(z, [dot(picks[h], flat) for h in range(z.subs)])).astype(BF16)


def update_kernel(z, *refs):
    arrived, picks, start_modes, inner, left_t, right_t, before, after, first_got, second_got = refs[:10]
    chosen, message = refs[10:]
    rows = picked_rows(z, arrived, picks)
    chosen[...] = rows
    m = z.modes
    parts = []
    for s in range(z.subs):
        faces = sides(z, before, after, first_got, second_got, s)
        both = shares(z, s, rows, faces)
        total = dot(inner[s], rows[(s + 1) * m : (s + 2) * m])
        parts.append(total + dot(left_t[s], both[0].astype(BF16)) + dot(right_t[s], both[1].astype(BF16)))
    modes = (start_modes[...] - select(z, parts)).astype(BF16)
    for k in range(z.n):
        message[k] = modes


def pick_kernel(z, *refs):
    arrived, picks, before, after, first_got, second_got = refs[:6]
    base_before, base_after, base_first, base_second, out = refs[6:]
    chosen = picked_rows(z, arrived, picks)
    near = chosen.shape[0]
    lefts, rights = [], []
    for s in range(z.subs):
        values = sides(z, before, after, first_got, second_got, s)
        bases = sides(z, base_before, base_after, base_first, base_second, s)
        left, right = shares(z, s, chosen, values, bases)
        lefts.append(left)
        rights.append(right)
    out[:near] = chosen
    out[near : near + z.face] = select(z, lefts).astype(BF16)
    out[near + z.face :] = select(z, rights).astype(BF16)


def last_kernel(z, *refs):
    chosen, values = refs[: z.group], refs[z.group : 2 * z.group]
    tall, left_rows, right_rows, second_pass, final_residual = refs[2 * z.group :]
    start = piece_start(z, 0, z.own)
    near = (z.subs + 2) * z.modes
    lefts, rights = [], []
    for s in range(z.subs):
        scatter = scatter_matrix(z, left_rows[s : s + 1, :], start, z.own)
        lefts.append(jnp.concatenate([tall[s, pl.ds(start, z.own), :], scatter], axis=1))
        rights.append(scatter_matrix(z, right_rows[s : s + 1, :], start, z.own))
    done = [jnp.zeros((z.own, z.lanes), F32) for _ in range(2 * z.subs)]
    for k in range(z.group):
        rows = chosen[k][:near]
        left, right = chosen[k][near : near + z.face], chosen[k][near + z.face :]
        steps, images = [], []
        for s in range(z.subs):
            total = dot(lefts[s], correction_side(z, rows, s, left))
            steps.append(total[:, z.lanes :])
            images.append(total[:, : z.lanes] + dot(rights[s], right))
        pair = values[k][0] + select(z, steps), values[k][1] - select(z, images)
        place = lax.rem(lax.axis_index(GROUP) + k, z.group)
        for at, packed in enumerate(pair):
            for s in range(z.subs):
                turn = lax.rem((place - s + z.subs * z.group) * z.width, z.lanes)
                turned = pltpu.roll(packed, turn, 1)
                here = at * z.subs + s
                done[here] = jnp.where(lane_mask(z, place, turned.shape), turned, done[here])
    for s in range(z.subs):
        second_pass[s] = done[s][:, : z.cases]
        final_residual[s] = done[z.subs + s][:, : z.cases]


def call(kernel, outs, operands, flops, scratch=(), late=(), resident=(), loose=(), name=None):
    moved = sum(int(np.prod(x.shape)) * x.dtype.itemsize for x in (*operands, *outs))
    n_in, n_out = len(operands), len(outs)

    brought = [i for i in range(n_in) if i not in resident]

    def whole(*refs):
        given, refs = refs[: n_in + n_out], refs[n_in + n_out :]
        inside, refs = list(given), list(refs)
        for i in [*brought, *range(n_in, n_in + n_out)]:
            inside[i] = refs.pop(0)
        in_sems, out_sems, *rest = refs
        arriving = {i: pltpu.make_async_copy(given[i], inside[i], in_sems.at[i]) for i in brought}
        for i in sorted(brought, key=lambda i: i in late):
            arriving[i].start()
        for i in brought:
            if i not in late:
                arriving[i].wait()
        extra = [lambda i: arriving[i].wait()] if late else []
        kernel(*extra, *inside, *rest)
        leaving = [pltpu.make_async_copy(inside[n_in + i], given[n_in + i], out_sems.at[i]) for i in range(n_out)]
        for copy in leaving:
            copy.start()
        for copy in leaving:
            copy.wait()

    hbm_spec = pl.BlockSpec(memory_space=pltpu.HBM)
    any_spec = pl.BlockSpec(memory_space=pl.ANY)
    vmem_spec = pl.BlockSpec(memory_space=pltpu.VMEM)
    placed = [
        x if i in loose or i in resident else pltpu.with_memory_space_constraint(x, pltpu.HBM) for i, x in enumerate(operands)
    ]
    return pl.pallas_call(
        whole,
        out_shape=[pltpu.HBM(o.shape, o.dtype) for o in outs],
        in_specs=[
            vmem_spec if i in resident else any_spec if i in loose else hbm_spec for i in range(n_in)
        ],
        out_specs=[hbm_spec] * n_out,
        scratch_shapes=[
            *[pltpu.VMEM(x.shape, x.dtype) for x in (*[operands[i] for i in brought], *outs)],
            pltpu.SemaphoreType.DMA((n_in,)),
            pltpu.SemaphoreType.DMA((n_out,)),
            *scratch,
        ],
        compiler_params=pltpu.CompilerParams(vmem_limit_bytes=VMEM_BYTES),
        cost_estimate=pl.CostEstimate(flops=flops, bytes_accessed=moved, transcendentals=0),
        name=name,
    )(*placed)


def shape(dims, dtype):
    return jax.ShapeDtypeStruct(dims, dtype)


def pieces_of(block, group):
    out = [block]
    for k in range(1, group):
        out.append(lax.ppermute(block, GROUP, [((g + k) % group, g) for g in range(group)]))
    return out


def body(loads, stiffness, local_inverse, coarse_basis, coarse_inverse, coarse_index, left_rows, right_rows):
    z = Sizes(loads, stiffness, coarse_basis, coarse_inverse, left_rows)
    n, group, subs, rows, lanes, modes, face = z.n, z.group, z.subs, z.rows, z.lanes, z.modes, z.face
    basis_pieces = pieces_of(jnp.swapaxes(coarse_basis, 1, 2), group)
    basis_pieces, local_inverse, stiffness = lax.optimization_barrier((basis_pieces, local_inverse, stiffness))
    column = np.arange(z.columns)
    repeat = jnp.asarray(np.arange(lanes)[:, None] == column[None, :] % modes, BF16)
    own_row = jnp.asarray(np.arange(n)[:, None] == column[None, :] // modes, F32)
    place = jnp.asarray(
        (column // modes * z.owned + column % modes)[None, :] + np.arange(subs)[:, None] * modes, jnp.int32
    )
    packed_f = shape((rows, lanes), F32)
    packed_b = shape((rows, lanes), BF16)
    copies = shape((n, modes, lanes), BF16)
    tall = shape((subs, rows, lanes), BF16)
    spread = functools.partial(lax.all_to_all, axis_name="sub", split_axis=0, concat_axis=0)
    first_pairs = [(i, i + 1 if i % 2 == 0 else i - 1) for i in range(n)]
    second_pairs = [(i, (i + (1 if i % 2 else -1)) % n) for i in range(n)]
    work = 4 * subs * rows * rows * lanes

    (message,) = call(
        functools.partial(open_kernel, z),
        [shape((n, modes + DIGIT_ROWS, lanes), BF16)],
        [*basis_pieces, loads, coarse_index],
        4 * rows * lanes * lanes,
        [pltpu.VMEM((DIGIT_ROWS, lanes), F32), pltpu.VMEM((subs, modes, rows), BF16)],
        loose=range(1, group),
        name="open",
    )
    inverse_columns = pieces_of(coarse_inverse, group)
    inverse_pieces = pieces_of(local_inverse, group)
    stiffness_pieces = pieces_of(stiffness, group)
    restricted = spread(message)
    faces = shape((subs, face, lanes), BF16)
    outer = shape((face, lanes), BF16)
    side = shape((subs, modes, face), BF16)
    (
        load_rows, solved, image, before, after, first_pair, second_pair, tall, left_t, right_t, inner, start_modes
    ) = call(
        functools.partial(first_image_kernel, z),
        [
            packed_b, packed_f, packed_f, faces, faces, outer, outer, tall, side, side,
            shape((subs, modes, modes), BF16), shape((modes, lanes), F32),
        ],
        [*inverse_pieces, *stiffness_pieces, *basis_pieces, loads, left_rows, right_rows],
        work,
        [
            pltpu.VMEM((rows, lanes), BF16), pltpu.VMEM((subs, modes, rows), BF16),
            pltpu.VMEM((subs, rows, 2 * lanes), BF16), pltpu.VMEM((subs, rows, 2 * lanes), BF16),
        ],
        late=[0, group],
        resident=[*range(1, group), *range(group + 1, 2 * group)],
        loose=range(2 * group + 1, 3 * group),
        name="first_image",
    )
    second_got = lax.ppermute(second_pair, "sub", second_pairs)
    restricted, second_pair = lax.optimization_barrier((restricted, second_pair))
    near = (subs + 2) * modes
    ordered_inverse, picks, message = call(
        functools.partial(order_kernel, z),
        [shape((subs, z.owned, z.columns), BF16), shape((subs, near, z.columns), BF16), copies],
        [*inverse_columns, restricted, repeat, own_row, place],
        2 * z.owned * z.total * z.total,
        loose=range(1, group + 1),
        name="order",
    )
    coarse = spread(message)
    first_got = lax.ppermute(first_pair, "sub", first_pairs)
    chosen, message = call(
        functools.partial(update_kernel, z),
        [shape((near, lanes), BF16), copies],
        [coarse, picks, start_modes, inner, left_t, right_t, before, after, first_got, second_got],
        work // 64,
        loose=[0, 8, 9],
        name="update",
    )
    restricted = spread(message)

    bases = [before, after, first_got, second_got]
    before, after, first_pair, second_pair, *values = call(
        functools.partial(second_image_kernel, z),
        [faces, faces, outer, outer, *[shape((2, z.own, lanes), F32)] * group],
        [
            *inverse_pieces, *stiffness_pieces, load_rows, image, tall, solved, chosen,
            *bases, left_rows, right_rows,
        ],
        work,
        [pltpu.VMEM((rows, lanes), F32), pltpu.VMEM((rows, lanes), BF16), pltpu.VMEM((rows, lanes), BF16)],
        late=[0, group],
        resident=[*range(1, group), *range(group + 1, 2 * group)],
        loose=[2 * group + 7, 2 * group + 8],
        name="second_image",
    )
    second_got = lax.ppermute(second_pair, "sub", second_pairs)
    restricted, before = lax.optimization_barrier((restricted, before))
    (message,) = call(
        functools.partial(coarse_kernel, z),
        [copies],
        [restricted, ordered_inverse],
        work // 64,
        loose=[0],
        name="coarse",
    )
    coarse = spread(message)
    first_got = lax.ppermute(first_pair, "sub", first_pairs)
    swapped = [values[0]]
    for k in range(1, group):
        swapped.append(lax.ppermute(values[k], GROUP, [(g, (g + k) % group) for g in range(group)]))
    swapped = [swapped[(group - k) % group] for k in range(group)]
    (chosen,) = call(
        functools.partial(pick_kernel, z),
        [shape((near + 2 * face, lanes), BF16)],
        [coarse, picks, before, after, first_got, second_got, *bases],
        work // 64,
        loose=[0, 4, 5, 8, 9],
        name="pick",
    )
    out = shape((subs, z.own, z.cases), F32)
    return tuple(
        call(
            functools.partial(last_kernel, z),
            [out, out],
            [*pieces_of(chosen, group), *swapped, tall, left_rows, right_rows],
            work // 8,
            loose=[*range(1, group), *range(group + 1, 2 * group)],
            name="last",
        )
    )


def solution(mesh):
    return jax.shard_map(
        body,
        mesh=mesh,
        in_specs=(
            P("sub", None, None),
            P("sub", GROUP, None),
            P("sub", GROUP, None),
            P("sub", GROUP, None),
            P("sub", GROUP),
            P("sub", None),
            P("sub", None),
            P("sub", None),
        ),
        out_specs=(P("sub", GROUP, None), P("sub", GROUP, None)),
        check_vma=False,
    )
```

```python
import functools

import jax
import jax.numpy as jnp
import numpy as np
from jax import lax
from jax.experimental import pallas as pl
from jax.experimental.pallas import tpu as pltpu
from jax.sharding import PartitionSpec as P

GROUP = ("crow", "ccol")
F32 = jnp.float32
BF16 = jnp.bfloat16
VMEM_BYTES = 48 * 1024 * 1024
DIGIT_ROWS = 16
DIGIT_BITS = 8
DIGIT = 1 << DIGIT_BITS


def dot(a, b):
    return lax.dot_general(a, b, (((1,), (0,)), ((), ())), preferred_element_type=F32)


def dot_tn(a, b):
    return lax.dot_general(a, b, (((0,), (0,)), ((), ())), preferred_element_type=F32)


def dot_nt(a, b):
    return lax.dot_general(a, b, (((1,), (1,)), ((), ())), preferred_element_type=F32)


class Sizes:
    def __init__(self, loads, stiffness, coarse_basis, coarse_inverse, left_rows):
        self.n = lax.axis_size("sub")
        self.group = lax.axis_size(GROUP)
        self.subs, self.rows, self.cases = loads.shape
        self.own = stiffness.shape[1]
        self.modes = coarse_basis.shape[2]
        self.owned, self.block = coarse_inverse.shape
        self.total = self.block * self.group
        self.face = left_rows.shape[1]
        self.width = self.cases // self.group
        self.lanes = max(self.cases, -(-self.subs * self.width // 128) * 128)
        self.columns = self.n * self.modes


def lane_mask(z, block, shape):
    lane = lax.broadcasted_iota(jnp.int32, shape, len(shape) - 1)
    return (lane >= block * z.width) & (lane < (block + 1) * z.width)


def select(z, parts):
    out = jnp.zeros_like(parts[0])
    for s, part in enumerate(parts):
        out = jnp.where(lane_mask(z, s, part.shape), part, out)
    return out


def fold(z, packed):
    if z.lanes == z.subs * z.width:
        out = packed
        for k in range(1, z.subs):
            out = out + pltpu.roll(packed, k * z.width, 1)
        return out
    out = packed
    for k in range(1, z.subs):
        out = out + pltpu.roll(packed, k * z.width, 1)
        out = out + pltpu.roll(packed, z.lanes - k * z.width, 1)
    return out


def lane_matrix(z, source, target, width=None):
    row = lax.broadcasted_iota(jnp.int32, (z.lanes, z.lanes), 0)
    lane = lax.broadcasted_iota(jnp.int32, (z.lanes, z.lanes), 1)
    hit = (row - source == lane - target) & (lane >= target) & (lane < target + (width or z.width))
    return jnp.where(hit, 1.0, 0.0).astype(BF16)


def piece_start(z, k, size):
    place = lax.rem(lax.axis_index(GROUP) + k, z.group)
    return pl.multiple_of(place * size, size)


def pick_matrix(z, rows_of):
    column = jnp.transpose(jnp.broadcast_to(rows_of.astype(F32), (z.face, z.face)))[:, 0:1].astype(jnp.int32)
    row = lax.broadcasted_iota(jnp.int32, (z.face, z.rows), 1)
    return jnp.where(row == column, 1.0, 0.0).astype(BF16)


def even():
    return lax.rem(lax.axis_index("sub"), 2) == 0


def case_matrix(z, s):
    row = lax.broadcasted_iota(jnp.int32, (z.cases, z.lanes), 0)
    lane = lax.broadcasted_iota(jnp.int32, (z.cases, z.lanes), 1)
    hit = (row - lax.axis_index(GROUP) * z.width == lane - s * z.width) & lane_mask(z, s, row.shape)
    return jnp.where(hit, 1.0, 0.0).astype(BF16)


def join_basis(z, pieces, basis_t):
    for k, piece in enumerate(pieces):
        basis_t[:, :, pl.ds(piece_start(z, k, z.own), z.own)] = piece[...]


def open_kernel(z, *refs):
    pieces = refs[: z.group]
    loads, index, message, digits, basis_t = refs[z.group :]
    join_basis(z, pieces, basis_t)
    total = jnp.zeros((z.modes, z.lanes), F32)
    for s in range(z.subs):
        total = total + dot(dot(basis_t[s], loads[s]).astype(BF16), case_matrix(z, s))
    modes = total.astype(BF16)
    digits[...] = jnp.zeros(digits.shape, F32)
    for s in range(z.subs):
        places = index[s : s + 1, :]
        digits[2 * s : 2 * s + 1, : z.modes] = (places >> DIGIT_BITS).astype(F32)
        digits[2 * s + 1 : 2 * s + 2, : z.modes] = (places & (DIGIT - 1)).astype(F32)
    for k in range(z.n):
        message[k, : z.modes, :] = modes
        message[k, z.modes :, :] = digits[...].astype(BF16)


def multiply(z, pieces, vector, store, wait):
    for k, piece in enumerate(pieces):
        wait(k)
        parts = [dot(piece[s], vector) for s in range(z.subs)]
        store(k, piece_start(z, k, z.own), select(z, parts))


def pick_both(z, left_rows, right_rows, s):
    return jnp.concatenate(
        [pick_matrix(z, left_rows[s : s + 1, :]), pick_matrix(z, right_rows[s : s + 1, :])], axis=0
    )


def store_faces(z, before, after, first_pair, second_pair):
    first, last = before[0], after[z.subs - 1]
    first_pair[...] = jnp.where(even(), last, first)
    second_pair[...] = jnp.where(even(), first, last)


def sides(z, before, after, first_pair, second_pair, s):
    if s == 0:
        from_before = jnp.where(even(), second_pair[...], first_pair[...])
    else:
        from_before = after[s - 1]
    if s == z.subs - 1:
        from_after = jnp.where(even(), first_pair[...], second_pair[...])
    else:
        from_after = before[s + 1]
    return from_before, from_after


def shares(z, s, chosen, faces, bases=None):
    m, half = z.modes, z.lanes // 2
    moved = lane_matrix(z, 0, s * z.width)
    out = []
    for side, at in ((0, s), (1, s + 2)):
        own = chosen[at * m : (at + 1) * m]
        below = jnp.concatenate([own, jnp.zeros((half - m, z.lanes), BF16)], axis=0)
        if bases is None:
            total = dot(faces[side], jnp.concatenate([moved[:half], below], axis=0))
        else:
            above = jnp.zeros((half, z.lanes), BF16)
            total = dot(faces[side], moved) + dot(bases[side], jnp.concatenate([above, below], axis=0))
        out.append(total)
    return out


def correction_side(z, chosen, s, share):
    m, half = z.modes, z.lanes // 2
    own = chosen[(s + 1) * m : (s + 2) * m]
    none = jnp.zeros((half - m, z.lanes), BF16)
    nil = jnp.zeros((half, z.lanes), BF16)
    image = jnp.concatenate([own, none, nil, share], axis=0)
    step = jnp.concatenate([nil, own, none, jnp.zeros((z.face, z.lanes), BF16)], axis=0)
    return jnp.concatenate([image, step], axis=1)


def scatter_matrix(z, rows_of, start, count):
    row = lax.broadcasted_iota(jnp.int32, (count, z.face), 0) + start
    return jnp.where(row == rows_of, 1.0, 0.0).astype(BF16)


def first_image_kernel(z, wait, *refs):
    inverse, stiffness = refs[: z.group], refs[z.group : 2 * z.group]
    pieces = refs[2 * z.group : 3 * z.group]
    loads, left_rows, right_rows = refs[3 * z.group : 3 * z.group + 3]
    load_rows, solved, image, before, after, first_pair, second_pair = refs[3 * z.group + 3 : 3 * z.group + 10]
    tall, basis_t, rounded, both, images = refs[3 * z.group + 10 :]
    join_basis(z, pieces, basis_t)
    packed = dot(loads[0], case_matrix(z, 0))
    for s in range(1, z.subs):
        packed = packed + dot(loads[s], case_matrix(z, s))
    load_rows[...] = packed.astype(BF16)

    def store_solved(k, start, value):
        solved[pl.ds(start, z.own), :] = value
        rounded[pl.ds(start, z.own), :] = value.astype(BF16)

    multiply(z, inverse, load_rows[...], store_solved, wait)
    solved_b = rounded[...]
    half = z.lanes // 2
    for s in range(z.subs):
        basis = jnp.transpose(basis_t[s].astype(F32)).astype(BF16)
        tall[s, :, half : half + z.modes] = basis
        tall[s, :, half + z.modes :] = jnp.zeros((z.rows, half - z.modes), BF16)
        both[s, :, : z.lanes] = solved_b
        both[s, :, z.lanes : z.lanes + z.modes] = basis
        both[s, :, z.lanes + z.modes :] = jnp.zeros((z.rows, z.lanes - z.modes), BF16)
    for k, piece in enumerate(stiffness):
        wait(z.group + k)
        start = piece_start(z, k, z.own)
        parts = [dot(piece[s], both[s]) for s in range(z.subs)]
        image[pl.ds(start, z.own), :] = select(z, [part[:, : z.lanes] for part in parts])
        for s in range(z.subs):
            images[s, pl.ds(start, z.own), :] = parts[s].astype(BF16)
    for s in range(z.subs):
        tall[s, :, :half] = images[s, :, z.lanes : z.lanes + half]
        picked = dot(pick_both(z, left_rows, right_rows, s), images[s]).astype(BF16)
        faces = dot(picked[:, : z.lanes], lane_matrix(z, s * z.width, 0))
        faces = (faces + dot(picked[:, z.lanes :], lane_matrix(z, 0, half, z.modes))).astype(BF16)
        before[s] = faces[: z.face]
        after[s] = faces[z.face :]
    store_faces(z, before, after, first_pair, second_pair)


def begin_kernel(z, load_rows, image, tall, basis_t, left_rows, right_rows, left_t, right_t, inner, start_modes):
    left = (load_rows[...].astype(F32) - image[...]).astype(BF16)
    begun = []
    for s in range(z.subs):
        restricted = dot(basis_t[s], jnp.concatenate([left, tall[s]], axis=1))
        begun.append(restricted[:, : z.lanes])
        inner[s] = restricted[:, z.lanes : z.lanes + z.modes].astype(BF16)
        sides_t = dot_nt(basis_t[s], pick_both(z, left_rows, right_rows, s)).astype(BF16)
        left_t[s] = sides_t[:, : z.face]
        right_t[s] = sides_t[:, z.face :]
    start_modes[...] = select(z, begun)


def second_image_kernel(z, wait, *refs):
    inverse, stiffness = refs[: z.group], refs[z.group : 2 * z.group]
    rest = refs[2 * z.group :]
    load_rows, old_image, tall, old_solved, chosen = rest[:5]
    before, after, first_got, second_got, left_rows, right_rows = rest[5:11]
    new_before, new_after, first_pair, second_pair = rest[11:15]
    values = rest[15 : 15 + z.group]
    base, rounded, image = rest[15 + z.group :]
    steps, images = [], []
    for s in range(z.subs):
        faces = sides(z, before, after, first_got, second_got, s)
        both = [share.astype(BF16) for share in shares(z, s, chosen, faces)]
        left = jnp.concatenate([tall[s], scatter_matrix(z, left_rows[s : s + 1, :], 0, z.rows)], axis=1)
        total = dot(left, correction_side(z, chosen, s, both[0]))
        steps.append(total[:, z.lanes :])
        images.append(total[:, : z.lanes] + dot(scatter_matrix(z, right_rows[s : s + 1, :], 0, z.rows), both[1]))
    residual = (load_rows[...].astype(F32) - old_image[...] - select(z, images)).astype(BF16)
    base[...] = old_solved[...] + select(z, steps)

    def store_solved(k, start, value):
        value = value + base[pl.ds(start, z.own), :]
        values[k][0] = value
        rounded[pl.ds(start, z.own), :] = value.astype(BF16)

    multiply(z, inverse, residual, store_solved, wait)

    def store_image(k, start, value):
        place = pl.ds(start, z.own)
        values[k][1] = load_rows[place, :].astype(F32) - value
        image[place, :] = value.astype(BF16)

    multiply(z, stiffness, rounded[...], store_image, lambda k: wait(z.group + k))
    pick = jnp.concatenate([pick_both(z, left_rows, right_rows, s) for s in range(z.subs)], axis=0)
    picked = dot(pick, image[...]).astype(BF16)
    for s in range(z.subs):
        own = picked[2 * s * z.face : 2 * (s + 1) * z.face]
        faces = dot(own, lane_matrix(z, s * z.width, 0)).astype(BF16)
        new_before[s] = faces[: z.face]
        new_after[s] = faces[z.face :]
    store_faces(z, new_before, new_after, first_pair, second_pair)


def digit_row(shape, row):
    return lax.broadcasted_iota(jnp.int32, shape, 1) == row


def coarse_rows(z, ordered_inverse, arrived, message):
    flat = arrived[:, : z.modes, :].reshape(z.columns, z.lanes)
    rows = fold(z, select(z, [dot(ordered_inverse[s], flat) for s in range(z.subs)]))
    packed = select(z, [rows[s * z.modes : (s + 1) * z.modes, :] for s in range(z.subs)]).astype(BF16)
    for k in range(z.n):
        message[k] = packed


def order_kernel(z, *refs):
    blocks = refs[: z.group]
    arrived, repeat, own_row, place, ordered_inverse, picks, message = refs[z.group :]
    digits = arrived[:, z.modes :, :].astype(F32)
    index = []
    for s in range(z.subs):
        high = jnp.sum(jnp.where(digit_row(digits.shape, 2 * s), digits, 0.0), axis=1)
        low = jnp.sum(jnp.where(digit_row(digits.shape, 2 * s + 1), digits, 0.0), axis=1)
        index.append(high * DIGIT + low)
        spread = dot(high.astype(BF16), repeat[...]) * DIGIT + dot(low.astype(BF16), repeat[...])
        places = jnp.sum(spread * own_row[...], axis=0, keepdims=True).astype(jnp.int32)
        for at in range(0, z.columns, 768):
            wide = min(768, z.columns - at)
            total = jnp.zeros((z.owned, wide), F32)
            for k, block in enumerate(blocks):
                inside = (places[:, at : at + wide] - piece_start(z, k, z.block)).astype(jnp.int16)
                for first in range(0, z.block, 768):
                    deep = min(768, z.block - first)
                    row = lax.broadcasted_iota(jnp.int16, (deep, wide), 0) + jnp.int16(first)
                    hot = jnp.where(row == inside, jnp.ones((), BF16), jnp.zeros((), BF16))
                    total = total + dot(block[:, first : first + deep], hot)
            ordered_inverse[s, :, at : at + wide] = total.astype(BF16)
    coarse_rows(z, ordered_inverse, arrived, message)
    here = lax.axis_index("sub")
    device = lax.broadcasted_iota(jnp.int32, (z.n, z.lanes), 0)
    for t in range(z.subs + 2):
        if t == 0:
            s, owner = z.subs - 1, lax.rem(here + z.n - 1, z.n)
        elif t == z.subs + 1:
            s, owner = 0, lax.rem(here + 1, z.n)
        else:
            s, owner = t - 1, here
        row = jnp.sum(jnp.where(device == owner, index[s], 0.0), axis=0, keepdims=True)
        column = jnp.transpose(jnp.broadcast_to(row, (z.lanes, z.lanes)))[: z.modes, 0:1].astype(jnp.int32)
        for h in range(z.subs):
            hit = column == place[h : h + 1, :]
            picks[h, t * z.modes : (t + 1) * z.modes, :] = jnp.where(hit, 1.0, 0.0).astype(BF16)


def coarse_kernel(z, arrived, ordered_inverse, message):
    coarse_rows(z, ordered_inverse, arrived, message)


def picked_rows(z, arrived, picks):
    flat = arrived[...].reshape(z.columns, z.lanes)
    return fold(z, select(z, [dot(picks[h], flat) for h in range(z.subs)])).astype(BF16)


def update_kernel(z, *refs):
    arrived, picks, start_modes, inner, left_t, right_t, before, after, first_got, second_got = refs[:10]
    chosen, message = refs[10:]
    rows = picked_rows(z, arrived, picks)
    chosen[...] = rows
    m = z.modes
    parts = []
    for s in range(z.subs):
        faces = sides(z, before, after, first_got, second_got, s)
        both = shares(z, s, rows, faces)
        total = dot(inner[s], rows[(s + 1) * m : (s + 2) * m])
        parts.append(total + dot(left_t[s], both[0].astype(BF16)) + dot(right_t[s], both[1].astype(BF16)))
    modes = (start_modes[...] - select(z, parts)).astype(BF16)
    for k in range(z.n):
        message[k] = modes


def pick_kernel(z, *refs):
    arrived, picks, before, after, first_got, second_got = refs[:6]
    base_before, base_after, base_first, base_second, out = refs[6:]
    chosen = picked_rows(z, arrived, picks)
    near = chosen.shape[0]
    lefts, rights = [], []
    for s in range(z.subs):
        values = sides(z, before, after, first_got, second_got, s)
        bases = sides(z, base_before, base_after, base_first, base_second, s)
        left, right = shares(z, s, chosen, values, bases)
        lefts.append(left)
        rights.append(right)
    out[:near] = chosen
    out[near : near + z.face] = select(z, lefts).astype(BF16)
    out[near + z.face :] = select(z, rights).astype(BF16)


def last_kernel(z, *refs):
    chosen, values = refs[: z.group], refs[z.group : 2 * z.group]
    tall, left_rows, right_rows, second_pass, final_residual = refs[2 * z.group :]
    start = piece_start(z, 0, z.own)
    near = (z.subs + 2) * z.modes
    lefts, rights = [], []
    for s in range(z.subs):
        scatter = scatter_matrix(z, left_rows[s : s + 1, :], start, z.own)
        lefts.append(jnp.concatenate([tall[s, pl.ds(start, z.own), :], scatter], axis=1))
        rights.append(scatter_matrix(z, right_rows[s : s + 1, :], start, z.own))
    done = [jnp.zeros((z.own, z.lanes), F32) for _ in range(2 * z.subs)]
    for k in range(z.group):
        rows = chosen[k][:near]
        left, right = chosen[k][near : near + z.face], chosen[k][near + z.face :]
        steps, images = [], []
        for s in range(z.subs):
            total = dot(lefts[s], correction_side(z, rows, s, left))
            steps.append(total[:, z.lanes :])
            images.append(total[:, : z.lanes] + dot(rights[s], right))
        pair = values[k][0] + select(z, steps), values[k][1] - select(z, images)
        place = lax.rem(lax.axis_index(GROUP) + k, z.group)
        for at, packed in enumerate(pair):
            for s in range(z.subs):
                turn = lax.rem((place - s + z.subs * z.group) * z.width, z.lanes)
                turned = pltpu.roll(packed, turn, 1)
                here = at * z.subs + s
                done[here] = jnp.where(lane_mask(z, place, turned.shape), turned, done[here])
    for s in range(z.subs):
        second_pass[s] = done[s][:, : z.cases]
        final_residual[s] = done[z.subs + s][:, : z.cases]


def call(kernel, outs, operands, flops, scratch=(), late=(), loose=(), name=None):
    moved = sum(int(np.prod(x.shape)) * x.dtype.itemsize for x in (*operands, *outs))
    n_in, n_out = len(operands), len(outs)

    def whole(*refs):
        hbm, refs = refs[: n_in + n_out], refs[n_in + n_out :]
        vmem, refs = refs[: n_in + n_out], refs[n_in + n_out :]
        in_sems, out_sems, *rest = refs
        arriving = [pltpu.make_async_copy(hbm[i], vmem[i], in_sems.at[i]) for i in range(n_in)]
        for i in sorted(range(n_in), key=lambda i: i in late):
            arriving[i].start()
        for i, copy in enumerate(arriving):
            if i not in late:
                copy.wait()
        extra = [lambda i: arriving[i].wait()] if late else []
        kernel(*extra, *vmem, *rest)
        leaving = [pltpu.make_async_copy(vmem[n_in + i], hbm[n_in + i], out_sems.at[i]) for i in range(n_out)]
        for copy in leaving:
            copy.start()
        for copy in leaving:
            copy.wait()

    hbm_spec = pl.BlockSpec(memory_space=pltpu.HBM)
    any_spec = pl.BlockSpec(memory_space=pl.ANY)
    placed = [
        x if i in loose else pltpu.with_memory_space_constraint(x, pltpu.HBM) for i, x in enumerate(operands)
    ]
    return pl.pallas_call(
        whole,
        out_shape=[pltpu.HBM(o.shape, o.dtype) for o in outs],
        in_specs=[any_spec if i in loose else hbm_spec for i in range(n_in)],
        out_specs=[hbm_spec] * n_out,
        scratch_shapes=[
            *[pltpu.VMEM(x.shape, x.dtype) for x in (*operands, *outs)],
            pltpu.SemaphoreType.DMA((n_in,)),
            pltpu.SemaphoreType.DMA((n_out,)),
            *scratch,
        ],
        compiler_params=pltpu.CompilerParams(vmem_limit_bytes=VMEM_BYTES),
        cost_estimate=pl.CostEstimate(flops=flops, bytes_accessed=moved, transcendentals=0),
        name=name,
    )(*placed)


def shape(dims, dtype):
    return jax.ShapeDtypeStruct(dims, dtype)


def pieces_of(block, group):
    out = [block]
    for k in range(1, group):
        out.append(lax.ppermute(block, GROUP, [((g + k) % group, g) for g in range(group)]))
    return out


def body(loads, stiffness, local_inverse, coarse_basis, coarse_inverse, coarse_index, left_rows, right_rows):
    z = Sizes(loads, stiffness, coarse_basis, coarse_inverse, left_rows)
    n, group, subs, rows, lanes, modes, face = z.n, z.group, z.subs, z.rows, z.lanes, z.modes, z.face
    basis_pieces = pieces_of(jnp.swapaxes(coarse_basis, 1, 2), group)
    inverse_columns = pieces_of(coarse_inverse, group)
    basis_pieces, inverse_columns, local_inverse, stiffness = lax.optimization_barrier(
        (basis_pieces, inverse_columns, local_inverse, stiffness)
    )
    column = np.arange(z.columns)
    repeat = jnp.asarray(np.arange(lanes)[:, None] == column[None, :] % modes, BF16)
    own_row = jnp.asarray(np.arange(n)[:, None] == column[None, :] // modes, F32)
    place = jnp.asarray(
        (column // modes * z.owned + column % modes)[None, :] + np.arange(subs)[:, None] * modes, jnp.int32
    )
    packed_f = shape((rows, lanes), F32)
    packed_b = shape((rows, lanes), BF16)
    copies = shape((n, modes, lanes), BF16)
    tall = shape((subs, rows, lanes), BF16)
    spread = functools.partial(lax.all_to_all, axis_name="sub", split_axis=0, concat_axis=0)
    first_pairs = [(i, i + 1 if i % 2 == 0 else i - 1) for i in range(n)]
    second_pairs = [(i, (i + (1 if i % 2 else -1)) % n) for i in range(n)]
    work = 4 * subs * rows * rows * lanes

    (message,) = call(
        functools.partial(open_kernel, z),
        [shape((n, modes + DIGIT_ROWS, lanes), BF16)],
        [*basis_pieces, loads, coarse_index],
        4 * rows * lanes * lanes,
        [pltpu.VMEM((DIGIT_ROWS, lanes), F32), pltpu.VMEM((subs, modes, rows), BF16)],
        loose=range(1, group),
        name="open",
    )
    inverse_pieces = pieces_of(local_inverse, group)
    stiffness_pieces = pieces_of(stiffness, group)
    restricted = spread(message)
    arrivals = [*range(1, group), *range(group + 1, 2 * group)]
    faces = shape((subs, face, lanes), BF16)
    outer = shape((face, lanes), BF16)
    (
        load_rows, solved, image, before, after, first_pair, second_pair, tall, basis_t
    ) = call(
        functools.partial(first_image_kernel, z),
        [
            packed_b, packed_f, packed_f, faces, faces, outer, outer, tall, shape((subs, modes, rows), BF16),
        ],
        [*inverse_pieces, *stiffness_pieces, *basis_pieces, loads, left_rows, right_rows],
        work,
        [
            pltpu.VMEM((rows, lanes), BF16),
            pltpu.VMEM((subs, rows, 2 * lanes), BF16), pltpu.VMEM((subs, rows, 2 * lanes), BF16),
        ],
        late=range(2 * group),
        loose=[*arrivals, *range(2 * group + 1, 3 * group)],
        name="first_image",
    )
    second_got = lax.ppermute(second_pair, "sub", second_pairs)
    side = shape((subs, modes, face), BF16)
    left_t, right_t, inner, start_modes = call(
        functools.partial(begin_kernel, z),
        [side, side, shape((subs, modes, modes), BF16), shape((modes, lanes), F32)],
        [load_rows, image, tall, basis_t, left_rows, right_rows],
        work // 16,
        name="begin",
    )
    restricted, second_pair = lax.optimization_barrier((restricted, second_pair))
    near = (subs + 2) * modes
    ordered_inverse, picks, message = call(
        functools.partial(order_kernel, z),
        [shape((subs, z.owned, z.columns), BF16), shape((subs, near, z.columns), BF16), copies],
        [*inverse_columns, restricted, repeat, own_row, place],
        2 * z.owned * z.total * z.total,
        loose=range(1, group + 1),
        name="order",
    )
    coarse = spread(message)
    first_got = lax.ppermute(first_pair, "sub", first_pairs)
    chosen, message = call(
        functools.partial(update_kernel, z),
        [shape((near, lanes), BF16), copies],
        [coarse, picks, start_modes, inner, left_t, right_t, before, after, first_got, second_got],
        work // 64,
        loose=[0, 8, 9],
        name="update",
    )
    restricted = spread(message)

    bases = [before, after, first_got, second_got]
    before, after, first_pair, second_pair, *values = call(
        functools.partial(second_image_kernel, z),
        [faces, faces, outer, outer, *[shape((2, z.own, lanes), F32)] * group],
        [
            *inverse_pieces, *stiffness_pieces, load_rows, image, tall, solved, chosen,
            *bases, left_rows, right_rows,
        ],
        work,
        [pltpu.VMEM((rows, lanes), F32), pltpu.VMEM((rows, lanes), BF16), pltpu.VMEM((rows, lanes), BF16)],
        late=range(2 * group),
        loose=[*arrivals, 2 * group + 7, 2 * group + 8],
        name="second_image",
    )
    second_got = lax.ppermute(second_pair, "sub", second_pairs)
    restricted, before = lax.optimization_barrier((restricted, before))
    (message,) = call(
        functools.partial(coarse_kernel, z),
        [copies],
        [restricted, ordered_inverse],
        work // 64,
        loose=[0],
        name="coarse",
    )
    coarse = spread(message)
    first_got = lax.ppermute(first_pair, "sub", first_pairs)
    swapped = [values[0]]
    for k in range(1, group):
        swapped.append(lax.ppermute(values[k], GROUP, [(g, (g + k) % group) for g in range(group)]))
    swapped = [swapped[(group - k) % group] for k in range(group)]
    (chosen,) = call(
        functools.partial(pick_kernel, z),
        [shape((near + 2 * face, lanes), BF16)],
        [coarse, picks, before, after, first_got, second_got, *bases],
        work // 64,
        loose=[0, 4, 5, 8, 9],
        name="pick",
    )
    out = shape((subs, z.own, z.cases), F32)
    return tuple(
        call(
            functools.partial(last_kernel, z),
            [out, out],
            [*pieces_of(chosen, group), *swapped, tall, left_rows, right_rows],
            work // 8,
            loose=[*range(1, group), *range(group + 1, 2 * group)],
            name="last",
        )
    )


def solution(mesh):
    return jax.shard_map(
        body,
        mesh=mesh,
        in_specs=(
            P("sub", None, None),
            P("sub", GROUP, None),
            P("sub", GROUP, None),
            P("sub", GROUP, None),
            P("sub", GROUP),
            P("sub", None),
            P("sub", None),
            P("sub", None),
        ),
        out_specs=(P("sub", GROUP, None), P("sub", GROUP, None)),
        check_vma=False,
    )
```

```python
import functools

import jax
import jax.numpy as jnp
import numpy as np
from jax import lax
from jax.experimental import pallas as pl
from jax.experimental.pallas import tpu as pltpu
from jax.sharding import PartitionSpec as P

GROUP = ("crow", "ccol")
F32 = jnp.float32
BF16 = jnp.bfloat16
VMEM_BYTES = 48 * 1024 * 1024
DIGIT_ROWS = 16
DIGIT_BITS = 8
DIGIT = 1 << DIGIT_BITS


def dot(a, b):
    return lax.dot_general(a, b, (((1,), (0,)), ((), ())), preferred_element_type=F32)


def dot_tn(a, b):
    return lax.dot_general(a, b, (((0,), (0,)), ((), ())), preferred_element_type=F32)


def dot_nt(a, b):
    return lax.dot_general(a, b, (((1,), (1,)), ((), ())), preferred_element_type=F32)


class Sizes:
    def __init__(self, loads, stiffness, coarse_basis, coarse_inverse, left_rows):
        self.n = lax.axis_size("sub")
        self.group = lax.axis_size(GROUP)
        self.subs, self.rows, self.cases = loads.shape
        self.own = stiffness.shape[1]
        self.modes = coarse_basis.shape[2]
        self.owned, self.block = coarse_inverse.shape
        self.total = self.block * self.group
        self.face = left_rows.shape[1]
        self.width = self.cases // self.group
        self.lanes = max(self.cases, -(-self.subs * self.width // 128) * 128)
        self.columns = self.n * self.modes


def lane_mask(z, block, shape):
    lane = lax.broadcasted_iota(jnp.int32, shape, len(shape) - 1)
    return (lane >= block * z.width) & (lane < (block + 1) * z.width)


def select(z, parts):
    out = jnp.zeros_like(parts[0])
    for s, part in enumerate(parts):
        out = jnp.where(lane_mask(z, s, part.shape), part, out)
    return out


def fold(z, packed):
    if z.lanes == z.subs * z.width:
        out = packed
        for k in range(1, z.subs):
            out = out + pltpu.roll(packed, k * z.width, 1)
        return out
    out = packed
    for k in range(1, z.subs):
        out = out + pltpu.roll(packed, k * z.width, 1)
        out = out + pltpu.roll(packed, z.lanes - k * z.width, 1)
    return out


def lane_matrix(z, source, target, width=None):
    row = lax.broadcasted_iota(jnp.int32, (z.lanes, z.lanes), 0)
    lane = lax.broadcasted_iota(jnp.int32, (z.lanes, z.lanes), 1)
    hit = (row - source == lane - target) & (lane >= target) & (lane < target + (width or z.width))
    return jnp.where(hit, 1.0, 0.0).astype(BF16)


def piece_start(z, k, size):
    place = lax.rem(lax.axis_index(GROUP) + k, z.group)
    return pl.multiple_of(place * size, size)


def pick_matrix(z, rows_of):
    column = jnp.transpose(jnp.broadcast_to(rows_of.astype(F32), (z.face, z.face)))[:, 0:1].astype(jnp.int32)
    row = lax.broadcasted_iota(jnp.int32, (z.face, z.rows), 1)
    return jnp.where(row == column, 1.0, 0.0).astype(BF16)


def even():
    return lax.rem(lax.axis_index("sub"), 2) == 0


def case_matrix(z, s):
    row = lax.broadcasted_iota(jnp.int32, (z.cases, z.lanes), 0)
    lane = lax.broadcasted_iota(jnp.int32, (z.cases, z.lanes), 1)
    hit = (row - lax.axis_index(GROUP) * z.width == lane - s * z.width) & lane_mask(z, s, row.shape)
    return jnp.where(hit, 1.0, 0.0).astype(BF16)


def join_basis(z, pieces, basis_t):
    for k, piece in enumerate(pieces):
        basis_t[:, :, pl.ds(piece_start(z, k, z.own), z.own)] = piece[...]


def open_kernel(z, *refs):
    pieces = refs[: z.group]
    loads, index, message, digits, basis_t = refs[z.group :]
    join_basis(z, pieces, basis_t)
    total = jnp.zeros((z.modes, z.lanes), F32)
    for s in range(z.subs):
        total = total + dot(dot(basis_t[s], loads[s]).astype(BF16), case_matrix(z, s))
    modes = total.astype(BF16)
    digits[...] = jnp.zeros(digits.shape, F32)
    for s in range(z.subs):
        places = index[s : s + 1, :]
        digits[2 * s : 2 * s + 1, : z.modes] = (places >> DIGIT_BITS).astype(F32)
        digits[2 * s + 1 : 2 * s + 2, : z.modes] = (places & (DIGIT - 1)).astype(F32)
    for k in range(z.n):
        message[k, : z.modes, :] = modes
        message[k, z.modes :, :] = digits[...].astype(BF16)


def multiply(z, pieces, vector, store, wait):
    for k in range(z.group):
        wait(k)
    for k, piece in enumerate(pieces):
        parts = [dot(piece[s], vector) for s in range(z.subs)]
        store(k, piece_start(z, k, z.own), select(z, parts))


def pick_both(z, left_rows, right_rows, s):
    return jnp.concatenate(
        [pick_matrix(z, left_rows[s : s + 1, :]), pick_matrix(z, right_rows[s : s + 1, :])], axis=0
    )


def store_faces(z, before, after, first_pair, second_pair):
    first, last = before[0], after[z.subs - 1]
    first_pair[...] = jnp.where(even(), last, first)
    second_pair[...] = jnp.where(even(), first, last)


def sides(z, before, after, first_pair, second_pair, s):
    if s == 0:
        from_before = jnp.where(even(), second_pair[...], first_pair[...])
    else:
        from_before = after[s - 1]
    if s == z.subs - 1:
        from_after = jnp.where(even(), first_pair[...], second_pair[...])
    else:
        from_after = before[s + 1]
    return from_before, from_after


def shares(z, s, chosen, faces, bases=None):
    m, half = z.modes, z.lanes // 2
    moved = lane_matrix(z, 0, s * z.width)
    out = []
    for side, at in ((0, s), (1, s + 2)):
        own = chosen[at * m : (at + 1) * m]
        below = jnp.concatenate([own, jnp.zeros((half - m, z.lanes), BF16)], axis=0)
        if bases is None:
            total = dot(faces[side], jnp.concatenate([moved[:half], below], axis=0))
        else:
            above = jnp.zeros((half, z.lanes), BF16)
            total = dot(faces[side], moved) + dot(bases[side], jnp.concatenate([above, below], axis=0))
        out.append(total)
    return out


def correction_side(z, chosen, s, share):
    m, half = z.modes, z.lanes // 2
    own = chosen[(s + 1) * m : (s + 2) * m]
    none = jnp.zeros((half - m, z.lanes), BF16)
    nil = jnp.zeros((half, z.lanes), BF16)
    image = jnp.concatenate([own, none, nil, share], axis=0)
    step = jnp.concatenate([nil, own, none, jnp.zeros((z.face, z.lanes), BF16)], axis=0)
    return jnp.concatenate([image, step], axis=1)


def scatter_matrix(z, rows_of, start, count):
    row = lax.broadcasted_iota(jnp.int32, (count, z.face), 0) + start
    return jnp.where(row == rows_of, 1.0, 0.0).astype(BF16)


def first_image_kernel(z, wait, *refs):
    inverse, stiffness = refs[: z.group], refs[z.group : 2 * z.group]
    pieces = refs[2 * z.group : 3 * z.group]
    loads, left_rows, right_rows = refs[3 * z.group : 3 * z.group + 3]
    load_rows, solved, image, before, after, first_pair, second_pair = refs[3 * z.group + 3 : 3 * z.group + 10]
    tall, basis_t, rounded, both, images = refs[3 * z.group + 10 :]
    join_basis(z, pieces, basis_t)
    packed = dot(loads[0], case_matrix(z, 0))
    for s in range(1, z.subs):
        packed = packed + dot(loads[s], case_matrix(z, s))
    load_rows[...] = packed.astype(BF16)

    def store_solved(k, start, value):
        solved[pl.ds(start, z.own), :] = value
        rounded[pl.ds(start, z.own), :] = value.astype(BF16)

    multiply(z, inverse, load_rows[...], store_solved, wait)
    solved_b = rounded[...]
    half = z.lanes // 2
    for s in range(z.subs):
        basis = jnp.transpose(basis_t[s].astype(F32)).astype(BF16)
        tall[s, :, half : half + z.modes] = basis
        tall[s, :, half + z.modes :] = jnp.zeros((z.rows, half - z.modes), BF16)
        both[s, :, : z.lanes] = solved_b
        both[s, :, z.lanes : z.lanes + z.modes] = basis
        both[s, :, z.lanes + z.modes :] = jnp.zeros((z.rows, z.lanes - z.modes), BF16)
    for k, piece in enumerate(stiffness):
        wait(z.group + k)
        start = piece_start(z, k, z.own)
        parts = [dot(piece[s], both[s]) for s in range(z.subs)]
        image[pl.ds(start, z.own), :] = select(z, [part[:, : z.lanes] for part in parts])
        for s in range(z.subs):
            images[s, pl.ds(start, z.own), :] = parts[s].astype(BF16)
    for s in range(z.subs):
        tall[s, :, :half] = images[s, :, z.lanes : z.lanes + half]
        picked = dot(pick_both(z, left_rows, right_rows, s), images[s]).astype(BF16)
        faces = dot(picked[:, : z.lanes], lane_matrix(z, s * z.width, 0))
        faces = (faces + dot(picked[:, z.lanes :], lane_matrix(z, 0, half, z.modes))).astype(BF16)
        before[s] = faces[: z.face]
        after[s] = faces[z.face :]
    store_faces(z, before, after, first_pair, second_pair)


def begin_kernel(z, load_rows, image, tall, basis_t, left_rows, right_rows, left_t, right_t, inner, start_modes):
    left = (load_rows[...].astype(F32) - image[...]).astype(BF16)
    begun = []
    for s in range(z.subs):
        restricted = dot(basis_t[s], jnp.concatenate([left, tall[s]], axis=1))
        begun.append(restricted[:, : z.lanes])
        inner[s] = restricted[:, z.lanes : z.lanes + z.modes].astype(BF16)
        sides_t = dot_nt(basis_t[s], pick_both(z, left_rows, right_rows, s)).astype(BF16)
        left_t[s] = sides_t[:, : z.face]
        right_t[s] = sides_t[:, z.face :]
    start_modes[...] = select(z, begun)


def second_image_kernel(z, wait, *refs):
    inverse, stiffness = refs[: z.group], refs[z.group : 2 * z.group]
    rest = refs[2 * z.group :]
    load_rows, old_image, tall, old_solved, chosen = rest[:5]
    before, after, first_got, second_got, left_rows, right_rows = rest[5:11]
    new_before, new_after, first_pair, second_pair = rest[11:15]
    values = rest[15 : 15 + z.group]
    base, rounded, image = rest[15 + z.group :]
    steps, images = [], []
    for s in range(z.subs):
        faces = sides(z, before, after, first_got, second_got, s)
        both = [share.astype(BF16) for share in shares(z, s, chosen, faces)]
        left = jnp.concatenate([tall[s], scatter_matrix(z, left_rows[s : s + 1, :], 0, z.rows)], axis=1)
        total = dot(left, correction_side(z, chosen, s, both[0]))
        steps.append(total[:, z.lanes :])
        images.append(total[:, : z.lanes] + dot(scatter_matrix(z, right_rows[s : s + 1, :], 0, z.rows), both[1]))
    residual = (load_rows[...].astype(F32) - old_image[...] - select(z, images)).astype(BF16)
    base[...] = old_solved[...] + select(z, steps)

    def store_solved(k, start, value):
        value = value + base[pl.ds(start, z.own), :]
        values[k][0] = value
        rounded[pl.ds(start, z.own), :] = value.astype(BF16)

    multiply(z, inverse, residual, store_solved, wait)

    def store_image(k, start, value):
        place = pl.ds(start, z.own)
        values[k][1] = load_rows[place, :].astype(F32) - value
        image[place, :] = value.astype(BF16)

    multiply(z, stiffness, rounded[...], store_image, lambda k: wait(z.group + k))
    pick = jnp.concatenate([pick_both(z, left_rows, right_rows, s) for s in range(z.subs)], axis=0)
    picked = dot(pick, image[...]).astype(BF16)
    for s in range(z.subs):
        own = picked[2 * s * z.face : 2 * (s + 1) * z.face]
        faces = dot(own, lane_matrix(z, s * z.width, 0)).astype(BF16)
        new_before[s] = faces[: z.face]
        new_after[s] = faces[z.face :]
    store_faces(z, new_before, new_after, first_pair, second_pair)


def digit_row(shape, row):
    return lax.broadcasted_iota(jnp.int32, shape, 1) == row


def coarse_rows(z, ordered_inverse, arrived, message):
    flat = arrived[:, : z.modes, :].reshape(z.columns, z.lanes)
    rows = fold(z, select(z, [dot(ordered_inverse[s], flat) for s in range(z.subs)]))
    packed = select(z, [rows[s * z.modes : (s + 1) * z.modes, :] for s in range(z.subs)]).astype(BF16)
    for k in range(z.n):
        message[k] = packed


def order_kernel(z, *refs):
    blocks = refs[: z.group]
    arrived, repeat, own_row, place, ordered_inverse, picks, message = refs[z.group :]
    digits = arrived[:, z.modes :, :].astype(F32)
    index = []
    for s in range(z.subs):
        high = jnp.sum(jnp.where(digit_row(digits.shape, 2 * s), digits, 0.0), axis=1)
        low = jnp.sum(jnp.where(digit_row(digits.shape, 2 * s + 1), digits, 0.0), axis=1)
        index.append(high * DIGIT + low)
        spread = dot(high.astype(BF16), repeat[...]) * DIGIT + dot(low.astype(BF16), repeat[...])
        places = jnp.sum(spread * own_row[...], axis=0, keepdims=True).astype(jnp.int32)
        for at in range(0, z.columns, 768):
            wide = min(768, z.columns - at)
            total = jnp.zeros((z.owned, wide), F32)
            for k, block in enumerate(blocks):
                inside = (places[:, at : at + wide] - piece_start(z, k, z.block)).astype(jnp.int16)
                for first in range(0, z.block, 768):
                    deep = min(768, z.block - first)
                    row = lax.broadcasted_iota(jnp.int16, (deep, wide), 0) + jnp.int16(first)
                    hot = jnp.where(row == inside, jnp.ones((), BF16), jnp.zeros((), BF16))
                    total = total + dot(block[:, first : first + deep], hot)
            ordered_inverse[s, :, at : at + wide] = total.astype(BF16)
    coarse_rows(z, ordered_inverse, arrived, message)
    here = lax.axis_index("sub")
    device = lax.broadcasted_iota(jnp.int32, (z.n, z.lanes), 0)
    for t in range(z.subs + 2):
        if t == 0:
            s, owner = z.subs - 1, lax.rem(here + z.n - 1, z.n)
        elif t == z.subs + 1:
            s, owner = 0, lax.rem(here + 1, z.n)
        else:
            s, owner = t - 1, here
        row = jnp.sum(jnp.where(device == owner, index[s], 0.0), axis=0, keepdims=True)
        column = jnp.transpose(jnp.broadcast_to(row, (z.lanes, z.lanes)))[: z.modes, 0:1].astype(jnp.int32)
        for h in range(z.subs):
            hit = column == place[h : h + 1, :]
            picks[h, t * z.modes : (t + 1) * z.modes, :] = jnp.where(hit, 1.0, 0.0).astype(BF16)


def coarse_kernel(z, arrived, ordered_inverse, message):
    coarse_rows(z, ordered_inverse, arrived, message)


def picked_rows(z, arrived, picks):
    flat = arrived[...].reshape(z.columns, z.lanes)
    return fold(z, select(z, [dot(picks[h], flat) for h in range(z.subs)])).astype(BF16)


def update_kernel(z, *refs):
    arrived, picks, start_modes, inner, left_t, right_t, before, after, first_got, second_got = refs[:10]
    chosen, message = refs[10:]
    rows = picked_rows(z, arrived, picks)
    chosen[...] = rows
    m = z.modes
    parts = []
    for s in range(z.subs):
        faces = sides(z, before, after, first_got, second_got, s)
        both = shares(z, s, rows, faces)
        total = dot(inner[s], rows[(s + 1) * m : (s + 2) * m])
        parts.append(total + dot(left_t[s], both[0].astype(BF16)) + dot(right_t[s], both[1].astype(BF16)))
    modes = (start_modes[...] - select(z, parts)).astype(BF16)
    for k in range(z.n):
        message[k] = modes


def pick_kernel(z, arrived, picks, before, after, base_before, base_after, base_first, base_second, out):
    chosen = picked_rows(z, arrived, picks)
    near = chosen.shape[0]
    none = jnp.zeros((z.face, z.lanes), BF16)
    lefts, rights = [], []
    for s in range(z.subs):
        values = (none if s == 0 else after[s - 1]), (none if s == z.subs - 1 else before[s + 1])
        bases = sides(z, base_before, base_after, base_first, base_second, s)
        left, right = shares(z, s, chosen, values, bases)
        lefts.append(left)
        rights.append(right)
    out[:near] = chosen
    out[near : near + z.face] = select(z, lefts).astype(BF16)
    out[near + z.face :] = select(z, rights).astype(BF16)


def last_kernel(z, *refs):
    chosen, values = refs[: z.group], refs[z.group : 2 * z.group]
    firsts, seconds = refs[2 * z.group : 3 * z.group], refs[3 * z.group : 4 * z.group]
    tall, left_rows, right_rows, second_pass, final_residual = refs[4 * z.group :]
    start = piece_start(z, 0, z.own)
    near = (z.subs + 2) * z.modes
    lefts, rights = [], []
    for s in range(z.subs):
        scatter = scatter_matrix(z, left_rows[s : s + 1, :], start, z.own)
        lefts.append(jnp.concatenate([tall[s, pl.ds(start, z.own), :], scatter], axis=1))
        rights.append(scatter_matrix(z, right_rows[s : s + 1, :], start, z.own))
    done = [jnp.zeros((z.own, z.lanes), F32) for _ in range(2 * z.subs)]
    for k in range(z.group):
        rows = chosen[k][:near]
        from_before = dot(jnp.where(even(), seconds[k][...], firsts[k][...]), lane_matrix(z, 0, 0))
        from_after = dot(
            jnp.where(even(), firsts[k][...], seconds[k][...]), lane_matrix(z, 0, (z.subs - 1) * z.width)
        )
        left = (chosen[k][near : near + z.face].astype(F32) + from_before).astype(BF16)
        right = (chosen[k][near + z.face :].astype(F32) + from_after).astype(BF16)
        steps, images = [], []
        for s in range(z.subs):
            total = dot(lefts[s], correction_side(z, rows, s, left))
            steps.append(total[:, z.lanes :])
            images.append(total[:, : z.lanes] + dot(rights[s], right))
        pair = values[k][0] + select(z, steps), values[k][1] - select(z, images)
        place = lax.rem(lax.axis_index(GROUP) + k, z.group)
        for at, packed in enumerate(pair):
            for s in range(z.subs):
                turn = lax.rem((place - s + z.subs * z.group) * z.width, z.lanes)
                turned = pltpu.roll(packed, turn, 1)
                here = at * z.subs + s
                done[here] = jnp.where(lane_mask(z, place, turned.shape), turned, done[here])
    for s in range(z.subs):
        second_pass[s] = done[s][:, : z.cases]
        final_residual[s] = done[z.subs + s][:, : z.cases]


def call(kernel, outs, operands, flops, scratch=(), late=(), loose=(), name=None):
    moved = sum(int(np.prod(x.shape)) * x.dtype.itemsize for x in (*operands, *outs))
    n_in, n_out = len(operands), len(outs)

    def whole(*refs):
        hbm, refs = refs[: n_in + n_out], refs[n_in + n_out :]
        vmem, refs = refs[: n_in + n_out], refs[n_in + n_out :]
        in_sems, out_sems, *rest = refs
        arriving = [pltpu.make_async_copy(hbm[i], vmem[i], in_sems.at[i]) for i in range(n_in)]
        for i in sorted(range(n_in), key=lambda i: i in late):
            arriving[i].start()
        for i, copy in enumerate(arriving):
            if i not in late:
                copy.wait()
        extra = [lambda i: arriving[i].wait()] if late else []
        kernel(*extra, *vmem, *rest)
        leaving = [pltpu.make_async_copy(vmem[n_in + i], hbm[n_in + i], out_sems.at[i]) for i in range(n_out)]
        for copy in leaving:
            copy.start()
        for copy in leaving:
            copy.wait()

    hbm_spec = pl.BlockSpec(memory_space=pltpu.HBM)
    any_spec = pl.BlockSpec(memory_space=pl.ANY)
    placed = [
        x if i in loose else pltpu.with_memory_space_constraint(x, pltpu.HBM) for i, x in enumerate(operands)
    ]
    return pl.pallas_call(
        whole,
        out_shape=[pltpu.HBM(o.shape, o.dtype) for o in outs],
        in_specs=[any_spec if i in loose else hbm_spec for i in range(n_in)],
        out_specs=[hbm_spec] * n_out,
        scratch_shapes=[
            *[pltpu.VMEM(x.shape, x.dtype) for x in (*operands, *outs)],
            pltpu.SemaphoreType.DMA((n_in,)),
            pltpu.SemaphoreType.DMA((n_out,)),
            *scratch,
        ],
        compiler_params=pltpu.CompilerParams(vmem_limit_bytes=VMEM_BYTES),
        cost_estimate=pl.CostEstimate(flops=flops, bytes_accessed=moved, transcendentals=0),
        name=name,
    )(*placed)


def shape(dims, dtype):
    return jax.ShapeDtypeStruct(dims, dtype)


def pieces_of(block, group):
    out = [block]
    for k in range(1, group):
        out.append(lax.ppermute(block, GROUP, [((g + k) % group, g) for g in range(group)]))
    return out


def body(loads, stiffness, local_inverse, coarse_basis, coarse_inverse, coarse_index, left_rows, right_rows):
    z = Sizes(loads, stiffness, coarse_basis, coarse_inverse, left_rows)
    n, group, subs, rows, lanes, modes, face = z.n, z.group, z.subs, z.rows, z.lanes, z.modes, z.face
    basis_pieces = pieces_of(jnp.swapaxes(coarse_basis, 1, 2), group)
    inverse_columns = pieces_of(coarse_inverse, group)
    basis_pieces, inverse_columns, local_inverse, stiffness = lax.optimization_barrier(
        (basis_pieces, inverse_columns, local_inverse, stiffness)
    )
    column = np.arange(z.columns)
    repeat = jnp.asarray(np.arange(lanes)[:, None] == column[None, :] % modes, BF16)
    own_row = jnp.asarray(np.arange(n)[:, None] == column[None, :] // modes, F32)
    place = jnp.asarray(
        (column // modes * z.owned + column % modes)[None, :] + np.arange(subs)[:, None] * modes, jnp.int32
    )
    packed_f = shape((rows, lanes), F32)
    packed_b = shape((rows, lanes), BF16)
    copies = shape((n, modes, lanes), BF16)
    tall = shape((subs, rows, lanes), BF16)
    spread = functools.partial(lax.all_to_all, axis_name="sub", split_axis=0, concat_axis=0)
    first_pairs = [(i, i + 1 if i % 2 == 0 else i - 1) for i in range(n)]
    second_pairs = [(i, (i + (1 if i % 2 else -1)) % n) for i in range(n)]
    work = 4 * subs * rows * rows * lanes

    (message,) = call(
        functools.partial(open_kernel, z),
        [shape((n, modes + DIGIT_ROWS, lanes), BF16)],
        [*basis_pieces, loads, coarse_index],
        4 * rows * lanes * lanes,
        [pltpu.VMEM((DIGIT_ROWS, lanes), F32), pltpu.VMEM((subs, modes, rows), BF16)],
        loose=range(1, group),
        name="open",
    )
    inverse_pieces = pieces_of(local_inverse, group)
    stiffness_pieces = pieces_of(stiffness, group)
    restricted = spread(message)
    arrivals = [*range(1, group), *range(group + 1, 2 * group)]
    faces = shape((subs, face, lanes), BF16)
    outer = shape((face, lanes), BF16)
    (
        load_rows, solved, image, before, after, first_pair, second_pair, tall, basis_t
    ) = call(
        functools.partial(first_image_kernel, z),
        [
            packed_b, packed_f, packed_f, faces, faces, outer, outer, tall, shape((subs, modes, rows), BF16),
        ],
        [*inverse_pieces, *stiffness_pieces, *basis_pieces, loads, left_rows, right_rows],
        work,
        [
            pltpu.VMEM((rows, lanes), BF16),
            pltpu.VMEM((subs, rows, 2 * lanes), BF16), pltpu.VMEM((subs, rows, 2 * lanes), BF16),
        ],
        late=range(2 * group),
        loose=[*arrivals, *range(2 * group + 1, 3 * group)],
        name="first_image",
    )
    second_got = lax.ppermute(second_pair, "sub", second_pairs)
    side = shape((subs, modes, face), BF16)
    left_t, right_t, inner, start_modes = call(
        functools.partial(begin_kernel, z),
        [side, side, shape((subs, modes, modes), BF16), shape((modes, lanes), F32)],
        [load_rows, image, tall, basis_t, left_rows, right_rows],
        work // 16,
        name="begin",
    )
    restricted, second_pair = lax.optimization_barrier((restricted, second_pair))
    near = (subs + 2) * modes
    ordered_inverse, picks, message = call(
        functools.partial(order_kernel, z),
        [shape((subs, z.owned, z.columns), BF16), shape((subs, near, z.columns), BF16), copies],
        [*inverse_columns, restricted, repeat, own_row, place],
        2 * z.owned * z.total * z.total,
        loose=range(1, group + 1),
        name="order",
    )
    coarse = spread(message)
    first_got = lax.ppermute(first_pair, "sub", first_pairs)
    chosen, message = call(
        functools.partial(update_kernel, z),
        [shape((near, lanes), BF16), copies],
        [coarse, picks, start_modes, inner, left_t, right_t, before, after, first_got, second_got],
        work // 64,
        loose=[0, 8, 9],
        name="update",
    )
    restricted = spread(message)

    bases = [before, after, first_got, second_got]
    before, after, first_pair, second_pair, *values = call(
        functools.partial(second_image_kernel, z),
        [faces, faces, outer, outer, *[shape((2, z.own, lanes), F32)] * group],
        [
            *inverse_pieces, *stiffness_pieces, load_rows, image, tall, solved, chosen,
            *bases, left_rows, right_rows,
        ],
        work,
        [pltpu.VMEM((rows, lanes), F32), pltpu.VMEM((rows, lanes), BF16), pltpu.VMEM((rows, lanes), BF16)],
        late=range(2 * group),
        loose=[*arrivals, 2 * group + 7, 2 * group + 8],
        name="second_image",
    )
    second_got = lax.ppermute(second_pair, "sub", second_pairs)
    restricted, before = lax.optimization_barrier((restricted, before))
    (message,) = call(
        functools.partial(coarse_kernel, z),
        [copies],
        [restricted, ordered_inverse],
        work // 64,
        loose=[0],
        name="coarse",
    )
    coarse = spread(message)
    first_got = lax.ppermute(first_pair, "sub", first_pairs)
    swapped = [values[0]]
    for k in range(1, group):
        swapped.append(lax.ppermute(values[k], GROUP, [(g, (g + k) % group) for g in range(group)]))
    swapped = [swapped[(group - k) % group] for k in range(group)]
    (chosen,) = call(
        functools.partial(pick_kernel, z),
        [shape((near + 2 * face, lanes), BF16)],
        [coarse, picks, before, after, *bases],
        work // 64,
        loose=[0, 6, 7],
        name="pick",
    )
    out = shape((subs, z.own, z.cases), F32)
    return tuple(
        call(
            functools.partial(last_kernel, z),
            [out, out],
            [
                *pieces_of(chosen, group), *swapped, *pieces_of(first_got, group), *pieces_of(second_got, group),
                tall, left_rows, right_rows,
            ],
            work // 8,
            loose=[*range(1, group), *range(group + 1, 4 * group)],
            name="last",
        )
    )


def solution(mesh):
    return jax.shard_map(
        body,
        mesh=mesh,
        in_specs=(
            P("sub", None, None),
            P("sub", GROUP, None),
            P("sub", GROUP, None),
            P("sub", GROUP, None),
            P("sub", GROUP),
            P("sub", None),
            P("sub", None),
            P("sub", None),
        ),
        out_specs=(P("sub", GROUP, None), P("sub", GROUP, None)),
        check_vma=False,
    )
```

```python
import functools

import jax
import jax.numpy as jnp
import numpy as np
from jax import lax
from jax.experimental import pallas as pl
from jax.experimental.pallas import tpu as pltpu
from jax.sharding import PartitionSpec as P

GROUP = ("crow", "ccol")
F32 = jnp.float32
BF16 = jnp.bfloat16
VMEM_BYTES = 48 * 1024 * 1024
DIGIT_ROWS = 16
DIGIT_BITS = 8
DIGIT = 1 << DIGIT_BITS


def dot(a, b):
    return lax.dot_general(a, b, (((1,), (0,)), ((), ())), preferred_element_type=F32)


def dot_tn(a, b):
    return lax.dot_general(a, b, (((0,), (0,)), ((), ())), preferred_element_type=F32)


def dot_nt(a, b):
    return lax.dot_general(a, b, (((1,), (1,)), ((), ())), preferred_element_type=F32)


class Sizes:
    def __init__(self, loads, stiffness, coarse_basis, coarse_inverse, left_rows):
        self.n = lax.axis_size("sub")
        self.group = lax.axis_size(GROUP)
        self.subs, self.rows, self.cases = loads.shape
        self.own = stiffness.shape[1]
        self.modes = coarse_basis.shape[2]
        self.owned, self.block = coarse_inverse.shape
        self.total = self.block * self.group
        self.face = left_rows.shape[1]
        self.width = self.cases // self.group
        self.lanes = max(self.cases, -(-self.subs * self.width // 128) * 128)
        self.columns = self.n * self.modes


def lane_mask(z, block, shape):
    lane = lax.broadcasted_iota(jnp.int32, shape, len(shape) - 1)
    return (lane >= block * z.width) & (lane < (block + 1) * z.width)


def select(z, parts):
    out = jnp.zeros_like(parts[0])
    for s, part in enumerate(parts):
        out = jnp.where(lane_mask(z, s, part.shape), part, out)
    return out


def fold(z, packed):
    if z.lanes == z.subs * z.width:
        out = packed
        for k in range(1, z.subs):
            out = out + pltpu.roll(packed, k * z.width, 1)
        return out
    out = packed
    for k in range(1, z.subs):
        out = out + pltpu.roll(packed, k * z.width, 1)
        out = out + pltpu.roll(packed, z.lanes - k * z.width, 1)
    return out


def lane_matrix(z, source, target, width=None):
    row = lax.broadcasted_iota(jnp.int32, (z.lanes, z.lanes), 0)
    lane = lax.broadcasted_iota(jnp.int32, (z.lanes, z.lanes), 1)
    hit = (row - source == lane - target) & (lane >= target) & (lane < target + (width or z.width))
    return jnp.where(hit, 1.0, 0.0).astype(BF16)


def piece_start(z, k, size):
    place = lax.rem(lax.axis_index(GROUP) + k, z.group)
    return pl.multiple_of(place * size, size)


def pick_matrix(z, rows_of):
    column = jnp.transpose(jnp.broadcast_to(rows_of.astype(F32), (z.face, z.face)))[:, 0:1].astype(jnp.int32)
    row = lax.broadcasted_iota(jnp.int32, (z.face, z.rows), 1)
    return jnp.where(row == column, 1.0, 0.0).astype(BF16)


def even():
    return lax.rem(lax.axis_index("sub"), 2) == 0


def case_matrix(z, s):
    row = lax.broadcasted_iota(jnp.int32, (z.cases, z.lanes), 0)
    lane = lax.broadcasted_iota(jnp.int32, (z.cases, z.lanes), 1)
    hit = (row - lax.axis_index(GROUP) * z.width == lane - s * z.width) & lane_mask(z, s, row.shape)
    return jnp.where(hit, 1.0, 0.0).astype(BF16)


def join_basis(z, pieces, basis_t):
    for k, piece in enumerate(pieces):
        basis_t[:, :, pl.ds(piece_start(z, k, z.own), z.own)] = piece[...]


def open_kernel(z, *refs):
    pieces = refs[: z.group]
    loads, index, message, digits, basis_t = refs[z.group :]
    join_basis(z, pieces, basis_t)
    total = jnp.zeros((z.modes, z.lanes), F32)
    for s in range(z.subs):
        total = total + dot(dot(basis_t[s], loads[s]).astype(BF16), case_matrix(z, s))
    modes = total.astype(BF16)
    digits[...] = jnp.zeros(digits.shape, F32)
    for s in range(z.subs):
        places = index[s : s + 1, :]
        digits[2 * s : 2 * s + 1, : z.modes] = (places >> DIGIT_BITS).astype(F32)
        digits[2 * s + 1 : 2 * s + 2, : z.modes] = (places & (DIGIT - 1)).astype(F32)
    for k in range(z.n):
        message[k, : z.modes, :] = modes
        message[k, z.modes :, :] = digits[...].astype(BF16)


def multiply(z, pieces, vector, store, wait):
    for k in range(z.group):
        wait(k)
    for k, piece in enumerate(pieces):
        parts = [dot(piece[s], vector) for s in range(z.subs)]
        store(k, piece_start(z, k, z.own), select(z, parts))


def pick_both(z, left_rows, right_rows, s):
    return jnp.concatenate(
        [pick_matrix(z, left_rows[s : s + 1, :]), pick_matrix(z, right_rows[s : s + 1, :])], axis=0
    )


def store_faces(z, before, after, first_pair, second_pair):
    first, last = before[0], after[z.subs - 1]
    first_pair[...] = jnp.where(even(), last, first)
    second_pair[...] = jnp.where(even(), first, last)


def sides(z, before, after, first_pair, second_pair, s):
    if s == 0:
        from_before = jnp.where(even(), second_pair[...], first_pair[...])
    else:
        from_before = after[s - 1]
    if s == z.subs - 1:
        from_after = jnp.where(even(), first_pair[...], second_pair[...])
    else:
        from_after = before[s + 1]
    return from_before, from_after


def shares(z, s, chosen, faces, bases=None):
    m, half = z.modes, z.lanes // 2
    moved = lane_matrix(z, 0, s * z.width)
    out = []
    for side, at in ((0, s), (1, s + 2)):
        own = chosen[at * m : (at + 1) * m]
        below = jnp.concatenate([own, jnp.zeros((half - m, z.lanes), BF16)], axis=0)
        if bases is None:
            total = dot(faces[side], jnp.concatenate([moved[:half], below], axis=0))
        else:
            above = jnp.zeros((half, z.lanes), BF16)
            total = dot(faces[side], moved) + dot(bases[side], jnp.concatenate([above, below], axis=0))
        out.append(total)
    return out


def correction_side(z, chosen, s, share):
    m, half = z.modes, z.lanes // 2
    own = chosen[(s + 1) * m : (s + 2) * m]
    none = jnp.zeros((half - m, z.lanes), BF16)
    nil = jnp.zeros((half, z.lanes), BF16)
    image = jnp.concatenate([own, none, nil, share], axis=0)
    step = jnp.concatenate([nil, own, none, jnp.zeros((z.face, z.lanes), BF16)], axis=0)
    return jnp.concatenate([image, step], axis=1)


def scatter_matrix(z, rows_of, start, count):
    row = lax.broadcasted_iota(jnp.int32, (count, z.face), 0) + start
    return jnp.where(row == rows_of, 1.0, 0.0).astype(BF16)


def first_image_kernel(z, wait, *refs):
    inverse, stiffness = refs[: z.group], refs[z.group : 2 * z.group]
    pieces = refs[2 * z.group : 3 * z.group]
    loads, left_rows, right_rows = refs[3 * z.group : 3 * z.group + 3]
    load_rows, solved, image, before, after, first_pair, second_pair = refs[3 * z.group + 3 : 3 * z.group + 10]
    tall, basis_t, rounded, both, images = refs[3 * z.group + 10 :]
    join_basis(z, pieces, basis_t)
    packed = dot(loads[0], case_matrix(z, 0))
    for s in range(1, z.subs):
        packed = packed + dot(loads[s], case_matrix(z, s))
    load_rows[...] = packed.astype(BF16)

    def store_solved(k, start, value):
        solved[pl.ds(start, z.own), :] = value
        rounded[pl.ds(start, z.own), :] = value.astype(BF16)

    multiply(z, inverse, load_rows[...], store_solved, wait)
    solved_b = rounded[...]
    half = z.lanes // 2
    for s in range(z.subs):
        basis = jnp.transpose(basis_t[s].astype(F32)).astype(BF16)
        tall[s, :, half : half + z.modes] = basis
        tall[s, :, half + z.modes :] = jnp.zeros((z.rows, half - z.modes), BF16)
        both[s, :, : z.lanes] = solved_b
        both[s, :, z.lanes : z.lanes + z.modes] = basis
        both[s, :, z.lanes + z.modes :] = jnp.zeros((z.rows, z.lanes - z.modes), BF16)
    for k, piece in enumerate(stiffness):
        wait(z.group + k)
        start = piece_start(z, k, z.own)
        parts = [dot(piece[s], both[s]) for s in range(z.subs)]
        image[pl.ds(start, z.own), :] = select(z, [part[:, : z.lanes] for part in parts])
        for s in range(z.subs):
            images[s, pl.ds(start, z.own), :] = parts[s].astype(BF16)
    for s in range(z.subs):
        tall[s, :, :half] = images[s, :, z.lanes : z.lanes + half]
        picked = dot(pick_both(z, left_rows, right_rows, s), images[s]).astype(BF16)
        faces = dot(picked[:, : z.lanes], lane_matrix(z, s * z.width, 0))
        faces = (faces + dot(picked[:, z.lanes :], lane_matrix(z, 0, half, z.modes))).astype(BF16)
        before[s] = faces[: z.face]
        after[s] = faces[z.face :]
    store_faces(z, before, after, first_pair, second_pair)


def begin_kernel(z, *refs):
    load_rows, image, tall, basis_t, left_rows, right_rows, index, place = refs[:8]
    left_t, right_t, inner, start_modes, picks = refs[8:]
    left = (load_rows[...].astype(F32) - image[...]).astype(BF16)
    begun = []
    for s in range(z.subs):
        restricted = dot(basis_t[s], jnp.concatenate([left, tall[s]], axis=1))
        begun.append(restricted[:, : z.lanes])
        inner[s] = restricted[:, z.lanes : z.lanes + z.modes].astype(BF16)
        sides_t = dot_nt(basis_t[s], pick_both(z, left_rows, right_rows, s)).astype(BF16)
        left_t[s] = sides_t[:, : z.face]
        right_t[s] = sides_t[:, z.face :]
    start_modes[...] = select(z, begun)
    here = lax.axis_index("sub")
    device = lax.broadcasted_iota(jnp.int32, (z.n, z.lanes), 0)
    for t in range(z.subs + 2):
        if t == 0:
            s, owner = z.subs - 1, lax.rem(here + z.n - 1, z.n)
        elif t == z.subs + 1:
            s, owner = 0, lax.rem(here + 1, z.n)
        else:
            s, owner = t - 1, here
        row = jnp.sum(jnp.where(device == owner, index[s], 0.0), axis=0, keepdims=True)
        column = jnp.transpose(jnp.broadcast_to(row, (z.lanes, z.lanes)))[: z.modes, 0:1].astype(jnp.int32)
        for h in range(z.subs):
            hit = column == place[h : h + 1, :]
            picks[h, t * z.modes : (t + 1) * z.modes, :] = jnp.where(hit, 1.0, 0.0).astype(BF16)


def second_image_kernel(z, wait, *refs):
    inverse, stiffness = refs[: z.group], refs[z.group : 2 * z.group]
    rest = refs[2 * z.group :]
    load_rows, old_image, tall, old_solved, chosen = rest[:5]
    before, after, first_got, second_got, left_rows, right_rows = rest[5:11]
    new_before, new_after, first_pair, second_pair = rest[11:15]
    values = rest[15 : 15 + z.group]
    base, rounded, image = rest[15 + z.group :]
    steps, images = [], []
    for s in range(z.subs):
        faces = sides(z, before, after, first_got, second_got, s)
        both = [share.astype(BF16) for share in shares(z, s, chosen, faces)]
        left = jnp.concatenate([tall[s], scatter_matrix(z, left_rows[s : s + 1, :], 0, z.rows)], axis=1)
        total = dot(left, correction_side(z, chosen, s, both[0]))
        steps.append(total[:, z.lanes :])
        images.append(total[:, : z.lanes] + dot(scatter_matrix(z, right_rows[s : s + 1, :], 0, z.rows), both[1]))
    residual = (load_rows[...].astype(F32) - old_image[...] - select(z, images)).astype(BF16)
    base[...] = old_solved[...] + select(z, steps)

    def store_solved(k, start, value):
        value = value + base[pl.ds(start, z.own), :]
        values[k][0] = value
        rounded[pl.ds(start, z.own), :] = value.astype(BF16)

    multiply(z, inverse, residual, store_solved, wait)

    def store_image(k, start, value):
        place = pl.ds(start, z.own)
        values[k][1] = load_rows[place, :].astype(F32) - value
        image[place, :] = value.astype(BF16)

    multiply(z, stiffness, rounded[...], store_image, lambda k: wait(z.group + k))
    pick = jnp.concatenate([pick_both(z, left_rows, right_rows, s) for s in range(z.subs)], axis=0)
    picked = dot(pick, image[...]).astype(BF16)
    for s in range(z.subs):
        own = picked[2 * s * z.face : 2 * (s + 1) * z.face]
        faces = dot(own, lane_matrix(z, s * z.width, 0)).astype(BF16)
        new_before[s] = faces[: z.face]
        new_after[s] = faces[z.face :]
    store_faces(z, new_before, new_after, first_pair, second_pair)


def digit_row(shape, row):
    return lax.broadcasted_iota(jnp.int32, shape, 1) == row


def coarse_rows(z, ordered_inverse, arrived, message):
    flat = arrived[:, : z.modes, :].reshape(z.columns, z.lanes)
    rows = fold(z, select(z, [dot(ordered_inverse[s], flat) for s in range(z.subs)]))
    packed = select(z, [rows[s * z.modes : (s + 1) * z.modes, :] for s in range(z.subs)]).astype(BF16)
    for k in range(z.n):
        message[k] = packed


def order_kernel(z, *refs):
    blocks = refs[: z.group]
    arrived, repeat, own_row, ordered_inverse, index, message = refs[z.group :]
    digits = arrived[:, z.modes :, :].astype(F32)
    for s in range(z.subs):
        high = jnp.sum(jnp.where(digit_row(digits.shape, 2 * s), digits, 0.0), axis=1)
        low = jnp.sum(jnp.where(digit_row(digits.shape, 2 * s + 1), digits, 0.0), axis=1)
        index[s] = high * DIGIT + low
        spread = dot(high.astype(BF16), repeat[...]) * DIGIT + dot(low.astype(BF16), repeat[...])
        places = jnp.sum(spread * own_row[...], axis=0, keepdims=True).astype(jnp.int32)
        for at in range(0, z.columns, 768):
            wide = min(768, z.columns - at)
            total = jnp.zeros((z.owned, wide), F32)
            for k, block in enumerate(blocks):
                inside = (places[:, at : at + wide] - piece_start(z, k, z.block)).astype(jnp.int16)
                for first in range(0, z.block, 768):
                    deep = min(768, z.block - first)
                    row = lax.broadcasted_iota(jnp.int16, (deep, wide), 0) + jnp.int16(first)
                    hot = jnp.where(row == inside, jnp.ones((), BF16), jnp.zeros((), BF16))
                    total = total + dot(block[:, first : first + deep], hot)
            ordered_inverse[s, :, at : at + wide] = total.astype(BF16)
    coarse_rows(z, ordered_inverse, arrived, message)


def coarse_kernel(z, arrived, ordered_inverse, message):
    coarse_rows(z, ordered_inverse, arrived, message)


def picked_rows(z, arrived, picks):
    flat = arrived[...].reshape(z.columns, z.lanes)
    return fold(z, select(z, [dot(picks[h], flat) for h in range(z.subs)])).astype(BF16)


def update_kernel(z, *refs):
    arrived, picks, start_modes, inner, left_t, right_t, before, after, first_got, second_got = refs[:10]
    chosen, message = refs[10:]
    rows = picked_rows(z, arrived, picks)
    chosen[...] = rows
    m = z.modes
    parts = []
    for s in range(z.subs):
        faces = sides(z, before, after, first_got, second_got, s)
        both = shares(z, s, rows, faces)
        total = dot(inner[s], rows[(s + 1) * m : (s + 2) * m])
        parts.append(total + dot(left_t[s], both[0].astype(BF16)) + dot(right_t[s], both[1].astype(BF16)))
    modes = (start_modes[...] - select(z, parts)).astype(BF16)
    for k in range(z.n):
        message[k] = modes


def pick_kernel(z, *refs):
    arrived, picks, before, after, first_got, second_got = refs[:6]
    base_before, base_after, base_first, base_second, out = refs[6:]
    chosen = picked_rows(z, arrived, picks)
    near = chosen.shape[0]
    lefts, rights = [], []
    for s in range(z.subs):
        values = sides(z, before, after, first_got, second_got, s)
        bases = sides(z, base_before, base_after, base_first, base_second, s)
        left, right = shares(z, s, chosen, values, bases)
        lefts.append(left)
        rights.append(right)
    out[:near] = chosen
    out[near : near + z.face] = select(z, lefts).astype(BF16)
    out[near + z.face :] = select(z, rights).astype(BF16)


def last_kernel(z, *refs):
    chosen, values = refs[: z.group], refs[z.group : 2 * z.group]
    tall, left_rows, right_rows, second_pass, final_residual = refs[2 * z.group :]
    start = piece_start(z, 0, z.own)
    near = (z.subs + 2) * z.modes
    lefts, rights = [], []
    for s in range(z.subs):
        scatter = scatter_matrix(z, left_rows[s : s + 1, :], start, z.own)
        lefts.append(jnp.concatenate([tall[s, pl.ds(start, z.own), :], scatter], axis=1))
        rights.append(scatter_matrix(z, right_rows[s : s + 1, :], start, z.own))
    done = [jnp.zeros((z.own, z.lanes), F32) for _ in range(2 * z.subs)]
    for k in range(z.group):
        rows = chosen[k][:near]
        left, right = chosen[k][near : near + z.face], chosen[k][near + z.face :]
        steps, images = [], []
        for s in range(z.subs):
            total = dot(lefts[s], correction_side(z, rows, s, left))
            steps.append(total[:, z.lanes :])
            images.append(total[:, : z.lanes] + dot(rights[s], right))
        pair = values[k][0] + select(z, steps), values[k][1] - select(z, images)
        place = lax.rem(lax.axis_index(GROUP) + k, z.group)
        for at, packed in enumerate(pair):
            for s in range(z.subs):
                turn = lax.rem((place - s + z.subs * z.group) * z.width, z.lanes)
                turned = pltpu.roll(packed, turn, 1)
                here = at * z.subs + s
                done[here] = jnp.where(lane_mask(z, place, turned.shape), turned, done[here])
    for s in range(z.subs):
        second_pass[s] = done[s][:, : z.cases]
        final_residual[s] = done[z.subs + s][:, : z.cases]


def call(kernel, outs, operands, flops, scratch=(), late=(), loose=(), name=None):
    moved = sum(int(np.prod(x.shape)) * x.dtype.itemsize for x in (*operands, *outs))
    n_in, n_out = len(operands), len(outs)

    def whole(*refs):
        hbm, refs = refs[: n_in + n_out], refs[n_in + n_out :]
        vmem, refs = refs[: n_in + n_out], refs[n_in + n_out :]
        in_sems, out_sems, *rest = refs
        arriving = [pltpu.make_async_copy(hbm[i], vmem[i], in_sems.at[i]) for i in range(n_in)]
        for i in sorted(range(n_in), key=lambda i: i in late):
            arriving[i].start()
        for i, copy in enumerate(arriving):
            if i not in late:
                copy.wait()
        extra = [lambda i: arriving[i].wait()] if late else []
        kernel(*extra, *vmem, *rest)
        leaving = [pltpu.make_async_copy(vmem[n_in + i], hbm[n_in + i], out_sems.at[i]) for i in range(n_out)]
        for copy in leaving:
            copy.start()
        for copy in leaving:
            copy.wait()

    hbm_spec = pl.BlockSpec(memory_space=pltpu.HBM)
    any_spec = pl.BlockSpec(memory_space=pl.ANY)
    placed = [
        x if i in loose else pltpu.with_memory_space_constraint(x, pltpu.HBM) for i, x in enumerate(operands)
    ]
    return pl.pallas_call(
        whole,
        out_shape=[pltpu.HBM(o.shape, o.dtype) for o in outs],
        in_specs=[any_spec if i in loose else hbm_spec for i in range(n_in)],
        out_specs=[hbm_spec] * n_out,
        scratch_shapes=[
            *[pltpu.VMEM(x.shape, x.dtype) for x in (*operands, *outs)],
            pltpu.SemaphoreType.DMA((n_in,)),
            pltpu.SemaphoreType.DMA((n_out,)),
            *scratch,
        ],
        compiler_params=pltpu.CompilerParams(vmem_limit_bytes=VMEM_BYTES),
        cost_estimate=pl.CostEstimate(flops=flops, bytes_accessed=moved, transcendentals=0),
        name=name,
    )(*placed)


def shape(dims, dtype):
    return jax.ShapeDtypeStruct(dims, dtype)


def pieces_of(block, group):
    out = [block]
    for k in range(1, group):
        out.append(lax.ppermute(block, GROUP, [((g + k) % group, g) for g in range(group)]))
    return out


def body(loads, stiffness, local_inverse, coarse_basis, coarse_inverse, coarse_index, left_rows, right_rows):
    z = Sizes(loads, stiffness, coarse_basis, coarse_inverse, left_rows)
    n, group, subs, rows, lanes, modes, face = z.n, z.group, z.subs, z.rows, z.lanes, z.modes, z.face
    basis_pieces = pieces_of(jnp.swapaxes(coarse_basis, 1, 2), group)
    inverse_columns = pieces_of(coarse_inverse, group)
    basis_pieces, inverse_columns, local_inverse, stiffness = lax.optimization_barrier(
        (basis_pieces, inverse_columns, local_inverse, stiffness)
    )
    column = np.arange(z.columns)
    repeat = jnp.asarray(np.arange(lanes)[:, None] == column[None, :] % modes, BF16)
    own_row = jnp.asarray(np.arange(n)[:, None] == column[None, :] // modes, F32)
    place = jnp.asarray(
        (column // modes * z.owned + column % modes)[None, :] + np.arange(subs)[:, None] * modes, jnp.int32
    )
    packed_f = shape((rows, lanes), F32)
    packed_b = shape((rows, lanes), BF16)
    copies = shape((n, modes, lanes), BF16)
    tall = shape((subs, rows, lanes), BF16)
    spread = functools.partial(lax.all_to_all, axis_name="sub", split_axis=0, concat_axis=0)
    first_pairs = [(i, i + 1 if i % 2 == 0 else i - 1) for i in range(n)]
    second_pairs = [(i, (i + (1 if i % 2 else -1)) % n) for i in range(n)]
    work = 4 * subs * rows * rows * lanes

    (message,) = call(
        functools.partial(open_kernel, z),
        [shape((n, modes + DIGIT_ROWS, lanes), BF16)],
        [*basis_pieces, loads, coarse_index],
        4 * rows * lanes * lanes,
        [pltpu.VMEM((DIGIT_ROWS, lanes), F32), pltpu.VMEM((subs, modes, rows), BF16)],
        loose=range(1, group),
        name="open",
    )
    inverse_pieces = pieces_of(local_inverse, group)
    stiffness_pieces = pieces_of(stiffness, group)
    restricted = spread(message)
    arrivals = [*range(1, group), *range(group + 1, 2 * group)]
    faces = shape((subs, face, lanes), BF16)
    outer = shape((face, lanes), BF16)
    (
        load_rows, solved, image, before, after, first_pair, second_pair, tall, basis_t
    ) = call(
        functools.partial(first_image_kernel, z),
        [
            packed_b, packed_f, packed_f, faces, faces, outer, outer, tall, shape((subs, modes, rows), BF16),
        ],
        [*inverse_pieces, *stiffness_pieces, *basis_pieces, loads, left_rows, right_rows],
        work,
        [
            pltpu.VMEM((rows, lanes), BF16),
            pltpu.VMEM((subs, rows, 2 * lanes), BF16), pltpu.VMEM((subs, rows, 2 * lanes), BF16),
        ],
        late=range(2 * group),
        loose=[*arrivals, *range(2 * group + 1, 3 * group)],
        name="first_image",
    )
    second_got = lax.ppermute(second_pair, "sub", second_pairs)
    restricted, second_pair = lax.optimization_barrier((restricted, second_pair))
    near = (subs + 2) * modes
    ordered_inverse, index, message = call(
        functools.partial(order_kernel, z),
        [shape((subs, z.owned, z.columns), BF16), shape((subs, n, lanes), F32), copies],
        [*inverse_columns, restricted, repeat, own_row],
        2 * z.owned * z.total * z.total,
        loose=range(1, group + 1),
        name="order",
    )
    coarse = spread(message)
    first_got = lax.ppermute(first_pair, "sub", first_pairs)
    side = shape((subs, modes, face), BF16)
    left_t, right_t, inner, start_modes, picks = call(
        functools.partial(begin_kernel, z),
        [
            side, side, shape((subs, modes, modes), BF16), shape((modes, lanes), F32),
            shape((subs, near, z.columns), BF16),
        ],
        [load_rows, image, tall, basis_t, left_rows, right_rows, index, place],
        work // 16,
        name="begin",
    )
    chosen, message = call(
        functools.partial(update_kernel, z),
        [shape((near, lanes), BF16), copies],
        [coarse, picks, start_modes, inner, left_t, right_t, before, after, first_got, second_got],
        work // 64,
        loose=[0, 8, 9],
        name="update",
    )
    restricted = spread(message)

    bases = [before, after, first_got, second_got]
    before, after, first_pair, second_pair, *values = call(
        functools.partial(second_image_kernel, z),
        [faces, faces, outer, outer, *[shape((2, z.own, lanes), F32)] * group],
        [
            *inverse_pieces, *stiffness_pieces, load_rows, image, tall, solved, chosen,
            *bases, left_rows, right_rows,
        ],
        work,
        [pltpu.VMEM((rows, lanes), F32), pltpu.VMEM((rows, lanes), BF16), pltpu.VMEM((rows, lanes), BF16)],
        late=range(2 * group),
        loose=[*arrivals, 2 * group + 7, 2 * group + 8],
        name="second_image",
    )
    second_got = lax.ppermute(second_pair, "sub", second_pairs)
    restricted, before = lax.optimization_barrier((restricted, before))
    (message,) = call(
        functools.partial(coarse_kernel, z),
        [copies],
        [restricted, ordered_inverse],
        work // 64,
        loose=[0],
        name="coarse",
    )
    coarse = spread(message)
    first_got = lax.ppermute(first_pair, "sub", first_pairs)
    swapped = [values[0]]
    for k in range(1, group):
        swapped.append(lax.ppermute(values[k], GROUP, [(g, (g + k) % group) for g in range(group)]))
    swapped = [swapped[(group - k) % group] for k in range(group)]
    (chosen,) = call(
        functools.partial(pick_kernel, z),
        [shape((near + 2 * face, lanes), BF16)],
        [coarse, picks, before, after, first_got, second_got, *bases],
        work // 64,
        loose=[0, 4, 5, 8, 9],
        name="pick",
    )
    out = shape((subs, z.own, z.cases), F32)
    return tuple(
        call(
            functools.partial(last_kernel, z),
            [out, out],
            [*pieces_of(chosen, group), *swapped, tall, left_rows, right_rows],
            work // 8,
            loose=[*range(1, group), *range(group + 1, 2 * group)],
            name="last",
        )
    )


def solution(mesh):
    return jax.shard_map(
        body,
        mesh=mesh,
        in_specs=(
            P("sub", None, None),
            P("sub", GROUP, None),
            P("sub", GROUP, None),
            P("sub", GROUP, None),
            P("sub", GROUP),
            P("sub", None),
            P("sub", None),
            P("sub", None),
        ),
        out_specs=(P("sub", GROUP, None), P("sub", GROUP, None)),
        check_vma=False,
    )
```

```python
import functools

import jax
import jax.numpy as jnp
import numpy as np
from jax import lax
from jax.experimental import pallas as pl
from jax.experimental.pallas import tpu as pltpu
from jax.sharding import PartitionSpec as P

GROUP = ("crow", "ccol")
F32 = jnp.float32
BF16 = jnp.bfloat16
VMEM_BYTES = 48 * 1024 * 1024
DIGIT_ROWS = 16
DIGIT_BITS = 8
DIGIT = 1 << DIGIT_BITS


def dot(a, b):
    return lax.dot_general(a, b, (((1,), (0,)), ((), ())), preferred_element_type=F32)


def dot_tn(a, b):
    return lax.dot_general(a, b, (((0,), (0,)), ((), ())), preferred_element_type=F32)


def dot_nt(a, b):
    return lax.dot_general(a, b, (((1,), (1,)), ((), ())), preferred_element_type=F32)


class Sizes:
    def __init__(self, loads, stiffness, coarse_basis, coarse_inverse, left_rows):
        self.n = lax.axis_size("sub")
        self.group = lax.axis_size(GROUP)
        self.subs, self.rows, self.cases = loads.shape
        self.own = stiffness.shape[1]
        self.modes = coarse_basis.shape[2]
        self.owned, self.block = coarse_inverse.shape
        self.total = self.block * self.group
        self.face = left_rows.shape[1]
        self.width = self.cases // self.group
        self.lanes = max(self.cases, -(-self.subs * self.width // 128) * 128)
        self.columns = self.n * self.modes


def lane_mask(z, block, shape):
    lane = lax.broadcasted_iota(jnp.int32, shape, len(shape) - 1)
    return (lane >= block * z.width) & (lane < (block + 1) * z.width)


def select(z, parts):
    out = jnp.zeros_like(parts[0])
    for s, part in enumerate(parts):
        out = jnp.where(lane_mask(z, s, part.shape), part, out)
    return out


def fold(z, packed):
    if z.lanes == z.subs * z.width:
        out = packed
        for k in range(1, z.subs):
            out = out + pltpu.roll(packed, k * z.width, 1)
        return out
    out = packed
    for k in range(1, z.subs):
        out = out + pltpu.roll(packed, k * z.width, 1)
        out = out + pltpu.roll(packed, z.lanes - k * z.width, 1)
    return out


def lane_matrix(z, source, target, width=None):
    row = lax.broadcasted_iota(jnp.int32, (z.lanes, z.lanes), 0)
    lane = lax.broadcasted_iota(jnp.int32, (z.lanes, z.lanes), 1)
    hit = (row - source == lane - target) & (lane >= target) & (lane < target + (width or z.width))
    return jnp.where(hit, 1.0, 0.0).astype(BF16)


def piece_start(z, k, size):
    place = lax.rem(lax.axis_index(GROUP) + k, z.group)
    return pl.multiple_of(place * size, size)


def pick_matrix(z, rows_of):
    column = jnp.transpose(jnp.broadcast_to(rows_of.astype(F32), (z.face, z.face)))[:, 0:1].astype(jnp.int32)
    row = lax.broadcasted_iota(jnp.int32, (z.face, z.rows), 1)
    return jnp.where(row == column, 1.0, 0.0).astype(BF16)


def even():
    return lax.rem(lax.axis_index("sub"), 2) == 0


def case_matrix(z, s):
    row = lax.broadcasted_iota(jnp.int32, (z.cases, z.lanes), 0)
    lane = lax.broadcasted_iota(jnp.int32, (z.cases, z.lanes), 1)
    hit = (row - lax.axis_index(GROUP) * z.width == lane - s * z.width) & lane_mask(z, s, row.shape)
    return jnp.where(hit, 1.0, 0.0).astype(BF16)


def join_basis(z, pieces, basis_t):
    for k, piece in enumerate(pieces):
        basis_t[:, :, pl.ds(piece_start(z, k, z.own), z.own)] = piece[...]


def open_kernel(z, *refs):
    pieces = refs[: z.group]
    loads, index, message, digits, basis_t = refs[z.group :]
    join_basis(z, pieces, basis_t)
    total = jnp.zeros((z.modes, z.lanes), F32)
    for s in range(z.subs):
        total = total + dot(dot(basis_t[s], loads[s]).astype(BF16), case_matrix(z, s))
    modes = total.astype(BF16)
    digits[...] = jnp.zeros(digits.shape, F32)
    for s in range(z.subs):
        places = index[s : s + 1, :]
        digits[2 * s : 2 * s + 1, : z.modes] = (places >> DIGIT_BITS).astype(F32)
        digits[2 * s + 1 : 2 * s + 2, : z.modes] = (places & (DIGIT - 1)).astype(F32)
    for k in range(z.n):
        message[k, : z.modes, :] = modes
        message[k, z.modes :, :] = digits[...].astype(BF16)


def multiply(z, pieces, vector, store, wait):
    for k in range(z.group):
        wait(k)
    for k, piece in enumerate(pieces):
        parts = [dot(piece[s], vector) for s in range(z.subs)]
        store(k, piece_start(z, k, z.own), select(z, parts))


def pick_both(z, left_rows, right_rows, s):
    return jnp.concatenate(
        [pick_matrix(z, left_rows[s : s + 1, :]), pick_matrix(z, right_rows[s : s + 1, :])], axis=0
    )


def store_faces(z, before, after, first_pair, second_pair):
    first, last = before[0], after[z.subs - 1]
    first_pair[...] = jnp.where(even(), last, first)
    second_pair[...] = jnp.where(even(), first, last)


def sides(z, before, after, first_pair, second_pair, s):
    if s == 0:
        from_before = jnp.where(even(), second_pair[...], first_pair[...])
    else:
        from_before = after[s - 1]
    if s == z.subs - 1:
        from_after = jnp.where(even(), first_pair[...], second_pair[...])
    else:
        from_after = before[s + 1]
    return from_before, from_after


def shares(z, s, chosen, faces, bases=None):
    m, half = z.modes, z.lanes // 2
    moved = lane_matrix(z, 0, s * z.width)
    out = []
    for side, at in ((0, s), (1, s + 2)):
        own = chosen[at * m : (at + 1) * m]
        below = jnp.concatenate([own, jnp.zeros((half - m, z.lanes), BF16)], axis=0)
        if bases is None:
            total = dot(faces[side], jnp.concatenate([moved[:half], below], axis=0))
        else:
            above = jnp.zeros((half, z.lanes), BF16)
            total = dot(faces[side], moved) + dot(bases[side], jnp.concatenate([above, below], axis=0))
        out.append(total)
    return out


def correction_side(z, chosen, s, share):
    m, half = z.modes, z.lanes // 2
    own = chosen[(s + 1) * m : (s + 2) * m]
    none = jnp.zeros((half - m, z.lanes), BF16)
    nil = jnp.zeros((half, z.lanes), BF16)
    image = jnp.concatenate([own, none, nil, share], axis=0)
    step = jnp.concatenate([nil, own, none, jnp.zeros((z.face, z.lanes), BF16)], axis=0)
    return jnp.concatenate([image, step], axis=1)


def scatter_matrix(z, rows_of, start, count):
    row = lax.broadcasted_iota(jnp.int32, (count, z.face), 0) + start
    return jnp.where(row == rows_of, 1.0, 0.0).astype(BF16)


def first_image_kernel(z, wait, *refs):
    inverse, stiffness = refs[: z.group], refs[z.group : 2 * z.group]
    pieces = refs[2 * z.group : 3 * z.group]
    loads, left_rows, right_rows = refs[3 * z.group : 3 * z.group + 3]
    load_rows, solved, image, before, after, first_pair, second_pair = refs[3 * z.group + 3 : 3 * z.group + 10]
    tall, basis_t, rounded, both, images = refs[3 * z.group + 10 :]
    join_basis(z, pieces, basis_t)
    packed = dot(loads[0], case_matrix(z, 0))
    for s in range(1, z.subs):
        packed = packed + dot(loads[s], case_matrix(z, s))
    load_rows[...] = packed.astype(BF16)

    def store_solved(k, start, value):
        solved[pl.ds(start, z.own), :] = value
        rounded[pl.ds(start, z.own), :] = value.astype(BF16)

    multiply(z, inverse, load_rows[...], store_solved, wait)
    solved_b = rounded[...]
    half = z.lanes // 2
    for s in range(z.subs):
        basis = jnp.transpose(basis_t[s].astype(F32)).astype(BF16)
        tall[s, :, half : half + z.modes] = basis
        tall[s, :, half + z.modes :] = jnp.zeros((z.rows, half - z.modes), BF16)
        both[s, :, : z.lanes] = solved_b
        both[s, :, z.lanes : z.lanes + z.modes] = basis
        both[s, :, z.lanes + z.modes :] = jnp.zeros((z.rows, z.lanes - z.modes), BF16)
    for k, piece in enumerate(stiffness):
        wait(z.group + k)
        start = piece_start(z, k, z.own)
        parts = [dot(piece[s], both[s]) for s in range(z.subs)]
        image[pl.ds(start, z.own), :] = select(z, [part[:, : z.lanes] for part in parts])
        for s in range(z.subs):
            images[s, pl.ds(start, z.own), :] = parts[s].astype(BF16)
    for s in range(z.subs):
        tall[s, :, :half] = images[s, :, z.lanes : z.lanes + half]
        picked = dot(pick_both(z, left_rows, right_rows, s), images[s]).astype(BF16)
        faces = dot(picked[:, : z.lanes], lane_matrix(z, s * z.width, 0))
        faces = (faces + dot(picked[:, z.lanes :], lane_matrix(z, 0, half, z.modes))).astype(BF16)
        before[s] = faces[: z.face]
        after[s] = faces[z.face :]
    store_faces(z, before, after, first_pair, second_pair)


def begin_kernel(z, *refs):
    load_rows, image, tall, basis_t, left_rows, right_rows, index, place = refs[:8]
    left_t, right_t, inner, start_modes, picks = refs[8:]
    left = (load_rows[...].astype(F32) - image[...]).astype(BF16)
    begun = []
    for s in range(z.subs):
        restricted = dot(basis_t[s], jnp.concatenate([left, tall[s]], axis=1))
        begun.append(restricted[:, : z.lanes])
        inner[s] = restricted[:, z.lanes : z.lanes + z.modes].astype(BF16)
        sides_t = dot_nt(basis_t[s], pick_both(z, left_rows, right_rows, s)).astype(BF16)
        left_t[s] = sides_t[:, : z.face]
        right_t[s] = sides_t[:, z.face :]
    start_modes[...] = select(z, begun)
    here = lax.axis_index("sub")
    device = lax.broadcasted_iota(jnp.int32, (z.n, z.lanes), 0)
    for t in range(z.subs + 2):
        if t == 0:
            s, owner = z.subs - 1, lax.rem(here + z.n - 1, z.n)
        elif t == z.subs + 1:
            s, owner = 0, lax.rem(here + 1, z.n)
        else:
            s, owner = t - 1, here
        row = jnp.sum(jnp.where(device == owner, index[s], 0.0), axis=0, keepdims=True)
        column = jnp.transpose(jnp.broadcast_to(row, (z.lanes, z.lanes)))[: z.modes, 0:1].astype(jnp.int32)
        for h in range(z.subs):
            hit = column == place[h : h + 1, :]
            picks[h, t * z.modes : (t + 1) * z.modes, :] = jnp.where(hit, 1.0, 0.0).astype(BF16)


def second_image_kernel(z, wait, *refs):
    inverse, stiffness = refs[: z.group], refs[z.group : 2 * z.group]
    rest = refs[2 * z.group :]
    load_rows, old_image, tall, old_solved, chosen = rest[:5]
    before, after, first_got, second_got, left_rows, right_rows = rest[5:11]
    new_before, new_after, first_pair, second_pair = rest[11:15]
    values = rest[15 : 15 + z.group]
    base, rounded, image = rest[15 + z.group :]
    steps, images = [], []
    for s in range(z.subs):
        faces = sides(z, before, after, first_got, second_got, s)
        both = [share.astype(BF16) for share in shares(z, s, chosen, faces)]
        left = jnp.concatenate([tall[s], scatter_matrix(z, left_rows[s : s + 1, :], 0, z.rows)], axis=1)
        total = dot(left, correction_side(z, chosen, s, both[0]))
        steps.append(total[:, z.lanes :])
        images.append(total[:, : z.lanes] + dot(scatter_matrix(z, right_rows[s : s + 1, :], 0, z.rows), both[1]))
    residual = (load_rows[...].astype(F32) - old_image[...] - select(z, images)).astype(BF16)
    base[...] = old_solved[...] + select(z, steps)

    def store_solved(k, start, value):
        value = value + base[pl.ds(start, z.own), :]
        values[k][0] = value
        rounded[pl.ds(start, z.own), :] = value.astype(BF16)

    multiply(z, inverse, residual, store_solved, wait)

    def store_image(k, start, value):
        place = pl.ds(start, z.own)
        values[k][1] = load_rows[place, :].astype(F32) - value
        image[place, :] = value.astype(BF16)

    multiply(z, stiffness, rounded[...], store_image, lambda k: wait(z.group + k))
    pick = jnp.concatenate([pick_both(z, left_rows, right_rows, s) for s in range(z.subs)], axis=0)
    picked = dot(pick, image[...]).astype(BF16)
    for s in range(z.subs):
        own = picked[2 * s * z.face : 2 * (s + 1) * z.face]
        faces = dot(own, lane_matrix(z, s * z.width, 0)).astype(BF16)
        new_before[s] = faces[: z.face]
        new_after[s] = faces[z.face :]
    store_faces(z, new_before, new_after, first_pair, second_pair)


def digit_row(shape, row):
    return lax.broadcasted_iota(jnp.int32, shape, 1) == row


def coarse_rows(z, ordered_inverse, arrived, message):
    flat = arrived[:, : z.modes, :].reshape(z.columns, z.lanes)
    rows = fold(z, select(z, [dot(ordered_inverse[s], flat) for s in range(z.subs)]))
    packed = select(z, [rows[s * z.modes : (s + 1) * z.modes, :] for s in range(z.subs)]).astype(BF16)
    for k in range(z.n):
        message[k] = packed


def order_kernel(z, *refs):
    blocks = refs[: z.group]
    arrived, repeat, own_row, ordered_inverse, index, message = refs[z.group :]
    digits = arrived[:, z.modes :, :].astype(F32)
    for s in range(z.subs):
        high = jnp.sum(jnp.where(digit_row(digits.shape, 2 * s), digits, 0.0), axis=1)
        low = jnp.sum(jnp.where(digit_row(digits.shape, 2 * s + 1), digits, 0.0), axis=1)
        index[s] = high * DIGIT + low
        spread = dot(high.astype(BF16), repeat[...]) * DIGIT + dot(low.astype(BF16), repeat[...])
        places = jnp.sum(spread * own_row[...], axis=0, keepdims=True).astype(jnp.int32)
        for at in range(0, z.columns, 768):
            wide = min(768, z.columns - at)
            total = jnp.zeros((z.owned, wide), F32)
            for k, block in enumerate(blocks):
                inside = (places[:, at : at + wide] - piece_start(z, k, z.block)).astype(jnp.int16)
                for first in range(0, z.block, 768):
                    deep = min(768, z.block - first)
                    row = lax.broadcasted_iota(jnp.int16, (deep, wide), 0) + jnp.int16(first)
                    hot = jnp.where(row == inside, jnp.ones((), BF16), jnp.zeros((), BF16))
                    total = total + dot(block[:, first : first + deep], hot)
            ordered_inverse[s, :, at : at + wide] = total.astype(BF16)
    coarse_rows(z, ordered_inverse, arrived, message)


def coarse_kernel(z, arrived, ordered_inverse, message):
    coarse_rows(z, ordered_inverse, arrived, message)


def picked_rows(z, arrived, picks):
    flat = arrived[...].reshape(z.columns, z.lanes)
    return fold(z, select(z, [dot(picks[h], flat) for h in range(z.subs)])).astype(BF16)


def update_kernel(z, *refs):
    arrived, picks, start_modes, inner, left_t, right_t, before, after, first_got, second_got = refs[:10]
    chosen, message = refs[10:]
    rows = picked_rows(z, arrived, picks)
    chosen[...] = rows
    m = z.modes
    parts = []
    for s in range(z.subs):
        faces = sides(z, before, after, first_got, second_got, s)
        both = shares(z, s, rows, faces)
        total = dot(inner[s], rows[(s + 1) * m : (s + 2) * m])
        parts.append(total + dot(left_t[s], both[0].astype(BF16)) + dot(right_t[s], both[1].astype(BF16)))
    modes = (start_modes[...] - select(z, parts)).astype(BF16)
    for k in range(z.n):
        message[k] = modes


def pick_kernel(z, *refs):
    arrived, picks, before, after, first_got, second_got = refs[:6]
    base_before, base_after, base_first, base_second, out = refs[6:]
    chosen = picked_rows(z, arrived, picks)
    near = chosen.shape[0]
    lefts, rights = [], []
    for s in range(z.subs):
        values = sides(z, before, after, first_got, second_got, s)
        bases = sides(z, base_before, base_after, base_first, base_second, s)
        left, right = shares(z, s, chosen, values, bases)
        lefts.append(left)
        rights.append(right)
    out[:near] = chosen
    out[near : near + z.face] = select(z, lefts).astype(BF16)
    out[near + z.face :] = select(z, rights).astype(BF16)


def base_kernel(z, *refs):
    *values, out = refs
    for at in range(2):
        for s in range(z.subs):
            total = jnp.zeros((z.own, z.lanes), F32)
            for k, value in enumerate(values):
                place = lax.rem(lax.axis_index(GROUP) + k, z.group)
                turn = lax.rem((place - s + z.subs * z.group) * z.width, z.lanes)
                turned = pltpu.roll(value[at], turn, 1)
                total = jnp.where(lane_mask(z, place, turned.shape), turned, total)
            out[at, s] = total


def last_kernel(z, *refs):
    chosen = refs[: z.group]
    base, tall, left_rows, right_rows, second_pass, final_residual = refs[z.group :]
    start = piece_start(z, 0, z.own)
    near = (z.subs + 2) * z.modes

    def all_cases(rows, source):
        total = jnp.zeros((rows.stop - rows.start, z.lanes), F32)
        for k, piece in enumerate(chosen):
            place = lax.rem(lax.axis_index(GROUP) + k, z.group)
            total = total + dot(piece[rows, :], lane_matrix(z, source, place * z.width))
        return total.astype(BF16)

    modes = all_cases(slice(0, near), 0)
    for s in range(z.subs):
        left = all_cases(slice(near, near + z.face), s * z.width)
        right = all_cases(slice(near + z.face, near + 2 * z.face), s * z.width)
        scatter = scatter_matrix(z, left_rows[s : s + 1, :], start, z.own)
        wide = jnp.concatenate([tall[s, pl.ds(start, z.own), :], scatter], axis=1)
        total = dot(wide, correction_side(z, modes, s, left))
        image = total[:, : z.lanes] + dot(scatter_matrix(z, right_rows[s : s + 1, :], start, z.own), right)
        second_pass[s] = (base[0, s] + total[:, z.lanes :])[:, : z.cases]
        final_residual[s] = (base[1, s] - image)[:, : z.cases]


def call(kernel, outs, operands, flops, scratch=(), late=(), loose=(), name=None):
    moved = sum(int(np.prod(x.shape)) * x.dtype.itemsize for x in (*operands, *outs))
    n_in, n_out = len(operands), len(outs)

    def whole(*refs):
        hbm, refs = refs[: n_in + n_out], refs[n_in + n_out :]
        vmem, refs = refs[: n_in + n_out], refs[n_in + n_out :]
        in_sems, out_sems, *rest = refs
        arriving = [pltpu.make_async_copy(hbm[i], vmem[i], in_sems.at[i]) for i in range(n_in)]
        for i in sorted(range(n_in), key=lambda i: i in late):
            arriving[i].start()
        for i, copy in enumerate(arriving):
            if i not in late:
                copy.wait()
        extra = [lambda i: arriving[i].wait()] if late else []
        kernel(*extra, *vmem, *rest)
        leaving = [pltpu.make_async_copy(vmem[n_in + i], hbm[n_in + i], out_sems.at[i]) for i in range(n_out)]
        for copy in leaving:
            copy.start()
        for copy in leaving:
            copy.wait()

    hbm_spec = pl.BlockSpec(memory_space=pltpu.HBM)
    any_spec = pl.BlockSpec(memory_space=pl.ANY)
    placed = [
        x if i in loose else pltpu.with_memory_space_constraint(x, pltpu.HBM) for i, x in enumerate(operands)
    ]
    return pl.pallas_call(
        whole,
        out_shape=[pltpu.HBM(o.shape, o.dtype) for o in outs],
        in_specs=[any_spec if i in loose else hbm_spec for i in range(n_in)],
        out_specs=[hbm_spec] * n_out,
        scratch_shapes=[
            *[pltpu.VMEM(x.shape, x.dtype) for x in (*operands, *outs)],
            pltpu.SemaphoreType.DMA((n_in,)),
            pltpu.SemaphoreType.DMA((n_out,)),
            *scratch,
        ],
        compiler_params=pltpu.CompilerParams(vmem_limit_bytes=VMEM_BYTES),
        cost_estimate=pl.CostEstimate(flops=flops, bytes_accessed=moved, transcendentals=0),
        name=name,
    )(*placed)


def shape(dims, dtype):
    return jax.ShapeDtypeStruct(dims, dtype)


def pieces_of(block, group):
    out = [block]
    for k in range(1, group):
        out.append(lax.ppermute(block, GROUP, [((g + k) % group, g) for g in range(group)]))
    return out


def body(loads, stiffness, local_inverse, coarse_basis, coarse_inverse, coarse_index, left_rows, right_rows):
    z = Sizes(loads, stiffness, coarse_basis, coarse_inverse, left_rows)
    n, group, subs, rows, lanes, modes, face = z.n, z.group, z.subs, z.rows, z.lanes, z.modes, z.face
    basis_pieces = pieces_of(jnp.swapaxes(coarse_basis, 1, 2), group)
    inverse_columns = pieces_of(coarse_inverse, group)
    basis_pieces, inverse_columns, local_inverse, stiffness = lax.optimization_barrier(
        (basis_pieces, inverse_columns, local_inverse, stiffness)
    )
    column = np.arange(z.columns)
    repeat = jnp.asarray(np.arange(lanes)[:, None] == column[None, :] % modes, BF16)
    own_row = jnp.asarray(np.arange(n)[:, None] == column[None, :] // modes, F32)
    place = jnp.asarray(
        (column // modes * z.owned + column % modes)[None, :] + np.arange(subs)[:, None] * modes, jnp.int32
    )
    packed_f = shape((rows, lanes), F32)
    packed_b = shape((rows, lanes), BF16)
    copies = shape((n, modes, lanes), BF16)
    tall = shape((subs, rows, lanes), BF16)
    spread = functools.partial(lax.all_to_all, axis_name="sub", split_axis=0, concat_axis=0)
    first_pairs = [(i, i + 1 if i % 2 == 0 else i - 1) for i in range(n)]
    second_pairs = [(i, (i + (1 if i % 2 else -1)) % n) for i in range(n)]
    work = 4 * subs * rows * rows * lanes

    (message,) = call(
        functools.partial(open_kernel, z),
        [shape((n, modes + DIGIT_ROWS, lanes), BF16)],
        [*basis_pieces, loads, coarse_index],
        4 * rows * lanes * lanes,
        [pltpu.VMEM((DIGIT_ROWS, lanes), F32), pltpu.VMEM((subs, modes, rows), BF16)],
        loose=range(1, group),
        name="open",
    )
    inverse_pieces = pieces_of(local_inverse, group)
    stiffness_pieces = pieces_of(stiffness, group)
    restricted = spread(message)
    arrivals = [*range(1, group), *range(group + 1, 2 * group)]
    faces = shape((subs, face, lanes), BF16)
    outer = shape((face, lanes), BF16)
    (
        load_rows, solved, image, before, after, first_pair, second_pair, tall, basis_t
    ) = call(
        functools.partial(first_image_kernel, z),
        [
            packed_b, packed_f, packed_f, faces, faces, outer, outer, tall, shape((subs, modes, rows), BF16),
        ],
        [*inverse_pieces, *stiffness_pieces, *basis_pieces, loads, left_rows, right_rows],
        work,
        [
            pltpu.VMEM((rows, lanes), BF16),
            pltpu.VMEM((subs, rows, 2 * lanes), BF16), pltpu.VMEM((subs, rows, 2 * lanes), BF16),
        ],
        late=range(2 * group),
        loose=[*arrivals, *range(2 * group + 1, 3 * group)],
        name="first_image",
    )
    second_got = lax.ppermute(second_pair, "sub", second_pairs)
    restricted, second_pair = lax.optimization_barrier((restricted, second_pair))
    near = (subs + 2) * modes
    ordered_inverse, index, message = call(
        functools.partial(order_kernel, z),
        [shape((subs, z.owned, z.columns), BF16), shape((subs, n, lanes), F32), copies],
        [*inverse_columns, restricted, repeat, own_row],
        2 * z.owned * z.total * z.total,
        loose=range(1, group + 1),
        name="order",
    )
    coarse = spread(message)
    first_got = lax.ppermute(first_pair, "sub", first_pairs)
    side = shape((subs, modes, face), BF16)
    left_t, right_t, inner, start_modes, picks = call(
        functools.partial(begin_kernel, z),
        [
            side, side, shape((subs, modes, modes), BF16), shape((modes, lanes), F32),
            shape((subs, near, z.columns), BF16),
        ],
        [load_rows, image, tall, basis_t, left_rows, right_rows, index, place],
        work // 16,
        name="begin",
    )
    chosen, message = call(
        functools.partial(update_kernel, z),
        [shape((near, lanes), BF16), copies],
        [coarse, picks, start_modes, inner, left_t, right_t, before, after, first_got, second_got],
        work // 64,
        loose=[0, 8, 9],
        name="update",
    )
    restricted = spread(message)

    bases = [before, after, first_got, second_got]
    before, after, first_pair, second_pair, *values = call(
        functools.partial(second_image_kernel, z),
        [faces, faces, outer, outer, *[shape((2, z.own, lanes), F32)] * group],
        [
            *inverse_pieces, *stiffness_pieces, load_rows, image, tall, solved, chosen,
            *bases, left_rows, right_rows,
        ],
        work,
        [pltpu.VMEM((rows, lanes), F32), pltpu.VMEM((rows, lanes), BF16), pltpu.VMEM((rows, lanes), BF16)],
        late=range(2 * group),
        loose=[*arrivals, 2 * group + 7, 2 * group + 8],
        name="second_image",
    )
    second_got = lax.ppermute(second_pair, "sub", second_pairs)
    restricted, before = lax.optimization_barrier((restricted, before))
    (message,) = call(
        functools.partial(coarse_kernel, z),
        [copies],
        [restricted, ordered_inverse],
        work // 64,
        loose=[0],
        name="coarse",
    )
    coarse = spread(message)
    first_got = lax.ppermute(first_pair, "sub", first_pairs)
    swapped = [values[0]]
    for k in range(1, group):
        swapped.append(lax.ppermute(values[k], GROUP, [(g, (g + k) % group) for g in range(group)]))
    swapped = [swapped[(group - k) % group] for k in range(group)]
    (base,) = call(
        functools.partial(base_kernel, z),
        [shape((2, subs, z.own, lanes), F32)],
        swapped,
        work // 64,
        loose=range(1, group),
        name="base",
    )
    coarse, base = lax.optimization_barrier((coarse, base))
    (chosen,) = call(
        functools.partial(pick_kernel, z),
        [shape((near + 2 * face, lanes), BF16)],
        [coarse, picks, before, after, first_got, second_got, *bases],
        work // 64,
        loose=[0, 4, 5, 8, 9],
        name="pick",
    )
    out = shape((subs, z.own, z.cases), F32)
    return tuple(
        call(
            functools.partial(last_kernel, z),
            [out, out],
            [*pieces_of(chosen, group), base, tall, left_rows, right_rows],
            work // 8,
            loose=range(1, group),
            name="last",
        )
    )


def solution(mesh):
    return jax.shard_map(
        body,
        mesh=mesh,
        in_specs=(
            P("sub", None, None),
            P("sub", GROUP, None),
            P("sub", GROUP, None),
            P("sub", GROUP, None),
            P("sub", GROUP),
            P("sub", None),
            P("sub", None),
            P("sub", None),
        ),
        out_specs=(P("sub", GROUP, None), P("sub", GROUP, None)),
        check_vma=False,
    )
```

```python
import functools

import jax
import jax.numpy as jnp
import numpy as np
from jax import lax
from jax.experimental import pallas as pl
from jax.experimental.pallas import tpu as pltpu
from jax.sharding import PartitionSpec as P

GROUP = ("crow", "ccol")
F32 = jnp.float32
BF16 = jnp.bfloat16
VMEM_BYTES = 48 * 1024 * 1024
DIGIT_ROWS = 16
DIGIT_BITS = 8
DIGIT = 1 << DIGIT_BITS


def dot(a, b):
    return lax.dot_general(a, b, (((1,), (0,)), ((), ())), preferred_element_type=F32)


def dot_tn(a, b):
    return lax.dot_general(a, b, (((0,), (0,)), ((), ())), preferred_element_type=F32)


def dot_nt(a, b):
    return lax.dot_general(a, b, (((1,), (1,)), ((), ())), preferred_element_type=F32)


class Sizes:
    def __init__(self, loads, stiffness, coarse_basis, coarse_inverse, left_rows):
        self.n = lax.axis_size("sub")
        self.group = lax.axis_size(GROUP)
        self.subs, self.rows, self.cases = loads.shape
        self.own = stiffness.shape[1]
        self.modes = coarse_basis.shape[2]
        self.owned, self.block = coarse_inverse.shape
        self.total = self.block * self.group
        self.face = left_rows.shape[1]
        self.width = self.cases // self.group
        self.lanes = max(self.cases, -(-self.subs * self.width // 128) * 128)
        self.columns = self.n * self.modes


def lane_mask(z, block, shape):
    lane = lax.broadcasted_iota(jnp.int32, shape, len(shape) - 1)
    return (lane >= block * z.width) & (lane < (block + 1) * z.width)


def select(z, parts):
    out = jnp.zeros_like(parts[0])
    for s, part in enumerate(parts):
        out = jnp.where(lane_mask(z, s, part.shape), part, out)
    return out


def fold(z, packed):
    if z.lanes == z.subs * z.width:
        out = packed
        for k in range(1, z.subs):
            out = out + pltpu.roll(packed, k * z.width, 1)
        return out
    out = packed
    for k in range(1, z.subs):
        out = out + pltpu.roll(packed, k * z.width, 1)
        out = out + pltpu.roll(packed, z.lanes - k * z.width, 1)
    return out


def lane_matrix(z, source, target, width=None):
    row = lax.broadcasted_iota(jnp.int32, (z.lanes, z.lanes), 0)
    lane = lax.broadcasted_iota(jnp.int32, (z.lanes, z.lanes), 1)
    hit = (row - source == lane - target) & (lane >= target) & (lane < target + (width or z.width))
    return jnp.where(hit, 1.0, 0.0).astype(BF16)


def piece_start(z, k, size):
    place = lax.rem(lax.axis_index(GROUP) + k, z.group)
    return pl.multiple_of(place * size, size)


def pick_matrix(z, rows_of):
    column = jnp.transpose(jnp.broadcast_to(rows_of.astype(F32), (z.face, z.face)))[:, 0:1].astype(jnp.int32)
    row = lax.broadcasted_iota(jnp.int32, (z.face, z.rows), 1)
    return jnp.where(row == column, 1.0, 0.0).astype(BF16)


def even():
    return lax.rem(lax.axis_index("sub"), 2) == 0


def case_matrix(z, s):
    row = lax.broadcasted_iota(jnp.int32, (z.cases, z.lanes), 0)
    lane = lax.broadcasted_iota(jnp.int32, (z.cases, z.lanes), 1)
    hit = (row - lax.axis_index(GROUP) * z.width == lane - s * z.width) & lane_mask(z, s, row.shape)
    return jnp.where(hit, 1.0, 0.0).astype(BF16)


def join_basis(z, pieces, basis_t):
    for k, piece in enumerate(pieces):
        basis_t[:, :, pl.ds(piece_start(z, k, z.own), z.own)] = piece[...]


def open_kernel(z, *refs):
    pieces = refs[: z.group]
    loads, index, message, digits, basis_t = refs[z.group :]
    join_basis(z, pieces, basis_t)
    total = jnp.zeros((z.modes, z.lanes), F32)
    for s in range(z.subs):
        total = total + dot(dot(basis_t[s], loads[s]).astype(BF16), case_matrix(z, s))
    modes = total.astype(BF16)
    digits[...] = jnp.zeros(digits.shape, F32)
    for s in range(z.subs):
        places = index[s : s + 1, :]
        digits[2 * s : 2 * s + 1, : z.modes] = (places >> DIGIT_BITS).astype(F32)
        digits[2 * s + 1 : 2 * s + 2, : z.modes] = (places & (DIGIT - 1)).astype(F32)
    for k in range(z.n):
        message[k, : z.modes, :] = modes
        message[k, z.modes :, :] = digits[...].astype(BF16)


def multiply(z, pieces, vector, store, wait):
    for k in range(z.group):
        wait(k)
    for k, piece in enumerate(pieces):
        parts = [dot(piece[s], vector) for s in range(z.subs)]
        store(k, piece_start(z, k, z.own), select(z, parts))


def pick_both(z, left_rows, right_rows, s):
    return jnp.concatenate(
        [pick_matrix(z, left_rows[s : s + 1, :]), pick_matrix(z, right_rows[s : s + 1, :])], axis=0
    )


def store_faces(z, before, after, first_pair, second_pair):
    first, last = before[0], after[z.subs - 1]
    first_pair[...] = jnp.where(even(), last, first)
    second_pair[...] = jnp.where(even(), first, last)


def sides(z, before, after, first_pair, second_pair, s):
    if s == 0:
        from_before = jnp.where(even(), second_pair[...], first_pair[...])
    else:
        from_before = after[s - 1]
    if s == z.subs - 1:
        from_after = jnp.where(even(), first_pair[...], second_pair[...])
    else:
        from_after = before[s + 1]
    return from_before, from_after


def shares(z, s, chosen, faces, bases=None):
    m, half = z.modes, z.lanes // 2
    moved = lane_matrix(z, 0, s * z.width)
    out = []
    for side, at in ((0, s), (1, s + 2)):
        own = chosen[at * m : (at + 1) * m]
        below = jnp.concatenate([own, jnp.zeros((half - m, z.lanes), BF16)], axis=0)
        if bases is None:
            total = dot(faces[side], jnp.concatenate([moved[:half], below], axis=0))
        else:
            above = jnp.zeros((half, z.lanes), BF16)
            total = dot(faces[side], moved) + dot(bases[side], jnp.concatenate([above, below], axis=0))
        out.append(total)
    return out


def correction_side(z, chosen, s, share):
    m, half = z.modes, z.lanes // 2
    own = chosen[(s + 1) * m : (s + 2) * m]
    none = jnp.zeros((half - m, z.lanes), BF16)
    nil = jnp.zeros((half, z.lanes), BF16)
    image = jnp.concatenate([own, none, nil, share], axis=0)
    step = jnp.concatenate([nil, own, none, jnp.zeros((z.face, z.lanes), BF16)], axis=0)
    return jnp.concatenate([image, step], axis=1)


def scatter_matrix(z, rows_of, start, count):
    row = lax.broadcasted_iota(jnp.int32, (count, z.face), 0) + start
    return jnp.where(row == rows_of, 1.0, 0.0).astype(BF16)


def first_image_kernel(z, wait, *refs):
    inverse, stiffness = refs[: z.group], refs[z.group : 2 * z.group]
    pieces = refs[2 * z.group : 3 * z.group]
    loads, left_rows, right_rows = refs[3 * z.group : 3 * z.group + 3]
    load_rows, solved, image, before, after, first_pair, second_pair = refs[3 * z.group + 3 : 3 * z.group + 10]
    tall, basis_t, rounded, both, images = refs[3 * z.group + 10 :]
    join_basis(z, pieces, basis_t)
    packed = dot(loads[0], case_matrix(z, 0))
    for s in range(1, z.subs):
        packed = packed + dot(loads[s], case_matrix(z, s))
    load_rows[...] = packed.astype(BF16)

    def store_solved(k, start, value):
        solved[pl.ds(start, z.own), :] = value
        rounded[pl.ds(start, z.own), :] = value.astype(BF16)

    multiply(z, inverse, load_rows[...], store_solved, wait)
    solved_b = rounded[...]
    half = z.lanes // 2
    for s in range(z.subs):
        basis = jnp.transpose(basis_t[s].astype(F32)).astype(BF16)
        tall[s, :, half : half + z.modes] = basis
        tall[s, :, half + z.modes :] = jnp.zeros((z.rows, half - z.modes), BF16)
        both[s, :, : z.lanes] = solved_b
        both[s, :, z.lanes : z.lanes + z.modes] = basis
        both[s, :, z.lanes + z.modes :] = jnp.zeros((z.rows, z.lanes - z.modes), BF16)
    for k, piece in enumerate(stiffness):
        wait(z.group + k)
        start = piece_start(z, k, z.own)
        parts = [dot(piece[s], both[s]) for s in range(z.subs)]
        image[pl.ds(start, z.own), :] = select(z, [part[:, : z.lanes] for part in parts])
        for s in range(z.subs):
            images[s, pl.ds(start, z.own), :] = parts[s].astype(BF16)
    for s in range(z.subs):
        tall[s, :, :half] = images[s, :, z.lanes : z.lanes + half]
        picked = dot(pick_both(z, left_rows, right_rows, s), images[s]).astype(BF16)
        faces = dot(picked[:, : z.lanes], lane_matrix(z, s * z.width, 0))
        faces = (faces + dot(picked[:, z.lanes :], lane_matrix(z, 0, half, z.modes))).astype(BF16)
        before[s] = faces[: z.face]
        after[s] = faces[z.face :]
    store_faces(z, before, after, first_pair, second_pair)


def begin_kernel(z, *refs):
    load_rows, image, tall, basis_t, left_rows, right_rows, index, place = refs[:8]
    left_t, right_t, inner, start_modes, picks = refs[8:]
    left = (load_rows[...].astype(F32) - image[...]).astype(BF16)
    begun = []
    for s in range(z.subs):
        restricted = dot(basis_t[s], jnp.concatenate([left, tall[s]], axis=1))
        begun.append(restricted[:, : z.lanes])
        inner[s] = restricted[:, z.lanes : z.lanes + z.modes].astype(BF16)
        sides_t = dot_nt(basis_t[s], pick_both(z, left_rows, right_rows, s)).astype(BF16)
        left_t[s] = sides_t[:, : z.face]
        right_t[s] = sides_t[:, z.face :]
    start_modes[...] = select(z, begun)
    here = lax.axis_index("sub")
    device = lax.broadcasted_iota(jnp.int32, (z.n, z.lanes), 0)
    for t in range(z.subs + 2):
        if t == 0:
            s, owner = z.subs - 1, lax.rem(here + z.n - 1, z.n)
        elif t == z.subs + 1:
            s, owner = 0, lax.rem(here + 1, z.n)
        else:
            s, owner = t - 1, here
        row = jnp.sum(jnp.where(device == owner, index[s], 0.0), axis=0, keepdims=True)
        column = jnp.transpose(jnp.broadcast_to(row, (z.lanes, z.lanes)))[: z.modes, 0:1].astype(jnp.int32)
        for h in range(z.subs):
            hit = column == place[h : h + 1, :]
            picks[h, t * z.modes : (t + 1) * z.modes, :] = jnp.where(hit, 1.0, 0.0).astype(BF16)


def second_image_kernel(z, wait, *refs):
    inverse, stiffness = refs[: z.group], refs[z.group : 2 * z.group]
    rest = refs[2 * z.group :]
    load_rows, old_image, tall, old_solved, chosen = rest[:5]
    before, after, first_got, second_got, left_rows, right_rows = rest[5:11]
    first_pair, second_pair = rest[11:13]
    values = rest[13 : 13 + z.group]
    base, rounded, image, new_before, new_after = rest[13 + z.group :]
    steps, images = [], []
    for s in range(z.subs):
        faces = sides(z, before, after, first_got, second_got, s)
        both = [share.astype(BF16) for share in shares(z, s, chosen, faces)]
        left = jnp.concatenate([tall[s], scatter_matrix(z, left_rows[s : s + 1, :], 0, z.rows)], axis=1)
        total = dot(left, correction_side(z, chosen, s, both[0]))
        steps.append(total[:, z.lanes :])
        images.append(total[:, : z.lanes] + dot(scatter_matrix(z, right_rows[s : s + 1, :], 0, z.rows), both[1]))
    residual = (load_rows[...].astype(F32) - old_image[...] - select(z, images)).astype(BF16)
    base[...] = old_solved[...] + select(z, steps)

    def store_solved(k, start, value):
        value = value + base[pl.ds(start, z.own), :]
        values[k][0] = value
        rounded[pl.ds(start, z.own), :] = value.astype(BF16)

    multiply(z, inverse, residual, store_solved, wait)

    def store_image(k, start, value):
        place = pl.ds(start, z.own)
        values[k][1] = load_rows[place, :].astype(F32) - value
        image[place, :] = value.astype(BF16)

    multiply(z, stiffness, rounded[...], store_image, lambda k: wait(z.group + k))
    pick = jnp.concatenate([pick_both(z, left_rows, right_rows, s) for s in range(z.subs)], axis=0)
    picked = dot(pick, image[...]).astype(BF16)
    for s in range(z.subs):
        own = picked[2 * s * z.face : 2 * (s + 1) * z.face]
        faces = dot(own, lane_matrix(z, s * z.width, 0)).astype(BF16)
        new_before[s] = faces[: z.face]
        new_after[s] = faces[z.face :]
    store_faces(z, new_before, new_after, first_pair, second_pair)
    inner = []
    for s in range(z.subs):
        move = lane_matrix(z, 0, s * z.width)
        total = jnp.zeros((z.rows, z.lanes), F32)
        if s > 0:
            share = dot(new_after[s - 1], move).astype(BF16)
            total = total + dot(scatter_matrix(z, left_rows[s : s + 1, :], 0, z.rows), share)
        if s < z.subs - 1:
            share = dot(new_before[s + 1], move).astype(BF16)
            total = total + dot(scatter_matrix(z, right_rows[s : s + 1, :], 0, z.rows), share)
        inner.append(total)
    base[...] = select(z, inner)
    for k in range(z.group):
        values[k][1] = values[k][1] - base[pl.ds(piece_start(z, k, z.own), z.own), :]


def digit_row(shape, row):
    return lax.broadcasted_iota(jnp.int32, shape, 1) == row


def coarse_rows(z, ordered_inverse, arrived, message):
    flat = arrived[:, : z.modes, :].reshape(z.columns, z.lanes)
    rows = fold(z, select(z, [dot(ordered_inverse[s], flat) for s in range(z.subs)]))
    packed = select(z, [rows[s * z.modes : (s + 1) * z.modes, :] for s in range(z.subs)]).astype(BF16)
    for k in range(z.n):
        message[k] = packed


def order_kernel(z, *refs):
    blocks = refs[: z.group]
    arrived, repeat, own_row, ordered_inverse, index, message = refs[z.group :]
    digits = arrived[:, z.modes :, :].astype(F32)
    for s in range(z.subs):
        high = jnp.sum(jnp.where(digit_row(digits.shape, 2 * s), digits, 0.0), axis=1)
        low = jnp.sum(jnp.where(digit_row(digits.shape, 2 * s + 1), digits, 0.0), axis=1)
        index[s] = high * DIGIT + low
        spread = dot(high.astype(BF16), repeat[...]) * DIGIT + dot(low.astype(BF16), repeat[...])
        places = jnp.sum(spread * own_row[...], axis=0, keepdims=True).astype(jnp.int32)
        for at in range(0, z.columns, 768):
            wide = min(768, z.columns - at)
            total = jnp.zeros((z.owned, wide), F32)
            for k, block in enumerate(blocks):
                inside = (places[:, at : at + wide] - piece_start(z, k, z.block)).astype(jnp.int16)
                for first in range(0, z.block, 768):
                    deep = min(768, z.block - first)
                    row = lax.broadcasted_iota(jnp.int16, (deep, wide), 0) + jnp.int16(first)
                    hot = jnp.where(row == inside, jnp.ones((), BF16), jnp.zeros((), BF16))
                    total = total + dot(block[:, first : first + deep], hot)
            ordered_inverse[s, :, at : at + wide] = total.astype(BF16)
    coarse_rows(z, ordered_inverse, arrived, message)


def coarse_kernel(z, arrived, ordered_inverse, message):
    coarse_rows(z, ordered_inverse, arrived, message)


def picked_rows(z, arrived, picks):
    flat = arrived[...].reshape(z.columns, z.lanes)
    return fold(z, select(z, [dot(picks[h], flat) for h in range(z.subs)])).astype(BF16)


def update_kernel(z, *refs):
    arrived, picks, start_modes, inner, left_t, right_t, before, after, first_got, second_got = refs[:10]
    chosen, message = refs[10:]
    rows = picked_rows(z, arrived, picks)
    chosen[...] = rows
    m = z.modes
    parts = []
    for s in range(z.subs):
        faces = sides(z, before, after, first_got, second_got, s)
        both = shares(z, s, rows, faces)
        total = dot(inner[s], rows[(s + 1) * m : (s + 2) * m])
        parts.append(total + dot(left_t[s], both[0].astype(BF16)) + dot(right_t[s], both[1].astype(BF16)))
    modes = (start_modes[...] - select(z, parts)).astype(BF16)
    for k in range(z.n):
        message[k] = modes


def base_kernel(z, *refs):
    *values, out = refs
    for at in range(2):
        for s in range(z.subs):
            total = jnp.zeros((z.own, z.lanes), F32)
            for k, value in enumerate(values):
                place = lax.rem(lax.axis_index(GROUP) + k, z.group)
                turn = lax.rem((place - s + z.subs * z.group) * z.width, z.lanes)
                turned = pltpu.roll(value[at], turn, 1)
                total = jnp.where(lane_mask(z, place, turned.shape), turned, total)
            out[at, s] = total


def last_kernel(z, wait, *refs):
    arrived, firsts, seconds = refs[: z.group], refs[z.group : 2 * z.group], refs[2 * z.group : 3 * z.group]
    picks, face_before, face_after, face_first, face_second, left_rows, right_rows = refs[3 * z.group : 3 * z.group + 7]
    tall, base, second_pass, final_residual = refs[3 * z.group + 7 :]
    start = piece_start(z, 0, z.own)
    m, half = z.modes, z.lanes // 2
    places = [lax.rem(lax.axis_index(GROUP) + k, z.group) * z.width for k in range(z.group)]
    moves = [lane_matrix(z, 0, place) for place in places]

    def all_cases(parts):
        return sum(dot(part, move) for part, move in zip(parts, moves))

    modes = all_cases([picked_rows(z, piece, picks) for piece in arrived]).astype(BF16)
    swaps = list(zip(firsts, seconds))
    outer_before = all_cases([jnp.where(even(), b[...], a[...]) for a, b in swaps])
    outer_after = all_cases([jnp.where(even(), a[...], b[...]) for a, b in swaps])
    wait(3 * z.group + 7)
    totals = []
    for s in range(z.subs):
        faces = sides(z, face_before, face_after, face_first, face_second, s)
        both = []
        for side, at in ((0, s), (1, s + 2)):
            above = jnp.zeros((half, z.lanes), BF16)
            below = jnp.zeros((half - m, z.lanes), BF16)
            both.append(dot(faces[side], jnp.concatenate([above, modes[at * m : (at + 1) * m], below], axis=0)))
        if s == 0:
            both[0] = both[0] + outer_before
        if s == z.subs - 1:
            both[1] = both[1] + outer_after
        scatter = scatter_matrix(z, left_rows[s : s + 1, :], start, z.own)
        wide = jnp.concatenate([tall[s, pl.ds(start, z.own), :], scatter], axis=1)
        total = dot(wide, correction_side(z, modes, s, both[0].astype(BF16)))
        image = dot(scatter_matrix(z, right_rows[s : s + 1, :], start, z.own), both[1].astype(BF16))
        totals.append((total[:, z.lanes :], total[:, : z.lanes] + image))
    wait(3 * z.group + 8)
    for s, (step, image) in enumerate(totals):
        second_pass[s] = (base[0, s] + step)[:, : z.cases]
        final_residual[s] = (base[1, s] - image)[:, : z.cases]


def call(kernel, outs, operands, flops, scratch=(), late=(), loose=(), name=None):
    moved = sum(int(np.prod(x.shape)) * x.dtype.itemsize for x in (*operands, *outs))
    n_in, n_out = len(operands), len(outs)

    def whole(*refs):
        hbm, refs = refs[: n_in + n_out], refs[n_in + n_out :]
        vmem, refs = refs[: n_in + n_out], refs[n_in + n_out :]
        in_sems, out_sems, *rest = refs
        arriving = [pltpu.make_async_copy(hbm[i], vmem[i], in_sems.at[i]) for i in range(n_in)]
        for i in sorted(range(n_in), key=lambda i: i in late):
            arriving[i].start()
        for i, copy in enumerate(arriving):
            if i not in late:
                copy.wait()
        extra = [lambda i: arriving[i].wait()] if late else []
        kernel(*extra, *vmem, *rest)
        leaving = [pltpu.make_async_copy(vmem[n_in + i], hbm[n_in + i], out_sems.at[i]) for i in range(n_out)]
        for copy in leaving:
            copy.start()
        for copy in leaving:
            copy.wait()

    hbm_spec = pl.BlockSpec(memory_space=pltpu.HBM)
    any_spec = pl.BlockSpec(memory_space=pl.ANY)
    placed = [
        x if i in loose else pltpu.with_memory_space_constraint(x, pltpu.HBM) for i, x in enumerate(operands)
    ]
    return pl.pallas_call(
        whole,
        out_shape=[pltpu.HBM(o.shape, o.dtype) for o in outs],
        in_specs=[any_spec if i in loose else hbm_spec for i in range(n_in)],
        out_specs=[hbm_spec] * n_out,
        scratch_shapes=[
            *[pltpu.VMEM(x.shape, x.dtype) for x in (*operands, *outs)],
            pltpu.SemaphoreType.DMA((n_in,)),
            pltpu.SemaphoreType.DMA((n_out,)),
            *scratch,
        ],
        compiler_params=pltpu.CompilerParams(vmem_limit_bytes=VMEM_BYTES),
        cost_estimate=pl.CostEstimate(flops=flops, bytes_accessed=moved, transcendentals=0),
        name=name,
    )(*placed)


def shape(dims, dtype):
    return jax.ShapeDtypeStruct(dims, dtype)


def pieces_of(block, group):
    out = [block]
    for k in range(1, group):
        out.append(lax.ppermute(block, GROUP, [((g + k) % group, g) for g in range(group)]))
    return out


def body(loads, stiffness, local_inverse, coarse_basis, coarse_inverse, coarse_index, left_rows, right_rows):
    z = Sizes(loads, stiffness, coarse_basis, coarse_inverse, left_rows)
    n, group, subs, rows, lanes, modes, face = z.n, z.group, z.subs, z.rows, z.lanes, z.modes, z.face
    basis_pieces = pieces_of(jnp.swapaxes(coarse_basis, 1, 2), group)
    inverse_columns = pieces_of(coarse_inverse, group)
    basis_pieces, inverse_columns, local_inverse, stiffness = lax.optimization_barrier(
        (basis_pieces, inverse_columns, local_inverse, stiffness)
    )
    column = np.arange(z.columns)
    repeat = jnp.asarray(np.arange(lanes)[:, None] == column[None, :] % modes, BF16)
    own_row = jnp.asarray(np.arange(n)[:, None] == column[None, :] // modes, F32)
    place = jnp.asarray(
        (column // modes * z.owned + column % modes)[None, :] + np.arange(subs)[:, None] * modes, jnp.int32
    )
    packed_f = shape((rows, lanes), F32)
    packed_b = shape((rows, lanes), BF16)
    copies = shape((n, modes, lanes), BF16)
    tall = shape((subs, rows, lanes), BF16)
    spread = functools.partial(lax.all_to_all, axis_name="sub", split_axis=0, concat_axis=0)
    first_pairs = [(i, i + 1 if i % 2 == 0 else i - 1) for i in range(n)]
    second_pairs = [(i, (i + (1 if i % 2 else -1)) % n) for i in range(n)]
    work = 4 * subs * rows * rows * lanes

    (message,) = call(
        functools.partial(open_kernel, z),
        [shape((n, modes + DIGIT_ROWS, lanes), BF16)],
        [*basis_pieces, loads, coarse_index],
        4 * rows * lanes * lanes,
        [pltpu.VMEM((DIGIT_ROWS, lanes), F32), pltpu.VMEM((subs, modes, rows), BF16)],
        loose=range(1, group),
        name="open",
    )
    inverse_pieces = pieces_of(local_inverse, group)
    stiffness_pieces = pieces_of(stiffness, group)
    restricted = spread(message)
    arrivals = [*range(1, group), *range(group + 1, 2 * group)]
    faces = shape((subs, face, lanes), BF16)
    outer = shape((face, lanes), BF16)
    (
        load_rows, solved, image, before, after, first_pair, second_pair, tall, basis_t
    ) = call(
        functools.partial(first_image_kernel, z),
        [
            packed_b, packed_f, packed_f, faces, faces, outer, outer, tall, shape((subs, modes, rows), BF16),
        ],
        [*inverse_pieces, *stiffness_pieces, *basis_pieces, loads, left_rows, right_rows],
        work,
        [
            pltpu.VMEM((rows, lanes), BF16),
            pltpu.VMEM((subs, rows, 2 * lanes), BF16), pltpu.VMEM((subs, rows, 2 * lanes), BF16),
        ],
        late=range(2 * group),
        loose=[*arrivals, *range(2 * group + 1, 3 * group)],
        name="first_image",
    )
    second_got = lax.ppermute(second_pair, "sub", second_pairs)
    restricted, second_pair = lax.optimization_barrier((restricted, second_pair))
    near = (subs + 2) * modes
    ordered_inverse, index, message = call(
        functools.partial(order_kernel, z),
        [shape((subs, z.owned, z.columns), BF16), shape((subs, n, lanes), F32), copies],
        [*inverse_columns, restricted, repeat, own_row],
        2 * z.owned * z.total * z.total,
        loose=range(1, group + 1),
        name="order",
    )
    coarse = spread(message)
    first_got = lax.ppermute(first_pair, "sub", first_pairs)
    side = shape((subs, modes, face), BF16)
    left_t, right_t, inner, start_modes, picks = call(
        functools.partial(begin_kernel, z),
        [
            side, side, shape((subs, modes, modes), BF16), shape((modes, lanes), F32),
            shape((subs, near, z.columns), BF16),
        ],
        [load_rows, image, tall, basis_t, left_rows, right_rows, index, place],
        work // 16,
        name="begin",
    )
    chosen, message = call(
        functools.partial(update_kernel, z),
        [shape((near, lanes), BF16), copies],
        [coarse, picks, start_modes, inner, left_t, right_t, before, after, first_got, second_got],
        work // 64,
        loose=[0, 8, 9],
        name="update",
    )
    restricted = spread(message)

    bases = [before, after, first_got, second_got]
    first_pair, second_pair, *values = call(
        functools.partial(second_image_kernel, z),
        [outer, outer, *[shape((2, z.own, lanes), F32)] * group],
        [
            *inverse_pieces, *stiffness_pieces, load_rows, image, tall, solved, chosen,
            *bases, left_rows, right_rows,
        ],
        work,
        [
            pltpu.VMEM((rows, lanes), F32), pltpu.VMEM((rows, lanes), BF16), pltpu.VMEM((rows, lanes), BF16),
            pltpu.VMEM((subs, face, lanes), BF16), pltpu.VMEM((subs, face, lanes), BF16),
        ],
        late=range(2 * group),
        loose=[*arrivals, 2 * group + 7, 2 * group + 8],
        name="second_image",
    )
    second_got = lax.ppermute(second_pair, "sub", second_pairs)
    restricted, second_pair = lax.optimization_barrier((restricted, second_pair))
    (message,) = call(
        functools.partial(coarse_kernel, z),
        [copies],
        [restricted, ordered_inverse],
        work // 64,
        loose=[0],
        name="coarse",
    )
    coarse = spread(message)
    first_got = lax.ppermute(first_pair, "sub", first_pairs)
    swapped = [values[0]]
    for k in range(1, group):
        swapped.append(lax.ppermute(values[k], GROUP, [(g, (g + k) % group) for g in range(group)]))
    swapped = [swapped[(group - k) % group] for k in range(group)]
    (base,) = call(
        functools.partial(base_kernel, z),
        [shape((2, subs, z.own, lanes), F32)],
        swapped,
        work // 64,
        loose=range(1, group),
        name="base",
    )
    coarse, base, first_got, second_got = lax.optimization_barrier((coarse, base, first_got, second_got))
    out = shape((subs, z.own, z.cases), F32)
    return tuple(
        call(
            functools.partial(last_kernel, z),
            [out, out],
            [
                *pieces_of(coarse, group), *pieces_of(first_got, group), *pieces_of(second_got, group),
                picks, *bases, left_rows, right_rows, tall, base,
            ],
            work // 8,
            late=[3 * group + 7, 3 * group + 8],
            loose=[*range(3 * group), 3 * group + 3, 3 * group + 4],
            name="last",
        )
    )


def solution(mesh):
    return jax.shard_map(
        body,
        mesh=mesh,
        in_specs=(
            P("sub", None, None),
            P("sub", GROUP, None),
            P("sub", GROUP, None),
            P("sub", GROUP, None),
            P("sub", GROUP),
            P("sub", None),
            P("sub", None),
            P("sub", None),
        ),
        out_specs=(P("sub", GROUP, None), P("sub", GROUP, None)),
        check_vma=False,
    )
```

```python
import functools

import jax
import jax.numpy as jnp
import numpy as np
from jax import lax
from jax.experimental import pallas as pl
from jax.experimental.pallas import tpu as pltpu
from jax.sharding import PartitionSpec as P

GROUP = ("crow", "ccol")
F32 = jnp.float32
BF16 = jnp.bfloat16
VMEM_BYTES = 48 * 1024 * 1024
DIGIT_ROWS = 16
DIGIT_BITS = 8
DIGIT = 1 << DIGIT_BITS


def dot(a, b):
    return lax.dot_general(a, b, (((1,), (0,)), ((), ())), preferred_element_type=F32)


def dot_tn(a, b):
    return lax.dot_general(a, b, (((0,), (0,)), ((), ())), preferred_element_type=F32)


def dot_nt(a, b):
    return lax.dot_general(a, b, (((1,), (1,)), ((), ())), preferred_element_type=F32)


class Sizes:
    def __init__(self, loads, stiffness, coarse_basis, coarse_inverse, left_rows):
        self.n = lax.axis_size("sub")
        self.group = lax.axis_size(GROUP)
        self.subs, self.rows, self.cases = loads.shape
        self.own = stiffness.shape[1]
        self.modes = coarse_basis.shape[2]
        self.owned, self.block = coarse_inverse.shape
        self.total = self.block * self.group
        self.face = left_rows.shape[1]
        self.width = self.cases // self.group
        self.lanes = max(self.cases, -(-self.subs * self.width // 128) * 128)
        self.columns = self.n * self.modes


def lane_mask(z, block, shape):
    lane = lax.broadcasted_iota(jnp.int32, shape, len(shape) - 1)
    return (lane >= block * z.width) & (lane < (block + 1) * z.width)


def select(z, parts):
    out = jnp.zeros_like(parts[0])
    for s, part in enumerate(parts):
        out = jnp.where(lane_mask(z, s, part.shape), part, out)
    return out


def fold(z, packed):
    if z.lanes == z.subs * z.width:
        out = packed
        for k in range(1, z.subs):
            out = out + pltpu.roll(packed, k * z.width, 1)
        return out
    out = packed
    for k in range(1, z.subs):
        out = out + pltpu.roll(packed, k * z.width, 1)
        out = out + pltpu.roll(packed, z.lanes - k * z.width, 1)
    return out


def lane_matrix(z, source, target, width=None):
    row = lax.broadcasted_iota(jnp.int32, (z.lanes, z.lanes), 0)
    lane = lax.broadcasted_iota(jnp.int32, (z.lanes, z.lanes), 1)
    hit = (row - source == lane - target) & (lane >= target) & (lane < target + (width or z.width))
    return jnp.where(hit, 1.0, 0.0).astype(BF16)


def piece_start(z, k, size):
    place = lax.rem(lax.axis_index(GROUP) + k, z.group)
    return pl.multiple_of(place * size, size)


def pick_matrix(z, rows_of):
    column = jnp.transpose(jnp.broadcast_to(rows_of.astype(F32), (z.face, z.face)))[:, 0:1].astype(jnp.int32)
    row = lax.broadcasted_iota(jnp.int32, (z.face, z.rows), 1)
    return jnp.where(row == column, 1.0, 0.0).astype(BF16)


def even():
    return lax.rem(lax.axis_index("sub"), 2) == 0


def case_matrix(z, s):
    row = lax.broadcasted_iota(jnp.int32, (z.cases, z.lanes), 0)
    lane = lax.broadcasted_iota(jnp.int32, (z.cases, z.lanes), 1)
    hit = (row - lax.axis_index(GROUP) * z.width == lane - s * z.width) & lane_mask(z, s, row.shape)
    return jnp.where(hit, 1.0, 0.0).astype(BF16)


def join_basis(z, pieces, basis_t):
    for k, piece in enumerate(pieces):
        basis_t[:, :, pl.ds(piece_start(z, k, z.own), z.own)] = piece[...]


def open_kernel(z, *refs):
    pieces = refs[: z.group]
    loads, index, message, digits, basis_t = refs[z.group :]
    join_basis(z, pieces, basis_t)
    total = jnp.zeros((z.modes, z.lanes), F32)
    for s in range(z.subs):
        total = total + dot(dot(basis_t[s], loads[s]).astype(BF16), case_matrix(z, s))
    modes = total.astype(BF16)
    digits[...] = jnp.zeros(digits.shape, F32)
    for s in range(z.subs):
        places = index[s : s + 1, :]
        digits[2 * s : 2 * s + 1, : z.modes] = (places >> DIGIT_BITS).astype(F32)
        digits[2 * s + 1 : 2 * s + 2, : z.modes] = (places & (DIGIT - 1)).astype(F32)
    for k in range(z.n):
        message[k, : z.modes, :] = modes
        message[k, z.modes :, :] = digits[...].astype(BF16)


def multiply(z, pieces, vector, store, wait):
    for k in range(z.group):
        wait(k)
    for k, piece in enumerate(pieces):
        parts = [dot(piece[s], vector) for s in range(z.subs)]
        store(k, piece_start(z, k, z.own), select(z, parts))


def pick_both(z, left_rows, right_rows, s):
    return jnp.concatenate(
        [pick_matrix(z, left_rows[s : s + 1, :]), pick_matrix(z, right_rows[s : s + 1, :])], axis=0
    )


def halves(z, face):
    part = z.face // 2
    return (face[:part].astype(F32) + dot(face[part:], lane_matrix(z, 0, z.lanes // 2))).astype(BF16)


def store_faces(z, before, after, first_pair, second_pair):
    first, last = before[0], after[z.subs - 1]
    first_pair[...] = jnp.where(even(), last, first)
    second_pair[...] = jnp.where(even(), first, last)


def sides(z, before, after, first_pair, second_pair, s):
    if s == 0:
        from_before = jnp.where(even(), second_pair[...], first_pair[...])
    else:
        from_before = after[s - 1]
    if s == z.subs - 1:
        from_after = jnp.where(even(), first_pair[...], second_pair[...])
    else:
        from_after = before[s + 1]
    return from_before, from_after


def shares(z, s, chosen, faces, bases=None):
    m, half = z.modes, z.lanes // 2
    moved = lane_matrix(z, 0, s * z.width)
    out = []
    for side, at in ((0, s), (1, s + 2)):
        own = chosen[at * m : (at + 1) * m]
        below = jnp.concatenate([own, jnp.zeros((half - m, z.lanes), BF16)], axis=0)
        if bases is None:
            total = dot(faces[side], jnp.concatenate([moved[:half], below], axis=0))
        else:
            above = jnp.zeros((half, z.lanes), BF16)
            total = dot(faces[side], moved) + dot(bases[side], jnp.concatenate([above, below], axis=0))
        out.append(total)
    return out


def correction_side(z, chosen, s, share):
    m, half = z.modes, z.lanes // 2
    own = chosen[(s + 1) * m : (s + 2) * m]
    none = jnp.zeros((half - m, z.lanes), BF16)
    nil = jnp.zeros((half, z.lanes), BF16)
    image = jnp.concatenate([own, none, nil, share], axis=0)
    step = jnp.concatenate([nil, own, none, jnp.zeros((z.face, z.lanes), BF16)], axis=0)
    return jnp.concatenate([image, step], axis=1)


def scatter_matrix(z, rows_of, start, count):
    row = lax.broadcasted_iota(jnp.int32, (count, z.face), 0) + start
    return jnp.where(row == rows_of, 1.0, 0.0).astype(BF16)


def first_image_kernel(z, wait, *refs):
    inverse, stiffness = refs[: z.group], refs[z.group : 2 * z.group]
    pieces = refs[2 * z.group : 3 * z.group]
    loads, left_rows, right_rows = refs[3 * z.group : 3 * z.group + 3]
    load_rows, solved, image, before, after, first_pair, second_pair = refs[3 * z.group + 3 : 3 * z.group + 10]
    tall, basis_t, rounded, both, images = refs[3 * z.group + 10 :]
    join_basis(z, pieces, basis_t)
    packed = dot(loads[0], case_matrix(z, 0))
    for s in range(1, z.subs):
        packed = packed + dot(loads[s], case_matrix(z, s))
    load_rows[...] = packed.astype(BF16)

    def store_solved(k, start, value):
        solved[pl.ds(start, z.own), :] = value
        rounded[pl.ds(start, z.own), :] = value.astype(BF16)

    multiply(z, inverse, load_rows[...], store_solved, wait)
    solved_b = rounded[...]
    half = z.lanes // 2
    for s in range(z.subs):
        basis = jnp.transpose(basis_t[s].astype(F32)).astype(BF16)
        tall[s, :, half : half + z.modes] = basis
        tall[s, :, half + z.modes :] = jnp.zeros((z.rows, half - z.modes), BF16)
        both[s, :, : z.lanes] = solved_b
        both[s, :, z.lanes : z.lanes + z.modes] = basis
        both[s, :, z.lanes + z.modes :] = jnp.zeros((z.rows, z.lanes - z.modes), BF16)
    for k, piece in enumerate(stiffness):
        wait(z.group + k)
        start = piece_start(z, k, z.own)
        parts = [dot(piece[s], both[s]) for s in range(z.subs)]
        image[pl.ds(start, z.own), :] = select(z, [part[:, : z.lanes] for part in parts])
        for s in range(z.subs):
            images[s, pl.ds(start, z.own), :] = parts[s].astype(BF16)
    for s in range(z.subs):
        tall[s, :, :half] = images[s, :, z.lanes : z.lanes + half]
        picked = dot(pick_both(z, left_rows, right_rows, s), images[s]).astype(BF16)
        faces = dot(picked[:, : z.lanes], lane_matrix(z, s * z.width, 0))
        faces = (faces + dot(picked[:, z.lanes :], lane_matrix(z, 0, half, z.modes))).astype(BF16)
        before[s] = faces[: z.face]
        after[s] = faces[z.face :]
    store_faces(z, before, after, first_pair, second_pair)


def begin_kernel(z, *refs):
    load_rows, image, tall, basis_t, left_rows, right_rows, index, place = refs[:8]
    left_t, right_t, inner, start_modes, picks = refs[8:]
    left = (load_rows[...].astype(F32) - image[...]).astype(BF16)
    begun = []
    for s in range(z.subs):
        restricted = dot(basis_t[s], jnp.concatenate([left, tall[s]], axis=1))
        begun.append(restricted[:, : z.lanes])
        inner[s] = restricted[:, z.lanes : z.lanes + z.modes].astype(BF16)
        sides_t = dot_nt(basis_t[s], pick_both(z, left_rows, right_rows, s)).astype(BF16)
        left_t[s] = sides_t[:, : z.face]
        right_t[s] = sides_t[:, z.face :]
    start_modes[...] = select(z, begun)
    here = lax.axis_index("sub")
    device = lax.broadcasted_iota(jnp.int32, (z.n, z.lanes), 0)
    for t in range(z.subs + 2):
        if t == 0:
            s, owner = z.subs - 1, lax.rem(here + z.n - 1, z.n)
        elif t == z.subs + 1:
            s, owner = 0, lax.rem(here + 1, z.n)
        else:
            s, owner = t - 1, here
        row = jnp.sum(jnp.where(device == owner, index[s], 0.0), axis=0, keepdims=True)
        column = jnp.transpose(jnp.broadcast_to(row, (z.lanes, z.lanes)))[: z.modes, 0:1].astype(jnp.int32)
        for h in range(z.subs):
            hit = column == place[h : h + 1, :]
            picks[h, t * z.modes : (t + 1) * z.modes, :] = jnp.where(hit, 1.0, 0.0).astype(BF16)


def second_image_kernel(z, wait, *refs):
    inverse, stiffness = refs[: z.group], refs[z.group : 2 * z.group]
    rest = refs[2 * z.group :]
    load_rows, old_image, tall, old_solved, chosen = rest[:5]
    before, after, first_got, second_got, left_rows, right_rows = rest[5:11]
    first_pair, second_pair = rest[11:13]
    values = rest[13 : 13 + z.group]
    base, rounded, image, new_before, new_after = rest[13 + z.group :]
    steps, images = [], []
    for s in range(z.subs):
        faces = sides(z, before, after, first_got, second_got, s)
        both = [share.astype(BF16) for share in shares(z, s, chosen, faces)]
        left = jnp.concatenate([tall[s], scatter_matrix(z, left_rows[s : s + 1, :], 0, z.rows)], axis=1)
        total = dot(left, correction_side(z, chosen, s, both[0]))
        steps.append(total[:, z.lanes :])
        images.append(total[:, : z.lanes] + dot(scatter_matrix(z, right_rows[s : s + 1, :], 0, z.rows), both[1]))
    residual = (load_rows[...].astype(F32) - old_image[...] - select(z, images)).astype(BF16)
    base[...] = old_solved[...] + select(z, steps)

    def store_solved(k, start, value):
        value = value + base[pl.ds(start, z.own), :]
        values[k][0] = value
        rounded[pl.ds(start, z.own), :] = value.astype(BF16)

    multiply(z, inverse, residual, store_solved, wait)

    def store_image(k, start, value):
        place = pl.ds(start, z.own)
        values[k][1] = load_rows[place, :].astype(F32) - value
        image[place, :] = value.astype(BF16)

    multiply(z, stiffness, rounded[...], store_image, lambda k: wait(z.group + k))
    pick = jnp.concatenate([pick_both(z, left_rows, right_rows, s) for s in range(z.subs)], axis=0)
    picked = dot(pick, image[...]).astype(BF16)
    for s in range(z.subs):
        own = picked[2 * s * z.face : 2 * (s + 1) * z.face]
        faces = dot(own, lane_matrix(z, s * z.width, 0)).astype(BF16)
        new_before[s] = faces[: z.face]
        new_after[s] = faces[z.face :]
    first = halves(z, new_before[0])
    last = halves(z, new_after[z.subs - 1])
    first_pair[...] = jnp.where(even(), last, first)
    second_pair[...] = jnp.where(even(), first, last)
    inner = []
    for s in range(z.subs):
        move = lane_matrix(z, 0, s * z.width)
        total = jnp.zeros((z.rows, z.lanes), F32)
        if s > 0:
            share = dot(new_after[s - 1], move).astype(BF16)
            total = total + dot(scatter_matrix(z, left_rows[s : s + 1, :], 0, z.rows), share)
        if s < z.subs - 1:
            share = dot(new_before[s + 1], move).astype(BF16)
            total = total + dot(scatter_matrix(z, right_rows[s : s + 1, :], 0, z.rows), share)
        inner.append(total)
    base[...] = select(z, inner)
    for k in range(z.group):
        values[k][1] = values[k][1] - base[pl.ds(piece_start(z, k, z.own), z.own), :]


def digit_row(shape, row):
    return lax.broadcasted_iota(jnp.int32, shape, 1) == row


def coarse_rows(z, ordered_inverse, arrived, message):
    flat = arrived[:, : z.modes, :].reshape(z.columns, z.lanes)
    rows = fold(z, select(z, [dot(ordered_inverse[s], flat) for s in range(z.subs)]))
    packed = select(z, [rows[s * z.modes : (s + 1) * z.modes, :] for s in range(z.subs)]).astype(BF16)
    for k in range(z.n):
        message[k] = packed


def order_kernel(z, *refs):
    blocks = refs[: z.group]
    arrived, repeat, own_row, ordered_inverse, index, message = refs[z.group :]
    digits = arrived[:, z.modes :, :].astype(F32)
    for s in range(z.subs):
        high = jnp.sum(jnp.where(digit_row(digits.shape, 2 * s), digits, 0.0), axis=1)
        low = jnp.sum(jnp.where(digit_row(digits.shape, 2 * s + 1), digits, 0.0), axis=1)
        index[s] = high * DIGIT + low
        spread = dot(high.astype(BF16), repeat[...]) * DIGIT + dot(low.astype(BF16), repeat[...])
        places = jnp.sum(spread * own_row[...], axis=0, keepdims=True).astype(jnp.int32)
        for at in range(0, z.columns, 768):
            wide = min(768, z.columns - at)
            total = jnp.zeros((z.owned, wide), F32)
            for k, block in enumerate(blocks):
                inside = (places[:, at : at + wide] - piece_start(z, k, z.block)).astype(jnp.int16)
                for first in range(0, z.block, 768):
                    deep = min(768, z.block - first)
                    row = lax.broadcasted_iota(jnp.int16, (deep, wide), 0) + jnp.int16(first)
                    hot = jnp.where(row == inside, jnp.ones((), BF16), jnp.zeros((), BF16))
                    total = total + dot(block[:, first : first + deep], hot)
            ordered_inverse[s, :, at : at + wide] = total.astype(BF16)
    coarse_rows(z, ordered_inverse, arrived, message)


def coarse_kernel(z, arrived, ordered_inverse, message):
    coarse_rows(z, ordered_inverse, arrived, message)


def picked_rows(z, arrived, picks):
    flat = arrived[...].reshape(z.columns, z.lanes)
    return fold(z, select(z, [dot(picks[h], flat) for h in range(z.subs)])).astype(BF16)


def update_kernel(z, *refs):
    arrived, picks, start_modes, inner, left_t, right_t, before, after, first_got, second_got = refs[:10]
    chosen, message = refs[10:]
    rows = picked_rows(z, arrived, picks)
    chosen[...] = rows
    m = z.modes
    parts = []
    for s in range(z.subs):
        faces = sides(z, before, after, first_got, second_got, s)
        both = shares(z, s, rows, faces)
        total = dot(inner[s], rows[(s + 1) * m : (s + 2) * m])
        parts.append(total + dot(left_t[s], both[0].astype(BF16)) + dot(right_t[s], both[1].astype(BF16)))
    modes = (start_modes[...] - select(z, parts)).astype(BF16)
    for k in range(z.n):
        message[k] = modes


def base_kernel(z, *refs):
    *values, out = refs
    for at in range(2):
        for s in range(z.subs):
            total = jnp.zeros((z.own, z.lanes), F32)
            for k, value in enumerate(values):
                place = lax.rem(lax.axis_index(GROUP) + k, z.group)
                turn = lax.rem((place - s + z.subs * z.group) * z.width, z.lanes)
                turned = pltpu.roll(value[at], turn, 1)
                total = jnp.where(lane_mask(z, place, turned.shape), turned, total)
            out[at, s] = total


def last_kernel(z, wait, *refs):
    arrived, firsts, seconds = refs[: z.group], refs[z.group : 2 * z.group], refs[2 * z.group : 3 * z.group]
    picks, face_before, face_after, face_first, face_second, left_rows, right_rows = refs[3 * z.group : 3 * z.group + 7]
    tall, base, second_pass, final_residual = refs[3 * z.group + 7 :]
    start = piece_start(z, 0, z.own)
    m, half = z.modes, z.lanes // 2
    places = [lax.rem(lax.axis_index(GROUP) + k, z.group) * z.width for k in range(z.group)]

    def all_cases(parts, source=0):
        return sum(dot(part, lane_matrix(z, source, place)) for part, place in zip(parts, places))

    def whole_face(parts):
        return jnp.concatenate([all_cases(parts), all_cases(parts, half)], axis=0)

    modes = all_cases([picked_rows(z, piece, picks) for piece in arrived]).astype(BF16)
    swaps = list(zip(firsts, seconds))
    outer_before = whole_face([jnp.where(even(), b[...], a[...]) for a, b in swaps])
    outer_after = whole_face([jnp.where(even(), a[...], b[...]) for a, b in swaps])
    wait(3 * z.group + 7)
    totals = []
    for s in range(z.subs):
        faces = sides(z, face_before, face_after, face_first, face_second, s)
        both = []
        for side, at in ((0, s), (1, s + 2)):
            above = jnp.zeros((half, z.lanes), BF16)
            below = jnp.zeros((half - m, z.lanes), BF16)
            both.append(dot(faces[side], jnp.concatenate([above, modes[at * m : (at + 1) * m], below], axis=0)))
        if s == 0:
            both[0] = both[0] + outer_before
        if s == z.subs - 1:
            both[1] = both[1] + outer_after
        scatter = scatter_matrix(z, left_rows[s : s + 1, :], start, z.own)
        wide = jnp.concatenate([tall[s, pl.ds(start, z.own), :], scatter], axis=1)
        total = dot(wide, correction_side(z, modes, s, both[0].astype(BF16)))
        image = dot(scatter_matrix(z, right_rows[s : s + 1, :], start, z.own), both[1].astype(BF16))
        totals.append((total[:, z.lanes :], total[:, : z.lanes] + image))
    wait(3 * z.group + 8)
    for s, (step, image) in enumerate(totals):
        second_pass[s] = (base[0, s] + step)[:, : z.cases]
        final_residual[s] = (base[1, s] - image)[:, : z.cases]


def call(kernel, outs, operands, flops, scratch=(), late=(), loose=(), name=None):
    moved = sum(int(np.prod(x.shape)) * x.dtype.itemsize for x in (*operands, *outs))
    n_in, n_out = len(operands), len(outs)

    def whole(*refs):
        hbm, refs = refs[: n_in + n_out], refs[n_in + n_out :]
        vmem, refs = refs[: n_in + n_out], refs[n_in + n_out :]
        in_sems, out_sems, *rest = refs
        arriving = [pltpu.make_async_copy(hbm[i], vmem[i], in_sems.at[i]) for i in range(n_in)]
        for i in sorted(range(n_in), key=lambda i: i in late):
            arriving[i].start()
        for i, copy in enumerate(arriving):
            if i not in late:
                copy.wait()
        extra = [lambda i: arriving[i].wait()] if late else []
        kernel(*extra, *vmem, *rest)
        leaving = [pltpu.make_async_copy(vmem[n_in + i], hbm[n_in + i], out_sems.at[i]) for i in range(n_out)]
        for copy in leaving:
            copy.start()
        for copy in leaving:
            copy.wait()

    hbm_spec = pl.BlockSpec(memory_space=pltpu.HBM)
    any_spec = pl.BlockSpec(memory_space=pl.ANY)
    placed = [
        x if i in loose else pltpu.with_memory_space_constraint(x, pltpu.HBM) for i, x in enumerate(operands)
    ]
    return pl.pallas_call(
        whole,
        out_shape=[pltpu.HBM(o.shape, o.dtype) for o in outs],
        in_specs=[any_spec if i in loose else hbm_spec for i in range(n_in)],
        out_specs=[hbm_spec] * n_out,
        scratch_shapes=[
            *[pltpu.VMEM(x.shape, x.dtype) for x in (*operands, *outs)],
            pltpu.SemaphoreType.DMA((n_in,)),
            pltpu.SemaphoreType.DMA((n_out,)),
            *scratch,
        ],
        compiler_params=pltpu.CompilerParams(vmem_limit_bytes=VMEM_BYTES),
        cost_estimate=pl.CostEstimate(flops=flops, bytes_accessed=moved, transcendentals=0),
        name=name,
    )(*placed)


def shape(dims, dtype):
    return jax.ShapeDtypeStruct(dims, dtype)


def pieces_of(block, group):
    out = [block]
    for k in range(1, group):
        out.append(lax.ppermute(block, GROUP, [((g + k) % group, g) for g in range(group)]))
    return out


def body(loads, stiffness, local_inverse, coarse_basis, coarse_inverse, coarse_index, left_rows, right_rows):
    z = Sizes(loads, stiffness, coarse_basis, coarse_inverse, left_rows)
    n, group, subs, rows, lanes, modes, face = z.n, z.group, z.subs, z.rows, z.lanes, z.modes, z.face
    basis_pieces = pieces_of(jnp.swapaxes(coarse_basis, 1, 2), group)
    inverse_columns = pieces_of(coarse_inverse, group)
    basis_pieces, inverse_columns, local_inverse, stiffness = lax.optimization_barrier(
        (basis_pieces, inverse_columns, local_inverse, stiffness)
    )
    column = np.arange(z.columns)
    repeat = jnp.asarray(np.arange(lanes)[:, None] == column[None, :] % modes, BF16)
    own_row = jnp.asarray(np.arange(n)[:, None] == column[None, :] // modes, F32)
    place = jnp.asarray(
        (column // modes * z.owned + column % modes)[None, :] + np.arange(subs)[:, None] * modes, jnp.int32
    )
    packed_f = shape((rows, lanes), F32)
    packed_b = shape((rows, lanes), BF16)
    copies = shape((n, modes, lanes), BF16)
    tall = shape((subs, rows, lanes), BF16)
    spread = functools.partial(lax.all_to_all, axis_name="sub", split_axis=0, concat_axis=0)
    first_pairs = [(i, i + 1 if i % 2 == 0 else i - 1) for i in range(n)]
    second_pairs = [(i, (i + (1 if i % 2 else -1)) % n) for i in range(n)]
    work = 4 * subs * rows * rows * lanes

    (message,) = call(
        functools.partial(open_kernel, z),
        [shape((n, modes + DIGIT_ROWS, lanes), BF16)],
        [*basis_pieces, loads, coarse_index],
        4 * rows * lanes * lanes,
        [pltpu.VMEM((DIGIT_ROWS, lanes), F32), pltpu.VMEM((subs, modes, rows), BF16)],
        loose=range(1, group),
        name="open",
    )
    inverse_pieces = pieces_of(local_inverse, group)
    stiffness_pieces = pieces_of(stiffness, group)
    restricted = spread(message)
    arrivals = [*range(1, group), *range(group + 1, 2 * group)]
    faces = shape((subs, face, lanes), BF16)
    outer = shape((face, lanes), BF16)
    (
        load_rows, solved, image, before, after, first_pair, second_pair, tall, basis_t
    ) = call(
        functools.partial(first_image_kernel, z),
        [
            packed_b, packed_f, packed_f, faces, faces, outer, outer, tall, shape((subs, modes, rows), BF16),
        ],
        [*inverse_pieces, *stiffness_pieces, *basis_pieces, loads, left_rows, right_rows],
        work,
        [
            pltpu.VMEM((rows, lanes), BF16),
            pltpu.VMEM((subs, rows, 2 * lanes), BF16), pltpu.VMEM((subs, rows, 2 * lanes), BF16),
        ],
        late=range(2 * group),
        loose=[*arrivals, *range(2 * group + 1, 3 * group)],
        name="first_image",
    )
    second_got = lax.ppermute(second_pair, "sub", second_pairs)
    restricted, second_pair = lax.optimization_barrier((restricted, second_pair))
    near = (subs + 2) * modes
    ordered_inverse, index, message = call(
        functools.partial(order_kernel, z),
        [shape((subs, z.owned, z.columns), BF16), shape((subs, n, lanes), F32), copies],
        [*inverse_columns, restricted, repeat, own_row],
        2 * z.owned * z.total * z.total,
        loose=range(1, group + 1),
        name="order",
    )
    coarse = spread(message)
    first_got = lax.ppermute(first_pair, "sub", first_pairs)
    side = shape((subs, modes, face), BF16)
    left_t, right_t, inner, start_modes, picks = call(
        functools.partial(begin_kernel, z),
        [
            side, side, shape((subs, modes, modes), BF16), shape((modes, lanes), F32),
            shape((subs, near, z.columns), BF16),
        ],
        [load_rows, image, tall, basis_t, left_rows, right_rows, index, place],
        work // 16,
        name="begin",
    )
    chosen, message = call(
        functools.partial(update_kernel, z),
        [shape((near, lanes), BF16), copies],
        [coarse, picks, start_modes, inner, left_t, right_t, before, after, first_got, second_got],
        work // 64,
        loose=[0, 8, 9],
        name="update",
    )
    restricted = spread(message)

    bases = [before, after, first_got, second_got]
    half_face = shape((face // 2, lanes), BF16)
    first_pair, second_pair, *values = call(
        functools.partial(second_image_kernel, z),
        [half_face, half_face, *[shape((2, z.own, lanes), F32)] * group],
        [
            *inverse_pieces, *stiffness_pieces, load_rows, image, tall, solved, chosen,
            *bases, left_rows, right_rows,
        ],
        work,
        [
            pltpu.VMEM((rows, lanes), F32), pltpu.VMEM((rows, lanes), BF16), pltpu.VMEM((rows, lanes), BF16),
            pltpu.VMEM((subs, face, lanes), BF16), pltpu.VMEM((subs, face, lanes), BF16),
        ],
        late=range(2 * group),
        loose=[*arrivals, 2 * group + 7, 2 * group + 8],
        name="second_image",
    )
    second_got = lax.ppermute(second_pair, "sub", second_pairs)
    restricted, second_pair = lax.optimization_barrier((restricted, second_pair))
    (message,) = call(
        functools.partial(coarse_kernel, z),
        [copies],
        [restricted, ordered_inverse],
        work // 64,
        loose=[0],
        name="coarse",
    )
    coarse = spread(message)
    first_got = lax.ppermute(first_pair, "sub", first_pairs)
    swapped = [values[0]]
    for k in range(1, group):
        swapped.append(lax.ppermute(values[k], GROUP, [(g, (g + k) % group) for g in range(group)]))
    swapped = [swapped[(group - k) % group] for k in range(group)]
    (base,) = call(
        functools.partial(base_kernel, z),
        [shape((2, subs, z.own, lanes), F32)],
        swapped,
        work // 64,
        loose=range(1, group),
        name="base",
    )
    coarse, base, first_got, second_got = lax.optimization_barrier((coarse, base, first_got, second_got))
    out = shape((subs, z.own, z.cases), F32)
    return tuple(
        call(
            functools.partial(last_kernel, z),
            [out, out],
            [
                *pieces_of(coarse, group), *pieces_of(first_got, group), *pieces_of(second_got, group),
                picks, *bases, left_rows, right_rows, tall, base,
            ],
            work // 8,
            late=[3 * group + 7, 3 * group + 8],
            loose=[*range(3 * group), 3 * group + 3, 3 * group + 4],
            name="last",
        )
    )


def solution(mesh):
    return jax.shard_map(
        body,
        mesh=mesh,
        in_specs=(
            P("sub", None, None),
            P("sub", GROUP, None),
            P("sub", GROUP, None),
            P("sub", GROUP, None),
            P("sub", GROUP),
            P("sub", None),
            P("sub", None),
            P("sub", None),
        ),
        out_specs=(P("sub", GROUP, None), P("sub", GROUP, None)),
        check_vma=False,
    )
```

```python
import functools

import jax
import jax.numpy as jnp
import numpy as np
from jax import lax
from jax.experimental import pallas as pl
from jax.experimental.pallas import tpu as pltpu
from jax.sharding import PartitionSpec as P

GROUP = ("crow", "ccol")
F32 = jnp.float32
BF16 = jnp.bfloat16
VMEM_BYTES = 48 * 1024 * 1024
DIGIT_ROWS = 16
DIGIT_BITS = 8
DIGIT = 1 << DIGIT_BITS


def dot(a, b):
    return lax.dot_general(a, b, (((1,), (0,)), ((), ())), preferred_element_type=F32)


def dot_tn(a, b):
    return lax.dot_general(a, b, (((0,), (0,)), ((), ())), preferred_element_type=F32)


def dot_nt(a, b):
    return lax.dot_general(a, b, (((1,), (1,)), ((), ())), preferred_element_type=F32)


class Sizes:
    def __init__(self, loads, stiffness, coarse_basis, coarse_inverse, left_rows):
        self.n = lax.axis_size("sub")
        self.group = lax.axis_size(GROUP)
        self.subs, self.rows, self.cases = loads.shape
        self.own = stiffness.shape[1]
        self.modes = coarse_basis.shape[2]
        self.owned, self.block = coarse_inverse.shape
        self.total = self.block * self.group
        self.face = left_rows.shape[1]
        self.width = self.cases // self.group
        self.lanes = max(self.cases, -(-self.subs * self.width // 128) * 128)
        self.columns = self.n * self.modes


def lane_mask(z, block, shape):
    lane = lax.broadcasted_iota(jnp.int32, shape, len(shape) - 1)
    return (lane >= block * z.width) & (lane < (block + 1) * z.width)


def select(z, parts):
    out = jnp.zeros_like(parts[0])
    for s, part in enumerate(parts):
        out = jnp.where(lane_mask(z, s, part.shape), part, out)
    return out


def fold(z, packed):
    if z.lanes == z.subs * z.width:
        out = packed
        for k in range(1, z.subs):
            out = out + pltpu.roll(packed, k * z.width, 1)
        return out
    out = packed
    for k in range(1, z.subs):
        out = out + pltpu.roll(packed, k * z.width, 1)
        out = out + pltpu.roll(packed, z.lanes - k * z.width, 1)
    return out


def lane_matrix(z, source, target, width=None):
    row = lax.broadcasted_iota(jnp.int32, (z.lanes, z.lanes), 0)
    lane = lax.broadcasted_iota(jnp.int32, (z.lanes, z.lanes), 1)
    hit = (row - source == lane - target) & (lane >= target) & (lane < target + (width or z.width))
    return jnp.where(hit, 1.0, 0.0).astype(BF16)


def piece_start(z, k, size):
    place = lax.rem(lax.axis_index(GROUP) + k, z.group)
    return pl.multiple_of(place * size, size)


def pick_matrix(z, rows_of):
    column = jnp.transpose(jnp.broadcast_to(rows_of.astype(F32), (z.face, z.face)))[:, 0:1].astype(jnp.int32)
    row = lax.broadcasted_iota(jnp.int32, (z.face, z.rows), 1)
    return jnp.where(row == column, 1.0, 0.0).astype(BF16)


def even():
    return lax.rem(lax.axis_index("sub"), 2) == 0


def case_matrix(z, s):
    row = lax.broadcasted_iota(jnp.int32, (z.cases, z.lanes), 0)
    lane = lax.broadcasted_iota(jnp.int32, (z.cases, z.lanes), 1)
    hit = (row - lax.axis_index(GROUP) * z.width == lane - s * z.width) & lane_mask(z, s, row.shape)
    return jnp.where(hit, 1.0, 0.0).astype(BF16)


def join_basis(z, pieces, basis_t):
    for k, piece in enumerate(pieces):
        basis_t[:, :, pl.ds(piece_start(z, k, z.own), z.own)] = piece[...]


def open_kernel(z, *refs):
    pieces = refs[: z.group]
    loads, index, message, digits, basis_t = refs[z.group :]
    join_basis(z, pieces, basis_t)
    total = jnp.zeros((z.modes, z.lanes), F32)
    for s in range(z.subs):
        total = total + dot(dot(basis_t[s], loads[s]).astype(BF16), case_matrix(z, s))
    modes = total.astype(BF16)
    digits[...] = jnp.zeros(digits.shape, F32)
    for s in range(z.subs):
        places = index[s : s + 1, :]
        digits[2 * s : 2 * s + 1, : z.modes] = (places >> DIGIT_BITS).astype(F32)
        digits[2 * s + 1 : 2 * s + 2, : z.modes] = (places & (DIGIT - 1)).astype(F32)
    for k in range(z.n):
        message[k, : z.modes, :] = modes
        message[k, z.modes :, :] = digits[...].astype(BF16)


def multiply(z, pieces, vector, store, wait):
    for k in range(z.group):
        wait(k)
    for k, piece in enumerate(pieces):
        parts = [dot(piece[s], vector) for s in range(z.subs)]
        store(k, piece_start(z, k, z.own), select(z, parts))


def pick_both(z, left_rows, right_rows, s):
    return jnp.concatenate(
        [pick_matrix(z, left_rows[s : s + 1, :]), pick_matrix(z, right_rows[s : s + 1, :])], axis=0
    )


def halves(z, face):
    part = z.face // 2
    return (face[:part].astype(F32) + dot(face[part:], lane_matrix(z, 0, z.lanes // 2))).astype(BF16)


def store_faces(z, before, after, first_pair, second_pair):
    first, last = before[0], after[z.subs - 1]
    first_pair[...] = jnp.where(even(), last, first)
    second_pair[...] = jnp.where(even(), first, last)


def sides(z, before, after, first_pair, second_pair, s):
    if s == 0:
        from_before = jnp.where(even(), second_pair[...], first_pair[...])
    else:
        from_before = after[s - 1]
    if s == z.subs - 1:
        from_after = jnp.where(even(), first_pair[...], second_pair[...])
    else:
        from_after = before[s + 1]
    return from_before, from_after


def shares(z, s, chosen, faces, bases=None):
    m, half = z.modes, z.lanes // 2
    moved = lane_matrix(z, 0, s * z.width)
    out = []
    for side, at in ((0, s), (1, s + 2)):
        own = chosen[at * m : (at + 1) * m]
        below = jnp.concatenate([own, jnp.zeros((half - m, z.lanes), BF16)], axis=0)
        if bases is None:
            total = dot(faces[side], jnp.concatenate([moved[:half], below], axis=0))
        else:
            above = jnp.zeros((half, z.lanes), BF16)
            total = dot(faces[side], moved) + dot(bases[side], jnp.concatenate([above, below], axis=0))
        out.append(total)
    return out


def correction_side(z, chosen, s, share):
    m, half = z.modes, z.lanes // 2
    own = chosen[(s + 1) * m : (s + 2) * m]
    none = jnp.zeros((half - m, z.lanes), BF16)
    nil = jnp.zeros((half, z.lanes), BF16)
    image = jnp.concatenate([own, none, nil, share], axis=0)
    step = jnp.concatenate([nil, own, none, jnp.zeros((z.face, z.lanes), BF16)], axis=0)
    return jnp.concatenate([image, step], axis=1)


def scatter_matrix(z, rows_of, start, count):
    row = lax.broadcasted_iota(jnp.int32, (count, z.face), 0) + start
    return jnp.where(row == rows_of, 1.0, 0.0).astype(BF16)


def first_image_kernel(z, wait, *refs):
    inverse, stiffness = refs[: z.group], refs[z.group : 2 * z.group]
    pieces = refs[2 * z.group : 3 * z.group]
    loads, left_rows, right_rows = refs[3 * z.group : 3 * z.group + 3]
    load_rows, solved, image, before, after, first_pair, second_pair = refs[3 * z.group + 3 : 3 * z.group + 10]
    tall, basis_t, rounded, both, images = refs[3 * z.group + 10 :]
    join_basis(z, pieces, basis_t)
    packed = dot(loads[0], case_matrix(z, 0))
    for s in range(1, z.subs):
        packed = packed + dot(loads[s], case_matrix(z, s))
    load_rows[...] = packed.astype(BF16)

    def store_solved(k, start, value):
        solved[pl.ds(start, z.own), :] = value
        rounded[pl.ds(start, z.own), :] = value.astype(BF16)

    multiply(z, inverse, load_rows[...], store_solved, wait)
    solved_b = rounded[...]
    half = z.lanes // 2
    for s in range(z.subs):
        basis = jnp.transpose(basis_t[s].astype(F32)).astype(BF16)
        tall[s, :, half : half + z.modes] = basis
        tall[s, :, half + z.modes :] = jnp.zeros((z.rows, half - z.modes), BF16)
        both[s, :, : z.lanes] = solved_b
        both[s, :, z.lanes : z.lanes + z.modes] = basis
        both[s, :, z.lanes + z.modes :] = jnp.zeros((z.rows, z.lanes - z.modes), BF16)
    for k, piece in enumerate(stiffness):
        wait(z.group + k)
        start = piece_start(z, k, z.own)
        parts = [dot(piece[s], both[s]) for s in range(z.subs)]
        image[pl.ds(start, z.own), :] = select(z, [part[:, : z.lanes] for part in parts])
        for s in range(z.subs):
            images[s, pl.ds(start, z.own), :] = parts[s].astype(BF16)
    for s in range(z.subs):
        tall[s, :, :half] = images[s, :, z.lanes : z.lanes + half]
        picked = dot(pick_both(z, left_rows, right_rows, s), images[s]).astype(BF16)
        faces = dot(picked[:, : z.lanes], lane_matrix(z, s * z.width, 0))
        faces = (faces + dot(picked[:, z.lanes :], lane_matrix(z, 0, half, z.modes))).astype(BF16)
        before[s] = faces[: z.face]
        after[s] = faces[z.face :]
    store_faces(z, before, after, first_pair, second_pair)


def begin_kernel(z, *refs):
    load_rows, image, tall, basis_t, left_rows, right_rows, index, place = refs[:8]
    left_t, right_t, inner, start_modes, picks = refs[8:]
    left = (load_rows[...].astype(F32) - image[...]).astype(BF16)
    begun = []
    for s in range(z.subs):
        restricted = dot(basis_t[s], jnp.concatenate([left, tall[s]], axis=1))
        begun.append(restricted[:, : z.lanes])
        inner[s] = restricted[:, z.lanes : z.lanes + z.modes].astype(BF16)
        sides_t = dot_nt(basis_t[s], pick_both(z, left_rows, right_rows, s)).astype(BF16)
        left_t[s] = sides_t[:, : z.face]
        right_t[s] = sides_t[:, z.face :]
    start_modes[...] = select(z, begun)
    here = lax.axis_index("sub")
    device = lax.broadcasted_iota(jnp.int32, (z.n, z.lanes), 0)
    for t in range(z.subs + 2):
        if t == 0:
            s, owner = z.subs - 1, lax.rem(here + z.n - 1, z.n)
        elif t == z.subs + 1:
            s, owner = 0, lax.rem(here + 1, z.n)
        else:
            s, owner = t - 1, here
        row = jnp.sum(jnp.where(device == owner, index[s], 0.0), axis=0, keepdims=True)
        column = jnp.transpose(jnp.broadcast_to(row, (z.lanes, z.lanes)))[: z.modes, 0:1].astype(jnp.int32)
        for h in range(z.subs):
            hit = column == place[h : h + 1, :]
            picks[h, t * z.modes : (t + 1) * z.modes, :] = jnp.where(hit, 1.0, 0.0).astype(BF16)


def second_image_kernel(z, wait, *refs):
    inverse, stiffness = refs[: z.group], refs[z.group : 2 * z.group]
    rest = refs[2 * z.group :]
    load_rows, old_image, tall, old_solved, chosen = rest[:5]
    before, after, first_got, second_got, left_rows, right_rows = rest[5:11]
    first_pair, second_pair = rest[11:13]
    values = rest[13 : 13 + z.group]
    base, rounded, image, new_before, new_after = rest[13 + z.group :]
    steps, images = [], []
    for s in range(z.subs):
        faces = sides(z, before, after, first_got, second_got, s)
        both = [share.astype(BF16) for share in shares(z, s, chosen, faces)]
        left = jnp.concatenate([tall[s], scatter_matrix(z, left_rows[s : s + 1, :], 0, z.rows)], axis=1)
        total = dot(left, correction_side(z, chosen, s, both[0]))
        steps.append(total[:, z.lanes :])
        images.append(total[:, : z.lanes] + dot(scatter_matrix(z, right_rows[s : s + 1, :], 0, z.rows), both[1]))
    residual = (load_rows[...].astype(F32) - old_image[...] - select(z, images)).astype(BF16)
    base[...] = old_solved[...] + select(z, steps)

    def store_solved(k, start, value):
        value = value + base[pl.ds(start, z.own), :]
        values[k][0] = value
        rounded[pl.ds(start, z.own), :] = value.astype(BF16)

    multiply(z, inverse, residual, store_solved, wait)

    def store_image(k, start, value):
        place = pl.ds(start, z.own)
        values[k][1] = load_rows[place, :].astype(F32) - value
        image[place, :] = value.astype(BF16)

    multiply(z, stiffness, rounded[...], store_image, lambda k: wait(z.group + k))
    pick = jnp.concatenate([pick_both(z, left_rows, right_rows, s) for s in range(z.subs)], axis=0)
    picked = dot(pick, image[...]).astype(BF16)
    for s in range(z.subs):
        own = picked[2 * s * z.face : 2 * (s + 1) * z.face]
        faces = dot(own, lane_matrix(z, s * z.width, 0)).astype(BF16)
        new_before[s] = faces[: z.face]
        new_after[s] = faces[z.face :]
    first = halves(z, new_before[0])
    last = halves(z, new_after[z.subs - 1])
    first_pair[...] = jnp.where(even(), last, first)
    second_pair[...] = jnp.where(even(), first, last)
    inner = []
    for s in range(z.subs):
        move = lane_matrix(z, 0, s * z.width)
        total = jnp.zeros((z.rows, z.lanes), F32)
        if s > 0:
            share = dot(new_after[s - 1], move).astype(BF16)
            total = total + dot(scatter_matrix(z, left_rows[s : s + 1, :], 0, z.rows), share)
        if s < z.subs - 1:
            share = dot(new_before[s + 1], move).astype(BF16)
            total = total + dot(scatter_matrix(z, right_rows[s : s + 1, :], 0, z.rows), share)
        inner.append(total)
    base[...] = select(z, inner)
    for k in range(z.group):
        values[k][1] = values[k][1] - base[pl.ds(piece_start(z, k, z.own), z.own), :]


def digit_row(shape, row):
    return lax.broadcasted_iota(jnp.int32, shape, 1) == row


def coarse_rows(z, ordered_inverse, arrived, message):
    flat = arrived[:, : z.modes, :].reshape(z.columns, z.lanes)
    rows = fold(z, select(z, [dot(ordered_inverse[s], flat) for s in range(z.subs)]))
    packed = select(z, [rows[s * z.modes : (s + 1) * z.modes, :] for s in range(z.subs)]).astype(BF16)
    for k in range(z.n):
        message[k] = packed


def order_kernel(z, *refs):
    blocks = refs[: z.group]
    arrived, repeat, own_row, ordered_inverse, index, message = refs[z.group :]
    digits = arrived[:, z.modes :, :].astype(F32)
    for s in range(z.subs):
        high = jnp.sum(jnp.where(digit_row(digits.shape, 2 * s), digits, 0.0), axis=1)
        low = jnp.sum(jnp.where(digit_row(digits.shape, 2 * s + 1), digits, 0.0), axis=1)
        index[s] = high * DIGIT + low
        spread = dot(high.astype(BF16), repeat[...]) * DIGIT + dot(low.astype(BF16), repeat[...])
        places = jnp.sum(spread * own_row[...], axis=0, keepdims=True).astype(jnp.int32)
        for at in range(0, z.columns, 768):
            wide = min(768, z.columns - at)
            total = jnp.zeros((z.owned, wide), F32)
            for k, block in enumerate(blocks):
                inside = (places[:, at : at + wide] - piece_start(z, k, z.block)).astype(jnp.int16)
                for first in range(0, z.block, 768):
                    deep = min(768, z.block - first)
                    row = lax.broadcasted_iota(jnp.int16, (deep, wide), 0) + jnp.int16(first)
                    hot = jnp.where(row == inside, jnp.ones((), BF16), jnp.zeros((), BF16))
                    total = total + dot(block[:, first : first + deep], hot)
            ordered_inverse[s, :, at : at + wide] = total.astype(BF16)
    coarse_rows(z, ordered_inverse, arrived, message)


def coarse_kernel(z, arrived, ordered_inverse, message):
    coarse_rows(z, ordered_inverse, arrived, message)


def picked_rows(z, arrived, picks):
    flat = arrived[...].reshape(z.columns, z.lanes)
    return fold(z, select(z, [dot(picks[h], flat) for h in range(z.subs)])).astype(BF16)


def update_kernel(z, *refs):
    arrived, picks, start_modes, inner, left_t, right_t, before, after, first_got, second_got = refs[:10]
    chosen, message = refs[10:]
    rows = picked_rows(z, arrived, picks)
    chosen[...] = rows
    m = z.modes
    parts = []
    for s in range(z.subs):
        faces = sides(z, before, after, first_got, second_got, s)
        both = shares(z, s, rows, faces)
        total = dot(inner[s], rows[(s + 1) * m : (s + 2) * m])
        parts.append(total + dot(left_t[s], both[0].astype(BF16)) + dot(right_t[s], both[1].astype(BF16)))
    modes = (start_modes[...] - select(z, parts)).astype(BF16)
    for k in range(z.n):
        message[k] = modes


def base_kernel(z, *refs):
    *values, out = refs
    for at in range(2):
        for s in range(z.subs):
            total = jnp.zeros((z.own, z.lanes), F32)
            for k, value in enumerate(values):
                place = lax.rem(lax.axis_index(GROUP) + k, z.group)
                turn = lax.rem((place - s + z.subs * z.group) * z.width, z.lanes)
                turned = pltpu.roll(value[at], turn, 1)
                total = jnp.where(lane_mask(z, place, turned.shape), turned, total)
            out[at, s] = total


def last_kernel(z, wait, send, *refs):
    arrived, firsts, seconds = refs[: z.group], refs[z.group : 2 * z.group], refs[2 * z.group : 3 * z.group]
    picks, face_before, face_after, face_first, face_second, left_rows, right_rows = refs[3 * z.group : 3 * z.group + 7]
    tall, base, second_pass, final_residual = refs[3 * z.group + 7 :]
    start = piece_start(z, 0, z.own)
    m, half = z.modes, z.lanes // 2
    places = [lax.rem(lax.axis_index(GROUP) + k, z.group) * z.width for k in range(z.group)]

    def all_cases(parts, source=0):
        return sum(dot(part, lane_matrix(z, source, place)) for part, place in zip(parts, places))

    def whole_face(parts):
        return jnp.concatenate([all_cases(parts), all_cases(parts, half)], axis=0)

    modes = all_cases([picked_rows(z, piece, picks) for piece in arrived]).astype(BF16)
    swaps = list(zip(firsts, seconds))
    outer_before = whole_face([jnp.where(even(), b[...], a[...]) for a, b in swaps])
    outer_after = whole_face([jnp.where(even(), a[...], b[...]) for a, b in swaps])
    wait(3 * z.group + 7)
    for s in range(z.subs):
        faces = sides(z, face_before, face_after, face_first, face_second, s)
        both = []
        for side, at in ((0, s), (1, s + 2)):
            above = jnp.zeros((half, z.lanes), BF16)
            below = jnp.zeros((half - m, z.lanes), BF16)
            both.append(dot(faces[side], jnp.concatenate([above, modes[at * m : (at + 1) * m], below], axis=0)))
        if s == 0:
            both[0] = both[0] + outer_before
        if s == z.subs - 1:
            both[1] = both[1] + outer_after
        scatter = scatter_matrix(z, left_rows[s : s + 1, :], start, z.own)
        wide = jnp.concatenate([tall[s, pl.ds(start, z.own), :], scatter], axis=1)
        total = dot(wide, correction_side(z, modes, s, both[0].astype(BF16)))
        image = dot(scatter_matrix(z, right_rows[s : s + 1, :], start, z.own), both[1].astype(BF16))
        if s == 0:
            wait(3 * z.group + 8)
        second_pass[s] = (base[0, s] + total[:, z.lanes :])[:, : z.cases]
        send(0, s)
        final_residual[s] = (base[1, s] - total[:, : z.lanes] - image)[:, : z.cases]
        send(1, s)


def call(kernel, outs, operands, flops, scratch=(), late=(), loose=(), early=False, name=None):
    moved = sum(int(np.prod(x.shape)) * x.dtype.itemsize for x in (*operands, *outs))
    n_in, n_out = len(operands), len(outs)
    blocks = outs[0].shape[0] if early else 1

    def whole(*refs):
        hbm, refs = refs[: n_in + n_out], refs[n_in + n_out :]
        vmem, refs = refs[: n_in + n_out], refs[n_in + n_out :]
        in_sems, out_sems, *rest = refs
        arriving = [pltpu.make_async_copy(hbm[i], vmem[i], in_sems.at[i]) for i in range(n_in)]
        for i in sorted(range(n_in), key=lambda i: i in late):
            arriving[i].start()
        for i, copy in enumerate(arriving):
            if i not in late:
                copy.wait()
        extra = [lambda i: arriving[i].wait()] if late else []
        if early:
            leaving = [
                [
                    pltpu.make_async_copy(vmem[n_in + i].at[at], hbm[n_in + i].at[at], out_sems.at[i * blocks + at])
                    for at in range(blocks)
                ]
                for i in range(n_out)
            ]
            kernel(*extra, lambda i, at: leaving[i][at].start(), *vmem, *rest)
            leaving = sum(leaving, [])
        else:
            leaving = [pltpu.make_async_copy(vmem[n_in + i], hbm[n_in + i], out_sems.at[i]) for i in range(n_out)]
            kernel(*extra, *vmem, *rest)
            for copy in leaving:
                copy.start()
        for copy in leaving:
            copy.wait()

    hbm_spec = pl.BlockSpec(memory_space=pltpu.HBM)
    any_spec = pl.BlockSpec(memory_space=pl.ANY)
    placed = [
        x if i in loose else pltpu.with_memory_space_constraint(x, pltpu.HBM) for i, x in enumerate(operands)
    ]
    return pl.pallas_call(
        whole,
        out_shape=[pltpu.HBM(o.shape, o.dtype) for o in outs],
        in_specs=[any_spec if i in loose else hbm_spec for i in range(n_in)],
        out_specs=[hbm_spec] * n_out,
        scratch_shapes=[
            *[pltpu.VMEM(x.shape, x.dtype) for x in (*operands, *outs)],
            pltpu.SemaphoreType.DMA((n_in,)),
            pltpu.SemaphoreType.DMA((n_out * blocks,)),
            *scratch,
        ],
        compiler_params=pltpu.CompilerParams(vmem_limit_bytes=VMEM_BYTES),
        cost_estimate=pl.CostEstimate(flops=flops, bytes_accessed=moved, transcendentals=0),
        name=name,
    )(*placed)


def shape(dims, dtype):
    return jax.ShapeDtypeStruct(dims, dtype)


def pieces_of(block, group):
    out = [block]
    for k in range(1, group):
        out.append(lax.ppermute(block, GROUP, [((g + k) % group, g) for g in range(group)]))
    return out


def body(loads, stiffness, local_inverse, coarse_basis, coarse_inverse, coarse_index, left_rows, right_rows):
    z = Sizes(loads, stiffness, coarse_basis, coarse_inverse, left_rows)
    n, group, subs, rows, lanes, modes, face = z.n, z.group, z.subs, z.rows, z.lanes, z.modes, z.face
    basis_pieces = pieces_of(jnp.swapaxes(coarse_basis, 1, 2), group)
    inverse_columns = pieces_of(coarse_inverse, group)
    basis_pieces, inverse_columns, local_inverse, stiffness = lax.optimization_barrier(
        (basis_pieces, inverse_columns, local_inverse, stiffness)
    )
    column = np.arange(z.columns)
    repeat = jnp.asarray(np.arange(lanes)[:, None] == column[None, :] % modes, BF16)
    own_row = jnp.asarray(np.arange(n)[:, None] == column[None, :] // modes, F32)
    place = jnp.asarray(
        (column // modes * z.owned + column % modes)[None, :] + np.arange(subs)[:, None] * modes, jnp.int32
    )
    packed_f = shape((rows, lanes), F32)
    packed_b = shape((rows, lanes), BF16)
    copies = shape((n, modes, lanes), BF16)
    tall = shape((subs, rows, lanes), BF16)
    spread = functools.partial(lax.all_to_all, axis_name="sub", split_axis=0, concat_axis=0)
    first_pairs = [(i, i + 1 if i % 2 == 0 else i - 1) for i in range(n)]
    second_pairs = [(i, (i + (1 if i % 2 else -1)) % n) for i in range(n)]
    work = 4 * subs * rows * rows * lanes

    (message,) = call(
        functools.partial(open_kernel, z),
        [shape((n, modes + DIGIT_ROWS, lanes), BF16)],
        [*basis_pieces, loads, coarse_index],
        4 * rows * lanes * lanes,
        [pltpu.VMEM((DIGIT_ROWS, lanes), F32), pltpu.VMEM((subs, modes, rows), BF16)],
        loose=range(1, group),
        name="open",
    )
    inverse_pieces = pieces_of(local_inverse, group)
    stiffness_pieces = pieces_of(stiffness, group)
    restricted = spread(message)
    arrivals = [*range(1, group), *range(group + 1, 2 * group)]
    faces = shape((subs, face, lanes), BF16)
    outer = shape((face, lanes), BF16)
    (
        load_rows, solved, image, before, after, first_pair, second_pair, tall, basis_t
    ) = call(
        functools.partial(first_image_kernel, z),
        [
            packed_b, packed_f, packed_f, faces, faces, outer, outer, tall, shape((subs, modes, rows), BF16),
        ],
        [*inverse_pieces, *stiffness_pieces, *basis_pieces, loads, left_rows, right_rows],
        work,
        [
            pltpu.VMEM((rows, lanes), BF16),
            pltpu.VMEM((subs, rows, 2 * lanes), BF16), pltpu.VMEM((subs, rows, 2 * lanes), BF16),
        ],
        late=range(2 * group),
        loose=[*arrivals, *range(2 * group + 1, 3 * group)],
        name="first_image",
    )
    second_got = lax.ppermute(second_pair, "sub", second_pairs)
    restricted, second_pair = lax.optimization_barrier((restricted, second_pair))
    near = (subs + 2) * modes
    ordered_inverse, index, message = call(
        functools.partial(order_kernel, z),
        [shape((subs, z.owned, z.columns), BF16), shape((subs, n, lanes), F32), copies],
        [*inverse_columns, restricted, repeat, own_row],
        2 * z.owned * z.total * z.total,
        loose=range(1, group + 1),
        name="order",
    )
    coarse = spread(message)
    first_got = lax.ppermute(first_pair, "sub", first_pairs)
    side = shape((subs, modes, face), BF16)
    left_t, right_t, inner, start_modes, picks = call(
        functools.partial(begin_kernel, z),
        [
            side, side, shape((subs, modes, modes), BF16), shape((modes, lanes), F32),
            shape((subs, near, z.columns), BF16),
        ],
        [load_rows, image, tall, basis_t, left_rows, right_rows, index, place],
        work // 16,
        name="begin",
    )
    chosen, message = call(
        functools.partial(update_kernel, z),
        [shape((near, lanes), BF16), copies],
        [coarse, picks, start_modes, inner, left_t, right_t, before, after, first_got, second_got],
        work // 64,
        loose=[0, 8, 9],
        name="update",
    )
    restricted = spread(message)

    bases = [before, after, first_got, second_got]
    half_face = shape((face // 2, lanes), BF16)
    first_pair, second_pair, *values = call(
        functools.partial(second_image_kernel, z),
        [half_face, half_face, *[shape((2, z.own, lanes), F32)] * group],
        [
            *inverse_pieces, *stiffness_pieces, load_rows, image, tall, solved, chosen,
            *bases, left_rows, right_rows,
        ],
        work,
        [
            pltpu.VMEM((rows, lanes), F32), pltpu.VMEM((rows, lanes), BF16), pltpu.VMEM((rows, lanes), BF16),
            pltpu.VMEM((subs, face, lanes), BF16), pltpu.VMEM((subs, face, lanes), BF16),
        ],
        late=range(2 * group),
        loose=[*arrivals, 2 * group + 7, 2 * group + 8],
        name="second_image",
    )
    second_got = lax.ppermute(second_pair, "sub", second_pairs)
    restricted, second_pair = lax.optimization_barrier((restricted, second_pair))
    (message,) = call(
        functools.partial(coarse_kernel, z),
        [copies],
        [restricted, ordered_inverse],
        work // 64,
        loose=[0],
        name="coarse",
    )
    coarse = spread(message)
    first_got = lax.ppermute(first_pair, "sub", first_pairs)
    swapped = [values[0]]
    for k in range(1, group):
        swapped.append(lax.ppermute(values[k], GROUP, [(g, (g + k) % group) for g in range(group)]))
    swapped = [swapped[(group - k) % group] for k in range(group)]
    (base,) = call(
        functools.partial(base_kernel, z),
        [shape((2, subs, z.own, lanes), F32)],
        swapped,
        work // 64,
        loose=range(1, group),
        name="base",
    )
    coarse, base, first_got, second_got = lax.optimization_barrier((coarse, base, first_got, second_got))
    out = shape((subs, z.own, z.cases), F32)
    return tuple(
        call(
            functools.partial(last_kernel, z),
            [out, out],
            [
                *pieces_of(coarse, group), *pieces_of(first_got, group), *pieces_of(second_got, group),
                picks, *bases, left_rows, right_rows, tall, base,
            ],
            work // 8,
            late=[3 * group + 7, 3 * group + 8],
            loose=[*range(3 * group), 3 * group + 3, 3 * group + 4],
            early=True,
            name="last",
        )
    )


def solution(mesh):
    return jax.shard_map(
        body,
        mesh=mesh,
        in_specs=(
            P("sub", None, None),
            P("sub", GROUP, None),
            P("sub", GROUP, None),
            P("sub", GROUP, None),
            P("sub", GROUP),
            P("sub", None),
            P("sub", None),
            P("sub", None),
        ),
        out_specs=(P("sub", GROUP, None), P("sub", GROUP, None)),
        check_vma=False,
    )
```

```python
import functools

import jax
import jax.numpy as jnp
import numpy as np
from jax import lax
from jax.experimental import pallas as pl
from jax.experimental.pallas import tpu as pltpu
from jax.sharding import PartitionSpec as P

GROUP = ("crow", "ccol")
F32 = jnp.float32
BF16 = jnp.bfloat16
VMEM_BYTES = 48 * 1024 * 1024
DIGIT_ROWS = 16
DIGIT_BITS = 8
DIGIT = 1 << DIGIT_BITS


def dot(a, b):
    return lax.dot_general(a, b, (((1,), (0,)), ((), ())), preferred_element_type=F32)


def dot_tn(a, b):
    return lax.dot_general(a, b, (((0,), (0,)), ((), ())), preferred_element_type=F32)


def dot_nt(a, b):
    return lax.dot_general(a, b, (((1,), (1,)), ((), ())), preferred_element_type=F32)


class Sizes:
    def __init__(self, loads, stiffness, coarse_basis, coarse_inverse, left_rows):
        self.n = lax.axis_size("sub")
        self.group = lax.axis_size(GROUP)
        self.subs, self.rows, self.cases = loads.shape
        self.own = stiffness.shape[1]
        self.modes = coarse_basis.shape[2]
        self.owned, self.block = coarse_inverse.shape
        self.total = self.block * self.group
        self.face = left_rows.shape[1]
        self.width = self.cases // self.group
        self.lanes = max(self.cases, -(-self.subs * self.width // 128) * 128)
        self.columns = self.n * self.modes


def lane_mask(z, block, shape):
    lane = lax.broadcasted_iota(jnp.int32, shape, len(shape) - 1)
    return (lane >= block * z.width) & (lane < (block + 1) * z.width)


def select(z, parts):
    out = jnp.zeros_like(parts[0])
    for s, part in enumerate(parts):
        out = jnp.where(lane_mask(z, s, part.shape), part, out)
    return out


def fold(z, packed):
    if z.lanes == z.subs * z.width:
        out = packed
        for k in range(1, z.subs):
            out = out + pltpu.roll(packed, k * z.width, 1)
        return out
    out = packed
    for k in range(1, z.subs):
        out = out + pltpu.roll(packed, k * z.width, 1)
        out = out + pltpu.roll(packed, z.lanes - k * z.width, 1)
    return out


def lane_matrix(z, source, target, width=None):
    row = lax.broadcasted_iota(jnp.int32, (z.lanes, z.lanes), 0)
    lane = lax.broadcasted_iota(jnp.int32, (z.lanes, z.lanes), 1)
    hit = (row - source == lane - target) & (lane >= target) & (lane < target + (width or z.width))
    return jnp.where(hit, 1.0, 0.0).astype(BF16)


def piece_start(z, k, size):
    place = lax.rem(lax.axis_index(GROUP) + k, z.group)
    return pl.multiple_of(place * size, size)


def pick_matrix(z, rows_of):
    column = jnp.transpose(jnp.broadcast_to(rows_of.astype(F32), (z.face, z.face)))[:, 0:1].astype(jnp.int32)
    row = lax.broadcasted_iota(jnp.int32, (z.face, z.rows), 1)
    return jnp.where(row == column, 1.0, 0.0).astype(BF16)


def even():
    return lax.rem(lax.axis_index("sub"), 2) == 0


def case_matrix(z, s):
    row = lax.broadcasted_iota(jnp.int32, (z.cases, z.lanes), 0)
    lane = lax.broadcasted_iota(jnp.int32, (z.cases, z.lanes), 1)
    hit = (row - lax.axis_index(GROUP) * z.width == lane - s * z.width) & lane_mask(z, s, row.shape)
    return jnp.where(hit, 1.0, 0.0).astype(BF16)


def join_basis(z, pieces, basis_t):
    for k, piece in enumerate(pieces):
        basis_t[:, :, pl.ds(piece_start(z, k, z.own), z.own)] = piece[...]


def open_kernel(z, *refs):
    pieces = refs[: z.group]
    loads, index, message, digits, basis_t = refs[z.group :]
    join_basis(z, pieces, basis_t)
    total = jnp.zeros((z.modes, z.lanes), F32)
    for s in range(z.subs):
        total = total + dot(dot(basis_t[s], loads[s]).astype(BF16), case_matrix(z, s))
    modes = total.astype(BF16)
    digits[...] = jnp.zeros(digits.shape, F32)
    for s in range(z.subs):
        places = index[s : s + 1, :]
        digits[2 * s : 2 * s + 1, : z.modes] = (places >> DIGIT_BITS).astype(F32)
        digits[2 * s + 1 : 2 * s + 2, : z.modes] = (places & (DIGIT - 1)).astype(F32)
    for k in range(z.n):
        message[k, : z.modes, :] = modes
        message[k, z.modes :, :] = digits[...].astype(BF16)


def multiply(z, pieces, vector, store, wait):
    for k in range(z.group):
        wait(k)
    for k, piece in enumerate(pieces):
        parts = [dot(piece[s], vector) for s in range(z.subs)]
        store(k, piece_start(z, k, z.own), select(z, parts))


def pick_both(z, left_rows, right_rows, s):
    return jnp.concatenate(
        [pick_matrix(z, left_rows[s : s + 1, :]), pick_matrix(z, right_rows[s : s + 1, :])], axis=0
    )


def halves(z, face):
    part = z.face // 2
    return (face[:part].astype(F32) + dot(face[part:], lane_matrix(z, 0, z.lanes // 2))).astype(BF16)


def store_faces(z, before, after, first_pair, second_pair):
    first, last = before[0], after[z.subs - 1]
    first_pair[...] = jnp.where(even(), last, first)
    second_pair[...] = jnp.where(even(), first, last)


def sides(z, before, after, first_pair, second_pair, s):
    if s == 0:
        from_before = jnp.where(even(), second_pair[...], first_pair[...])
    else:
        from_before = after[s - 1]
    if s == z.subs - 1:
        from_after = jnp.where(even(), first_pair[...], second_pair[...])
    else:
        from_after = before[s + 1]
    return from_before, from_after


def shares(z, s, chosen, faces, bases=None):
    m, half = z.modes, z.lanes // 2
    moved = lane_matrix(z, 0, s * z.width)
    out = []
    for side, at in ((0, s), (1, s + 2)):
        own = chosen[at * m : (at + 1) * m]
        below = jnp.concatenate([own, jnp.zeros((half - m, z.lanes), BF16)], axis=0)
        if bases is None:
            total = dot(faces[side], jnp.concatenate([moved[:half], below], axis=0))
        else:
            above = jnp.zeros((half, z.lanes), BF16)
            total = dot(faces[side], moved) + dot(bases[side], jnp.concatenate([above, below], axis=0))
        out.append(total)
    return out


def correction_side(z, chosen, s, share):
    m, half = z.modes, z.lanes // 2
    own = chosen[(s + 1) * m : (s + 2) * m]
    none = jnp.zeros((half - m, z.lanes), BF16)
    nil = jnp.zeros((half, z.lanes), BF16)
    image = jnp.concatenate([own, none, nil, share], axis=0)
    step = jnp.concatenate([nil, own, none, jnp.zeros((z.face, z.lanes), BF16)], axis=0)
    return jnp.concatenate([image, step], axis=1)


def scatter_matrix(z, rows_of, start, count):
    row = lax.broadcasted_iota(jnp.int32, (count, z.face), 0) + start
    return jnp.where(row == rows_of, 1.0, 0.0).astype(BF16)


def first_image_kernel(z, wait, *refs):
    inverse, stiffness = refs[: z.group], refs[z.group : 2 * z.group]
    pieces = refs[2 * z.group : 3 * z.group]
    loads, left_rows, right_rows = refs[3 * z.group : 3 * z.group + 3]
    load_rows, solved, image, before, after, first_pair, second_pair = refs[3 * z.group + 3 : 3 * z.group + 10]
    tall, basis_t, rounded, both, images = refs[3 * z.group + 10 :]
    join_basis(z, pieces, basis_t)
    packed = dot(loads[0], case_matrix(z, 0))
    for s in range(1, z.subs):
        packed = packed + dot(loads[s], case_matrix(z, s))
    load_rows[...] = packed.astype(BF16)

    def store_solved(k, start, value):
        solved[pl.ds(start, z.own), :] = value
        rounded[pl.ds(start, z.own), :] = value.astype(BF16)

    multiply(z, inverse, load_rows[...], store_solved, wait)
    solved_b = rounded[...]
    half = z.lanes // 2
    for s in range(z.subs):
        basis = jnp.transpose(basis_t[s].astype(F32)).astype(BF16)
        tall[s, :, half : half + z.modes] = basis
        tall[s, :, half + z.modes :] = jnp.zeros((z.rows, half - z.modes), BF16)
        both[s, :, : z.lanes] = solved_b
        both[s, :, z.lanes : z.lanes + z.modes] = basis
        both[s, :, z.lanes + z.modes :] = jnp.zeros((z.rows, z.lanes - z.modes), BF16)
    for k, piece in enumerate(stiffness):
        wait(z.group + k)
        start = piece_start(z, k, z.own)
        parts = [dot(piece[s], both[s]) for s in range(z.subs)]
        image[pl.ds(start, z.own), :] = select(z, [part[:, : z.lanes] for part in parts])
        for s in range(z.subs):
            images[s, pl.ds(start, z.own), :] = parts[s].astype(BF16)
    for s in range(z.subs):
        tall[s, :, :half] = images[s, :, z.lanes : z.lanes + half]
        picked = dot(pick_both(z, left_rows, right_rows, s), images[s]).astype(BF16)
        faces = dot(picked[:, : z.lanes], lane_matrix(z, s * z.width, 0))
        faces = (faces + dot(picked[:, z.lanes :], lane_matrix(z, 0, half, z.modes))).astype(BF16)
        before[s] = faces[: z.face]
        after[s] = faces[z.face :]
    store_faces(z, before, after, first_pair, second_pair)


def begin_kernel(z, *refs):
    load_rows, image, tall, basis_t, left_rows, right_rows, index, place = refs[:8]
    left_t, right_t, inner, start_modes, picks = refs[8:]
    left = (load_rows[...].astype(F32) - image[...]).astype(BF16)
    begun = []
    for s in range(z.subs):
        restricted = dot(basis_t[s], jnp.concatenate([left, tall[s]], axis=1))
        begun.append(restricted[:, : z.lanes])
        inner[s] = restricted[:, z.lanes : z.lanes + z.modes].astype(BF16)
        sides_t = dot_nt(basis_t[s], pick_both(z, left_rows, right_rows, s)).astype(BF16)
        left_t[s] = sides_t[:, : z.face]
        right_t[s] = sides_t[:, z.face :]
    start_modes[...] = select(z, begun)
    here = lax.axis_index("sub")
    device = lax.broadcasted_iota(jnp.int32, (z.n, z.lanes), 0)
    for t in range(z.subs + 2):
        if t == 0:
            s, owner = z.subs - 1, lax.rem(here + z.n - 1, z.n)
        elif t == z.subs + 1:
            s, owner = 0, lax.rem(here + 1, z.n)
        else:
            s, owner = t - 1, here
        row = jnp.sum(jnp.where(device == owner, index[s], 0.0), axis=0, keepdims=True)
        column = jnp.transpose(jnp.broadcast_to(row, (z.lanes, z.lanes)))[: z.modes, 0:1].astype(jnp.int32)
        for h in range(z.subs):
            hit = column == place[h : h + 1, :]
            picks[h, t * z.modes : (t + 1) * z.modes, :] = jnp.where(hit, 1.0, 0.0).astype(BF16)


def second_image_kernel(z, wait, *refs):
    inverse, stiffness = refs[: z.group], refs[z.group : 2 * z.group]
    rest = refs[2 * z.group :]
    load_rows, old_image, tall, old_solved, chosen = rest[:5]
    before, after, first_got, second_got, left_rows, right_rows = rest[5:11]
    first_pair, second_pair = rest[11:13]
    values = rest[13 : 13 + z.group]
    base, rounded, image, new_before, new_after = rest[13 + z.group :]
    steps, images = [], []
    for s in range(z.subs):
        faces = sides(z, before, after, first_got, second_got, s)
        both = [share.astype(BF16) for share in shares(z, s, chosen, faces)]
        left = jnp.concatenate([tall[s], scatter_matrix(z, left_rows[s : s + 1, :], 0, z.rows)], axis=1)
        total = dot(left, correction_side(z, chosen, s, both[0]))
        steps.append(total[:, z.lanes :])
        images.append(total[:, : z.lanes] + dot(scatter_matrix(z, right_rows[s : s + 1, :], 0, z.rows), both[1]))
    residual = (load_rows[...].astype(F32) - old_image[...] - select(z, images)).astype(BF16)
    base[...] = old_solved[...] + select(z, steps)

    def store_solved(k, start, value):
        value = value + base[pl.ds(start, z.own), :]
        values[k][0] = value
        rounded[pl.ds(start, z.own), :] = value.astype(BF16)

    multiply(z, inverse, residual, store_solved, wait)

    def store_image(k, start, value):
        place = pl.ds(start, z.own)
        values[k][1] = load_rows[place, :].astype(F32) - value
        image[place, :] = value.astype(BF16)

    multiply(z, stiffness, rounded[...], store_image, lambda k: wait(z.group + k))
    pick = jnp.concatenate([pick_both(z, left_rows, right_rows, s) for s in range(z.subs)], axis=0)
    picked = dot(pick, image[...]).astype(BF16)
    for s in range(z.subs):
        own = picked[2 * s * z.face : 2 * (s + 1) * z.face]
        faces = dot(own, lane_matrix(z, s * z.width, 0)).astype(BF16)
        new_before[s] = faces[: z.face]
        new_after[s] = faces[z.face :]
    first = halves(z, new_before[0])
    last = halves(z, new_after[z.subs - 1])
    first_pair[...] = jnp.where(even(), last, first)
    second_pair[...] = jnp.where(even(), first, last)
    inner = []
    for s in range(z.subs):
        move = lane_matrix(z, 0, s * z.width)
        total = jnp.zeros((z.rows, z.lanes), F32)
        if s > 0:
            share = dot(new_after[s - 1], move).astype(BF16)
            total = total + dot(scatter_matrix(z, left_rows[s : s + 1, :], 0, z.rows), share)
        if s < z.subs - 1:
            share = dot(new_before[s + 1], move).astype(BF16)
            total = total + dot(scatter_matrix(z, right_rows[s : s + 1, :], 0, z.rows), share)
        inner.append(total)
    base[...] = select(z, inner)
    for k in range(z.group):
        values[k][1] = values[k][1] - base[pl.ds(piece_start(z, k, z.own), z.own), :]


def digit_row(shape, row):
    return lax.broadcasted_iota(jnp.int32, shape, 1) == row


def coarse_rows(z, ordered_inverse, arrived, message):
    flat = arrived[:, : z.modes, :].reshape(z.columns, z.lanes)
    rows = fold(z, select(z, [dot(ordered_inverse[s], flat) for s in range(z.subs)]))
    packed = select(z, [rows[s * z.modes : (s + 1) * z.modes, :] for s in range(z.subs)]).astype(BF16)
    for k in range(z.n):
        message[k] = packed


def order_kernel(z, *refs):
    blocks = refs[: z.group]
    arrived, repeat, own_row, ordered_inverse, index, message = refs[z.group :]
    digits = arrived[:, z.modes :, :].astype(F32)
    for s in range(z.subs):
        high = jnp.sum(jnp.where(digit_row(digits.shape, 2 * s), digits, 0.0), axis=1)
        low = jnp.sum(jnp.where(digit_row(digits.shape, 2 * s + 1), digits, 0.0), axis=1)
        index[s] = high * DIGIT + low
        spread = dot(high.astype(BF16), repeat[...]) * DIGIT + dot(low.astype(BF16), repeat[...])
        places = jnp.sum(spread * own_row[...], axis=0, keepdims=True).astype(jnp.int32)
        for at in range(0, z.columns, 768):
            wide = min(768, z.columns - at)
            total = jnp.zeros((z.owned, wide), F32)
            for k, block in enumerate(blocks):
                inside = (places[:, at : at + wide] - piece_start(z, k, z.block)).astype(jnp.int16)
                for first in range(0, z.block, 768):
                    deep = min(768, z.block - first)
                    row = lax.broadcasted_iota(jnp.int16, (deep, wide), 0) + jnp.int16(first)
                    hot = jnp.where(row == inside, jnp.ones((), BF16), jnp.zeros((), BF16))
                    total = total + dot(block[:, first : first + deep], hot)
            ordered_inverse[s, :, at : at + wide] = total.astype(BF16)
    coarse_rows(z, ordered_inverse, arrived, message)


def coarse_kernel(z, arrived, ordered_inverse, message):
    coarse_rows(z, ordered_inverse, arrived, message)


def picked_rows(z, arrived, picks):
    flat = arrived[...].reshape(z.columns, z.lanes)
    return fold(z, select(z, [dot(picks[h], flat) for h in range(z.subs)])).astype(BF16)


def update_kernel(z, *refs):
    arrived, picks, start_modes, inner, left_t, right_t, before, after, first_got, second_got = refs[:10]
    chosen, message = refs[10:]
    rows = picked_rows(z, arrived, picks)
    chosen[...] = rows
    m = z.modes
    parts = []
    for s in range(z.subs):
        faces = sides(z, before, after, first_got, second_got, s)
        both = shares(z, s, rows, faces)
        total = dot(inner[s], rows[(s + 1) * m : (s + 2) * m])
        parts.append(total + dot(left_t[s], both[0].astype(BF16)) + dot(right_t[s], both[1].astype(BF16)))
    modes = (start_modes[...] - select(z, parts)).astype(BF16)
    for k in range(z.n):
        message[k] = modes


def base_kernel(z, *refs):
    *values, out = refs
    for at in range(2):
        for s in range(z.subs):
            total = jnp.zeros((z.own, z.lanes), F32)
            for k, value in enumerate(values):
                place = lax.rem(lax.axis_index(GROUP) + k, z.group)
                turn = lax.rem((place - s + z.subs * z.group) * z.width, z.lanes)
                turned = pltpu.roll(value[at], turn, 1)
                total = jnp.where(lane_mask(z, place, turned.shape), turned, total)
            out[at, s] = total


def last_kernel(z, wait, *refs):
    arrived, firsts, seconds = refs[: z.group], refs[z.group : 2 * z.group], refs[2 * z.group : 3 * z.group]
    picks, face_before, face_after, face_first, face_second, left_rows, right_rows = refs[3 * z.group : 3 * z.group + 7]
    tall, base, second_pass, final_residual = refs[3 * z.group + 7 :]
    start = piece_start(z, 0, z.own)
    m, half = z.modes, z.lanes // 2
    places = [lax.rem(lax.axis_index(GROUP) + k, z.group) * z.width for k in range(z.group)]

    def all_cases(parts, source=0):
        return sum(dot(part, lane_matrix(z, source, place)) for part, place in zip(parts, places))

    def whole_face(parts):
        return jnp.concatenate([all_cases(parts), all_cases(parts, half)], axis=0)

    modes = all_cases([picked_rows(z, piece, picks) for piece in arrived]).astype(BF16)
    swaps = list(zip(firsts, seconds))
    outer_before = whole_face([jnp.where(even(), b[...], a[...]) for a, b in swaps])
    outer_after = whole_face([jnp.where(even(), a[...], b[...]) for a, b in swaps])
    wait(3 * z.group + 7)
    totals = []
    for s in range(z.subs):
        faces = sides(z, face_before, face_after, face_first, face_second, s)
        both = []
        for side, at in ((0, s), (1, s + 2)):
            above = jnp.zeros((half, z.lanes), BF16)
            below = jnp.zeros((half - m, z.lanes), BF16)
            both.append(dot(faces[side], jnp.concatenate([above, modes[at * m : (at + 1) * m], below], axis=0)))
        if s == 0:
            both[0] = both[0] + outer_before
        if s == z.subs - 1:
            both[1] = both[1] + outer_after
        scatter = scatter_matrix(z, left_rows[s : s + 1, :], start, z.own)
        wide = jnp.concatenate([tall[s, pl.ds(start, z.own), :], scatter], axis=1)
        total = dot(wide, correction_side(z, modes, s, both[0].astype(BF16)))
        image = dot(scatter_matrix(z, right_rows[s : s + 1, :], start, z.own), both[1].astype(BF16))
        totals.append((total[:, z.lanes :], total[:, : z.lanes] + image))
    wait(3 * z.group + 8)
    for s, (step, image) in enumerate(totals):
        second_pass[s] = (base[0, s] + step)[:, : z.cases]
        final_residual[s] = (base[1, s] - image)[:, : z.cases]


def call(kernel, outs, operands, flops, scratch=(), late=(), loose=(), name=None):
    moved = sum(int(np.prod(x.shape)) * x.dtype.itemsize for x in (*operands, *outs))
    n_in, n_out = len(operands), len(outs)

    def whole(*refs):
        hbm, refs = refs[: n_in + n_out], refs[n_in + n_out :]
        vmem, refs = refs[: n_in + n_out], refs[n_in + n_out :]
        in_sems, out_sems, *rest = refs
        arriving = [pltpu.make_async_copy(hbm[i], vmem[i], in_sems.at[i]) for i in range(n_in)]
        for i in sorted(range(n_in), key=lambda i: i in late):
            arriving[i].start()
        for i, copy in enumerate(arriving):
            if i not in late:
                copy.wait()
        extra = [lambda i: arriving[i].wait()] if late else []
        kernel(*extra, *vmem, *rest)
        leaving = [pltpu.make_async_copy(vmem[n_in + i], hbm[n_in + i], out_sems.at[i]) for i in range(n_out)]
        for copy in leaving:
            copy.start()
        for copy in leaving:
            copy.wait()

    hbm_spec = pl.BlockSpec(memory_space=pltpu.HBM)
    any_spec = pl.BlockSpec(memory_space=pl.ANY)
    placed = [
        x if i in loose else pltpu.with_memory_space_constraint(x, pltpu.HBM) for i, x in enumerate(operands)
    ]
    return pl.pallas_call(
        whole,
        out_shape=[pltpu.HBM(o.shape, o.dtype) for o in outs],
        in_specs=[any_spec if i in loose else hbm_spec for i in range(n_in)],
        out_specs=[hbm_spec] * n_out,
        scratch_shapes=[
            *[pltpu.VMEM(x.shape, x.dtype) for x in (*operands, *outs)],
            pltpu.SemaphoreType.DMA((n_in,)),
            pltpu.SemaphoreType.DMA((n_out,)),
            *scratch,
        ],
        compiler_params=pltpu.CompilerParams(vmem_limit_bytes=VMEM_BYTES),
        cost_estimate=pl.CostEstimate(flops=flops, bytes_accessed=moved, transcendentals=0),
        name=name,
    )(*placed)


def shape(dims, dtype):
    return jax.ShapeDtypeStruct(dims, dtype)


def pieces_of(block, group):
    out = [block]
    for k in range(1, group):
        out.append(lax.ppermute(block, GROUP, [((g + k) % group, g) for g in range(group)]))
    return out


def body(loads, stiffness, local_inverse, coarse_basis, coarse_inverse, coarse_index, left_rows, right_rows):
    z = Sizes(loads, stiffness, coarse_basis, coarse_inverse, left_rows)
    n, group, subs, rows, lanes, modes, face = z.n, z.group, z.subs, z.rows, z.lanes, z.modes, z.face
    basis_pieces = pieces_of(jnp.swapaxes(coarse_basis, 1, 2), group)
    basis_pieces, coarse_inverse, local_inverse, stiffness = lax.optimization_barrier(
        (basis_pieces, coarse_inverse, local_inverse, stiffness)
    )
    inverse_columns = pieces_of(coarse_inverse, group)
    column = np.arange(z.columns)
    repeat = jnp.asarray(np.arange(lanes)[:, None] == column[None, :] % modes, BF16)
    own_row = jnp.asarray(np.arange(n)[:, None] == column[None, :] // modes, F32)
    place = jnp.asarray(
        (column // modes * z.owned + column % modes)[None, :] + np.arange(subs)[:, None] * modes, jnp.int32
    )
    packed_f = shape((rows, lanes), F32)
    packed_b = shape((rows, lanes), BF16)
    copies = shape((n, modes, lanes), BF16)
    tall = shape((subs, rows, lanes), BF16)
    spread = functools.partial(lax.all_to_all, axis_name="sub", split_axis=0, concat_axis=0)
    first_pairs = [(i, i + 1 if i % 2 == 0 else i - 1) for i in range(n)]
    second_pairs = [(i, (i + (1 if i % 2 else -1)) % n) for i in range(n)]
    work = 4 * subs * rows * rows * lanes

    (message,) = call(
        functools.partial(open_kernel, z),
        [shape((n, modes + DIGIT_ROWS, lanes), BF16)],
        [*basis_pieces, loads, coarse_index],
        4 * rows * lanes * lanes,
        [pltpu.VMEM((DIGIT_ROWS, lanes), F32), pltpu.VMEM((subs, modes, rows), BF16)],
        loose=range(1, group),
        name="open",
    )
    inverse_pieces = pieces_of(local_inverse, group)
    stiffness_pieces = pieces_of(stiffness, group)
    restricted = spread(message)
    arrivals = [*range(1, group), *range(group + 1, 2 * group)]
    faces = shape((subs, face, lanes), BF16)
    outer = shape((face, lanes), BF16)
    (
        load_rows, solved, image, before, after, first_pair, second_pair, tall, basis_t
    ) = call(
        functools.partial(first_image_kernel, z),
        [
            packed_b, packed_f, packed_f, faces, faces, outer, outer, tall, shape((subs, modes, rows), BF16),
        ],
        [*inverse_pieces, *stiffness_pieces, *basis_pieces, loads, left_rows, right_rows],
        work,
        [
            pltpu.VMEM((rows, lanes), BF16),
            pltpu.VMEM((subs, rows, 2 * lanes), BF16), pltpu.VMEM((subs, rows, 2 * lanes), BF16),
        ],
        late=range(2 * group),
        loose=[*arrivals, *range(2 * group + 1, 3 * group)],
        name="first_image",
    )
    first_got = lax.ppermute(first_pair, "sub", first_pairs)
    restricted, first_pair = lax.optimization_barrier((restricted, first_pair))
    near = (subs + 2) * modes
    ordered_inverse, index, message = call(
        functools.partial(order_kernel, z),
        [shape((subs, z.owned, z.columns), BF16), shape((subs, n, lanes), F32), copies],
        [*inverse_columns, restricted, repeat, own_row],
        2 * z.owned * z.total * z.total,
        loose=range(1, group + 1),
        name="order",
    )
    coarse = spread(message)
    second_got = lax.ppermute(second_pair, "sub", second_pairs)
    side = shape((subs, modes, face), BF16)
    left_t, right_t, inner, start_modes, picks = call(
        functools.partial(begin_kernel, z),
        [
            side, side, shape((subs, modes, modes), BF16), shape((modes, lanes), F32),
            shape((subs, near, z.columns), BF16),
        ],
        [load_rows, image, tall, basis_t, left_rows, right_rows, index, place],
        work // 16,
        name="begin",
    )
    chosen, message = call(
        functools.partial(update_kernel, z),
        [shape((near, lanes), BF16), copies],
        [coarse, picks, start_modes, inner, left_t, right_t, before, after, first_got, second_got],
        work // 64,
        loose=[0, 8, 9],
        name="update",
    )
    restricted = spread(message)

    bases = [before, after, first_got, second_got]
    half_face = shape((face // 2, lanes), BF16)
    first_pair, second_pair, *values = call(
        functools.partial(second_image_kernel, z),
        [half_face, half_face, *[shape((2, z.own, lanes), F32)] * group],
        [
            *inverse_pieces, *stiffness_pieces, load_rows, image, tall, solved, chosen,
            *bases, left_rows, right_rows,
        ],
        work,
        [
            pltpu.VMEM((rows, lanes), F32), pltpu.VMEM((rows, lanes), BF16), pltpu.VMEM((rows, lanes), BF16),
            pltpu.VMEM((subs, face, lanes), BF16), pltpu.VMEM((subs, face, lanes), BF16),
        ],
        late=range(2 * group),
        loose=[*arrivals, 2 * group + 7, 2 * group + 8],
        name="second_image",
    )
    first_got = lax.ppermute(first_pair, "sub", first_pairs)
    restricted, first_pair = lax.optimization_barrier((restricted, first_pair))
    (message,) = call(
        functools.partial(coarse_kernel, z),
        [copies],
        [restricted, ordered_inverse],
        work // 64,
        loose=[0],
        name="coarse",
    )
    coarse = spread(message)
    second_got = lax.ppermute(second_pair, "sub", second_pairs)
    swapped = [values[0]]
    for k in range(1, group):
        swapped.append(lax.ppermute(values[k], GROUP, [(g, (g + k) % group) for g in range(group)]))
    swapped = [swapped[(group - k) % group] for k in range(group)]
    (base,) = call(
        functools.partial(base_kernel, z),
        [shape((2, subs, z.own, lanes), F32)],
        swapped,
        work // 64,
        loose=range(1, group),
        name="base",
    )
    coarse, base, first_got, second_got = lax.optimization_barrier((coarse, base, first_got, second_got))
    out = shape((subs, z.own, z.cases), F32)
    return tuple(
        call(
            functools.partial(last_kernel, z),
            [out, out],
            [
                *pieces_of(coarse, group), *pieces_of(first_got, group), *pieces_of(second_got, group),
                picks, *bases, left_rows, right_rows, tall, base,
            ],
            work // 8,
            late=[3 * group + 7, 3 * group + 8],
            loose=[*range(3 * group), 3 * group + 3, 3 * group + 4],
            name="last",
        )
    )


def solution(mesh):
    return jax.shard_map(
        body,
        mesh=mesh,
        in_specs=(
            P("sub", None, None),
            P("sub", GROUP, None),
            P("sub", GROUP, None),
            P("sub", GROUP, None),
            P("sub", GROUP),
            P("sub", None),
            P("sub", None),
            P("sub", None),
        ),
        out_specs=(P("sub", GROUP, None), P("sub", GROUP, None)),
        check_vma=False,
    )
```

```python
import functools

import jax
import jax.numpy as jnp
import numpy as np
from jax import lax
from jax.experimental import pallas as pl
from jax.experimental.pallas import tpu as pltpu
from jax.sharding import PartitionSpec as P

GROUP = ("crow", "ccol")
F32 = jnp.float32
BF16 = jnp.bfloat16
VMEM_BYTES = 48 * 1024 * 1024
DIGIT_ROWS = 16
DIGIT_BITS = 8
DIGIT = 1 << DIGIT_BITS


def dot(a, b):
    return lax.dot_general(a, b, (((1,), (0,)), ((), ())), preferred_element_type=F32)


def dot_tn(a, b):
    return lax.dot_general(a, b, (((0,), (0,)), ((), ())), preferred_element_type=F32)


def dot_nt(a, b):
    return lax.dot_general(a, b, (((1,), (1,)), ((), ())), preferred_element_type=F32)


class Sizes:
    def __init__(self, loads, stiffness, coarse_basis, coarse_inverse, left_rows):
        self.n = lax.axis_size("sub")
        self.group = lax.axis_size(GROUP)
        self.subs, self.rows, self.cases = loads.shape
        self.own = stiffness.shape[1]
        self.modes = coarse_basis.shape[2]
        self.owned, self.block = coarse_inverse.shape
        self.total = self.block * self.group
        self.face = left_rows.shape[1]
        self.width = self.cases // self.group
        self.lanes = max(self.cases, -(-self.subs * self.width // 128) * 128)
        self.columns = self.n * self.modes


def lane_mask(z, block, shape):
    lane = lax.broadcasted_iota(jnp.int32, shape, len(shape) - 1)
    return (lane >= block * z.width) & (lane < (block + 1) * z.width)


def select(z, parts):
    out = jnp.zeros_like(parts[0])
    for s, part in enumerate(parts):
        out = jnp.where(lane_mask(z, s, part.shape), part, out)
    return out


def fold(z, packed):
    if z.lanes == z.subs * z.width:
        out = packed
        for k in range(1, z.subs):
            out = out + pltpu.roll(packed, k * z.width, 1)
        return out
    out = packed
    for k in range(1, z.subs):
        out = out + pltpu.roll(packed, k * z.width, 1)
        out = out + pltpu.roll(packed, z.lanes - k * z.width, 1)
    return out


def lane_matrix(z, source, target, width=None):
    row = lax.broadcasted_iota(jnp.int32, (z.lanes, z.lanes), 0)
    lane = lax.broadcasted_iota(jnp.int32, (z.lanes, z.lanes), 1)
    hit = (row - source == lane - target) & (lane >= target) & (lane < target + (width or z.width))
    return jnp.where(hit, 1.0, 0.0).astype(BF16)


def piece_start(z, k, size):
    place = lax.rem(lax.axis_index(GROUP) + k, z.group)
    return pl.multiple_of(place * size, size)


def pick_matrix(z, rows_of):
    column = jnp.transpose(jnp.broadcast_to(rows_of.astype(F32), (z.face, z.face)))[:, 0:1].astype(jnp.int32)
    row = lax.broadcasted_iota(jnp.int32, (z.face, z.rows), 1)
    return jnp.where(row == column, 1.0, 0.0).astype(BF16)


def even():
    return lax.rem(lax.axis_index("sub"), 2) == 0


def case_matrix(z, s):
    row = lax.broadcasted_iota(jnp.int32, (z.cases, z.lanes), 0)
    lane = lax.broadcasted_iota(jnp.int32, (z.cases, z.lanes), 1)
    hit = (row - lax.axis_index(GROUP) * z.width == lane - s * z.width) & lane_mask(z, s, row.shape)
    return jnp.where(hit, 1.0, 0.0).astype(BF16)


def join_basis(z, pieces, basis_t):
    for k, piece in enumerate(pieces):
        basis_t[:, :, pl.ds(piece_start(z, k, z.own), z.own)] = piece[...]


def open_kernel(z, *refs):
    pieces = refs[: z.group]
    loads, index, message, digits, basis_t = refs[z.group :]
    join_basis(z, pieces, basis_t)
    total = jnp.zeros((z.modes, z.lanes), F32)
    for s in range(z.subs):
        total = total + dot(dot(basis_t[s], loads[s]).astype(BF16), case_matrix(z, s))
    modes = total.astype(BF16)
    digits[...] = jnp.zeros(digits.shape, F32)
    for s in range(z.subs):
        places = index[s : s + 1, :]
        digits[2 * s : 2 * s + 1, : z.modes] = (places >> DIGIT_BITS).astype(F32)
        digits[2 * s + 1 : 2 * s + 2, : z.modes] = (places & (DIGIT - 1)).astype(F32)
    for k in range(z.n):
        message[k, : z.modes, :] = modes
        message[k, z.modes :, :] = digits[...].astype(BF16)


def multiply(z, pieces, vector, store, wait):
    for k in range(z.group):
        wait(k)
    for k, piece in enumerate(pieces):
        parts = [dot(piece[s], vector) for s in range(z.subs)]
        store(k, piece_start(z, k, z.own), select(z, parts))


def pick_both(z, left_rows, right_rows, s):
    return jnp.concatenate(
        [pick_matrix(z, left_rows[s : s + 1, :]), pick_matrix(z, right_rows[s : s + 1, :])], axis=0
    )


def halves(z, face):
    part = z.face // 2
    return (face[:part].astype(F32) + dot(face[part:], lane_matrix(z, 0, z.lanes // 2))).astype(BF16)


def store_faces(z, before, after, first_pair, second_pair):
    first, last = before[0], after[z.subs - 1]
    first_pair[...] = jnp.where(even(), last, first)
    second_pair[...] = jnp.where(even(), first, last)


def sides(z, before, after, first_pair, second_pair, s):
    if s == 0:
        from_before = jnp.where(even(), second_pair[...], first_pair[...])
    else:
        from_before = after[s - 1]
    if s == z.subs - 1:
        from_after = jnp.where(even(), first_pair[...], second_pair[...])
    else:
        from_after = before[s + 1]
    return from_before, from_after


def shares(z, s, chosen, faces, bases=None):
    m, half = z.modes, z.lanes // 2
    moved = lane_matrix(z, 0, s * z.width)
    out = []
    for side, at in ((0, s), (1, s + 2)):
        own = chosen[at * m : (at + 1) * m]
        below = jnp.concatenate([own, jnp.zeros((half - m, z.lanes), BF16)], axis=0)
        if bases is None:
            total = dot(faces[side], jnp.concatenate([moved[:half], below], axis=0))
        else:
            above = jnp.zeros((half, z.lanes), BF16)
            total = dot(faces[side], moved) + dot(bases[side], jnp.concatenate([above, below], axis=0))
        out.append(total)
    return out


def correction_side(z, chosen, s, share):
    m, half = z.modes, z.lanes // 2
    own = chosen[(s + 1) * m : (s + 2) * m]
    none = jnp.zeros((half - m, z.lanes), BF16)
    nil = jnp.zeros((half, z.lanes), BF16)
    image = jnp.concatenate([own, none, nil, share], axis=0)
    step = jnp.concatenate([nil, own, none, jnp.zeros((z.face, z.lanes), BF16)], axis=0)
    return jnp.concatenate([image, step], axis=1)


def scatter_matrix(z, rows_of, start, count):
    row = lax.broadcasted_iota(jnp.int32, (count, z.face), 0) + start
    return jnp.where(row == rows_of, 1.0, 0.0).astype(BF16)


def first_image_kernel(z, wait, *refs):
    inverse, stiffness = refs[: z.group], refs[z.group : 2 * z.group]
    pieces = refs[2 * z.group : 3 * z.group]
    loads, left_rows, right_rows = refs[3 * z.group : 3 * z.group + 3]
    load_rows, solved, image, before, after, first_pair, second_pair = refs[3 * z.group + 3 : 3 * z.group + 10]
    tall, basis_t, rounded, both, images = refs[3 * z.group + 10 :]
    join_basis(z, pieces, basis_t)
    packed = dot(loads[0], case_matrix(z, 0))
    for s in range(1, z.subs):
        packed = packed + dot(loads[s], case_matrix(z, s))
    load_rows[...] = packed.astype(BF16)

    def store_solved(k, start, value):
        solved[pl.ds(start, z.own), :] = value
        rounded[pl.ds(start, z.own), :] = value.astype(BF16)

    multiply(z, inverse, load_rows[...], store_solved, wait)
    solved_b = rounded[...]
    half = z.lanes // 2
    for s in range(z.subs):
        basis = jnp.transpose(basis_t[s].astype(F32)).astype(BF16)
        tall[s, :, half : half + z.modes] = basis
        tall[s, :, half + z.modes :] = jnp.zeros((z.rows, half - z.modes), BF16)
        both[s, :, : z.lanes] = solved_b
        both[s, :, z.lanes : z.lanes + z.modes] = basis
        both[s, :, z.lanes + z.modes :] = jnp.zeros((z.rows, z.lanes - z.modes), BF16)
    for k, piece in enumerate(stiffness):
        wait(z.group + k)
        start = piece_start(z, k, z.own)
        parts = [dot(piece[s], both[s]) for s in range(z.subs)]
        image[pl.ds(start, z.own), :] = select(z, [part[:, : z.lanes] for part in parts])
        for s in range(z.subs):
            images[s, pl.ds(start, z.own), :] = parts[s].astype(BF16)
    for s in range(z.subs):
        tall[s, :, :half] = images[s, :, z.lanes : z.lanes + half]
        picked = dot(pick_both(z, left_rows, right_rows, s), images[s]).astype(BF16)
        faces = dot(picked[:, : z.lanes], lane_matrix(z, s * z.width, 0))
        faces = (faces + dot(picked[:, z.lanes :], lane_matrix(z, 0, half, z.modes))).astype(BF16)
        before[s] = faces[: z.face]
        after[s] = faces[z.face :]
    store_faces(z, before, after, first_pair, second_pair)


def begin_kernel(z, *refs):
    load_rows, image, tall, basis_t, left_rows, right_rows, index, place = refs[:8]
    left_t, right_t, inner, start_modes, picks = refs[8:]
    left = (load_rows[...].astype(F32) - image[...]).astype(BF16)
    begun = []
    for s in range(z.subs):
        restricted = dot(basis_t[s], jnp.concatenate([left, tall[s]], axis=1))
        begun.append(restricted[:, : z.lanes])
        inner[s] = restricted[:, z.lanes : z.lanes + z.modes].astype(BF16)
        sides_t = dot_nt(basis_t[s], pick_both(z, left_rows, right_rows, s)).astype(BF16)
        left_t[s] = sides_t[:, : z.face]
        right_t[s] = sides_t[:, z.face :]
    start_modes[...] = select(z, begun)
    here = lax.axis_index("sub")
    device = lax.broadcasted_iota(jnp.int32, (z.n, z.lanes), 0)
    for t in range(z.subs + 2):
        if t == 0:
            s, owner = z.subs - 1, lax.rem(here + z.n - 1, z.n)
        elif t == z.subs + 1:
            s, owner = 0, lax.rem(here + 1, z.n)
        else:
            s, owner = t - 1, here
        row = jnp.sum(jnp.where(device == owner, index[s], 0.0), axis=0, keepdims=True)
        column = jnp.transpose(jnp.broadcast_to(row, (z.lanes, z.lanes)))[: z.modes, 0:1].astype(jnp.int32)
        for h in range(z.subs):
            hit = column == place[h : h + 1, :]
            picks[h, t * z.modes : (t + 1) * z.modes, :] = jnp.where(hit, 1.0, 0.0).astype(BF16)


def second_image_kernel(z, wait, *refs):
    inverse, stiffness = refs[: z.group], refs[z.group : 2 * z.group]
    rest = refs[2 * z.group :]
    load_rows, old_image, tall, old_solved, chosen = rest[:5]
    before, after, first_got, second_got, left_rows, right_rows = rest[5:11]
    first_pair, second_pair = rest[11:13]
    values = rest[13 : 13 + z.group]
    base, rounded, image, new_before, new_after = rest[13 + z.group :]
    steps, images = [], []
    for s in range(z.subs):
        faces = sides(z, before, after, first_got, second_got, s)
        both = [share.astype(BF16) for share in shares(z, s, chosen, faces)]
        left = jnp.concatenate([tall[s], scatter_matrix(z, left_rows[s : s + 1, :], 0, z.rows)], axis=1)
        total = dot(left, correction_side(z, chosen, s, both[0]))
        steps.append(total[:, z.lanes :])
        images.append(total[:, : z.lanes] + dot(scatter_matrix(z, right_rows[s : s + 1, :], 0, z.rows), both[1]))
    residual = (load_rows[...].astype(F32) - old_image[...] - select(z, images)).astype(BF16)
    base[...] = old_solved[...] + select(z, steps)

    def store_solved(k, start, value):
        value = value + base[pl.ds(start, z.own), :]
        values[k][0] = value
        rounded[pl.ds(start, z.own), :] = value.astype(BF16)

    multiply(z, inverse, residual, store_solved, wait)

    def store_image(k, start, value):
        place = pl.ds(start, z.own)
        values[k][1] = load_rows[place, :].astype(F32) - value
        image[place, :] = value.astype(BF16)

    multiply(z, stiffness, rounded[...], store_image, lambda k: wait(z.group + k))
    pick = jnp.concatenate([pick_both(z, left_rows, right_rows, s) for s in range(z.subs)], axis=0)
    picked = dot(pick, image[...]).astype(BF16)
    for s in range(z.subs):
        own = picked[2 * s * z.face : 2 * (s + 1) * z.face]
        faces = dot(own, lane_matrix(z, s * z.width, 0)).astype(BF16)
        new_before[s] = faces[: z.face]
        new_after[s] = faces[z.face :]
    first = halves(z, new_before[0])
    last = halves(z, new_after[z.subs - 1])
    first_pair[...] = jnp.where(even(), last, first)
    second_pair[...] = jnp.where(even(), first, last)
    inner = []
    for s in range(z.subs):
        move = lane_matrix(z, 0, s * z.width)
        total = jnp.zeros((z.rows, z.lanes), F32)
        if s > 0:
            share = dot(new_after[s - 1], move).astype(BF16)
            total = total + dot(scatter_matrix(z, left_rows[s : s + 1, :], 0, z.rows), share)
        if s < z.subs - 1:
            share = dot(new_before[s + 1], move).astype(BF16)
            total = total + dot(scatter_matrix(z, right_rows[s : s + 1, :], 0, z.rows), share)
        inner.append(total)
    base[...] = select(z, inner)
    for k in range(z.group):
        values[k][1] = values[k][1] - base[pl.ds(piece_start(z, k, z.own), z.own), :]


def digit_row(shape, row):
    return lax.broadcasted_iota(jnp.int32, shape, 1) == row


def coarse_rows(z, ordered_inverse, arrived, message):
    flat = arrived[:, : z.modes, :].reshape(z.columns, z.lanes)
    rows = fold(z, select(z, [dot(ordered_inverse[s], flat) for s in range(z.subs)]))
    packed = select(z, [rows[s * z.modes : (s + 1) * z.modes, :] for s in range(z.subs)]).astype(BF16)
    for k in range(z.n):
        message[k] = packed


def order_kernel(z, *refs):
    blocks = refs[: z.group]
    arrived, repeat, own_row, ordered_inverse, index, message = refs[z.group :]
    digits = arrived[:, z.modes :, :].astype(F32)
    for s in range(z.subs):
        high = jnp.sum(jnp.where(digit_row(digits.shape, 2 * s), digits, 0.0), axis=1)
        low = jnp.sum(jnp.where(digit_row(digits.shape, 2 * s + 1), digits, 0.0), axis=1)
        index[s] = high * DIGIT + low
        spread = dot(high.astype(BF16), repeat[...]) * DIGIT + dot(low.astype(BF16), repeat[...])
        places = jnp.sum(spread * own_row[...], axis=0, keepdims=True).astype(jnp.int32)
        for at in range(0, z.columns, 768):
            wide = min(768, z.columns - at)
            total = jnp.zeros((z.owned, wide), F32)
            for k, block in enumerate(blocks):
                inside = (places[:, at : at + wide] - piece_start(z, k, z.block)).astype(jnp.int16)
                for first in range(0, z.block, 768):
                    deep = min(768, z.block - first)
                    row = lax.broadcasted_iota(jnp.int16, (deep, wide), 0) + jnp.int16(first)
                    hot = jnp.where(row == inside, jnp.ones((), BF16), jnp.zeros((), BF16))
                    total = total + dot(block[:, first : first + deep], hot)
            ordered_inverse[s, :, at : at + wide] = total.astype(BF16)
    coarse_rows(z, ordered_inverse, arrived, message)


def coarse_kernel(z, arrived, ordered_inverse, message):
    coarse_rows(z, ordered_inverse, arrived, message)


def picked_rows(z, arrived, picks):
    flat = arrived[...].reshape(z.columns, z.lanes)
    return fold(z, select(z, [dot(picks[h], flat) for h in range(z.subs)])).astype(BF16)


def update_kernel(z, *refs):
    arrived, picks, start_modes, inner, left_t, right_t, before, after, first_got, second_got = refs[:10]
    chosen, message = refs[10:]
    rows = picked_rows(z, arrived, picks)
    chosen[...] = rows
    m = z.modes
    parts = []
    for s in range(z.subs):
        faces = sides(z, before, after, first_got, second_got, s)
        both = shares(z, s, rows, faces)
        total = dot(inner[s], rows[(s + 1) * m : (s + 2) * m])
        parts.append(total + dot(left_t[s], both[0].astype(BF16)) + dot(right_t[s], both[1].astype(BF16)))
    modes = (start_modes[...] - select(z, parts)).astype(BF16)
    for k in range(z.n):
        message[k] = modes


def base_kernel(z, *refs):
    *values, out = refs
    for at in range(2):
        for s in range(z.subs):
            total = jnp.zeros((z.own, z.lanes), F32)
            for k, value in enumerate(values):
                place = lax.rem(lax.axis_index(GROUP) + k, z.group)
                turn = lax.rem((place - s + z.subs * z.group) * z.width, z.lanes)
                turned = pltpu.roll(value[at], turn, 1)
                total = jnp.where(lane_mask(z, place, turned.shape), turned, total)
            out[at, s] = total


def last_kernel(z, wait, *refs):
    arrived, firsts, seconds = refs[: z.group], refs[z.group : 2 * z.group], refs[2 * z.group : 3 * z.group]
    picks, face_before, face_after, face_first, face_second, left_rows, right_rows = refs[3 * z.group : 3 * z.group + 7]
    tall, base, second_pass, final_residual = refs[3 * z.group + 7 :]
    start = piece_start(z, 0, z.own)
    m, half = z.modes, z.lanes // 2
    places = [lax.rem(lax.axis_index(GROUP) + k, z.group) * z.width for k in range(z.group)]

    def all_cases(parts, source=0):
        return sum(dot(part, lane_matrix(z, source, place)) for part, place in zip(parts, places))

    def whole_face(parts):
        return jnp.concatenate([all_cases(parts), all_cases(parts, half)], axis=0)

    modes = all_cases([picked_rows(z, piece, picks) for piece in arrived]).astype(BF16)
    swaps = list(zip(firsts, seconds))
    outer_before = whole_face([jnp.where(even(), b[...], a[...]) for a, b in swaps])
    outer_after = whole_face([jnp.where(even(), a[...], b[...]) for a, b in swaps])
    wait(3 * z.group + 7)
    totals = []
    for s in range(z.subs):
        faces = sides(z, face_before, face_after, face_first, face_second, s)
        both = []
        for side, at in ((0, s), (1, s + 2)):
            above = jnp.zeros((half, z.lanes), BF16)
            below = jnp.zeros((half - m, z.lanes), BF16)
            both.append(dot(faces[side], jnp.concatenate([above, modes[at * m : (at + 1) * m], below], axis=0)))
        if s == 0:
            both[0] = both[0] + outer_before
        if s == z.subs - 1:
            both[1] = both[1] + outer_after
        scatter = scatter_matrix(z, left_rows[s : s + 1, :], start, z.own)
        wide = jnp.concatenate([tall[s, pl.ds(start, z.own), :], scatter], axis=1)
        total = dot(wide, correction_side(z, modes, s, both[0].astype(BF16)))
        image = dot(scatter_matrix(z, right_rows[s : s + 1, :], start, z.own), both[1].astype(BF16))
        totals.append((total[:, z.lanes :], total[:, : z.lanes] + image))
    wait(3 * z.group + 8)
    for s, (step, image) in enumerate(totals):
        second_pass[s] = (base[0, s] + step)[:, : z.cases]
        final_residual[s] = (base[1, s] - image)[:, : z.cases]


def call(kernel, outs, operands, flops, scratch=(), late=(), loose=(), name=None):
    moved = sum(int(np.prod(x.shape)) * x.dtype.itemsize for x in (*operands, *outs))
    n_in, n_out = len(operands), len(outs)

    def whole(*refs):
        hbm, refs = refs[: n_in + n_out], refs[n_in + n_out :]
        vmem, refs = refs[: n_in + n_out], refs[n_in + n_out :]
        in_sems, out_sems, *rest = refs
        arriving = [pltpu.make_async_copy(hbm[i], vmem[i], in_sems.at[i]) for i in range(n_in)]
        for i in sorted(range(n_in), key=lambda i: i in late):
            arriving[i].start()
        for i, copy in enumerate(arriving):
            if i not in late:
                copy.wait()
        extra = [lambda i: arriving[i].wait()] if late else []
        kernel(*extra, *vmem, *rest)
        leaving = [pltpu.make_async_copy(vmem[n_in + i], hbm[n_in + i], out_sems.at[i]) for i in range(n_out)]
        for copy in leaving:
            copy.start()
        for copy in leaving:
            copy.wait()

    hbm_spec = pl.BlockSpec(memory_space=pltpu.HBM)
    any_spec = pl.BlockSpec(memory_space=pl.ANY)
    placed = [
        x if i in loose else pltpu.with_memory_space_constraint(x, pltpu.HBM) for i, x in enumerate(operands)
    ]
    return pl.pallas_call(
        whole,
        out_shape=[pltpu.HBM(o.shape, o.dtype) for o in outs],
        in_specs=[any_spec if i in loose else hbm_spec for i in range(n_in)],
        out_specs=[hbm_spec] * n_out,
        scratch_shapes=[
            *[pltpu.VMEM(x.shape, x.dtype) for x in (*operands, *outs)],
            pltpu.SemaphoreType.DMA((n_in,)),
            pltpu.SemaphoreType.DMA((n_out,)),
            *scratch,
        ],
        compiler_params=pltpu.CompilerParams(vmem_limit_bytes=VMEM_BYTES),
        cost_estimate=pl.CostEstimate(flops=flops, bytes_accessed=moved, transcendentals=0),
        name=name,
    )(*placed)


def shape(dims, dtype):
    return jax.ShapeDtypeStruct(dims, dtype)


def pieces_of(block, group):
    out = [block]
    for k in range(1, group):
        out.append(lax.ppermute(block, GROUP, [((g + k) % group, g) for g in range(group)]))
    return out


def body(loads, stiffness, local_inverse, coarse_basis, coarse_inverse, coarse_index, left_rows, right_rows):
    z = Sizes(loads, stiffness, coarse_basis, coarse_inverse, left_rows)
    n, group, subs, rows, lanes, modes, face = z.n, z.group, z.subs, z.rows, z.lanes, z.modes, z.face
    basis_pieces = pieces_of(jnp.swapaxes(coarse_basis, 1, 2), group)
    basis_pieces, coarse_inverse, local_inverse, stiffness = lax.optimization_barrier(
        (basis_pieces, coarse_inverse, local_inverse, stiffness)
    )
    inverse_columns = pieces_of(coarse_inverse, group)
    column = np.arange(z.columns)
    repeat = jnp.asarray(np.arange(lanes)[:, None] == column[None, :] % modes, BF16)
    own_row = jnp.asarray(np.arange(n)[:, None] == column[None, :] // modes, F32)
    place = jnp.asarray(
        (column // modes * z.owned + column % modes)[None, :] + np.arange(subs)[:, None] * modes, jnp.int32
    )
    packed_f = shape((rows, lanes), F32)
    packed_b = shape((rows, lanes), BF16)
    copies = shape((n, modes, lanes), BF16)
    tall = shape((subs, rows, lanes), BF16)
    spread = functools.partial(lax.all_to_all, axis_name="sub", split_axis=0, concat_axis=0)
    first_pairs = [(i, i + 1 if i % 2 == 0 else i - 1) for i in range(n)]
    second_pairs = [(i, (i + (1 if i % 2 else -1)) % n) for i in range(n)]
    work = 4 * subs * rows * rows * lanes

    (message,) = call(
        functools.partial(open_kernel, z),
        [shape((n, modes + DIGIT_ROWS, lanes), BF16)],
        [*basis_pieces, loads, coarse_index],
        4 * rows * lanes * lanes,
        [pltpu.VMEM((DIGIT_ROWS, lanes), F32), pltpu.VMEM((subs, modes, rows), BF16)],
        loose=range(1, group),
        name="open",
    )
    inverse_pieces = pieces_of(local_inverse, group)
    stiffness_pieces = pieces_of(stiffness, group)
    restricted = spread(message)
    arrivals = [*range(1, group), *range(group + 1, 2 * group)]
    faces = shape((subs, face, lanes), BF16)
    outer = shape((face, lanes), BF16)
    (
        load_rows, solved, image, before, after, first_pair, second_pair, tall, basis_t
    ) = call(
        functools.partial(first_image_kernel, z),
        [
            packed_b, packed_f, packed_f, faces, faces, outer, outer, tall, shape((subs, modes, rows), BF16),
        ],
        [*inverse_pieces, *stiffness_pieces, *basis_pieces, loads, left_rows, right_rows],
        work,
        [
            pltpu.VMEM((rows, lanes), BF16),
            pltpu.VMEM((subs, rows, 2 * lanes), BF16), pltpu.VMEM((subs, rows, 2 * lanes), BF16),
        ],
        late=range(2 * group),
        loose=[*arrivals, *range(2 * group + 1, 3 * group)],
        name="first_image",
    )
    first_got = lax.ppermute(first_pair, "sub", first_pairs)
    restricted, first_pair = lax.optimization_barrier((restricted, first_pair))
    near = (subs + 2) * modes
    ordered_inverse, index, message = call(
        functools.partial(order_kernel, z),
        [shape((subs, z.owned, z.columns), BF16), shape((subs, n, lanes), F32), copies],
        [*inverse_columns, restricted, repeat, own_row],
        2 * z.owned * z.total * z.total,
        loose=range(1, group + 1),
        name="order",
    )
    coarse = spread(message)
    second_got = lax.ppermute(second_pair, "sub", second_pairs)
    side = shape((subs, modes, face), BF16)
    left_t, right_t, inner, start_modes, picks = call(
        functools.partial(begin_kernel, z),
        [
            side, side, shape((subs, modes, modes), BF16), shape((modes, lanes), F32),
            shape((subs, near, z.columns), BF16),
        ],
        [load_rows, image, tall, basis_t, left_rows, right_rows, index, place],
        work // 16,
        name="begin",
    )
    chosen, message = call(
        functools.partial(update_kernel, z),
        [shape((near, lanes), BF16), copies],
        [coarse, picks, start_modes, inner, left_t, right_t, before, after, first_got, second_got],
        work // 64,
        loose=[0, 8, 9],
        name="update",
    )
    restricted = spread(message)

    bases = [before, after, first_got, second_got]
    half_face = shape((face // 2, lanes), BF16)
    first_pair, second_pair, *values = call(
        functools.partial(second_image_kernel, z),
        [half_face, half_face, *[shape((2, z.own, lanes), F32)] * group],
        [
            *inverse_pieces, *stiffness_pieces, load_rows, image, tall, solved, chosen,
            *bases, left_rows, right_rows,
        ],
        work,
        [
            pltpu.VMEM((rows, lanes), F32), pltpu.VMEM((rows, lanes), BF16), pltpu.VMEM((rows, lanes), BF16),
            pltpu.VMEM((subs, face, lanes), BF16), pltpu.VMEM((subs, face, lanes), BF16),
        ],
        late=range(2 * group),
        loose=[*arrivals, 2 * group + 7, 2 * group + 8],
        name="second_image",
    )
    first_got = lax.ppermute(first_pair, "sub", first_pairs)
    restricted, first_pair = lax.optimization_barrier((restricted, first_pair))
    (message,) = call(
        functools.partial(coarse_kernel, z),
        [copies],
        [restricted, ordered_inverse],
        work // 64,
        loose=[0],
        name="coarse",
    )
    coarse = spread(message)
    second_got = lax.ppermute(second_pair, "sub", second_pairs)
    swapped = [values[0]]
    for k in range(1, group):
        swapped.append(lax.ppermute(values[k], GROUP, [(g, (g + k) % group) for g in range(group)]))
    swapped = [swapped[(group - k) % group] for k in range(group)]
    (base,) = call(
        functools.partial(base_kernel, z),
        [shape((2, subs, z.own, lanes), F32)],
        swapped,
        work // 64,
        loose=range(1, group),
        name="base",
    )
    base, first_got, second_got = lax.optimization_barrier((base, first_got, second_got))
    out = shape((subs, z.own, z.cases), F32)
    return tuple(
        call(
            functools.partial(last_kernel, z),
            [out, out],
            [
                *pieces_of(coarse, group), *pieces_of(first_got, group), *pieces_of(second_got, group),
                picks, *bases, left_rows, right_rows, tall, base,
            ],
            work // 8,
            late=[3 * group + 7, 3 * group + 8],
            loose=[*range(3 * group), 3 * group + 3, 3 * group + 4],
            name="last",
        )
    )


def solution(mesh):
    return jax.shard_map(
        body,
        mesh=mesh,
        in_specs=(
            P("sub", None, None),
            P("sub", GROUP, None),
            P("sub", GROUP, None),
            P("sub", GROUP, None),
            P("sub", GROUP),
            P("sub", None),
            P("sub", None),
            P("sub", None),
        ),
        out_specs=(P("sub", GROUP, None), P("sub", GROUP, None)),
        check_vma=False,
    )
```

```python
import functools

import jax
import jax.numpy as jnp
import numpy as np
from jax import lax
from jax.experimental import pallas as pl
from jax.experimental.pallas import tpu as pltpu
from jax.sharding import PartitionSpec as P

GROUP = ("crow", "ccol")
F32 = jnp.float32
BF16 = jnp.bfloat16
VMEM_BYTES = 48 * 1024 * 1024
DIGIT_ROWS = 16
DIGIT_BITS = 8
DIGIT = 1 << DIGIT_BITS


def dot(a, b):
    return lax.dot_general(a, b, (((1,), (0,)), ((), ())), preferred_element_type=F32)


def dot_tn(a, b):
    return lax.dot_general(a, b, (((0,), (0,)), ((), ())), preferred_element_type=F32)


def dot_nt(a, b):
    return lax.dot_general(a, b, (((1,), (1,)), ((), ())), preferred_element_type=F32)


class Sizes:
    def __init__(self, loads, stiffness, coarse_basis, coarse_inverse, left_rows):
        self.n = lax.axis_size("sub")
        self.group = lax.axis_size(GROUP)
        self.subs, self.rows, self.cases = loads.shape
        self.own = stiffness.shape[1]
        self.modes = coarse_basis.shape[2]
        self.owned, self.block = coarse_inverse.shape
        self.total = self.block * self.group
        self.face = left_rows.shape[1]
        self.width = self.cases // self.group
        self.lanes = max(self.cases, -(-self.subs * self.width // 128) * 128)
        self.columns = self.n * self.modes


def lane_mask(z, block, shape):
    lane = lax.broadcasted_iota(jnp.int32, shape, len(shape) - 1)
    return (lane >= block * z.width) & (lane < (block + 1) * z.width)


def select(z, parts):
    out = jnp.zeros_like(parts[0])
    for s, part in enumerate(parts):
        out = jnp.where(lane_mask(z, s, part.shape), part, out)
    return out


def fold(z, packed):
    if z.lanes == z.subs * z.width:
        out = packed
        for k in range(1, z.subs):
            out = out + pltpu.roll(packed, k * z.width, 1)
        return out
    out = packed
    for k in range(1, z.subs):
        out = out + pltpu.roll(packed, k * z.width, 1)
        out = out + pltpu.roll(packed, z.lanes - k * z.width, 1)
    return out


def lane_matrix(z, source, target, width=None):
    row = lax.broadcasted_iota(jnp.int32, (z.lanes, z.lanes), 0)
    lane = lax.broadcasted_iota(jnp.int32, (z.lanes, z.lanes), 1)
    hit = (row - source == lane - target) & (lane >= target) & (lane < target + (width or z.width))
    return jnp.where(hit, 1.0, 0.0).astype(BF16)


def piece_start(z, k, size):
    place = lax.rem(lax.axis_index(GROUP) + k, z.group)
    return pl.multiple_of(place * size, size)


def pick_matrix(z, rows_of):
    column = jnp.transpose(jnp.broadcast_to(rows_of.astype(F32), (z.face, z.face)))[:, 0:1].astype(jnp.int32)
    row = lax.broadcasted_iota(jnp.int32, (z.face, z.rows), 1)
    return jnp.where(row == column, 1.0, 0.0).astype(BF16)


def even():
    return lax.rem(lax.axis_index("sub"), 2) == 0


def case_matrix(z, s):
    row = lax.broadcasted_iota(jnp.int32, (z.cases, z.lanes), 0)
    lane = lax.broadcasted_iota(jnp.int32, (z.cases, z.lanes), 1)
    hit = (row - lax.axis_index(GROUP) * z.width == lane - s * z.width) & lane_mask(z, s, row.shape)
    return jnp.where(hit, 1.0, 0.0).astype(BF16)


def join_basis(z, pieces, basis_t):
    for k, piece in enumerate(pieces):
        basis_t[:, :, pl.ds(piece_start(z, k, z.own), z.own)] = piece[...]


def open_kernel(z, *refs):
    pieces = refs[: z.group]
    loads, index, message, digits, basis_t = refs[z.group :]
    join_basis(z, pieces, basis_t)
    total = jnp.zeros((z.modes, z.lanes), F32)
    for s in range(z.subs):
        total = total + dot(dot(basis_t[s], loads[s]).astype(BF16), case_matrix(z, s))
    modes = total.astype(BF16)
    digits[...] = jnp.zeros(digits.shape, F32)
    for s in range(z.subs):
        places = index[s : s + 1, :]
        digits[2 * s : 2 * s + 1, : z.modes] = (places >> DIGIT_BITS).astype(F32)
        digits[2 * s + 1 : 2 * s + 2, : z.modes] = (places & (DIGIT - 1)).astype(F32)
    for k in range(z.n):
        message[k, : z.modes, :] = modes
        message[k, z.modes :, :] = digits[...].astype(BF16)


def multiply(z, pieces, vector, store, wait):
    for k in range(z.group):
        wait(k)
    for k, piece in enumerate(pieces):
        parts = [dot(piece[s], vector) for s in range(z.subs)]
        store(k, piece_start(z, k, z.own), select(z, parts))


def pick_both(z, left_rows, right_rows, s):
    return jnp.concatenate(
        [pick_matrix(z, left_rows[s : s + 1, :]), pick_matrix(z, right_rows[s : s + 1, :])], axis=0
    )


def halves(z, face):
    part = z.face // 2
    return (face[:part].astype(F32) + dot(face[part:], lane_matrix(z, 0, z.lanes // 2))).astype(BF16)


def store_faces(z, before, after, first_pair, second_pair):
    first, last = before[0], after[z.subs - 1]
    first_pair[...] = jnp.where(even(), last, first)
    second_pair[...] = jnp.where(even(), first, last)


def sides(z, before, after, first_pair, second_pair, s):
    if s == 0:
        from_before = jnp.where(even(), second_pair[...], first_pair[...])
    else:
        from_before = after[s - 1]
    if s == z.subs - 1:
        from_after = jnp.where(even(), first_pair[...], second_pair[...])
    else:
        from_after = before[s + 1]
    return from_before, from_after


def shares(z, s, chosen, faces, bases=None):
    m, half = z.modes, z.lanes // 2
    moved = lane_matrix(z, 0, s * z.width)
    out = []
    for side, at in ((0, s), (1, s + 2)):
        own = chosen[at * m : (at + 1) * m]
        below = jnp.concatenate([own, jnp.zeros((half - m, z.lanes), BF16)], axis=0)
        if bases is None:
            total = dot(faces[side], jnp.concatenate([moved[:half], below], axis=0))
        else:
            above = jnp.zeros((half, z.lanes), BF16)
            total = dot(faces[side], moved) + dot(bases[side], jnp.concatenate([above, below], axis=0))
        out.append(total)
    return out


def correction_side(z, chosen, s, share):
    m, half = z.modes, z.lanes // 2
    own = chosen[(s + 1) * m : (s + 2) * m]
    none = jnp.zeros((half - m, z.lanes), BF16)
    nil = jnp.zeros((half, z.lanes), BF16)
    image = jnp.concatenate([own, none, nil, share], axis=0)
    step = jnp.concatenate([nil, own, none, jnp.zeros((z.face, z.lanes), BF16)], axis=0)
    return jnp.concatenate([image, step], axis=1)


def scatter_matrix(z, rows_of, start, count):
    row = lax.broadcasted_iota(jnp.int32, (count, z.face), 0) + start
    return jnp.where(row == rows_of, 1.0, 0.0).astype(BF16)


def first_image_kernel(z, wait, *refs):
    inverse, stiffness = refs[: z.group], refs[z.group : 2 * z.group]
    pieces = refs[2 * z.group : 3 * z.group]
    loads, left_rows, right_rows = refs[3 * z.group : 3 * z.group + 3]
    load_rows, solved, image, before, after, first_pair, second_pair = refs[3 * z.group + 3 : 3 * z.group + 10]
    tall, basis_t, rounded, both, images = refs[3 * z.group + 10 :]
    join_basis(z, pieces, basis_t)
    packed = dot(loads[0], case_matrix(z, 0))
    for s in range(1, z.subs):
        packed = packed + dot(loads[s], case_matrix(z, s))
    load_rows[...] = packed.astype(BF16)

    def store_solved(k, start, value):
        solved[pl.ds(start, z.own), :] = value
        rounded[pl.ds(start, z.own), :] = value.astype(BF16)

    multiply(z, inverse, load_rows[...], store_solved, wait)
    solved_b = rounded[...]
    half = z.lanes // 2
    for s in range(z.subs):
        basis = jnp.transpose(basis_t[s].astype(F32)).astype(BF16)
        tall[s, :, half : half + z.modes] = basis
        tall[s, :, half + z.modes :] = jnp.zeros((z.rows, half - z.modes), BF16)
        both[s, :, : z.lanes] = solved_b
        both[s, :, z.lanes : z.lanes + z.modes] = basis
        both[s, :, z.lanes + z.modes :] = jnp.zeros((z.rows, z.lanes - z.modes), BF16)
    for k, piece in enumerate(stiffness):
        wait(z.group + k)
        start = piece_start(z, k, z.own)
        parts = [dot(piece[s], both[s]) for s in range(z.subs)]
        image[pl.ds(start, z.own), :] = select(z, [part[:, : z.lanes] for part in parts])
        for s in range(z.subs):
            images[s, pl.ds(start, z.own), :] = parts[s].astype(BF16)
    for s in range(z.subs):
        tall[s, :, :half] = images[s, :, z.lanes : z.lanes + half]
        picked = dot(pick_both(z, left_rows, right_rows, s), images[s]).astype(BF16)
        faces = dot(picked[:, : z.lanes], lane_matrix(z, s * z.width, 0))
        faces = (faces + dot(picked[:, z.lanes :], lane_matrix(z, 0, half, z.modes))).astype(BF16)
        before[s] = faces[: z.face]
        after[s] = faces[z.face :]
    store_faces(z, before, after, first_pair, second_pair)


def begin_kernel(z, *refs):
    load_rows, image, tall, basis_t, left_rows, right_rows, index, place = refs[:8]
    left_t, right_t, inner, start_modes, picks = refs[8:]
    left = (load_rows[...].astype(F32) - image[...]).astype(BF16)
    begun = []
    for s in range(z.subs):
        restricted = dot(basis_t[s], jnp.concatenate([left, tall[s]], axis=1))
        begun.append(restricted[:, : z.lanes])
        inner[s] = restricted[:, z.lanes : z.lanes + z.modes].astype(BF16)
        sides_t = dot_nt(basis_t[s], pick_both(z, left_rows, right_rows, s)).astype(BF16)
        left_t[s] = sides_t[:, : z.face]
        right_t[s] = sides_t[:, z.face :]
    start_modes[...] = select(z, begun)
    here = lax.axis_index("sub")
    device = lax.broadcasted_iota(jnp.int32, (z.n, z.lanes), 0)
    for t in range(z.subs + 2):
        if t == 0:
            s, owner = z.subs - 1, lax.rem(here + z.n - 1, z.n)
        elif t == z.subs + 1:
            s, owner = 0, lax.rem(here + 1, z.n)
        else:
            s, owner = t - 1, here
        row = jnp.sum(jnp.where(device == owner, index[s], 0.0), axis=0, keepdims=True)
        column = jnp.transpose(jnp.broadcast_to(row, (z.lanes, z.lanes)))[: z.modes, 0:1].astype(jnp.int32)
        for h in range(z.subs):
            hit = column == place[h : h + 1, :]
            picks[h, t * z.modes : (t + 1) * z.modes, :] = jnp.where(hit, 1.0, 0.0).astype(BF16)


def second_image_kernel(z, wait, *refs):
    inverse, stiffness = refs[: z.group], refs[z.group : 2 * z.group]
    rest = refs[2 * z.group :]
    load_rows, old_image, tall, old_solved, chosen = rest[:5]
    before, after, first_got, second_got, left_rows, right_rows = rest[5:11]
    first_pair, second_pair = rest[11:13]
    values = rest[13 : 13 + z.group]
    base, rounded, image, new_before, new_after = rest[13 + z.group :]
    steps, images = [], []
    for s in range(z.subs):
        faces = sides(z, before, after, first_got, second_got, s)
        both = [share.astype(BF16) for share in shares(z, s, chosen, faces)]
        left = jnp.concatenate([tall[s], scatter_matrix(z, left_rows[s : s + 1, :], 0, z.rows)], axis=1)
        total = dot(left, correction_side(z, chosen, s, both[0]))
        steps.append(total[:, z.lanes :])
        images.append(total[:, : z.lanes] + dot(scatter_matrix(z, right_rows[s : s + 1, :], 0, z.rows), both[1]))
    residual = (load_rows[...].astype(F32) - old_image[...] - select(z, images)).astype(BF16)
    base[...] = old_solved[...] + select(z, steps)

    def store_solved(k, start, value):
        value = value + base[pl.ds(start, z.own), :]
        values[k][0] = value
        rounded[pl.ds(start, z.own), :] = value.astype(BF16)

    multiply(z, inverse, residual, store_solved, wait)

    def store_image(k, start, value):
        place = pl.ds(start, z.own)
        values[k][1] = load_rows[place, :].astype(F32) - value
        image[place, :] = value.astype(BF16)

    multiply(z, stiffness, rounded[...], store_image, lambda k: wait(z.group + k))
    pick = jnp.concatenate([pick_both(z, left_rows, right_rows, s) for s in range(z.subs)], axis=0)
    picked = dot(pick, image[...]).astype(BF16)
    for s in range(z.subs):
        own = picked[2 * s * z.face : 2 * (s + 1) * z.face]
        faces = dot(own, lane_matrix(z, s * z.width, 0)).astype(BF16)
        new_before[s] = faces[: z.face]
        new_after[s] = faces[z.face :]
    first = halves(z, new_before[0])
    last = halves(z, new_after[z.subs - 1])
    first_pair[...] = jnp.where(even(), last, first)
    second_pair[...] = jnp.where(even(), first, last)
    inner = []
    for s in range(z.subs):
        move = lane_matrix(z, 0, s * z.width)
        total = jnp.zeros((z.rows, z.lanes), F32)
        if s > 0:
            share = dot(new_after[s - 1], move).astype(BF16)
            total = total + dot(scatter_matrix(z, left_rows[s : s + 1, :], 0, z.rows), share)
        if s < z.subs - 1:
            share = dot(new_before[s + 1], move).astype(BF16)
            total = total + dot(scatter_matrix(z, right_rows[s : s + 1, :], 0, z.rows), share)
        inner.append(total)
    base[...] = select(z, inner)
    for k in range(z.group):
        values[k][1] = values[k][1] - base[pl.ds(piece_start(z, k, z.own), z.own), :]


def digit_row(shape, row):
    return lax.broadcasted_iota(jnp.int32, shape, 1) == row


def coarse_rows(z, ordered_inverse, arrived, message):
    flat = arrived[:, : z.modes, :].reshape(z.columns, z.lanes)
    product = dot(ordered_inverse[...].reshape(z.subs * z.owned, z.columns), flat)
    rows = fold(z, select(z, [product[s * z.owned : (s + 1) * z.owned] for s in range(z.subs)]))
    packed = select(z, [rows[s * z.modes : (s + 1) * z.modes, :] for s in range(z.subs)]).astype(BF16)
    for k in range(z.n):
        message[k] = packed


def order_kernel(z, *refs):
    blocks = refs[: z.group]
    arrived, repeat, own_row, ordered_inverse, index, message = refs[z.group :]
    digits = arrived[:, z.modes :, :].astype(F32)
    pairs = []
    for s in range(z.subs):
        high = jnp.sum(jnp.where(digit_row(digits.shape, 2 * s), digits, 0.0), axis=1)
        low = jnp.sum(jnp.where(digit_row(digits.shape, 2 * s + 1), digits, 0.0), axis=1)
        index[s] = high * DIGIT + low
        pairs += [high.astype(BF16), low.astype(BF16)]
    spreads = dot(jnp.concatenate(pairs, axis=0), repeat[...])
    for s in range(z.subs):
        at_high, at_low = 2 * s * z.n, (2 * s + 1) * z.n
        spread = spreads[at_high : at_high + z.n] * DIGIT + spreads[at_low : at_low + z.n]
        places = jnp.sum(spread * own_row[...], axis=0, keepdims=True).astype(jnp.int32)
        for at in range(0, z.columns, 768):
            wide = min(768, z.columns - at)
            total = jnp.zeros((z.owned, wide), F32)
            for k, block in enumerate(blocks):
                inside = (places[:, at : at + wide] - piece_start(z, k, z.block)).astype(jnp.int16)
                for first in range(0, z.block, 768):
                    deep = min(768, z.block - first)
                    row = lax.broadcasted_iota(jnp.int16, (deep, wide), 0) + jnp.int16(first)
                    hot = jnp.where(row == inside, jnp.ones((), BF16), jnp.zeros((), BF16))
                    total = total + dot(block[:, first : first + deep], hot)
            ordered_inverse[s, :, at : at + wide] = total.astype(BF16)
    coarse_rows(z, ordered_inverse, arrived, message)


def coarse_kernel(z, arrived, ordered_inverse, message):
    coarse_rows(z, ordered_inverse, arrived, message)


def picked_rows(z, arrived, picks):
    flat = arrived[...].reshape(z.columns, z.lanes)
    near = picks.shape[1]
    product = dot(picks[...].reshape(z.subs * near, z.columns), flat)
    return fold(z, select(z, [product[h * near : (h + 1) * near] for h in range(z.subs)])).astype(BF16)


def update_kernel(z, *refs):
    arrived, picks, start_modes, inner, left_t, right_t, before, after, first_got, second_got = refs[:10]
    chosen, message = refs[10:]
    rows = picked_rows(z, arrived, picks)
    chosen[...] = rows
    m = z.modes
    parts = []
    for s in range(z.subs):
        faces = sides(z, before, after, first_got, second_got, s)
        both = shares(z, s, rows, faces)
        total = dot(inner[s], rows[(s + 1) * m : (s + 2) * m])
        parts.append(total + dot(left_t[s], both[0].astype(BF16)) + dot(right_t[s], both[1].astype(BF16)))
    modes = (start_modes[...] - select(z, parts)).astype(BF16)
    for k in range(z.n):
        message[k] = modes


def base_kernel(z, *refs):
    *values, out = refs
    for at in range(2):
        for s in range(z.subs):
            total = jnp.zeros((z.own, z.lanes), F32)
            for k, value in enumerate(values):
                place = lax.rem(lax.axis_index(GROUP) + k, z.group)
                turn = lax.rem((place - s + z.subs * z.group) * z.width, z.lanes)
                turned = pltpu.roll(value[at], turn, 1)
                total = jnp.where(lane_mask(z, place, turned.shape), turned, total)
            out[at, s] = total


def last_kernel(z, wait, *refs):
    arrived, firsts, seconds = refs[: z.group], refs[z.group : 2 * z.group], refs[2 * z.group : 3 * z.group]
    picks, face_before, face_after, face_first, face_second, left_rows, right_rows = refs[3 * z.group : 3 * z.group + 7]
    tall, base, second_pass, final_residual = refs[3 * z.group + 7 :]
    start = piece_start(z, 0, z.own)
    m, half = z.modes, z.lanes // 2
    places = [lax.rem(lax.axis_index(GROUP) + k, z.group) * z.width for k in range(z.group)]

    def all_cases(parts, source=0):
        return sum(dot(part, lane_matrix(z, source, place)) for part, place in zip(parts, places))

    def whole_face(parts):
        return jnp.concatenate([all_cases(parts), all_cases(parts, half)], axis=0)

    modes = all_cases([picked_rows(z, piece, picks) for piece in arrived]).astype(BF16)
    swaps = list(zip(firsts, seconds))
    outer_before = whole_face([jnp.where(even(), b[...], a[...]) for a, b in swaps])
    outer_after = whole_face([jnp.where(even(), a[...], b[...]) for a, b in swaps])
    wait(3 * z.group + 7)
    totals = []
    for s in range(z.subs):
        faces = sides(z, face_before, face_after, face_first, face_second, s)
        both = []
        for side, at in ((0, s), (1, s + 2)):
            above = jnp.zeros((half, z.lanes), BF16)
            below = jnp.zeros((half - m, z.lanes), BF16)
            both.append(dot(faces[side], jnp.concatenate([above, modes[at * m : (at + 1) * m], below], axis=0)))
        if s == 0:
            both[0] = both[0] + outer_before
        if s == z.subs - 1:
            both[1] = both[1] + outer_after
        scatter = scatter_matrix(z, left_rows[s : s + 1, :], start, z.own)
        wide = jnp.concatenate([tall[s, pl.ds(start, z.own), :], scatter], axis=1)
        total = dot(wide, correction_side(z, modes, s, both[0].astype(BF16)))
        image = dot(scatter_matrix(z, right_rows[s : s + 1, :], start, z.own), both[1].astype(BF16))
        totals.append((total[:, z.lanes :], total[:, : z.lanes] + image))
    wait(3 * z.group + 8)
    for s, (step, image) in enumerate(totals):
        second_pass[s] = (base[0, s] + step)[:, : z.cases]
        final_residual[s] = (base[1, s] - image)[:, : z.cases]


def call(kernel, outs, operands, flops, scratch=(), late=(), loose=(), name=None):
    moved = sum(int(np.prod(x.shape)) * x.dtype.itemsize for x in (*operands, *outs))
    n_in, n_out = len(operands), len(outs)

    def whole(*refs):
        hbm, refs = refs[: n_in + n_out], refs[n_in + n_out :]
        vmem, refs = refs[: n_in + n_out], refs[n_in + n_out :]
        in_sems, out_sems, *rest = refs
        arriving = [pltpu.make_async_copy(hbm[i], vmem[i], in_sems.at[i]) for i in range(n_in)]
        for i in sorted(range(n_in), key=lambda i: i in late):
            arriving[i].start()
        for i, copy in enumerate(arriving):
            if i not in late:
                copy.wait()
        extra = [lambda i: arriving[i].wait()] if late else []
        kernel(*extra, *vmem, *rest)
        leaving = [pltpu.make_async_copy(vmem[n_in + i], hbm[n_in + i], out_sems.at[i]) for i in range(n_out)]
        for copy in leaving:
            copy.start()
        for copy in leaving:
            copy.wait()

    hbm_spec = pl.BlockSpec(memory_space=pltpu.HBM)
    any_spec = pl.BlockSpec(memory_space=pl.ANY)
    placed = [
        x if i in loose else pltpu.with_memory_space_constraint(x, pltpu.HBM) for i, x in enumerate(operands)
    ]
    return pl.pallas_call(
        whole,
        out_shape=[pltpu.HBM(o.shape, o.dtype) for o in outs],
        in_specs=[any_spec if i in loose else hbm_spec for i in range(n_in)],
        out_specs=[hbm_spec] * n_out,
        scratch_shapes=[
            *[pltpu.VMEM(x.shape, x.dtype) for x in (*operands, *outs)],
            pltpu.SemaphoreType.DMA((n_in,)),
            pltpu.SemaphoreType.DMA((n_out,)),
            *scratch,
        ],
        compiler_params=pltpu.CompilerParams(vmem_limit_bytes=VMEM_BYTES),
        cost_estimate=pl.CostEstimate(flops=flops, bytes_accessed=moved, transcendentals=0),
        name=name,
    )(*placed)


def shape(dims, dtype):
    return jax.ShapeDtypeStruct(dims, dtype)


def pieces_of(block, group):
    out = [block]
    for k in range(1, group):
        out.append(lax.ppermute(block, GROUP, [((g + k) % group, g) for g in range(group)]))
    return out


def body(loads, stiffness, local_inverse, coarse_basis, coarse_inverse, coarse_index, left_rows, right_rows):
    z = Sizes(loads, stiffness, coarse_basis, coarse_inverse, left_rows)
    n, group, subs, rows, lanes, modes, face = z.n, z.group, z.subs, z.rows, z.lanes, z.modes, z.face
    basis_pieces = pieces_of(jnp.swapaxes(coarse_basis, 1, 2), group)
    basis_pieces, coarse_inverse, local_inverse, stiffness = lax.optimization_barrier(
        (basis_pieces, coarse_inverse, local_inverse, stiffness)
    )
    inverse_columns = pieces_of(coarse_inverse, group)
    column = np.arange(z.columns)
    repeat = jnp.asarray(np.arange(lanes)[:, None] == column[None, :] % modes, BF16)
    own_row = jnp.asarray(np.arange(n)[:, None] == column[None, :] // modes, F32)
    place = jnp.asarray(
        (column // modes * z.owned + column % modes)[None, :] + np.arange(subs)[:, None] * modes, jnp.int32
    )
    packed_f = shape((rows, lanes), F32)
    packed_b = shape((rows, lanes), BF16)
    copies = shape((n, modes, lanes), BF16)
    tall = shape((subs, rows, lanes), BF16)
    spread = functools.partial(lax.all_to_all, axis_name="sub", split_axis=0, concat_axis=0)
    first_pairs = [(i, i + 1 if i % 2 == 0 else i - 1) for i in range(n)]
    second_pairs = [(i, (i + (1 if i % 2 else -1)) % n) for i in range(n)]
    work = 4 * subs * rows * rows * lanes

    (message,) = call(
        functools.partial(open_kernel, z),
        [shape((n, modes + DIGIT_ROWS, lanes), BF16)],
        [*basis_pieces, loads, coarse_index],
        4 * rows * lanes * lanes,
        [pltpu.VMEM((DIGIT_ROWS, lanes), F32), pltpu.VMEM((subs, modes, rows), BF16)],
        loose=range(1, group),
        name="open",
    )
    inverse_pieces = pieces_of(local_inverse, group)
    stiffness_pieces = pieces_of(stiffness, group)
    restricted = spread(message)
    arrivals = [*range(1, group), *range(group + 1, 2 * group)]
    faces = shape((subs, face, lanes), BF16)
    outer = shape((face, lanes), BF16)
    (
        load_rows, solved, image, before, after, first_pair, second_pair, tall, basis_t
    ) = call(
        functools.partial(first_image_kernel, z),
        [
            packed_b, packed_f, packed_f, faces, faces, outer, outer, tall, shape((subs, modes, rows), BF16),
        ],
        [*inverse_pieces, *stiffness_pieces, *basis_pieces, loads, left_rows, right_rows],
        work,
        [
            pltpu.VMEM((rows, lanes), BF16),
            pltpu.VMEM((subs, rows, 2 * lanes), BF16), pltpu.VMEM((subs, rows, 2 * lanes), BF16),
        ],
        late=range(2 * group),
        loose=[*arrivals, *range(2 * group + 1, 3 * group)],
        name="first_image",
    )
    first_got = lax.ppermute(first_pair, "sub", first_pairs)
    restricted, first_pair = lax.optimization_barrier((restricted, first_pair))
    near = (subs + 2) * modes
    ordered_inverse, index, message = call(
        functools.partial(order_kernel, z),
        [shape((subs, z.owned, z.columns), BF16), shape((subs, n, lanes), F32), copies],
        [*inverse_columns, restricted, repeat, own_row],
        2 * z.owned * z.total * z.total,
        loose=range(1, group + 1),
        name="order",
    )
    coarse = spread(message)
    second_got = lax.ppermute(second_pair, "sub", second_pairs)
    side = shape((subs, modes, face), BF16)
    left_t, right_t, inner, start_modes, picks = call(
        functools.partial(begin_kernel, z),
        [
            side, side, shape((subs, modes, modes), BF16), shape((modes, lanes), F32),
            shape((subs, near, z.columns), BF16),
        ],
        [load_rows, image, tall, basis_t, left_rows, right_rows, index, place],
        work // 16,
        name="begin",
    )
    chosen, message = call(
        functools.partial(update_kernel, z),
        [shape((near, lanes), BF16), copies],
        [coarse, picks, start_modes, inner, left_t, right_t, before, after, first_got, second_got],
        work // 64,
        loose=[0, 8, 9],
        name="update",
    )
    restricted = spread(message)

    bases = [before, after, first_got, second_got]
    half_face = shape((face // 2, lanes), BF16)
    first_pair, second_pair, *values = call(
        functools.partial(second_image_kernel, z),
        [half_face, half_face, *[shape((2, z.own, lanes), F32)] * group],
        [
            *inverse_pieces, *stiffness_pieces, load_rows, image, tall, solved, chosen,
            *bases, left_rows, right_rows,
        ],
        work,
        [
            pltpu.VMEM((rows, lanes), F32), pltpu.VMEM((rows, lanes), BF16), pltpu.VMEM((rows, lanes), BF16),
            pltpu.VMEM((subs, face, lanes), BF16), pltpu.VMEM((subs, face, lanes), BF16),
        ],
        late=range(2 * group),
        loose=[*arrivals, 2 * group + 7, 2 * group + 8],
        name="second_image",
    )
    first_got = lax.ppermute(first_pair, "sub", first_pairs)
    restricted, first_pair = lax.optimization_barrier((restricted, first_pair))
    (message,) = call(
        functools.partial(coarse_kernel, z),
        [copies],
        [restricted, ordered_inverse],
        work // 64,
        loose=[0],
        name="coarse",
    )
    coarse = spread(message)
    second_got = lax.ppermute(second_pair, "sub", second_pairs)
    swapped = [values[0]]
    for k in range(1, group):
        swapped.append(lax.ppermute(values[k], GROUP, [(g, (g + k) % group) for g in range(group)]))
    swapped = [swapped[(group - k) % group] for k in range(group)]
    (base,) = call(
        functools.partial(base_kernel, z),
        [shape((2, subs, z.own, lanes), F32)],
        swapped,
        work // 64,
        loose=range(1, group),
        name="base",
    )
    coarse, base, first_got, second_got = lax.optimization_barrier((coarse, base, first_got, second_got))
    out = shape((subs, z.own, z.cases), F32)
    return tuple(
        call(
            functools.partial(last_kernel, z),
            [out, out],
            [
                *pieces_of(coarse, group), *pieces_of(first_got, group), *pieces_of(second_got, group),
                picks, *bases, left_rows, right_rows, tall, base,
            ],
            work // 8,
            late=[3 * group + 7, 3 * group + 8],
            loose=[*range(3 * group), 3 * group + 3, 3 * group + 4],
            name="last",
        )
    )


def solution(mesh):
    return jax.shard_map(
        body,
        mesh=mesh,
        in_specs=(
            P("sub", None, None),
            P("sub", GROUP, None),
            P("sub", GROUP, None),
            P("sub", GROUP, None),
            P("sub", GROUP),
            P("sub", None),
            P("sub", None),
            P("sub", None),
        ),
        out_specs=(P("sub", GROUP, None), P("sub", GROUP, None)),
        check_vma=False,
    )
```

```python
import functools

import jax
import jax.numpy as jnp
import numpy as np
from jax import lax
from jax.experimental import pallas as pl
from jax.experimental.pallas import tpu as pltpu
from jax.sharding import PartitionSpec as P

GROUP = ("crow", "ccol")
F32 = jnp.float32
BF16 = jnp.bfloat16
VMEM_BYTES = 48 * 1024 * 1024
DIGIT_ROWS = 16
DIGIT_BITS = 8
DIGIT = 1 << DIGIT_BITS


def dot(a, b):
    return lax.dot_general(a, b, (((1,), (0,)), ((), ())), preferred_element_type=F32)


def dot_tn(a, b):
    return lax.dot_general(a, b, (((0,), (0,)), ((), ())), preferred_element_type=F32)


def dot_nt(a, b):
    return lax.dot_general(a, b, (((1,), (1,)), ((), ())), preferred_element_type=F32)


class Sizes:
    def __init__(self, loads, stiffness, coarse_basis, coarse_inverse, left_rows):
        self.n = lax.axis_size("sub")
        self.group = lax.axis_size(GROUP)
        self.subs, self.rows, self.cases = loads.shape
        self.own = stiffness.shape[1]
        self.modes = coarse_basis.shape[2]
        self.owned, self.block = coarse_inverse.shape
        self.total = self.block * self.group
        self.face = left_rows.shape[1]
        self.width = self.cases // self.group
        self.lanes = max(self.cases, -(-self.subs * self.width // 128) * 128)
        self.columns = self.n * self.modes


def lane_mask(z, block, shape):
    lane = lax.broadcasted_iota(jnp.int32, shape, len(shape) - 1)
    return (lane >= block * z.width) & (lane < (block + 1) * z.width)


def select(z, parts):
    out = jnp.zeros_like(parts[0])
    for s, part in enumerate(parts):
        out = jnp.where(lane_mask(z, s, part.shape), part, out)
    return out


def fold(z, packed):
    if z.lanes == z.subs * z.width:
        out = packed
        for k in range(1, z.subs):
            out = out + pltpu.roll(packed, k * z.width, 1)
        return out
    out = packed
    for k in range(1, z.subs):
        out = out + pltpu.roll(packed, k * z.width, 1)
        out = out + pltpu.roll(packed, z.lanes - k * z.width, 1)
    return out


def lane_matrix(z, source, target, width=None):
    row = lax.broadcasted_iota(jnp.int32, (z.lanes, z.lanes), 0)
    lane = lax.broadcasted_iota(jnp.int32, (z.lanes, z.lanes), 1)
    hit = (row - source == lane - target) & (lane >= target) & (lane < target + (width or z.width))
    return jnp.where(hit, 1.0, 0.0).astype(BF16)


def piece_start(z, k, size):
    place = lax.rem(lax.axis_index(GROUP) + k, z.group)
    return pl.multiple_of(place * size, size)


def pick_matrix(z, rows_of):
    column = jnp.transpose(jnp.broadcast_to(rows_of.astype(F32), (z.face, z.face)))[:, 0:1].astype(jnp.int32)
    row = lax.broadcasted_iota(jnp.int32, (z.face, z.rows), 1)
    return jnp.where(row == column, 1.0, 0.0).astype(BF16)


def even():
    return lax.rem(lax.axis_index("sub"), 2) == 0


def case_matrix(z, s):
    row = lax.broadcasted_iota(jnp.int32, (z.cases, z.lanes), 0)
    lane = lax.broadcasted_iota(jnp.int32, (z.cases, z.lanes), 1)
    hit = (row - lax.axis_index(GROUP) * z.width == lane - s * z.width) & lane_mask(z, s, row.shape)
    return jnp.where(hit, 1.0, 0.0).astype(BF16)


def join_basis(z, pieces, basis_t):
    for k, piece in enumerate(pieces):
        basis_t[:, :, pl.ds(piece_start(z, k, z.own), z.own)] = piece[...]


def open_kernel(z, *refs):
    pieces = refs[: z.group]
    loads, index, message, digits, basis_t = refs[z.group :]
    join_basis(z, pieces, basis_t)
    total = jnp.zeros((z.modes, z.lanes), F32)
    for s in range(z.subs):
        total = total + dot(dot(basis_t[s], loads[s]).astype(BF16), case_matrix(z, s))
    modes = total.astype(BF16)
    digits[...] = jnp.zeros(digits.shape, F32)
    for s in range(z.subs):
        places = index[s : s + 1, :]
        digits[2 * s : 2 * s + 1, : z.modes] = (places >> DIGIT_BITS).astype(F32)
        digits[2 * s + 1 : 2 * s + 2, : z.modes] = (places & (DIGIT - 1)).astype(F32)
    for k in range(z.n):
        message[k, : z.modes, :] = modes
        message[k, z.modes :, :] = digits[...].astype(BF16)


def multiply(z, pieces, vector, store, wait):
    for k in range(z.group):
        wait(k)
    for k, piece in enumerate(pieces):
        parts = [dot(piece[s], vector) for s in range(z.subs)]
        store(k, piece_start(z, k, z.own), select(z, parts))


def pick_both(z, left_rows, right_rows, s):
    return jnp.concatenate(
        [pick_matrix(z, left_rows[s : s + 1, :]), pick_matrix(z, right_rows[s : s + 1, :])], axis=0
    )


def halves(z, face):
    part = z.face // 2
    return (face[:part].astype(F32) + dot(face[part:], lane_matrix(z, 0, z.lanes // 2))).astype(BF16)


def store_faces(z, before, after, first_pair, second_pair):
    first, last = before[0], after[z.subs - 1]
    first_pair[...] = jnp.where(even(), last, first)
    second_pair[...] = jnp.where(even(), first, last)


def sides(z, before, after, first_pair, second_pair, s):
    if s == 0:
        from_before = jnp.where(even(), second_pair[...], first_pair[...])
    else:
        from_before = after[s - 1]
    if s == z.subs - 1:
        from_after = jnp.where(even(), first_pair[...], second_pair[...])
    else:
        from_after = before[s + 1]
    return from_before, from_after


def shares(z, s, chosen, faces, bases=None):
    m, half = z.modes, z.lanes // 2
    moved = lane_matrix(z, 0, s * z.width)
    out = []
    for side, at in ((0, s), (1, s + 2)):
        own = chosen[at * m : (at + 1) * m]
        below = jnp.concatenate([own, jnp.zeros((half - m, z.lanes), BF16)], axis=0)
        if bases is None:
            total = dot(faces[side], jnp.concatenate([moved[:half], below], axis=0))
        else:
            above = jnp.zeros((half, z.lanes), BF16)
            total = dot(faces[side], moved) + dot(bases[side], jnp.concatenate([above, below], axis=0))
        out.append(total)
    return out


def correction_side(z, chosen, s, share):
    m, half = z.modes, z.lanes // 2
    own = chosen[(s + 1) * m : (s + 2) * m]
    none = jnp.zeros((half - m, z.lanes), BF16)
    nil = jnp.zeros((half, z.lanes), BF16)
    image = jnp.concatenate([own, none, nil, share], axis=0)
    step = jnp.concatenate([nil, own, none, jnp.zeros((z.face, z.lanes), BF16)], axis=0)
    return jnp.concatenate([image, step], axis=1)


def scatter_matrix(z, rows_of, start, count):
    row = lax.broadcasted_iota(jnp.int32, (count, z.face), 0) + start
    return jnp.where(row == rows_of, 1.0, 0.0).astype(BF16)


def first_image_kernel(z, wait, *refs):
    inverse, stiffness = refs[: z.group], refs[z.group : 2 * z.group]
    pieces = refs[2 * z.group : 3 * z.group]
    loads, left_rows, right_rows = refs[3 * z.group : 3 * z.group + 3]
    load_rows, solved, image, before, after, first_pair, second_pair = refs[3 * z.group + 3 : 3 * z.group + 10]
    tall, basis_t, rounded, both, images = refs[3 * z.group + 10 :]
    join_basis(z, pieces, basis_t)
    packed = dot(loads[0], case_matrix(z, 0))
    for s in range(1, z.subs):
        packed = packed + dot(loads[s], case_matrix(z, s))
    load_rows[...] = packed.astype(BF16)

    def store_solved(k, start, value):
        solved[pl.ds(start, z.own), :] = value
        rounded[pl.ds(start, z.own), :] = value.astype(BF16)

    multiply(z, inverse, load_rows[...], store_solved, wait)
    solved_b = rounded[...]
    half = z.lanes // 2
    for s in range(z.subs):
        basis = jnp.transpose(basis_t[s].astype(F32)).astype(BF16)
        tall[s, :, half : half + z.modes] = basis
        tall[s, :, half + z.modes :] = jnp.zeros((z.rows, half - z.modes), BF16)
        both[s, :, : z.lanes] = solved_b
        both[s, :, z.lanes : z.lanes + z.modes] = basis
        both[s, :, z.lanes + z.modes :] = jnp.zeros((z.rows, z.lanes - z.modes), BF16)
    for k, piece in enumerate(stiffness):
        wait(z.group + k)
        start = piece_start(z, k, z.own)
        parts = [dot(piece[s], both[s]) for s in range(z.subs)]
        image[pl.ds(start, z.own), :] = select(z, [part[:, : z.lanes] for part in parts])
        for s in range(z.subs):
            images[s, pl.ds(start, z.own), :] = parts[s].astype(BF16)
    for s in range(z.subs):
        tall[s, :, :half] = images[s, :, z.lanes : z.lanes + half]
        picked = dot(pick_both(z, left_rows, right_rows, s), images[s]).astype(BF16)
        faces = dot(picked[:, : z.lanes], lane_matrix(z, s * z.width, 0))
        faces = (faces + dot(picked[:, z.lanes :], lane_matrix(z, 0, half, z.modes))).astype(BF16)
        before[s] = faces[: z.face]
        after[s] = faces[z.face :]
    store_faces(z, before, after, first_pair, second_pair)


def begin_kernel(z, *refs):
    load_rows, image, tall, basis_t, left_rows, right_rows, index, place = refs[:8]
    left_t, right_t, inner, start_modes, picks = refs[8:]
    left = (load_rows[...].astype(F32) - image[...]).astype(BF16)
    begun = []
    for s in range(z.subs):
        restricted = dot(basis_t[s], jnp.concatenate([left, tall[s]], axis=1))
        begun.append(restricted[:, : z.lanes])
        inner[s] = restricted[:, z.lanes : z.lanes + z.modes].astype(BF16)
        sides_t = dot_nt(basis_t[s], pick_both(z, left_rows, right_rows, s)).astype(BF16)
        left_t[s] = sides_t[:, : z.face]
        right_t[s] = sides_t[:, z.face :]
    start_modes[...] = select(z, begun)
    here = lax.axis_index("sub")
    device = lax.broadcasted_iota(jnp.int32, (z.n, z.lanes), 0)
    for t in range(z.subs + 2):
        if t == 0:
            s, owner = z.subs - 1, lax.rem(here + z.n - 1, z.n)
        elif t == z.subs + 1:
            s, owner = 0, lax.rem(here + 1, z.n)
        else:
            s, owner = t - 1, here
        row = jnp.sum(jnp.where(device == owner, index[s], 0.0), axis=0, keepdims=True)
        column = jnp.transpose(jnp.broadcast_to(row, (z.lanes, z.lanes)))[: z.modes, 0:1].astype(jnp.int32)
        for h in range(z.subs):
            hit = column == place[h : h + 1, :]
            picks[h, t * z.modes : (t + 1) * z.modes, :] = jnp.where(hit, 1.0, 0.0).astype(BF16)


def second_image_kernel(z, wait, *refs):
    inverse, stiffness = refs[: z.group], refs[z.group : 2 * z.group]
    rest = refs[2 * z.group :]
    load_rows, old_image, tall, old_solved, chosen = rest[:5]
    before, after, first_got, second_got, left_rows, right_rows = rest[5:11]
    first_pair, second_pair = rest[11:13]
    values = rest[13 : 13 + z.group]
    base, rounded, image, new_before, new_after = rest[13 + z.group :]
    steps, images = [], []
    for s in range(z.subs):
        faces = sides(z, before, after, first_got, second_got, s)
        both = [share.astype(BF16) for share in shares(z, s, chosen, faces)]
        left = jnp.concatenate([tall[s], scatter_matrix(z, left_rows[s : s + 1, :], 0, z.rows)], axis=1)
        total = dot(left, correction_side(z, chosen, s, both[0]))
        steps.append(total[:, z.lanes :])
        images.append(total[:, : z.lanes] + dot(scatter_matrix(z, right_rows[s : s + 1, :], 0, z.rows), both[1]))
    residual = (load_rows[...].astype(F32) - old_image[...] - select(z, images)).astype(BF16)
    base[...] = old_solved[...] + select(z, steps)

    def store_solved(k, start, value):
        value = value + base[pl.ds(start, z.own), :]
        values[k][0] = value
        rounded[pl.ds(start, z.own), :] = value.astype(BF16)

    multiply(z, inverse, residual, store_solved, wait)

    def store_image(k, start, value):
        place = pl.ds(start, z.own)
        values[k][1] = load_rows[place, :].astype(F32) - value
        image[place, :] = value.astype(BF16)

    multiply(z, stiffness, rounded[...], store_image, lambda k: wait(z.group + k))
    pick = jnp.concatenate([pick_both(z, left_rows, right_rows, s) for s in range(z.subs)], axis=0)
    picked = dot(pick, image[...]).astype(BF16)
    for s in range(z.subs):
        own = picked[2 * s * z.face : 2 * (s + 1) * z.face]
        faces = dot(own, lane_matrix(z, s * z.width, 0)).astype(BF16)
        new_before[s] = faces[: z.face]
        new_after[s] = faces[z.face :]
    first = halves(z, new_before[0])
    last = halves(z, new_after[z.subs - 1])
    first_pair[...] = jnp.where(even(), last, first)
    second_pair[...] = jnp.where(even(), first, last)
    inner = []
    for s in range(z.subs):
        move = lane_matrix(z, 0, s * z.width)
        total = jnp.zeros((z.rows, z.lanes), F32)
        if s > 0:
            share = dot(new_after[s - 1], move).astype(BF16)
            total = total + dot(scatter_matrix(z, left_rows[s : s + 1, :], 0, z.rows), share)
        if s < z.subs - 1:
            share = dot(new_before[s + 1], move).astype(BF16)
            total = total + dot(scatter_matrix(z, right_rows[s : s + 1, :], 0, z.rows), share)
        inner.append(total)
    base[...] = select(z, inner)
    for k in range(z.group):
        values[k][1] = values[k][1] - base[pl.ds(piece_start(z, k, z.own), z.own), :]


def digit_row(shape, row):
    return lax.broadcasted_iota(jnp.int32, shape, 1) == row


def coarse_rows(z, ordered_inverse, arrived, message):
    flat = arrived[:, : z.modes, :].reshape(z.columns, z.lanes)
    product = dot(ordered_inverse[...].reshape(z.subs * z.owned, z.columns), flat)
    rows = fold(z, select(z, [product[s * z.owned : (s + 1) * z.owned] for s in range(z.subs)]))
    packed = select(z, [rows[s * z.modes : (s + 1) * z.modes, :] for s in range(z.subs)]).astype(BF16)
    for k in range(z.n):
        message[k] = packed


def order_kernel(z, *refs):
    blocks = refs[: z.group]
    arrived, repeat, own_row, ordered_inverse, index, message = refs[z.group :]
    digits = arrived[:, z.modes :, :].astype(F32)
    pairs = []
    for s in range(z.subs):
        high = jnp.sum(jnp.where(digit_row(digits.shape, 2 * s), digits, 0.0), axis=1)
        low = jnp.sum(jnp.where(digit_row(digits.shape, 2 * s + 1), digits, 0.0), axis=1)
        index[s] = high * DIGIT + low
        pairs += [high.astype(BF16), low.astype(BF16)]
    spreads = dot(jnp.concatenate(pairs, axis=0), repeat[...])
    for s in range(z.subs):
        at_high, at_low = 2 * s * z.n, (2 * s + 1) * z.n
        spread = spreads[at_high : at_high + z.n] * DIGIT + spreads[at_low : at_low + z.n]
        places = jnp.sum(spread * own_row[...], axis=0, keepdims=True).astype(jnp.int32)
        for at in range(0, z.columns, 768):
            wide = min(768, z.columns - at)
            total = jnp.zeros((z.owned, wide), F32)
            for k, block in enumerate(blocks):
                inside = (places[:, at : at + wide] - piece_start(z, k, z.block)).astype(jnp.int16)
                for first in range(0, z.block, 768):
                    deep = min(768, z.block - first)
                    row = lax.broadcasted_iota(jnp.int16, (deep, wide), 0) + jnp.int16(first)
                    hot = jnp.where(row == inside, jnp.ones((), BF16), jnp.zeros((), BF16))
                    total = total + dot(block[:, first : first + deep], hot)
            ordered_inverse[s, :, at : at + wide] = total.astype(BF16)
    coarse_rows(z, ordered_inverse, arrived, message)


def coarse_kernel(z, arrived, ordered_inverse, message):
    coarse_rows(z, ordered_inverse, arrived, message)


def picked_rows(z, arrived, picks):
    flat = arrived[...].reshape(z.columns, z.lanes)
    return fold(z, select(z, [dot(picks[h], flat) for h in range(z.subs)])).astype(BF16)


def update_kernel(z, *refs):
    arrived, picks, start_modes, inner, left_t, right_t, before, after, first_got, second_got = refs[:10]
    chosen, message = refs[10:]
    rows = picked_rows(z, arrived, picks)
    chosen[...] = rows
    m = z.modes
    parts = []
    for s in range(z.subs):
        faces = sides(z, before, after, first_got, second_got, s)
        both = shares(z, s, rows, faces)
        total = dot(inner[s], rows[(s + 1) * m : (s + 2) * m])
        parts.append(total + dot(left_t[s], both[0].astype(BF16)) + dot(right_t[s], both[1].astype(BF16)))
    modes = (start_modes[...] - select(z, parts)).astype(BF16)
    for k in range(z.n):
        message[k] = modes


def base_kernel(z, *refs):
    *values, out = refs
    for at in range(2):
        for s in range(z.subs):
            total = jnp.zeros((z.own, z.lanes), F32)
            for k, value in enumerate(values):
                place = lax.rem(lax.axis_index(GROUP) + k, z.group)
                turn = lax.rem((place - s + z.subs * z.group) * z.width, z.lanes)
                turned = pltpu.roll(value[at], turn, 1)
                total = jnp.where(lane_mask(z, place, turned.shape), turned, total)
            out[at, s] = total


def last_kernel(z, wait, *refs):
    arrived, firsts, seconds = refs[: z.group], refs[z.group : 2 * z.group], refs[2 * z.group : 3 * z.group]
    picks, face_before, face_after, face_first, face_second, left_rows, right_rows = refs[3 * z.group : 3 * z.group + 7]
    tall, base, second_pass, final_residual = refs[3 * z.group + 7 :]
    start = piece_start(z, 0, z.own)
    m, half = z.modes, z.lanes // 2
    places = [lax.rem(lax.axis_index(GROUP) + k, z.group) * z.width for k in range(z.group)]

    def all_cases(parts, source=0):
        return sum(dot(part, lane_matrix(z, source, place)) for part, place in zip(parts, places))

    def whole_face(parts):
        return jnp.concatenate([all_cases(parts), all_cases(parts, half)], axis=0)

    modes = all_cases([picked_rows(z, piece, picks) for piece in arrived]).astype(BF16)
    swaps = list(zip(firsts, seconds))
    outer_before = whole_face([jnp.where(even(), b[...], a[...]) for a, b in swaps])
    outer_after = whole_face([jnp.where(even(), a[...], b[...]) for a, b in swaps])
    wait(3 * z.group + 7)
    totals = []
    for s in range(z.subs):
        faces = sides(z, face_before, face_after, face_first, face_second, s)
        both = []
        for side, at in ((0, s), (1, s + 2)):
            above = jnp.zeros((half, z.lanes), BF16)
            below = jnp.zeros((half - m, z.lanes), BF16)
            both.append(dot(faces[side], jnp.concatenate([above, modes[at * m : (at + 1) * m], below], axis=0)))
        if s == 0:
            both[0] = both[0] + outer_before
        if s == z.subs - 1:
            both[1] = both[1] + outer_after
        scatter = scatter_matrix(z, left_rows[s : s + 1, :], start, z.own)
        wide = jnp.concatenate([tall[s, pl.ds(start, z.own), :], scatter], axis=1)
        total = dot(wide, correction_side(z, modes, s, both[0].astype(BF16)))
        image = dot(scatter_matrix(z, right_rows[s : s + 1, :], start, z.own), both[1].astype(BF16))
        totals.append((total[:, z.lanes :], total[:, : z.lanes] + image))
    wait(3 * z.group + 8)
    for s, (step, image) in enumerate(totals):
        second_pass[s] = (base[0, s] + step)[:, : z.cases]
        final_residual[s] = (base[1, s] - image)[:, : z.cases]


def call(kernel, outs, operands, flops, scratch=(), late=(), loose=(), name=None):
    moved = sum(int(np.prod(x.shape)) * x.dtype.itemsize for x in (*operands, *outs))
    n_in, n_out = len(operands), len(outs)

    def whole(*refs):
        hbm, refs = refs[: n_in + n_out], refs[n_in + n_out :]
        vmem, refs = refs[: n_in + n_out], refs[n_in + n_out :]
        in_sems, out_sems, *rest = refs
        arriving = [pltpu.make_async_copy(hbm[i], vmem[i], in_sems.at[i]) for i in range(n_in)]
        for i in sorted(range(n_in), key=lambda i: i in late):
            arriving[i].start()
        for i, copy in enumerate(arriving):
            if i not in late:
                copy.wait()
        extra = [lambda i: arriving[i].wait()] if late else []
        kernel(*extra, *vmem, *rest)
        leaving = [pltpu.make_async_copy(vmem[n_in + i], hbm[n_in + i], out_sems.at[i]) for i in range(n_out)]
        for copy in leaving:
            copy.start()
        for copy in leaving:
            copy.wait()

    hbm_spec = pl.BlockSpec(memory_space=pltpu.HBM)
    any_spec = pl.BlockSpec(memory_space=pl.ANY)
    placed = [
        x if i in loose else pltpu.with_memory_space_constraint(x, pltpu.HBM) for i, x in enumerate(operands)
    ]
    return pl.pallas_call(
        whole,
        out_shape=[pltpu.HBM(o.shape, o.dtype) for o in outs],
        in_specs=[any_spec if i in loose else hbm_spec for i in range(n_in)],
        out_specs=[hbm_spec] * n_out,
        scratch_shapes=[
            *[pltpu.VMEM(x.shape, x.dtype) for x in (*operands, *outs)],
            pltpu.SemaphoreType.DMA((n_in,)),
            pltpu.SemaphoreType.DMA((n_out,)),
            *scratch,
        ],
        compiler_params=pltpu.CompilerParams(vmem_limit_bytes=VMEM_BYTES),
        cost_estimate=pl.CostEstimate(flops=flops, bytes_accessed=moved, transcendentals=0),
        name=name,
    )(*placed)


def shape(dims, dtype):
    return jax.ShapeDtypeStruct(dims, dtype)


def pieces_of(block, group):
    out = [block]
    for k in range(1, group):
        out.append(lax.ppermute(block, GROUP, [((g + k) % group, g) for g in range(group)]))
    return out


def body(loads, stiffness, local_inverse, coarse_basis, coarse_inverse, coarse_index, left_rows, right_rows):
    z = Sizes(loads, stiffness, coarse_basis, coarse_inverse, left_rows)
    n, group, subs, rows, lanes, modes, face = z.n, z.group, z.subs, z.rows, z.lanes, z.modes, z.face
    basis_pieces = pieces_of(jnp.swapaxes(coarse_basis, 1, 2), group)
    basis_pieces, coarse_inverse, local_inverse, stiffness = lax.optimization_barrier(
        (basis_pieces, coarse_inverse, local_inverse, stiffness)
    )
    inverse_columns = pieces_of(coarse_inverse, group)
    column = np.arange(z.columns)
    repeat = jnp.asarray(np.arange(lanes)[:, None] == column[None, :] % modes, BF16)
    own_row = jnp.asarray(np.arange(n)[:, None] == column[None, :] // modes, F32)
    place = jnp.asarray(
        (column // modes * z.owned + column % modes)[None, :] + np.arange(subs)[:, None] * modes, jnp.int32
    )
    packed_f = shape((rows, lanes), F32)
    packed_b = shape((rows, lanes), BF16)
    copies = shape((n, modes, lanes), BF16)
    tall = shape((subs, rows, lanes), BF16)
    spread = functools.partial(lax.all_to_all, axis_name="sub", split_axis=0, concat_axis=0)
    first_pairs = [(i, i + 1 if i % 2 == 0 else i - 1) for i in range(n)]
    second_pairs = [(i, (i + (1 if i % 2 else -1)) % n) for i in range(n)]
    work = 4 * subs * rows * rows * lanes

    (message,) = call(
        functools.partial(open_kernel, z),
        [shape((n, modes + DIGIT_ROWS, lanes), BF16)],
        [*basis_pieces, loads, coarse_index],
        4 * rows * lanes * lanes,
        [pltpu.VMEM((DIGIT_ROWS, lanes), F32), pltpu.VMEM((subs, modes, rows), BF16)],
        loose=range(1, group),
        name="open",
    )
    inverse_pieces = pieces_of(local_inverse, group)
    stiffness_pieces = pieces_of(stiffness, group)
    restricted = spread(message)
    arrivals = [*range(1, group), *range(group + 1, 2 * group)]
    faces = shape((subs, face, lanes), BF16)
    outer = shape((face, lanes), BF16)
    (
        load_rows, solved, image, before, after, first_pair, second_pair, tall, basis_t
    ) = call(
        functools.partial(first_image_kernel, z),
        [
            packed_b, packed_f, packed_f, faces, faces, outer, outer, tall, shape((subs, modes, rows), BF16),
        ],
        [*inverse_pieces, *stiffness_pieces, *basis_pieces, loads, left_rows, right_rows],
        work,
        [
            pltpu.VMEM((rows, lanes), BF16),
            pltpu.VMEM((subs, rows, 2 * lanes), BF16), pltpu.VMEM((subs, rows, 2 * lanes), BF16),
        ],
        late=range(2 * group),
        loose=[*arrivals, *range(2 * group + 1, 3 * group)],
        name="first_image",
    )
    first_got = lax.ppermute(first_pair, "sub", first_pairs)
    restricted, first_pair = lax.optimization_barrier((restricted, first_pair))
    near = (subs + 2) * modes
    ordered_inverse, index, message = call(
        functools.partial(order_kernel, z),
        [shape((subs, z.owned, z.columns), BF16), shape((subs, n, lanes), F32), copies],
        [*inverse_columns, restricted, repeat, own_row],
        2 * z.owned * z.total * z.total,
        loose=range(1, group + 1),
        name="order",
    )
    coarse = spread(message)
    second_got = lax.ppermute(second_pair, "sub", second_pairs)
    side = shape((subs, modes, face), BF16)
    left_t, right_t, inner, start_modes, picks = call(
        functools.partial(begin_kernel, z),
        [
            side, side, shape((subs, modes, modes), BF16), shape((modes, lanes), F32),
            shape((subs, near, z.columns), BF16),
        ],
        [load_rows, image, tall, basis_t, left_rows, right_rows, index, place],
        work // 16,
        name="begin",
    )
    chosen, message = call(
        functools.partial(update_kernel, z),
        [shape((near, lanes), BF16), copies],
        [coarse, picks, start_modes, inner, left_t, right_t, before, after, first_got, second_got],
        work // 64,
        loose=[0, 8, 9],
        name="update",
    )
    restricted = spread(message)

    bases = [before, after, first_got, second_got]
    half_face = shape((face // 2, lanes), BF16)
    first_pair, second_pair, *values = call(
        functools.partial(second_image_kernel, z),
        [half_face, half_face, *[shape((2, z.own, lanes), F32)] * group],
        [
            *inverse_pieces, *stiffness_pieces, load_rows, image, tall, solved, chosen,
            *bases, left_rows, right_rows,
        ],
        work,
        [
            pltpu.VMEM((rows, lanes), F32), pltpu.VMEM((rows, lanes), BF16), pltpu.VMEM((rows, lanes), BF16),
            pltpu.VMEM((subs, face, lanes), BF16), pltpu.VMEM((subs, face, lanes), BF16),
        ],
        late=range(2 * group),
        loose=[*arrivals, 2 * group + 7, 2 * group + 8],
        name="second_image",
    )
    first_got = lax.ppermute(first_pair, "sub", first_pairs)
    restricted, first_pair = lax.optimization_barrier((restricted, first_pair))
    (message,) = call(
        functools.partial(coarse_kernel, z),
        [copies],
        [restricted, ordered_inverse],
        work // 64,
        loose=[0],
        name="coarse",
    )
    coarse = spread(message)
    second_got = lax.ppermute(second_pair, "sub", second_pairs)
    swapped = [values[0]]
    for k in range(1, group):
        swapped.append(lax.ppermute(values[k], GROUP, [(g, (g + k) % group) for g in range(group)]))
    swapped = [swapped[(group - k) % group] for k in range(group)]
    (base,) = call(
        functools.partial(base_kernel, z),
        [shape((2, subs, z.own, lanes), F32)],
        swapped,
        work // 64,
        loose=range(1, group),
        name="base",
    )
    coarse, base, first_got, second_got = lax.optimization_barrier((coarse, base, first_got, second_got))
    out = shape((subs, z.own, z.cases), F32)
    return tuple(
        call(
            functools.partial(last_kernel, z),
            [out, out],
            [
                *pieces_of(coarse, group), *pieces_of(first_got, group), *pieces_of(second_got, group),
                picks, *bases, left_rows, right_rows, tall, base,
            ],
            work // 8,
            late=[3 * group + 7, 3 * group + 8],
            loose=[*range(3 * group), 3 * group + 3, 3 * group + 4],
            name="last",
        )
    )


def solution(mesh):
    return jax.shard_map(
        body,
        mesh=mesh,
        in_specs=(
            P("sub", None, None),
            P("sub", GROUP, None),
            P("sub", GROUP, None),
            P("sub", GROUP, None),
            P("sub", GROUP),
            P("sub", None),
            P("sub", None),
            P("sub", None),
        ),
        out_specs=(P("sub", GROUP, None), P("sub", GROUP, None)),
        check_vma=False,
    )
```
